32 devices in a mesh: dp: 8 (over z, x), mp: 4 (over y, core).
Axes of the slice: x: 2, y: 2, z: 4, core: 2. Of those that a mesh axis runs over, the one named last changes fastest.
Arguments:
- tokens: bfloat16 [8192, 1024], P(('dp', 'mp')), may hold values from -6 to 6
- segment_ids: int32 [32, 256], P('dp'), may hold values from 0 to 7, as said below
- gsd_index: int32 [32, 256], P('dp'), may hold values from 0 to 7, as said below
- enc_qkv: bfloat16 [3, 1024, 1024], P(None, None, 'mp'), may hold values from -0.1875 to 0.1875
- enc_qv_bias: float32 [2, 1024], P(None, 'mp'), may hold values from -1.75 to 1.75
- enc_out_proj: bfloat16 [1024, 1024], P('mp'), may hold values from -0.5 to 0.5
- enc_up: bfloat16 [1024, 4096], P(None, 'mp'), may hold values from -0.1875 to 0.1875
- enc_up_bias: float32 [4096], P('mp'), may hold values from -1.75 to 1.75
- enc_down: bfloat16 [4096, 1024], P('mp'), may hold values from -0.125 to 0.125
- enc_out_bias: float32 [2, 1024], replicated, may hold values from -1.75 to 1.75
- enc_gain: float32 [2, 1024], replicated, may hold values from 0.5 to 1.5
- enc_norm_bias: float32 [2, 1024], replicated, may hold values from -1.75 to 1.75
- embed_weight: bfloat16 [1024, 512], P(None, 'mp'), may hold values from -0.1875 to 0.1875
- embed_bias: float32 [512], replicated, may hold values from -1.75 to 1.75
- dec_qkv: bfloat16 [3, 512, 512], P(None, None, 'mp'), may hold values from -0.25 to 0.25
- dec_qv_bias: float32 [2, 512], P(None, 'mp'), may hold values from -1.75 to 1.75
- dec_out_proj: bfloat16 [512, 512], P('mp'), may hold values from -0.75 to 0.75
- dec_up: bfloat16 [512, 2048], P(None, 'mp'), may hold values from -0.25 to 0.25
- dec_up_bias: float32 [2048], P('mp'), may hold values from -1.75 to 1.75
- dec_down: bfloat16 [2048, 512], P('mp'), may hold values from -0.1875 to 0.1875
- dec_out_bias: float32 [2, 512], replicated, may hold values from -1.75 to 1.75
- dec_gain: float32 [2, 512], replicated, may hold values from 0.5 to 1.5
- dec_norm_bias: float32 [2, 512], replicated, may hold values from -1.75 to 1.75
- cotangent: bfloat16 [8192, 512], P(('dp', 'mp')), may hold values from -6 to 6
Outputs:
- output: float32 [8192, 512], P(('dp', 'mp'))
- grad_tokens: float32 [8192, 1024], P(('dp', 'mp'))
- grad_enc_qkv: float32 [3, 1024, 1024], P(None, None, 'mp')
- grad_enc_qv_bias: float32 [2, 1024], P(None, 'mp')
- grad_enc_out_proj: float32 [1024, 1024], P('mp')
- grad_enc_up: float32 [1024, 4096], P(None, 'mp')
- grad_enc_up_bias: float32 [4096], P('mp')
- grad_enc_down: float32 [4096, 1024], P('mp')
- grad_enc_out_bias: float32 [2, 1024], replicated
- grad_enc_gain: float32 [2, 1024], replicated
- grad_enc_norm_bias: float32 [2, 1024], replicated
- grad_embed_weight: float32 [1024, 512], P(None, 'mp')
- grad_embed_bias: float32 [512], replicated
- grad_dec_qkv: float32 [3, 512, 512], P(None, None, 'mp')
- grad_dec_qv_bias: float32 [2, 512], P(None, 'mp')
- grad_dec_out_proj: float32 [512, 512], P('mp')
- grad_dec_up: float32 [512, 2048], P(None, 'mp')
- grad_dec_up_bias: float32 [2048], P('mp')
- grad_dec_down: float32 [2048, 512], P('mp')
- grad_dec_out_bias: float32 [2, 512], replicated
- grad_dec_gain: float32 [2, 512], replicated
- grad_dec_norm_bias: float32 [2, 512], replicated
The draws below stay inside these ranges and needn't reach their ends.
Inputs may be any that keep to these rules, and one draw needn't show every extreme that they name: `segment_ids`: in each row, images take consecutive positions numbered 1, 2, ... in order, each of 33 to 64 patches; 0 marks the padding after the last image. Some row holds the most images that fit. `gsd_index`: constant over the patches of one image; 0 on padding.
All inputs are finite; a program needn't handle non-finite values.
Results may differ from the reference program's by a relative error of at most 0.019.
Values may be sent and summed in bfloat16 or wider, within the bound.
No kernel may reach another device: no remote copies, remote signals or barrier semaphores. Data moves between devices by JAX's collectives and lax.ppermute only.
A program may use at most 128 MiB of HBM per device.

```python
import jax
import jax.numpy as jnp
from jax import lax

D = 1024
HEADS = 16
FF = 4096
DD = 512
DHEADS = 16
DFF = 2048
ROW_LEN = 256
ROWS = 32
TOKENS = 8192


def packing(key):
    lengths = jax.random.randint(key, (ROWS, 8), ROW_LEN // 8 + 1, ROW_LEN // 4 + 1)
    chosen_row = jax.random.randint(jax.random.fold_in(key, 7), (), 0, ROWS)
    row_numbers = jnp.arange(ROWS, dtype=jnp.int32)
    lengths = jnp.where(row_numbers[:, None] == chosen_row, ROW_LEN // 8 + 1, lengths)
    ends = jnp.cumsum(lengths, axis=1)
    fitted = jnp.max(jnp.where(ends <= ROW_LEN, ends, 0), axis=1)
    positions = jnp.arange(ROW_LEN, dtype=jnp.int32)
    image_number = 1 + jnp.sum(jnp.where(ends[:, None, :] <= positions[None, :, None], 1, 0), axis=-1)
    return jnp.where(positions[None, :] < fitted[:, None], image_number, 0).astype(jnp.int32)


def draw_segment_ids(key, part):
    segments = packing(key)
    return segments


def draw_gsd_index(key, part):
    segments = packing(key)
    key = jax.random.fold_in(key, 2)
    table = jax.random.randint(key, (ROWS, 8), 0, 8)
    numbers = jnp.arange(1, 9, dtype=jnp.int32)
    picked = jnp.where(segments[:, :, None] == numbers[None, None, :], table[:, None, :], 0)
    return jnp.sum(picked, axis=-1).astype(jnp.int32)


def block_scale(stream_key, extent, cuts, low, largest):
    def one(dim, parts):
        heights = jax.random.uniform(jax.random.fold_in(jax.random.fold_in(stream_key, 6), dim), (parts,), jnp.float32, low / len(cuts), largest / len(cuts))
        return jnp.repeat(jnp.exp(heights), extent[dim] // parts).reshape((-1,) + (1,) * (len(extent) - dim - 1))

    loudness = one(*cuts[0])
    for cut in cuts[1:]:
        loudness = loudness * one(*cut)
    return loudness


def scatter_about(rng, dims, spread, bound, shards=(), kind=jnp.bfloat16):
    gain = block_scale(rng, dims, shards, -0.22, 0.18) if shards else 1.0
    drawn = jax.random.normal(rng, dims, jnp.float32) * spread * gain
    return jnp.minimum(jnp.maximum(drawn, -bound), bound).astype(kind)


def setup_inputs(seed: int = 0) -> dict:
    keys = jax.random.split(jax.random.key(seed), 25)
    tokens = scatter_about(keys[0], (TOKENS, D), 1.0, 6.0, ((0, 32),))
    segment_ids = draw_segment_ids(jax.random.fold_in(keys[24], 71), 0)
    gsd_index = draw_gsd_index(jax.random.fold_in(keys[24], 71), 0)
    enc_qkv = scatter_about(keys[3], (3, D, D), D ** -0.5, 0.1875, ((2, 4),))
    enc_qv_bias = scatter_about(keys[4], (2, D), 0.3, 1.75, ((1, 4),), jnp.float32)
    enc_out_proj = scatter_about(keys[5], (D, D), (D // 8) ** -0.5, 0.5, ((0, 4),))
    enc_up = scatter_about(keys[6], (D, FF), D ** -0.5, 0.1875, ((1, 4),))
    enc_up_bias = scatter_about(keys[7], (FF,), 0.3, 1.75, ((0, 4),), jnp.float32)
    enc_down = scatter_about(keys[8], (FF, D), (FF // 2) ** -0.5, 0.125, ((0, 4),))
    enc_out_bias = scatter_about(keys[9], (2, D), 0.3, 1.75, (), jnp.float32)
    enc_gain = jnp.clip(1.0 + 0.1 * jax.random.normal(keys[10], (2, D), jnp.float32), 0.5, 1.5)
    enc_norm_bias = scatter_about(keys[11], (2, D), 0.3, 1.75, (), jnp.float32)
    embed_weight = scatter_about(keys[12], (D, DD), D ** -0.5, 0.1875, ((1, 4),))
    embed_bias = scatter_about(keys[13], (DD,), 0.3, 1.75, (), jnp.float32)
    dec_qkv = scatter_about(keys[14], (3, DD, DD), DD ** -0.5, 0.25, ((2, 4),))
    dec_qv_bias = scatter_about(keys[15], (2, DD), 0.3, 1.75, ((1, 4),), jnp.float32)
    dec_out_proj = scatter_about(keys[16], (DD, DD), (DD // 8) ** -0.5, 0.75, ((0, 4),))
    dec_up = scatter_about(keys[17], (DD, DFF), DD ** -0.5, 0.25, ((1, 4),))
    dec_up_bias = scatter_about(keys[18], (DFF,), 0.3, 1.75, ((0, 4),), jnp.float32)
    dec_down = scatter_about(keys[19], (DFF, DD), (DFF // 2) ** -0.5, 0.1875, ((0, 4),))
    dec_out_bias = scatter_about(keys[20], (2, DD), 0.3, 1.75, (), jnp.float32)
    dec_gain = jnp.clip(1.0 + 0.1 * jax.random.normal(keys[21], (2, DD), jnp.float32), 0.5, 1.5)
    dec_norm_bias = scatter_about(keys[22], (2, DD), 0.3, 1.75, (), jnp.float32)
    cotangent = scatter_about(keys[23], (TOKENS, DD), 1.0, 6.0, ((0, 32),))
    return dict(tokens=tokens, segment_ids=segment_ids, gsd_index=gsd_index, enc_qkv=enc_qkv, enc_qv_bias=enc_qv_bias, enc_out_proj=enc_out_proj, enc_up=enc_up, enc_up_bias=enc_up_bias, enc_down=enc_down, enc_out_bias=enc_out_bias, enc_gain=enc_gain, enc_norm_bias=enc_norm_bias, embed_weight=embed_weight, embed_bias=embed_bias, dec_qkv=dec_qkv, dec_qv_bias=dec_qv_bias, dec_out_proj=dec_out_proj, dec_up=dec_up, dec_up_bias=dec_up_bias, dec_down=dec_down, dec_out_bias=dec_out_bias, dec_gain=dec_gain, dec_norm_bias=dec_norm_bias, cotangent=cotangent)


@jax.custom_vjp
def low(v):
    return lax.optimization_barrier(v.astype(jnp.bfloat16)).astype(jnp.float32)

@jax.custom_vjp
def low_back(v):
    return v

def low_keep(v):
    return (low(v), None)

def low_pass(kept, grad):
    return (grad,)

def back_keep(v):
    return (v, None)

def back_low(kept, grad):
    return (low(grad),)
low.defvjp(low_keep, low_pass)
low_back.defvjp(back_keep, back_low)
norm_eps = 1e-06

def layer_norm(values, norm_gain, norm_shift):
    average = lax.optimization_barrier(jnp.mean(values, axis=-1, keepdims=True))
    centred = values - average
    variance = lax.optimization_barrier(jnp.mean(centred * centred, axis=-1, keepdims=True))
    return centred * lax.rsqrt(variance + norm_eps) * norm_gain + norm_shift

def scaled_places(segment_ids, gsd_index):
    length = segment_ids.shape[1]
    same_image = segment_ids[:, :, None] == segment_ids[:, None, :]
    positions = jnp.arange(length, dtype=jnp.int32)
    before = positions[None, :] < positions[:, None]
    ranks = lax.optimization_barrier(jnp.sum(jnp.where(same_image & before[None], 1, 0), axis=-1)).astype(jnp.float32)
    gsd_ratio = 0.5 + 0.25 * gsd_index.astype(jnp.float32)
    return (ranks * gsd_ratio).reshape(-1)

def sin_cos(scaled, model_width):
    half_width = model_width // 2
    frequency = jnp.power(10000.0, -jnp.arange(half_width, dtype=jnp.float32) / half_width)
    angles = scaled[:, None] * frequency[None, :]
    return jnp.concatenate([jnp.sin(angles), jnp.cos(angles)], axis=1)

def attend_row(pieces):
    query_heads, key_heads, value_heads, row_segments = pieces
    scale_factor = query_heads.shape[-1] ** (-0.5)
    scores = jnp.einsum('qhe,khe->hqk', query_heads, key_heads, precision=lax.Precision.HIGHEST) * scale_factor
    scores = low_back(scores)
    same_image = row_segments[:, None] == row_segments[None, :]
    scores = jnp.where(same_image[None], scores, -1000000000.0)
    soft_low = low(jax.nn.softmax(scores, axis=-1))
    return jnp.einsum('hqk,khe->qhe', soft_low, value_heads, precision=lax.Precision.HIGHEST)

def block(stream, weights, segment_ids, head_count):
    qkv, qv_bias, out_proj, up_proj, up_bias, down_proj, out_bias, norm_gain, norm_shift = weights
    token_count, model_width = stream.shape
    row_count, length = segment_ids.shape
    head_size = model_width // head_count
    normed = low(layer_norm(stream, norm_gain[0], norm_shift[0]))
    projected = low_back(jnp.einsum('tw,cwk->ctk', normed, qkv, precision=lax.Precision.HIGHEST))
    queries = low(projected[0] + qv_bias[0])
    key_rows = low(projected[1])
    values = low(projected[2] + qv_bias[1])
    split_shape = (row_count, length, head_count, head_size)
    mixture = lax.map(jax.checkpoint(attend_row), (queries.reshape(split_shape), key_rows.reshape(split_shape), values.reshape(split_shape), segment_ids))
    mixture = low(low_back(mixture.reshape(token_count, model_width)))
    middle = stream + low_back(jnp.dot(mixture, out_proj, precision=lax.Precision.HIGHEST)) + out_bias[0]
    normed_two = low(layer_norm(middle, norm_gain[1], norm_shift[1]))
    hidden_pre = low_back(jnp.dot(normed_two, up_proj, precision=lax.Precision.HIGHEST)) + up_bias
    hidden = low(jax.nn.gelu(hidden_pre))
    return middle + low_back(jnp.dot(hidden, down_proj, precision=lax.Precision.HIGHEST)) + out_bias[1]

def reference(tokens, segment_ids, gsd_index, enc_qkv, enc_qv_bias, enc_out_proj, enc_up, enc_up_bias, enc_down, enc_out_bias, enc_gain, enc_norm_bias, embed_weight, embed_bias, dec_qkv, dec_qv_bias, dec_out_proj, dec_up, dec_up_bias, dec_down, dec_out_bias, dec_gain, dec_norm_bias, cotangent):
    encoder = tuple((item.astype(jnp.float32) for item in (enc_qkv, enc_qv_bias, enc_out_proj, enc_up, enc_up_bias, enc_down, enc_out_bias, enc_gain, enc_norm_bias)))
    decoder = tuple((item.astype(jnp.float32) for item in (dec_qkv, dec_qv_bias, dec_out_proj, dec_up, dec_up_bias, dec_down, dec_out_bias, dec_gain, dec_norm_bias)))
    scaled = scaled_places(segment_ids, gsd_index)

    def forward(inputs, enc_weights, embed_matrix, embed_shift, dec_weights):
        stream = inputs + sin_cos(scaled, inputs.shape[1])
        encoded = block(stream, enc_weights, segment_ids, HEADS)
        embedded = low_back(jnp.dot(low(encoded), embed_matrix, precision=lax.Precision.HIGHEST)) + embed_shift
        dec_stream = embedded + sin_cos(scaled, embedded.shape[1])
        return block(dec_stream, dec_weights, segment_ids, DHEADS)
    output, pull_back = jax.vjp(forward, tokens.astype(jnp.float32), encoder, embed_weight.astype(jnp.float32), embed_bias.astype(jnp.float32), decoder)
    grad_tokens, enc_grads, grad_embed, grad_embed_bias, dec_grads = pull_back(cotangent.astype(jnp.float32))
    return (output, grad_tokens, enc_grads[0], enc_grads[1], enc_grads[2], enc_grads[3], enc_grads[4], enc_grads[5], enc_grads[6], enc_grads[7], enc_grads[8], grad_embed, grad_embed_bias, dec_grads[0], dec_grads[1], dec_grads[2], dec_grads[3], dec_grads[4], dec_grads[5], dec_grads[6], dec_grads[7], dec_grads[8])
```

```python
import jax
import jax.numpy as jnp
from jax import lax
from jax.sharding import PartitionSpec as P

HEADS = 16
DHEADS = 16
norm_eps = 1e-06
f32 = jnp.float32
bf16 = jnp.bfloat16


def swap(value, axis, mask):
    size = lax.axis_size(axis)
    return lax.ppermute(value, axis, [(i, i ^ mask) for i in range(size)])


def gather_blocks(block):
    far = swap(block, "mp", 2)
    near = swap(block, "mp", 1)
    far_near = swap(far, "mp", 1)
    return [block, near, far, far_near]


def scatter_blocks(parts):
    low = [part.astype(bf16) for part in parts]
    pair_far = low[2].astype(f32) + swap(low[3], "mp", 1).astype(f32)
    far = swap(pair_far.astype(bf16), "mp", 2)
    near = swap(low[1], "mp", 1)
    return parts[0].astype(f32) + near.astype(f32) + far.astype(f32)


def gather_rows(block):
    return jnp.concatenate(gather_blocks(block), axis=0)


def scatter_rows(partial):
    rows = partial.shape[0] // 4
    return scatter_blocks([partial[j * rows : (j + 1) * rows] for j in range(4)])


def sum_over_dp(value, order=None):
    size = lax.axis_size("dp")
    bits = []
    while 2 ** len(bits) < size:
        bits.append(2 ** len(bits))
    bits = bits if order is None else [bits[i] for i in order if i < len(bits)]
    me = lax.axis_index("dp")
    held = value.astype(bf16)
    for bit in bits:
        mine = (me & bit) != 0
        half = held.shape[0] // 2
        here = jnp.where(mine, half, 0)
        there = jnp.where(mine, 0, half)
        sent = swap(lax.dynamic_slice_in_dim(held, there, half, 0), "dp", bit)
        kept = lax.dynamic_slice_in_dim(held, here, half, 0)
        held = (kept.astype(f32) + sent.astype(f32)).astype(bf16)
    for bit in reversed(bits):
        mine = (me & bit) != 0
        other = swap(held, "dp", bit)
        held = jnp.where(
            mine,
            jnp.concatenate([other, held], axis=0),
            jnp.concatenate([held, other], axis=0),
        )
    return held.astype(f32)


def sum_over_all(vector):
    for axis in ("mp", "dp"):
        bit = 1
        while bit < lax.axis_size(axis):
            vector = vector + swap(vector, axis, bit)
            bit *= 2
    return vector


def norm_apply(values, norm_gain, norm_shift):
    average = jnp.mean(values, axis=-1, keepdims=True)
    centred = values - average
    variance = jnp.mean(centred * centred, axis=-1, keepdims=True)
    return centred * lax.rsqrt(variance + norm_eps) * norm_gain + norm_shift


def scaled_places(segment_ids, gsd_index):
    length = segment_ids.shape[1]
    same_image = segment_ids[:, :, None] == segment_ids[:, None, :]
    positions = jnp.arange(length, dtype=jnp.int32)
    before = positions[None, :] < positions[:, None]
    ranks = jnp.sum(jnp.where(same_image & before[None], 1, 0), axis=-1).astype(f32)
    gsd_ratio = 0.5 + 0.25 * gsd_index.astype(f32)
    return (ranks * gsd_ratio).reshape(-1)


def sin_cos(scaled, model_width):
    half_width = model_width // 2
    frequency = jnp.power(10000.0, -jnp.arange(half_width, dtype=f32) / half_width)
    angles = scaled[:, None] * frequency[None, :]
    return jnp.concatenate([jnp.sin(angles), jnp.cos(angles)], axis=1)


def split_heads(matrix, same_image, head_size):
    row_count, length = (same_image.shape[0], same_image.shape[1])
    return matrix.reshape(row_count, length, matrix.shape[1] // head_size, head_size)


def attention_scores(query_heads, key_heads, same_image, head_size):
    scores = jnp.einsum(
        "rqhe,rkhe->rhqk", query_heads, key_heads, preferred_element_type=f32
    ) * head_size ** (-0.5)
    return jnp.where(same_image[:, None], scores, -1000000000.0)


def attention_forward(queries, key_rows, values, same_image, head_size):
    query_heads = split_heads(queries, same_image, head_size)
    key_heads = split_heads(key_rows, same_image, head_size)
    value_heads = split_heads(values, same_image, head_size)
    scores = attention_scores(query_heads, key_heads, same_image, head_size)
    highest = jnp.max(scores, axis=-1, keepdims=True)
    log_total = highest + jnp.log(jnp.sum(jnp.exp(scores - highest), axis=-1, keepdims=True))
    soft_low = jnp.exp(scores - log_total).astype(bf16)
    mixture = jnp.einsum("rhqk,rkhe->rqhe", soft_low, value_heads, preferred_element_type=f32)
    return (mixture.reshape(queries.shape).astype(bf16), log_total)


def attention_backward(queries, key_rows, values, log_total, grad_mixture, same_image, head_size):
    query_heads = split_heads(queries, same_image, head_size)
    key_heads = split_heads(key_rows, same_image, head_size)
    value_heads = split_heads(values, same_image, head_size)
    grad_heads = split_heads(grad_mixture, same_image, head_size)
    scores = attention_scores(query_heads, key_heads, same_image, head_size)
    soft_full = jnp.exp(scores - log_total)
    soft_low = soft_full.astype(bf16)
    grad_values = jnp.einsum("rhqk,rqhe->rkhe", soft_low, grad_heads, preferred_element_type=f32)
    grad_probs = jnp.einsum("rqhe,rkhe->rhqk", grad_heads, value_heads, preferred_element_type=f32)
    row_delta = jnp.sum(grad_probs * soft_full, axis=-1, keepdims=True)
    grad_scores = (soft_full * (grad_probs - row_delta)).astype(bf16)
    scale_factor = head_size ** (-0.5)
    grad_queries = (
        jnp.einsum("rhqk,rkhe->rqhe", grad_scores, key_heads, preferred_element_type=f32)
        * scale_factor
    )
    grad_keys = (
        jnp.einsum("rhqk,rqhe->rkhe", grad_scores, query_heads, preferred_element_type=f32)
        * scale_factor
    )
    flat_shape = queries.shape
    return (
        grad_queries.reshape(flat_shape),
        grad_keys.reshape(flat_shape),
        grad_values.reshape(flat_shape),
    )


def block_forward(stream, weights, same_image, head_size, gather, scatter):
    qkv, qv_bias, out_proj, up_proj, up_bias, down_proj, out_bias, norm_gain, norm_shift = weights
    normed = norm_apply(stream, norm_gain[0], norm_shift[0]).astype(bf16)
    inputs = gather(normed)
    queries, key_rows, values = [
        jnp.dot(inputs, qkv[c], preferred_element_type=f32) for c in range(3)
    ]
    queries = (queries + qv_bias[0]).astype(bf16)
    key_rows = key_rows.astype(bf16)
    values = (values + qv_bias[1]).astype(bf16)
    mixture, log_total = attention_forward(queries, key_rows, values, same_image, head_size)
    middle = stream + scatter(jnp.dot(mixture, out_proj, preferred_element_type=f32)) + out_bias[0]
    normed_two = norm_apply(middle, norm_gain[1], norm_shift[1]).astype(bf16)
    inputs_two = gather(normed_two)
    hidden_pre = jnp.dot(inputs_two, up_proj, preferred_element_type=f32) + up_bias
    hidden = jax.nn.gelu(hidden_pre).astype(bf16)
    result = middle + scatter(jnp.dot(hidden, down_proj, preferred_element_type=f32)) + out_bias[1]
    return (
        result,
        (stream, middle, inputs, queries, key_rows, values, log_total, mixture, inputs_two, hidden_pre, hidden),
    )


def block_backward(grad_result, weights, kept_values, same_image, head_size, gather, scatter):
    qkv, qv_bias, out_proj, up_proj, up_bias, down_proj, out_bias, norm_gain, norm_shift = weights
    (stream, middle, inputs, queries, key_rows, values, log_total, mixture, inputs_two, hidden_pre, hidden) = kept_values
    grad_bias_mlp = jnp.sum(grad_result, axis=0)
    grad_branch = gather(grad_result.astype(bf16))
    grad_down = jnp.einsum("tf,tw->fw", hidden, grad_branch, preferred_element_type=f32)
    grad_hidden = jnp.einsum("tw,fw->tf", grad_branch, down_proj, preferred_element_type=f32)
    grad_pre = jax.vjp(jax.nn.gelu, hidden_pre)[1](grad_hidden)[0]
    grad_up_bias = jnp.sum(grad_pre, axis=0)
    grad_pre_low = grad_pre.astype(bf16)
    grad_up = jnp.einsum("tw,tf->wf", inputs_two, grad_pre_low, preferred_element_type=f32)
    grad_normed_two = scatter(
        jnp.einsum("tf,wf->tw", grad_pre_low, up_proj, preferred_element_type=f32)
    )
    pull_norm_two = jax.vjp(norm_apply, middle, norm_gain[1], norm_shift[1])[1]
    grad_mid_norm, grad_gain_two, grad_shift_two = pull_norm_two(grad_normed_two)
    grad_middle = grad_result + grad_mid_norm
    grad_bias_attn = jnp.sum(grad_middle, axis=0)
    grad_attn = gather(grad_middle.astype(bf16))
    grad_out_proj = jnp.einsum("tk,tw->kw", mixture, grad_attn, preferred_element_type=f32)
    grad_mixture = jnp.einsum("tw,kw->tk", grad_attn, out_proj, preferred_element_type=f32).astype(
        bf16
    )
    grad_queries, grad_keys, grad_values = attention_backward(
        queries, key_rows, values, log_total, grad_mixture, same_image, head_size
    )
    grad_qv_bias = jnp.stack([jnp.sum(grad_queries, axis=0), jnp.sum(grad_values, axis=0)])
    grad_projected = [g.astype(bf16) for g in (grad_queries, grad_keys, grad_values)]
    grad_qkv = [
        jnp.einsum("tw,tk->wk", inputs, g, preferred_element_type=f32) for g in grad_projected
    ]
    terms = [
        jnp.einsum("tk,wk->tw", grad_projected[c], qkv[c], preferred_element_type=f32)
        for c in range(3)
    ]
    grad_normed = scatter(terms[0] + terms[1] + terms[2])
    pull_norm = jax.vjp(norm_apply, stream, norm_gain[0], norm_shift[0])[1]
    grad_in_norm, grad_gain_one, grad_shift_one = pull_norm(grad_normed)
    grad_stream = grad_middle + grad_in_norm
    return (
        grad_stream,
        (
            grad_qkv,
            grad_qv_bias,
            grad_out_proj,
            grad_up,
            grad_up_bias,
            grad_down,
            jnp.stack([grad_bias_attn, grad_bias_mlp]),
            jnp.stack([grad_gain_one, grad_gain_two]),
            jnp.stack([grad_shift_one, grad_shift_two]),
        ),
    )


def per_device(
    tokens, segment_ids, gsd_index, enc_qkv, enc_qv_bias, enc_out_proj, enc_up, enc_up_bias,
    enc_down, enc_out_bias, enc_gain, enc_norm_bias, embed_weight, embed_bias, dec_qkv,
    dec_qv_bias, dec_out_proj, dec_up, dec_up_bias, dec_down, dec_out_bias, dec_gain,
    dec_norm_bias, cotangent,
):
    share_rows, width = tokens.shape
    rows, length = segment_ids.shape
    assert rows == 4 and share_rows == length and lax.axis_size("mp") == 4
    dec_width = cotangent.shape[1]
    slot = lax.axis_index("mp")
    order = [slot ^ j for j in range(4)]
    rows_here = jnp.concatenate(
        [lax.dynamic_slice_in_dim(segment_ids, o, 1, 0) for o in order], axis=0
    )
    same_image = rows_here[:, :, None] == rows_here[:, None, :]
    scaled = scaled_places(rows_here[:1], lax.dynamic_slice_in_dim(gsd_index, slot, 1, 0))

    wide = jnp.concatenate([dec_up, dec_down, dec_out_proj], axis=0)
    thin = jnp.concatenate([dec_qkv.reshape(-1, dec_qkv.shape[2]), embed_weight], axis=0)
    wides = gather_blocks(wide)
    thins = gather_blocks(thin)
    bias_share = dec_qv_bias.shape[1]
    bias_pack = gather_blocks(jnp.concatenate([dec_qv_bias.reshape(-1), dec_up_bias]))
    n_up, n_down = dec_up.shape[0], dec_down.shape[0]
    up_full = jnp.concatenate([w[:n_up] for w in wides], axis=1)
    down_full = jnp.concatenate([w[n_up : n_up + n_down] for w in wides], axis=0)
    out_full = jnp.concatenate([w[n_up + n_down :] for w in wides], axis=0)
    n_qkv = 3 * dec_qkv.shape[1]
    qkv_full = jnp.concatenate(
        [t[:n_qkv].reshape(dec_qkv.shape) for t in thins], axis=2
    )
    embed_full = jnp.concatenate([t[n_qkv:] for t in thins], axis=1)
    qv_full = jnp.concatenate(
        [b[: 2 * bias_share].reshape(2, bias_share) for b in bias_pack], axis=1
    )
    up_bias_full = jnp.concatenate([b[2 * bias_share :] for b in bias_pack], axis=0)

    def reorder(matrix):
        blocks = jnp.split(matrix, 4, axis=1)
        one = (slot & 1) != 0
        two = (slot & 2) != 0
        blocks = [jnp.where(one, blocks[j ^ 1], blocks[j]) for j in range(4)]
        blocks = [jnp.where(two, blocks[j ^ 2], blocks[j]) for j in range(4)]
        return jnp.concatenate(blocks, axis=1)

    encoder = (enc_qkv, enc_qv_bias, enc_out_proj, enc_up, enc_up_bias, enc_down, enc_out_bias, enc_gain, enc_norm_bias)
    decoder = (qkv_full, qv_full, out_full, up_full, up_bias_full, down_full, dec_out_bias, dec_gain, dec_norm_bias)

    def keep(value):
        return value

    enc_head = width // HEADS
    dec_head = dec_width // DHEADS
    stream = tokens.astype(f32) + sin_cos(scaled, width)
    encoded, enc_kept = block_forward(stream, encoder, same_image, enc_head, gather_rows, scatter_rows)
    encoded_low = encoded.astype(bf16)
    embedded = reorder(jnp.dot(encoded_low, embed_full, preferred_element_type=f32))
    dec_stream = embedded + embed_bias + sin_cos(scaled, dec_width)
    output, dec_kept = block_forward(dec_stream, decoder, same_image[:1], dec_head, keep, keep)
    grad_dec_in, dec_grads = block_backward(
        cotangent.astype(f32), decoder, dec_kept, same_image[:1], dec_head, keep, keep
    )
    grad_embed_bias = jnp.sum(grad_dec_in, axis=0)
    gz = reorder(grad_dec_in.astype(bf16))
    grad_embed = jnp.einsum("td,tc->dc", encoded_low, gz, preferred_element_type=f32)
    grad_encoded = jnp.einsum("tc,dc->td", gz, embed_full, preferred_element_type=f32)

    d_qkv, d_qv, d_out, d_up, d_up_bias, d_down, d_ob, d_gain, d_nb = dec_grads
    col = dec_qkv.shape[2]
    thin_parts, wide_parts = [], []
    for j in range(4):
        thin_parts.append(
            jnp.concatenate(
                [g[:, j * col : (j + 1) * col] for g in d_qkv]
                + [grad_embed[:, j * col : (j + 1) * col]],
                axis=0,
            ).astype(bf16)
        )
        wide_parts.append(
            jnp.concatenate(
                [
                    d_up[:, j * dec_up.shape[1] : (j + 1) * dec_up.shape[1]],
                    d_down[j * n_down : (j + 1) * n_down],
                    d_out[j * col : (j + 1) * col],
                ],
                axis=0,
            ).astype(bf16)
        )
    thin_sum = sum_over_dp(scatter_blocks(thin_parts))
    wide_sum = sum_over_dp(scatter_blocks(wide_parts))

    grad_tokens, enc_grads = block_backward(
        grad_encoded, encoder, enc_kept, same_image, enc_head, gather_rows, scatter_rows
    )
    e_qkv, e_qv, e_out, e_up, e_up_bias, e_down, e_ob, e_gain, e_nb = enc_grads
    e_down = sum_over_dp(e_down)
    e_up = sum_over_dp(e_up)
    e_out = sum_over_dp(e_out)
    e_qkv = sum_over_dp(jnp.concatenate(e_qkv, axis=0)).reshape(enc_qkv.shape)

    def own_place(share):
        out = jnp.zeros((4, share.size), f32)
        return lax.dynamic_update_slice(out, share.reshape(1, -1), (slot, 0)).reshape(-1)

    def in_order(full):
        return reorder(full.reshape(4, -1).reshape(1, -1)).reshape(-1)

    dec_blocks = jnp.concatenate(
        [d_qv.reshape(2, 4, -1).transpose(1, 0, 2).reshape(4, -1), d_up_bias.reshape(4, -1)], axis=1
    )
    pieces = [
        e_ob.reshape(-1), e_gain.reshape(-1), e_nb.reshape(-1), grad_embed_bias,
        d_ob.reshape(-1), d_gain.reshape(-1), d_nb.reshape(-1),
        own_place(jnp.concatenate([e_qv.reshape(-1), e_up_bias])),
        in_order(dec_blocks),
    ]
    packed = sum_over_all(jnp.concatenate(pieces))
    cut = []
    begin = 0
    for piece in pieces:
        cut.append(packed[begin : begin + piece.shape[0]])
        begin += piece.shape[0]
    e_share = lax.dynamic_slice_in_dim(cut[7].reshape(4, -1), slot, 1, 0)[0]
    d_share = lax.dynamic_slice_in_dim(cut[8].reshape(4, -1), slot, 1, 0)[0]
    return (
        output,
        grad_tokens,
        e_qkv,
        e_share[: e_qv.size].reshape(e_qv.shape),
        e_out,
        e_up,
        e_share[e_qv.size :],
        e_down,
        cut[0].reshape(e_ob.shape),
        cut[1].reshape(e_gain.shape),
        cut[2].reshape(e_nb.shape),
        thin_sum[n_qkv:],
        cut[3],
        thin_sum[:n_qkv].reshape(dec_qkv.shape),
        d_share[: 2 * bias_share].reshape(2, bias_share),
        wide_sum[n_up + n_down :],
        wide_sum[:n_up],
        d_share[2 * bias_share :],
        wide_sum[n_up : n_up + n_down],
        cut[4].reshape(d_ob.shape),
        cut[5].reshape(d_gain.shape),
        cut[6].reshape(d_nb.shape),
    )


def solution(mesh):
    return jax.shard_map(
        per_device,
        mesh=mesh,
        in_specs=(
            P(("dp", "mp"), None),
            P("dp", None),
            P("dp", None),
            P(None, None, "mp"),
            P(None, "mp"),
            P("mp", None),
            P(None, "mp"),
            P("mp"),
            P("mp", None),
            P(),
            P(),
            P(),
            P(None, "mp"),
            P(),
            P(None, None, "mp"),
            P(None, "mp"),
            P("mp", None),
            P(None, "mp"),
            P("mp"),
            P("mp", None),
            P(),
            P(),
            P(),
            P(("dp", "mp"), None),
        ),
        out_specs=(
            P(("dp", "mp"), None),
            P(("dp", "mp"), None),
            P(None, None, "mp"),
            P(None, "mp"),
            P("mp", None),
            P(None, "mp"),
            P("mp"),
            P("mp", None),
            P(),
            P(),
            P(),
            P(None, "mp"),
            P(),
            P(None, None, "mp"),
            P(None, "mp"),
            P("mp", None),
            P(None, "mp"),
            P("mp"),
            P("mp", None),
            P(),
            P(),
            P(),
        ),
        check_vma=False,
    )
```

```python
import jax
import jax.numpy as jnp
from jax import lax
from jax.sharding import PartitionSpec as P

HEADS = 16
DHEADS = 16
norm_eps = 1e-06
f32 = jnp.float32
bf16 = jnp.bfloat16


def swap(value, axis, mask):
    size = lax.axis_size(axis)
    return lax.ppermute(value, axis, [(i, i ^ mask) for i in range(size)])


def gather_blocks(block):
    far = swap(block, "mp", 2)
    near = swap(block, "mp", 1)
    far_near = swap(far, "mp", 1)
    return [block, near, far, far_near]


def scatter_blocks(parts):
    low = [part.astype(bf16) for part in parts]
    pair_far = low[2].astype(f32) + swap(low[3], "mp", 1).astype(f32)
    far = swap(pair_far.astype(bf16), "mp", 2)
    near = swap(low[1], "mp", 1)
    return parts[0].astype(f32) + near.astype(f32) + far.astype(f32)


def gather_rows(block):
    return jnp.concatenate(gather_blocks(block), axis=0)


def scatter_rows(partial):
    rows = partial.shape[0] // 4
    return scatter_blocks([partial[j * rows : (j + 1) * rows] for j in range(4)])


def sum_over_dp(value):
    share = lax.psum_scatter(value.astype(bf16), "dp", scatter_dimension=0, tiled=True)
    return lax.all_gather(share, "dp", axis=0, tiled=True).astype(f32)


def sum_over_all(vector):
    for axis in ("mp", "dp"):
        bit = 1
        while bit < lax.axis_size(axis):
            vector = vector + swap(vector, axis, bit)
            bit *= 2
    return vector


def norm_apply(values, norm_gain, norm_shift):
    average = jnp.mean(values, axis=-1, keepdims=True)
    centred = values - average
    variance = jnp.mean(centred * centred, axis=-1, keepdims=True)
    return centred * lax.rsqrt(variance + norm_eps) * norm_gain + norm_shift


def scaled_places(segment_ids, gsd_index):
    length = segment_ids.shape[1]
    same_image = segment_ids[:, :, None] == segment_ids[:, None, :]
    positions = jnp.arange(length, dtype=jnp.int32)
    before = positions[None, :] < positions[:, None]
    ranks = jnp.sum(jnp.where(same_image & before[None], 1, 0), axis=-1).astype(f32)
    gsd_ratio = 0.5 + 0.25 * gsd_index.astype(f32)
    return (ranks * gsd_ratio).reshape(-1)


def sin_cos(scaled, model_width):
    half_width = model_width // 2
    frequency = jnp.power(10000.0, -jnp.arange(half_width, dtype=f32) / half_width)
    angles = scaled[:, None] * frequency[None, :]
    return jnp.concatenate([jnp.sin(angles), jnp.cos(angles)], axis=1)


def split_heads(matrix, same_image, head_size):
    row_count, length = (same_image.shape[0], same_image.shape[1])
    return matrix.reshape(row_count, length, matrix.shape[1] // head_size, head_size)


def attention_scores(query_heads, key_heads, same_image, head_size):
    scores = jnp.einsum(
        "rqhe,rkhe->rhqk", query_heads, key_heads, preferred_element_type=f32
    ) * head_size ** (-0.5)
    return jnp.where(same_image[:, None], scores, -1000000000.0)


def attention_forward(queries, key_rows, values, same_image, head_size):
    query_heads = split_heads(queries, same_image, head_size)
    key_heads = split_heads(key_rows, same_image, head_size)
    value_heads = split_heads(values, same_image, head_size)
    scores = attention_scores(query_heads, key_heads, same_image, head_size)
    highest = jnp.max(scores, axis=-1, keepdims=True)
    log_total = highest + jnp.log(jnp.sum(jnp.exp(scores - highest), axis=-1, keepdims=True))
    soft_low = jnp.exp(scores - log_total).astype(bf16)
    mixture = jnp.einsum("rhqk,rkhe->rqhe", soft_low, value_heads, preferred_element_type=f32)
    return (mixture.reshape(queries.shape).astype(bf16), log_total)


def attention_backward(queries, key_rows, values, log_total, grad_mixture, same_image, head_size):
    query_heads = split_heads(queries, same_image, head_size)
    key_heads = split_heads(key_rows, same_image, head_size)
    value_heads = split_heads(values, same_image, head_size)
    grad_heads = split_heads(grad_mixture, same_image, head_size)
    scores = attention_scores(query_heads, key_heads, same_image, head_size)
    soft_full = jnp.exp(scores - log_total)
    soft_low = soft_full.astype(bf16)
    grad_values = jnp.einsum("rhqk,rqhe->rkhe", soft_low, grad_heads, preferred_element_type=f32)
    grad_probs = jnp.einsum("rqhe,rkhe->rhqk", grad_heads, value_heads, preferred_element_type=f32)
    row_delta = jnp.sum(grad_probs * soft_full, axis=-1, keepdims=True)
    grad_scores = (soft_full * (grad_probs - row_delta)).astype(bf16)
    scale_factor = head_size ** (-0.5)
    grad_queries = (
        jnp.einsum("rhqk,rkhe->rqhe", grad_scores, key_heads, preferred_element_type=f32)
        * scale_factor
    )
    grad_keys = (
        jnp.einsum("rhqk,rqhe->rkhe", grad_scores, query_heads, preferred_element_type=f32)
        * scale_factor
    )
    flat_shape = queries.shape
    return (
        grad_queries.reshape(flat_shape),
        grad_keys.reshape(flat_shape),
        grad_values.reshape(flat_shape),
    )


def block_forward(stream, weights, same_image, head_size, gather, scatter):
    qkv, qv_bias, out_proj, up_proj, up_bias, down_proj, out_bias, norm_gain, norm_shift = weights
    normed = norm_apply(stream, norm_gain[0], norm_shift[0]).astype(bf16)
    inputs = gather(normed)
    queries, key_rows, values = [
        jnp.dot(inputs, qkv[c], preferred_element_type=f32) for c in range(3)
    ]
    queries = (queries + qv_bias[0]).astype(bf16)
    key_rows = key_rows.astype(bf16)
    values = (values + qv_bias[1]).astype(bf16)
    mixture, log_total = attention_forward(queries, key_rows, values, same_image, head_size)
    middle = stream + scatter(jnp.dot(mixture, out_proj, preferred_element_type=f32)) + out_bias[0]
    normed_two = norm_apply(middle, norm_gain[1], norm_shift[1]).astype(bf16)
    inputs_two = gather(normed_two)
    hidden_pre = jnp.dot(inputs_two, up_proj, preferred_element_type=f32) + up_bias
    hidden = jax.nn.gelu(hidden_pre).astype(bf16)
    result = middle + scatter(jnp.dot(hidden, down_proj, preferred_element_type=f32)) + out_bias[1]
    return (
        result,
        (stream, middle, inputs, queries, key_rows, values, log_total, mixture, inputs_two, hidden_pre, hidden),
    )


def block_backward(grad_result, weights, kept_values, same_image, head_size, gather, scatter):
    qkv, qv_bias, out_proj, up_proj, up_bias, down_proj, out_bias, norm_gain, norm_shift = weights
    (stream, middle, inputs, queries, key_rows, values, log_total, mixture, inputs_two, hidden_pre, hidden) = kept_values
    grad_bias_mlp = jnp.sum(grad_result, axis=0)
    grad_branch = gather(grad_result.astype(bf16))
    grad_down = jnp.einsum("tf,tw->fw", hidden, grad_branch, preferred_element_type=f32)
    grad_hidden = jnp.einsum("tw,fw->tf", grad_branch, down_proj, preferred_element_type=f32)
    grad_pre = jax.vjp(jax.nn.gelu, hidden_pre)[1](grad_hidden)[0]
    grad_up_bias = jnp.sum(grad_pre, axis=0)
    grad_pre_low = grad_pre.astype(bf16)
    grad_up = jnp.einsum("tw,tf->wf", inputs_two, grad_pre_low, preferred_element_type=f32)
    grad_normed_two = scatter(
        jnp.einsum("tf,wf->tw", grad_pre_low, up_proj, preferred_element_type=f32)
    )
    pull_norm_two = jax.vjp(norm_apply, middle, norm_gain[1], norm_shift[1])[1]
    grad_mid_norm, grad_gain_two, grad_shift_two = pull_norm_two(grad_normed_two)
    grad_middle = grad_result + grad_mid_norm
    grad_bias_attn = jnp.sum(grad_middle, axis=0)
    grad_attn = gather(grad_middle.astype(bf16))
    grad_out_proj = jnp.einsum("tk,tw->kw", mixture, grad_attn, preferred_element_type=f32)
    grad_mixture = jnp.einsum("tw,kw->tk", grad_attn, out_proj, preferred_element_type=f32).astype(
        bf16
    )
    grad_queries, grad_keys, grad_values = attention_backward(
        queries, key_rows, values, log_total, grad_mixture, same_image, head_size
    )
    grad_qv_bias = jnp.stack([jnp.sum(grad_queries, axis=0), jnp.sum(grad_values, axis=0)])
    grad_projected = [g.astype(bf16) for g in (grad_queries, grad_keys, grad_values)]
    grad_qkv = [
        jnp.einsum("tw,tk->wk", inputs, g, preferred_element_type=f32) for g in grad_projected
    ]
    terms = [
        jnp.einsum("tk,wk->tw", grad_projected[c], qkv[c], preferred_element_type=f32)
        for c in range(3)
    ]
    grad_normed = scatter(terms[0] + terms[1] + terms[2])
    pull_norm = jax.vjp(norm_apply, stream, norm_gain[0], norm_shift[0])[1]
    grad_in_norm, grad_gain_one, grad_shift_one = pull_norm(grad_normed)
    grad_stream = grad_middle + grad_in_norm
    return (
        grad_stream,
        (
            grad_qkv,
            grad_qv_bias,
            grad_out_proj,
            grad_up,
            grad_up_bias,
            grad_down,
            jnp.stack([grad_bias_attn, grad_bias_mlp]),
            jnp.stack([grad_gain_one, grad_gain_two]),
            jnp.stack([grad_shift_one, grad_shift_two]),
        ),
    )


def per_device(
    tokens, segment_ids, gsd_index, enc_qkv, enc_qv_bias, enc_out_proj, enc_up, enc_up_bias,
    enc_down, enc_out_bias, enc_gain, enc_norm_bias, embed_weight, embed_bias, dec_qkv,
    dec_qv_bias, dec_out_proj, dec_up, dec_up_bias, dec_down, dec_out_bias, dec_gain,
    dec_norm_bias, cotangent,
):
    share_rows, width = tokens.shape
    rows, length = segment_ids.shape
    assert rows == 4 and share_rows == length and lax.axis_size("mp") == 4
    dec_width = cotangent.shape[1]
    slot = lax.axis_index("mp")
    order = [slot ^ j for j in range(4)]
    rows_here = jnp.concatenate(
        [lax.dynamic_slice_in_dim(segment_ids, o, 1, 0) for o in order], axis=0
    )
    same_image = rows_here[:, :, None] == rows_here[:, None, :]
    scaled = scaled_places(rows_here[:1], lax.dynamic_slice_in_dim(gsd_index, slot, 1, 0))

    wide = jnp.concatenate([dec_up, dec_down, dec_out_proj], axis=0)
    thin = jnp.concatenate([dec_qkv.reshape(-1, dec_qkv.shape[2]), embed_weight], axis=0)
    wides = gather_blocks(wide)
    thins = gather_blocks(thin)
    bias_share = dec_qv_bias.shape[1]
    bias_pack = gather_blocks(jnp.concatenate([dec_qv_bias.reshape(-1), dec_up_bias]))
    n_up, n_down = dec_up.shape[0], dec_down.shape[0]
    up_full = jnp.concatenate([w[:n_up] for w in wides], axis=1)
    down_full = jnp.concatenate([w[n_up : n_up + n_down] for w in wides], axis=0)
    out_full = jnp.concatenate([w[n_up + n_down :] for w in wides], axis=0)
    n_qkv = 3 * dec_qkv.shape[1]
    qkv_full = jnp.concatenate(
        [t[:n_qkv].reshape(dec_qkv.shape) for t in thins], axis=2
    )
    embed_full = jnp.concatenate([t[n_qkv:] for t in thins], axis=1)
    qv_full = jnp.concatenate(
        [b[: 2 * bias_share].reshape(2, bias_share) for b in bias_pack], axis=1
    )
    up_bias_full = jnp.concatenate([b[2 * bias_share :] for b in bias_pack], axis=0)

    def reorder(matrix):
        blocks = jnp.split(matrix, 4, axis=1)
        one = (slot & 1) != 0
        two = (slot & 2) != 0
        blocks = [jnp.where(one, blocks[j ^ 1], blocks[j]) for j in range(4)]
        blocks = [jnp.where(two, blocks[j ^ 2], blocks[j]) for j in range(4)]
        return jnp.concatenate(blocks, axis=1)

    encoder = (enc_qkv, enc_qv_bias, enc_out_proj, enc_up, enc_up_bias, enc_down, enc_out_bias, enc_gain, enc_norm_bias)
    decoder = (qkv_full, qv_full, out_full, up_full, up_bias_full, down_full, dec_out_bias, dec_gain, dec_norm_bias)

    def keep(value):
        return value

    enc_head = width // HEADS
    dec_head = dec_width // DHEADS
    stream = tokens.astype(f32) + sin_cos(scaled, width)
    encoded, enc_kept = block_forward(stream, encoder, same_image, enc_head, gather_rows, scatter_rows)
    encoded_low = encoded.astype(bf16)
    embedded = reorder(jnp.dot(encoded_low, embed_full, preferred_element_type=f32))
    dec_stream = embedded + embed_bias + sin_cos(scaled, dec_width)
    output, dec_kept = block_forward(dec_stream, decoder, same_image[:1], dec_head, keep, keep)
    grad_dec_in, dec_grads = block_backward(
        cotangent.astype(f32), decoder, dec_kept, same_image[:1], dec_head, keep, keep
    )
    grad_embed_bias = jnp.sum(grad_dec_in, axis=0)
    gz = reorder(grad_dec_in.astype(bf16))
    grad_embed = jnp.einsum("td,tc->dc", encoded_low, gz, preferred_element_type=f32)
    grad_encoded = jnp.einsum("tc,dc->td", gz, embed_full, preferred_element_type=f32)

    d_qkv, d_qv, d_out, d_up, d_up_bias, d_down, d_ob, d_gain, d_nb = dec_grads
    col = dec_qkv.shape[2]
    thin_parts, wide_parts = [], []
    for j in range(4):
        thin_parts.append(
            jnp.concatenate(
                [g[:, j * col : (j + 1) * col] for g in d_qkv]
                + [grad_embed[:, j * col : (j + 1) * col]],
                axis=0,
            ).astype(bf16)
        )
        wide_parts.append(
            jnp.concatenate(
                [
                    d_up[:, j * dec_up.shape[1] : (j + 1) * dec_up.shape[1]],
                    d_down[j * n_down : (j + 1) * n_down],
                    d_out[j * col : (j + 1) * col],
                ],
                axis=0,
            ).astype(bf16)
        )
    thin_sum = sum_over_dp(scatter_blocks(thin_parts))
    wide_sum = sum_over_dp(scatter_blocks(wide_parts))

    grad_tokens, enc_grads = block_backward(
        grad_encoded, encoder, enc_kept, same_image, enc_head, gather_rows, scatter_rows
    )
    e_qkv, e_qv, e_out, e_up, e_up_bias, e_down, e_ob, e_gain, e_nb = enc_grads
    e_down = sum_over_dp(e_down)
    e_up = sum_over_dp(e_up)
    e_out = sum_over_dp(e_out)
    e_qkv = sum_over_dp(jnp.concatenate(e_qkv, axis=0)).reshape(enc_qkv.shape)

    def own_place(share):
        out = jnp.zeros((4, share.size), f32)
        return lax.dynamic_update_slice(out, share.reshape(1, -1), (slot, 0)).reshape(-1)

    def in_order(full):
        return reorder(full.reshape(4, -1).reshape(1, -1)).reshape(-1)

    dec_blocks = jnp.concatenate(
        [d_qv.reshape(2, 4, -1).transpose(1, 0, 2).reshape(4, -1), d_up_bias.reshape(4, -1)], axis=1
    )
    pieces = [
        e_ob.reshape(-1), e_gain.reshape(-1), e_nb.reshape(-1), grad_embed_bias,
        d_ob.reshape(-1), d_gain.reshape(-1), d_nb.reshape(-1),
        own_place(jnp.concatenate([e_qv.reshape(-1), e_up_bias])),
        in_order(dec_blocks),
    ]
    packed = sum_over_all(jnp.concatenate(pieces))
    cut = []
    begin = 0
    for piece in pieces:
        cut.append(packed[begin : begin + piece.shape[0]])
        begin += piece.shape[0]
    e_share = lax.dynamic_slice_in_dim(cut[7].reshape(4, -1), slot, 1, 0)[0]
    d_share = lax.dynamic_slice_in_dim(cut[8].reshape(4, -1), slot, 1, 0)[0]
    return (
        output,
        grad_tokens,
        e_qkv,
        e_share[: e_qv.size].reshape(e_qv.shape),
        e_out,
        e_up,
        e_share[e_qv.size :],
        e_down,
        cut[0].reshape(e_ob.shape),
        cut[1].reshape(e_gain.shape),
        cut[2].reshape(e_nb.shape),
        thin_sum[n_qkv:],
        cut[3],
        thin_sum[:n_qkv].reshape(dec_qkv.shape),
        d_share[: 2 * bias_share].reshape(2, bias_share),
        wide_sum[n_up + n_down :],
        wide_sum[:n_up],
        d_share[2 * bias_share :],
        wide_sum[n_up : n_up + n_down],
        cut[4].reshape(d_ob.shape),
        cut[5].reshape(d_gain.shape),
        cut[6].reshape(d_nb.shape),
    )


def solution(mesh):
    return jax.shard_map(
        per_device,
        mesh=mesh,
        in_specs=(
            P(("dp", "mp"), None),
            P("dp", None),
            P("dp", None),
            P(None, None, "mp"),
            P(None, "mp"),
            P("mp", None),
            P(None, "mp"),
            P("mp"),
            P("mp", None),
            P(),
            P(),
            P(),
            P(None, "mp"),
            P(),
            P(None, None, "mp"),
            P(None, "mp"),
            P("mp", None),
            P(None, "mp"),
            P("mp"),
            P("mp", None),
            P(),
            P(),
            P(),
            P(("dp", "mp"), None),
        ),
        out_specs=(
            P(("dp", "mp"), None),
            P(("dp", "mp"), None),
            P(None, None, "mp"),
            P(None, "mp"),
            P("mp", None),
            P(None, "mp"),
            P("mp"),
            P("mp", None),
            P(),
            P(),
            P(),
            P(None, "mp"),
            P(),
            P(None, None, "mp"),
            P(None, "mp"),
            P("mp", None),
            P(None, "mp"),
            P("mp"),
            P("mp", None),
            P(),
            P(),
            P(),
        ),
        check_vma=False,
    )
```

```python
import functools
import math

import jax
import jax.numpy as jnp
from jax import lax
from jax.experimental import pallas as pl
from jax.experimental.pallas import tpu as pltpu
from jax.sharding import PartitionSpec as P

HEADS = 16
DHEADS = 16
norm_eps = 1e-06
f32 = jnp.float32
bf16 = jnp.bfloat16
MIB = 1 << 20
VMEM = pl.BlockSpec(memory_space=pltpu.VMEM)
SMEM = pl.BlockSpec(memory_space=pltpu.SMEM)


def shaped(dims, kind):
    return jax.ShapeDtypeStruct(dims, kind)


def run(body, outs, args, smem=0, scratch=(), limit=40, flops=0):
    moved = sum(a.size * a.dtype.itemsize for a in args)
    moved += sum(math.prod(o.shape) * jnp.dtype(o.dtype).itemsize for o in outs)
    return pl.pallas_call(
        body,
        out_shape=outs,
        in_specs=[SMEM] * smem + [VMEM] * (len(args) - smem),
        out_specs=[VMEM] * len(outs),
        scratch_shapes=scratch,
        compiler_params=pltpu.CompilerParams(vmem_limit_bytes=limit * MIB),
        cost_estimate=pl.CostEstimate(flops=flops, bytes_accessed=moved, transcendentals=0),
    )(*args)


def nn(a, b):
    return lax.dot_general(a, b, (((1,), (0,)), ((), ())), preferred_element_type=f32)


def nt(a, b):
    return lax.dot_general(a, b, (((1,), (1,)), ((), ())), preferred_element_type=f32)


def tn(a, b):
    return lax.dot_general(a, b, (((0,), (0,)), ((), ())), preferred_element_type=f32)


def swap(value, axis, mask):
    size = lax.axis_size(axis)
    return lax.ppermute(value, axis, [(i, i ^ mask) for i in range(size)])


def gather_blocks(block):
    far = swap(block, "mp", 2)
    near = swap(block, "mp", 1)
    far_near = swap(far, "mp", 1)
    return [block, near, far, far_near]


def scatter_blocks(parts):
    pair_far = parts[2].astype(f32) + swap(parts[3], "mp", 1).astype(f32)
    far = swap(pair_far.astype(bf16), "mp", 2)
    near = swap(parts[1], "mp", 1)
    return parts[0], near, far


def sum_over_all(vector):
    for axis in ("mp", "dp"):
        bit = 1
        while bit < lax.axis_size(axis):
            vector = vector + swap(vector, axis, bit)
            bit *= 2
    return vector


def norm_parts(values):
    average = jnp.mean(values, axis=-1, keepdims=True)
    centred = values - average
    variance = jnp.mean(centred * centred, axis=-1, keepdims=True)
    scale = lax.rsqrt(variance + norm_eps)
    return centred * scale, scale


def norm_back(normal, scale, gain, grad):
    wide = grad * gain
    one = jnp.mean(wide, axis=-1, keepdims=True)
    two = jnp.mean(wide * normal, axis=-1, keepdims=True)
    return scale * (wide - one - normal * two)


def gelu_both(v):
    slope = math.sqrt(2.0 / math.pi)
    square = v * v
    t = jnp.tanh(slope * v * (1.0 + 0.044715 * square))
    half = 0.5 * (1.0 + t)
    return v * half, half + 0.5 * slope * v * (1.0 - t * t) * (1.0 + 3.0 * 0.044715 * square)


def sin_cos(x):
    turn = jnp.floor(x * (2.0 / math.pi) + 0.5)
    r = ((x - turn * 1.5703125) - turn * 4.837512969970703125e-4) - turn * 7.54978995489188216e-8
    z = r * r
    s = r + r * z * (-1.6666654611e-1 + z * (8.3321608736e-3 + z * -1.9515295891e-4))
    c = 1.0 - 0.5 * z + z * z * (
        4.166664568298827e-2 + z * (-1.388731625493765e-3 + z * 2.443315711809948e-5)
    )
    quarter = turn.astype(jnp.int32)
    odd = (quarter & 1) != 0
    sine = jnp.where(odd, c, s)
    cosine = jnp.where(odd, s, c)
    sine = jnp.where((quarter & 2) != 0, -sine, sine)
    cosine = jnp.where(((quarter + 1) & 2) != 0, -cosine, cosine)
    return sine, cosine


def head_masks(heads):
    size = 256 // heads
    lane = lax.broadcasted_iota(jnp.int32, (1, 256), 1)
    return [
        jnp.where((lane >= h * size) & (lane < (h + 1) * size), 1.0, 0.0).astype(bf16)
        for h in range(heads)
    ]


def attend(q, k, v, bias, heads, scale, keep):
    size = 256 // heads
    vt = v.astype(f32).T.astype(bf16)
    mixes = []
    for h, mask in enumerate(head_masks(heads)):
        s = nt(k, q * mask) + bias
        top = jnp.max(s, axis=0, keepdims=True)
        p = jnp.exp2((s - top) * (scale * math.log2(math.e)))
        total = jnp.sum(p, axis=0, keepdims=True)
        p = (p * (1.0 / total)).astype(bf16)
        keep(h, p)
        mixes.append(nn(vt[h * size : (h + 1) * size], p))
    return jnp.concatenate(mixes, axis=0).T


def attend_back(q, k, v, gm, probs, heads, scale):
    size = 256 // heads
    kt = k.astype(f32).T.astype(bf16)
    gq, gk, gv = [], 0.0, 0.0
    for h, mask in enumerate(head_masks(heads)):
        gmh = gm * mask
        p = probs(h)
        wide = p.astype(f32)
        t = wide * nt(v, gmh)
        gs = (t - wide * jnp.sum(t, axis=0, keepdims=True)).astype(bf16)
        gk = gk + nn(gs, q * mask)
        gv = gv + nn(p, gmh)
        gq.append(nn(kt[h * size : (h + 1) * size], gs))
    return jnp.concatenate(gq, axis=0).T * scale, gk * scale, gv


def start_body(slot_ref, seg_ref, gsd_ref, tokens_ref, gain_ref, shift_ref, eb_ref, wf_ref, nf_ref,
               stream_ref, normed_ref, pos_ref, bias_ref):
    slot = slot_ref[0]
    n = seg_ref.shape[1]
    place = None
    for j in range(4):
        across = jnp.broadcast_to(seg_ref[pl.ds(slot ^ j, 1), :].astype(f32), (n, n))
        down = across.T
        same = across == down
        bias_ref[j] = jnp.where(same, 0.0, -1e30)
        if j == 0:
            earlier = lax.broadcasted_iota(jnp.int32, (n, n), 1) < lax.broadcasted_iota(
                jnp.int32, (n, n), 0
            )
            rank = jnp.sum(jnp.where(same & earlier, 1.0, 0.0), axis=1, keepdims=True)
            index = jnp.broadcast_to(gsd_ref[pl.ds(slot, 1), :].astype(f32), (n, n)).T[:, :1]
            place = rank * (0.5 + 0.25 * index)
    half = wf_ref.shape[1]
    sine, cosine = sin_cos(place * wf_ref[...])
    stream_ref[:, :half] = tokens_ref[:, :half].astype(f32) + sine
    stream_ref[:, half:] = tokens_ref[:, half:].astype(f32) + cosine
    normal, _ = norm_parts(stream_ref[...])
    normed_ref[...] = (normal * gain_ref[0:1] + shift_ref[0:1]).astype(bf16)
    sine, cosine = sin_cos(place * nf_ref[...])
    half = nf_ref.shape[1]
    pos_ref[:, :half] = sine + eb_ref[:, :half]
    pos_ref[:, half:] = cosine + eb_ref[:, half:]


def attn_body(first, scale, heads, xa_ref, xb_ref, bias_ref, w_ref, qvb_ref, o_ref,
              q_ref, k_ref, v_ref, p_ref, mix_ref, pa_ref, pb_ref):
    for r, (x_ref, part_ref) in enumerate(((xa_ref, pa_ref), (xb_ref, pb_ref))):
        x = x_ref[...]
        q = (nn(x, w_ref[0]) + qvb_ref[0:1]).astype(bf16)
        k = nn(x, w_ref[1]).astype(bf16)
        v = (nn(x, w_ref[2]) + qvb_ref[1:2]).astype(bf16)
        q_ref[r], k_ref[r], v_ref[r] = q, k, v

        def keep(h, p):
            p_ref[r, h] = p

        mix = attend(q, k, v, bias_ref[first + r], heads, scale, keep).astype(bf16)
        mix_ref[r] = mix
        part_ref[...] = nn(mix, o_ref[...]).astype(bf16)


def attn_back_body(scale, heads, ga_ref, gb_ref, q_ref, k_ref, v_ref, p_ref, w_ref, o_ref,
                   g3_ref, sums_ref, pa_ref, pb_ref):
    total_q, total_v = 0.0, 0.0
    for r, (g_ref, part_ref) in enumerate(((ga_ref, pa_ref), (gb_ref, pb_ref))):
        gm = nt(g_ref[...], o_ref[...]).astype(bf16)
        gq, gk, gv = attend_back(
            q_ref[r], k_ref[r], v_ref[r], gm, lambda h: p_ref[r, h], heads, scale
        )
        total_q = total_q + jnp.sum(gq, axis=0, keepdims=True)
        total_v = total_v + jnp.sum(gv, axis=0, keepdims=True)
        acc = 0.0
        for c, g in enumerate((gq, gk, gv)):
            low = g.astype(bf16)
            g3_ref[r, :, c * 256 : (c + 1) * 256] = low
            acc = acc + nt(low, w_ref[c])
        part_ref[...] = acc.astype(bf16)
    sums_ref[0:1] = total_q
    sums_ref[1:2] = total_v


def mid_body(stream_ref, p_ref, near_ref, far_ref, ob_ref, gain_ref, shift_ref, mid_ref, normed_ref):
    total = p_ref[...].astype(f32) + near_ref[...].astype(f32) + far_ref[...].astype(f32)
    middle = stream_ref[...] + total + ob_ref[0:1]
    mid_ref[...] = middle
    normal, _ = norm_parts(middle)
    normed_ref[...] = (normal * gain_ref[1:2] + shift_ref[1:2]).astype(bf16)


def mlp_body(xa_ref, xb_ref, up_ref, ub_ref, down_ref, hid_ref, dg_ref, pa_ref, pb_ref):
    width = up_ref.shape[1]
    for r, (x_ref, part_ref) in enumerate(((xa_ref, pa_ref), (xb_ref, pb_ref))):
        x = x_ref[...]
        for c in range(0, width, 256):
            cut = slice(c, c + 256)
            hidden, slope = gelu_both(nn(x, up_ref[:, cut]) + ub_ref[:, cut])
            hid_ref[r, :, cut] = hidden.astype(bf16)
            dg_ref[r, :, cut] = slope.astype(bf16)
        hidden = hid_ref[r]
        for c in range(0, down_ref.shape[1], 512):
            cut = slice(c, c + 512)
            part_ref[:, cut] = nn(hidden, down_ref[:, cut]).astype(bf16)


def mlp_back_body(ga_ref, gb_ref, dg_ref, up_ref, down_ref, gp_ref, sums_ref, pa_ref, pb_ref):
    width = up_ref.shape[1]
    for r, (g_ref, part_ref) in enumerate(((ga_ref, pa_ref), (gb_ref, pb_ref))):
        g = g_ref[...]
        for c in range(0, width, 256):
            cut = slice(c, c + 256)
            grad = nt(g, down_ref[cut]) * dg_ref[r, :, cut].astype(f32)
            gp_ref[r, :, cut] = grad.astype(bf16)
            total = jnp.sum(grad, axis=0, keepdims=True)
            sums_ref[:, cut] = total if r == 0 else sums_ref[:, cut] + total
        gp = gp_ref[r]
        for c in range(0, up_ref.shape[0], 512):
            cut = slice(c, c + 512)
            part_ref[:, cut] = nt(gp, up_ref[cut]).astype(bf16)


def mlp_end_body(slot_ref, ge_ref, p_ref, near_ref, far_ref, mid_ref, gain_ref, ua_ref, ub_ref, dec_ref,
                 gmid_ref, gm_ref, pack_ref):
    slot = slot_ref[0]
    grad = p_ref[...].astype(f32) + near_ref[...].astype(f32) + far_ref[...].astype(f32)
    normal, scale = norm_parts(mid_ref[...])
    gmid = ge_ref[...] + norm_back(normal, scale, gain_ref[1:2], grad)
    gmid_ref[...] = gmid
    gm_ref[...] = gmid.astype(bf16)
    pack_ref[...] = jnp.zeros(pack_ref.shape, f32)
    pack_ref[0:1] = jnp.sum(gmid, axis=0, keepdims=True)
    pack_ref[1:2] = jnp.sum(grad * normal, axis=0, keepdims=True)
    pack_ref[2:3] = jnp.sum(grad, axis=0, keepdims=True)
    pack_ref[pl.ds(4 + slot, 1), :] = ua_ref[...] + ub_ref[...]
    pack_ref[8:16] = dec_ref[...]


def last_body(slot_ref, gmid_ref, p_ref, near_ref, far_ref, stream_ref, gain_ref, sa_ref, sb_ref,
              gtok_ref, pack_ref):
    slot = slot_ref[0]
    grad = p_ref[...].astype(f32) + near_ref[...].astype(f32) + far_ref[...].astype(f32)
    normal, scale = norm_parts(stream_ref[...])
    gtok_ref[...] = gmid_ref[...] + norm_back(normal, scale, gain_ref[0:1], grad)
    pack_ref[...] = jnp.zeros(pack_ref.shape, f32)
    pack_ref[0:1] = jnp.sum(grad * normal, axis=0, keepdims=True)
    pack_ref[1:2] = jnp.sum(grad, axis=0, keepdims=True)
    share = sa_ref.shape[1]
    place = pl.ds(pl.multiple_of(slot * share, share), share)
    pack_ref[2:4, place] = sa_ref[...] + sb_ref[...]


def decoder_body(slot_ref, mid_ref, p_ref, near_ref, far_ref, eob_ref, w0, w1, w2, w3, t0, t1, t2, t3,
                 qvb_ref, upb_ref, pos_ref, bias_ref, dob_ref, dgain_ref, dnb_ref, cot_ref,
                 encl_ref, out_ref, x1_ref, x2_ref, hid_ref, mix_ref, gp_ref, gm_ref, g3_ref, gz_ref,
                 gel_ref, ge_ref, sums_ref,
                 wqkv, wout, wemb, pt, dg, qkv, wide):
    slot = slot_ref[0]
    wides, thins = (w0, w1, w2, w3), (t0, t1, t2, t3)
    width = cot_ref.shape[1]
    block = width // 4
    heads = DHEADS * 256 // width
    groups = width // 256
    scale = (width // DHEADS) ** -0.5

    def place(j, base=0):
        return pl.ds(pl.multiple_of(base + (slot ^ j) * block, block), block)

    for j in range(4):
        cut = slice(j * block, (j + 1) * block)
        for c in range(3):
            wqkv[c, :, cut] = thins[j][c * width : (c + 1) * width]
        wemb[:, cut] = thins[j][3 * width :]
        wout[cut] = wides[j][2 * width :]
    encoded = mid_ref[...] + eob_ref[1:2]
    encoded = encoded + p_ref[...].astype(f32) + near_ref[...].astype(f32) + far_ref[...].astype(f32)
    encl_ref[...] = encoded.astype(bf16)
    embedded = nn(encl_ref[...], wemb[...])
    for j in range(4):
        wide[:, place(j)] = embedded[:, j * block : (j + 1) * block]
    stream = wide[...] + pos_ref[...]
    normal1, scale1 = norm_parts(stream)
    x1_ref[...] = (normal1 * dgain_ref[0:1] + dnb_ref[0:1]).astype(bf16)
    x1 = x1_ref[...]
    qkv[0] = (nn(x1, wqkv[0]) + qvb_ref[0:1]).astype(bf16)
    qkv[1] = nn(x1, wqkv[1]).astype(bf16)
    qkv[2] = (nn(x1, wqkv[2]) + qvb_ref[1:2]).astype(bf16)
    bias = bias_ref[0]
    for g in range(groups):
        cut = slice(g * 256, (g + 1) * 256)

        def keep(h, p):
            pt[g * heads + h] = p

        mix_ref[:, cut] = attend(
            qkv[0, :, cut], qkv[1, :, cut], qkv[2, :, cut], bias, heads, scale, keep
        ).astype(bf16)
    middle = stream + nn(mix_ref[...], wout[...]) + dob_ref[0:1]
    normal2, scale2 = norm_parts(middle)
    x2_ref[...] = (normal2 * dgain_ref[1:2] + dnb_ref[1:2]).astype(bf16)
    x2 = x2_ref[...]
    result = middle + dob_ref[1:2]
    for j in range(4):
        cut = slice(j * width, (j + 1) * width)
        hidden, slope = gelu_both(nn(x2, wides[j][:width]) + upb_ref[:, cut])
        hid_ref[:, cut] = hidden.astype(bf16)
        dg[:, cut] = slope.astype(bf16)
        result = result + nn(hid_ref[:, cut], wides[j][width : 2 * width])
    out_ref[...] = result

    cot = cot_ref[...]
    grad = 0.0
    sums_ref[...] = jnp.zeros(sums_ref.shape, f32)
    for j in range(4):
        cut = slice(j * width, (j + 1) * width)
        pre = nt(cot, wides[j][width : 2 * width]) * dg[:, cut].astype(f32)
        gp_ref[:, cut] = pre.astype(bf16)
        block_sum = jnp.sum(pre, axis=0, keepdims=True)
        at = slot ^ j
        sums_ref[pl.ds(6 + (at >> 1), 1), pl.ds(pl.multiple_of((at & 1) * width, width), width)] = (
            block_sum
        )
        grad = grad + nt(gp_ref[:, cut], wides[j][:width])
    cotf = cot.astype(f32)
    gmid = cotf + norm_back(normal2, scale2, dgain_ref[1:2], grad)
    gm_ref[...] = gmid.astype(bf16)
    sums_ref[1:2, :width] = jnp.sum(gmid, axis=0, keepdims=True)
    sums_ref[2:3, :width] = jnp.sum(cotf, axis=0, keepdims=True)
    sums_ref[2:3, width:] = jnp.sum(grad * normal2, axis=0, keepdims=True)
    sums_ref[4:5, :width] = jnp.sum(grad, axis=0, keepdims=True)
    gmix = nt(gm_ref[...], wout[...]).astype(bf16)
    grad = 0.0
    for g in range(groups):
        cut = slice(g * 256, (g + 1) * 256)
        three = attend_back(
            qkv[0, :, cut], qkv[1, :, cut], qkv[2, :, cut], gmix[:, cut],
            lambda h: pt[g * heads + h], heads, scale,
        )
        for c, part in enumerate(three):
            begin = c * width + g * 256
            low = part.astype(bf16)
            g3_ref[:, begin : begin + 256] = low
            grad = grad + nt(low, wqkv[c, :, cut])
        for c, row, base in ((0, 4, width), (2, 5, width)):
            total = jnp.sum(three[c], axis=0, keepdims=True)
            for i in range(256 // block):
                sums_ref[row : row + 1, place(g * (256 // block) + i, base)] = (
                    total[:, i * block : (i + 1) * block]
                )
    gstream = gmid + norm_back(normal1, scale1, dgain_ref[0:1], grad)
    sums_ref[3:4, width:] = jnp.sum(gstream, axis=0, keepdims=True)
    sums_ref[1:2, width:] = jnp.sum(grad * normal1, axis=0, keepdims=True)
    sums_ref[3:4, :width] = jnp.sum(grad, axis=0, keepdims=True)
    wide[...] = gstream
    for j in range(4):
        gz_ref[:, j * block : (j + 1) * block] = wide[:, place(j)].astype(bf16)
    ge = nt(gz_ref[...], wemb[...])
    ge_ref[...] = ge
    gel_ref[...] = ge.astype(bf16)
    sums_ref[0:1] = jnp.sum(ge, axis=0, keepdims=True)


def decoder_weights_body(x1_ref, x2_ref, hid_ref, mix_ref, gp_ref, gm_ref, g3_ref, gz_ref, encl_ref, cot_ref,
                         ws_ref, ts_ref, wk_ref, tk_ref):
    width = cot_ref.shape[1]
    block = width // 4
    cot, gm, x2 = cot_ref[...], gm_ref[...], x2_ref[...]
    piece, thin = width // 8, block // 8
    step = 2 * piece + thin
    tall = encl_ref.shape[1] // 8
    jump = 3 * piece + tall

    def to(j):
        return (ws_ref, ts_ref) if j % 2 else (wk_ref, tk_ref)

    for j in (1, 3, 0, 2):
        w, t = to(j)
        i = j // 2
        cut = slice(j * width, (j + 1) * width)
        up = tn(x2, gp_ref[:, cut]).astype(bf16)
        down = tn(hid_ref[:, cut], cot).astype(bf16)
        out = tn(mix_ref[:, j * block : (j + 1) * block], gm).astype(bf16)
        for c in range(8):
            w[i, c * step : c * step + piece] = up[c * piece : (c + 1) * piece]
            w[i, c * step + piece : c * step + 2 * piece] = down[c * piece : (c + 1) * piece]
            w[i, c * step + 2 * piece : (c + 1) * step] = out[c * thin : (c + 1) * thin]
    x1 = x1_ref[...]
    for k in range(3):
        full = tn(x1, g3_ref[:, k * width : (k + 1) * width]).astype(bf16)
        for j in range(4):
            t = to(j)[1]
            for c in range(8):
                t[j // 2, c * jump + k * piece : c * jump + (k + 1) * piece] = (
                    full[c * piece : (c + 1) * piece, j * block : (j + 1) * block]
                )
    full = tn(encl_ref[...], gz_ref[...]).astype(bf16)
    for j in range(4):
        t = to(j)[1]
        for c in range(8):
            t[j // 2, c * jump + 3 * piece : (c + 1) * jump] = (
                full[c * tall : (c + 1) * tall, j * block : (j + 1) * block]
            )


def piece_of(refs, j):
    if len(refs) == 4:
        return refs[j][...]
    return refs[j // 2][j % 2]


def first_half_body(nx, ng, pick_ref, *refs):
    xs, gs, out_ref = refs[:nx], refs[nx : nx + ng], refs[nx + ng]
    acc = 0.0
    for j in range(4):
        acc = acc + tn(piece_of(xs, j), piece_of(gs, j))
    out_ref[...] = acc.astype(bf16)


def other_half_body(nx, ng, pick_ref, *refs):
    xs, gs, add_ref, send_ref, keep_ref = refs[:nx], refs[nx : nx + ng], *refs[nx + ng :]
    acc = add_ref[...].astype(f32)
    for j in range(4):
        acc = acc + tn(piece_of(xs, j), piece_of(gs, j))
    low = acc.astype(bf16)

    @pl.when(pl.program_id(0) == 0)
    def _():
        send_ref[...] = low

    @pl.when(pl.program_id(0) == 1)
    def _():
        keep_ref[...] = low


def weight_half(xs, gs, pick, add=None):
    cols, out_cols = xs[0].shape[-1], gs[0].shape[-1]
    tile = cols // 4

    def column(shape):
        lead = shape[:-1]
        return pl.BlockSpec(lead + (tile,), lambda i, p: (0,) * len(lead) + (p[i],))

    def whole(shape):
        return pl.BlockSpec(shape, lambda i, p: (0,) * len(shape))

    in_specs = [column(x.shape) for x in xs] + [whole(g.shape) for g in gs]
    args = list(xs) + list(gs)
    nx, ng = len(xs), len(gs)
    if add is None:
        body = functools.partial(first_half_body, nx, ng)
        outs = shaped((2 * tile, out_cols), bf16)
        out_specs = pl.BlockSpec((tile, out_cols), lambda i, p: (i, 0))
    else:
        body = functools.partial(other_half_body, nx, ng)
        in_specs.append(pl.BlockSpec((tile, out_cols), lambda i, p: (p[2 + i], 0)))
        args.append(add)
        outs = [shaped((tile, out_cols), bf16)] * 2
        out_specs = [pl.BlockSpec((tile, out_cols), lambda i, p: (0, 0))] * 2
    rows = sum(math.prod(x.shape[:-1]) for x in xs)
    return pl.pallas_call(
        body,
        out_shape=outs,
        grid_spec=pltpu.PrefetchScalarGridSpec(
            num_scalar_prefetch=1, grid=(2,), in_specs=in_specs, out_specs=out_specs
        ),
        compiler_params=pltpu.CompilerParams(vmem_limit_bytes=40 * MIB),
        cost_estimate=pl.CostEstimate(
            flops=2 * rows * 2 * tile * out_cols,
            bytes_accessed=2 * rows * (2 * tile + out_cols) + 8 * tile * out_cols,
            transcendentals=0,
        ),
    )(pick, *args)


def spread(near, far, place, outs, writes):
    chunk, width = near.shape[0] // 4, near.shape[1]

    def body(place_ref, near_ref, far_ref, *out_refs):
        def put(ref):
            for which, lead, row, rows, col, cols in writes:
                value = ref[row : row + rows, col : col + cols].astype(f32)
                if lead is None:
                    out_refs[which][...] = value
                else:
                    out_refs[which][lead] = value

        step = pl.program_id(0)

        @pl.when(step < 4)
        def _():
            put(near_ref)

        @pl.when(step >= 4)
        def _():
            put(far_ref)

    def out_block(dims):
        if len(dims) == 2:
            return pl.BlockSpec((dims[0] // 8, dims[1]), lambda i, p: (i ^ p[0], 0))
        return pl.BlockSpec((dims[0], dims[1] // 8, dims[2]), lambda i, p: (0, i ^ p[0], 0))

    return pl.pallas_call(
        body,
        out_shape=[shaped(dims, f32) for dims in outs],
        grid_spec=pltpu.PrefetchScalarGridSpec(
            num_scalar_prefetch=1,
            grid=(8,),
            in_specs=[
                pl.BlockSpec((chunk, width), lambda i, p: (jnp.minimum(i, 3), 0)),
                pl.BlockSpec((chunk, width), lambda i, p: (jnp.maximum(i - 4, 0), 0)),
            ],
            out_specs=[out_block(dims) for dims in outs],
        ),
        cost_estimate=pl.CostEstimate(
            flops=0, bytes_accessed=48 * chunk * width, transcendentals=0
        ),
    )(place, near, far)


class DpSum:
    def __init__(self):
        self.size = lax.axis_size("dp")
        me = lax.axis_index("dp").astype(jnp.int32)
        self.bit = [(me >> i) & 1 for i in range(3)]
        x, b2, b4 = self.bit
        if self.size == 8:
            self.place = (4 * x + 2 * b2 + b4).reshape(1)
        else:
            self.place = jnp.zeros((1,), jnp.int32)
        self.there = jnp.stack([2 * (1 - x), 2 * (1 - x) + 1])
        self.mine = jnp.stack([2 * x + 1 - b2, 2 * x + b2, 1 - b2, b2])

    def general(self, held):
        me = lax.axis_index("dp")
        bits = [1 << i for i in range(self.size.bit_length() - 1)]
        for bit in bits:
            mine = (me & bit) != 0
            half = held.shape[0] // 2
            other = lax.dynamic_slice_in_dim(held, jnp.where(mine, 0, half), half, 0)
            own = lax.dynamic_slice_in_dim(held, jnp.where(mine, half, 0), half, 0)
            held = (own.astype(f32) + swap(other, "dp", bit).astype(f32)).astype(bf16)
        for bit in reversed(bits):
            mine = (me & bit) != 0
            other = swap(held, "dp", bit)
            held = jnp.where(
                mine,
                jnp.concatenate([other, held], axis=0),
                jnp.concatenate([held, other], axis=0),
            )
        half = held.shape[0] // 2
        return held[:half], held[half:]

    def finish(self, send, keep):
        held = keep.astype(f32) + swap(send, "dp", 2).astype(f32)
        half = held.shape[0] // 2
        b4 = self.bit[2]
        other = lax.dynamic_slice_in_dim(held, (1 - b4) * half, half, 0).astype(bf16)
        own = lax.dynamic_slice_in_dim(held, b4 * half, half, 0)
        own = (own + swap(other, "dp", 4).astype(f32)).astype(bf16)
        two = jnp.concatenate([own, swap(own, "dp", 4)], axis=0)
        four = jnp.concatenate([two, swap(two, "dp", 2)], axis=0)
        return four, swap(four, "dp", 1)

    def product(self, xs, gs):
        if self.size != 8:
            first = weight_half(xs, gs, jnp.array([0, 1], jnp.int32))
            other = weight_half(xs, gs, jnp.array([2, 3], jnp.int32))
            return self.general(jnp.concatenate([first, other], axis=0))
        got = swap(weight_half(xs, gs, self.there), "dp", 1)
        send, keep = weight_half(xs, gs, self.mine, got)
        return self.finish(send, keep)

    def whole(self, value):
        if self.size != 8:
            return self.general(value.astype(bf16))
        half = value.shape[0] // 2
        x, b2, _ = self.bit
        other = lax.dynamic_slice_in_dim(value, (1 - x) * half, half, 0).astype(bf16)
        own = lax.dynamic_slice_in_dim(value, x * half, half, 0)
        held = own.astype(f32) + swap(other, "dp", 1).astype(f32)
        half = half // 2
        send = lax.dynamic_slice_in_dim(held, (1 - b2) * half, half, 0).astype(bf16)
        keep = lax.dynamic_slice_in_dim(held, b2 * half, half, 0)
        return self.finish(send, keep)


def out_weight_body(xa_ref, xb_ref, g0, g1, g2, g3, out_ref):
    acc = 0.0
    for j, g_ref in enumerate((g0, g1, g2, g3)):
        acc = acc + tn(piece_of((xa_ref, xb_ref), j), g_ref[...])
    out_ref[...] = acc.astype(bf16)


def per_device(
    tokens, segment_ids, gsd_index, enc_qkv, enc_qv_bias, enc_out_proj, enc_up, enc_up_bias,
    enc_down, enc_out_bias, enc_gain, enc_norm_bias, embed_weight, embed_bias, dec_qkv,
    dec_qv_bias, dec_out_proj, dec_up, dec_up_bias, dec_down, dec_out_bias, dec_gain,
    dec_norm_bias, cotangent,
):
    n, width = tokens.shape
    rows, length = segment_ids.shape
    assert rows == 4 and n == length == 256 and lax.axis_size("mp") == 4
    share, ff = enc_qkv.shape[2], enc_up.shape[1]
    dwidth, dff = cotangent.shape[1], dec_up.shape[1] * 4
    dshare = dwidth // 4
    heads = share // (width // HEADS)
    scale = (width // HEADS) ** -0.5
    slot = lax.axis_index("mp").astype(jnp.int32)
    at = slot.reshape(1)
    dp = DpSum()

    def waves(size):
        half = size // 2
        return jnp.power(10000.0, -jnp.arange(half, dtype=f32) / half).reshape(1, half)

    stream, normed, pos, bias = run(
        start_body,
        [shaped((n, width), f32), shaped((n, width), bf16), shaped((n, dwidth), f32), shaped((4, n, n), f32)],
        (at, segment_ids, gsd_index, tokens, enc_gain, enc_norm_bias, embed_bias.reshape(1, -1), waves(width), waves(dwidth)),
        smem=1,
    )
    x = gather_blocks(normed)

    def attention(first, xa, xb):
        return run(
            functools.partial(attn_body, first, scale, heads),
            [shaped((2, n, share), bf16)] * 3
            + [shaped((2, heads, n, n), bf16), shaped((2, n, share), bf16)]
            + [shaped((n, width), bf16)] * 2,
            (xa, xb, bias, enc_qkv, enc_qv_bias, enc_out_proj),
            flops=2 * 2 * n * width * 4 * share,
        )

    qa, ka, va, pa, mixa, part0, part1 = attention(0, x[0], x[1])
    qb, kb, vb, pb, mixb, part2, part3 = attention(2, x[2], x[3])
    middle, normed2 = run(
        mid_body,
        [shaped((n, width), f32), shaped((n, width), bf16)],
        (stream, *scatter_blocks([part0, part1, part2, part3]), enc_out_bias, enc_gain, enc_norm_bias),
    )
    y = gather_blocks(normed2)

    def feed(xa, xb):
        return run(
            mlp_body,
            [shaped((2, n, ff), bf16)] * 2 + [shaped((n, width), bf16)] * 2,
            (xa, xb, enc_up, enc_up_bias.reshape(1, -1), enc_down),
            flops=2 * 2 * n * width * 2 * ff,
        )

    hida, dga, part0, part1 = feed(y[0], y[1])
    hidb, dgb, part2, part3 = feed(y[2], y[3])
    terms = scatter_blocks([part0, part1, part2, part3])

    wide = jnp.concatenate([dec_up, dec_down, dec_out_proj], axis=0)
    thin = jnp.concatenate([dec_qkv.reshape(3 * dwidth, dshare), embed_weight], axis=0)
    wides, thins = gather_blocks(wide), gather_blocks(thin)
    small = gather_blocks(jnp.concatenate([dec_qv_bias.reshape(-1), dec_up_bias]).reshape(1, -1))
    qv_full = jnp.concatenate([b[:, : 2 * dshare].reshape(2, dshare) for b in small], axis=1)
    upb_full = jnp.concatenate([b[:, 2 * dshare :] for b in small], axis=1)
    dheads = DHEADS
    low = lambda *dims: shaped(dims, bf16)
    (enc_low, output, x1, x2, hid, mix, gp, gm, g3, gz, ge_low, ge, dec_sums) = run(
        decoder_body,
        [low(n, width), shaped((n, dwidth), f32), low(n, dwidth), low(n, dwidth), low(n, dff), low(n, dwidth),
         low(n, dff), low(n, dwidth), low(n, 3 * dwidth), low(n, dwidth), low(n, width), shaped((n, width), f32),
         shaped((8, width), f32)],
        (at, middle, *terms, enc_out_bias, *wides, *thins, qv_full, upb_full, pos, bias, dec_out_bias, dec_gain,
         dec_norm_bias, cotangent),
        smem=1,
        scratch=[
            pltpu.VMEM((3, dwidth, dwidth), bf16), pltpu.VMEM((dwidth, dwidth), bf16),
            pltpu.VMEM((width, dwidth), bf16), pltpu.VMEM((dheads, n, n), bf16),
            pltpu.VMEM((n, dff), bf16), pltpu.VMEM((3, n, dwidth), bf16), pltpu.VMEM((n, dwidth), f32),
        ],
        limit=56,
        flops=4 * n * 12 * dwidth * dwidth,
    )
    g = gather_blocks(ge_low)
    chunk_w, chunk_t = 9 * dwidth // 4, 3 * dwidth + width
    ws, ts, wk, tk = run(
        decoder_weights_body,
        [low(2, chunk_w, dwidth), low(2, chunk_t, dshare)] * 2,
        (x1, x2, hid, mix, gp, gm, g3, gz, enc_low, cotangent),
        limit=48,
        flops=2 * n * 12 * dwidth * dwidth,
    )

    def feed_back(ga, gb, slope):
        return run(
            mlp_back_body,
            [low(2, n, ff), shaped((1, ff), f32), low(n, width), low(n, width)],
            (ga, gb, slope, enc_up, enc_down),
            flops=2 * 2 * n * width * 2 * ff,
        )

    gpa, upa, part0, part1 = feed_back(g[0], g[1], dga)
    gpb, upb, part2, part3 = feed_back(g[2], g[3], dgb)
    grad_down = dp.product([hida, hidb], g)
    grad_up = dp.product(y, [gpa, gpb])
    grad_middle, gm_low, pack = run(
        mlp_end_body,
        [shaped((n, width), f32), low(n, width), shaped((16, width), f32)],
        (at, ge, *scatter_blocks([part0, part1, part2, part3]), middle, enc_gain, upa, upb, dec_sums),
        smem=1,
    )
    m = gather_blocks(gm_low)
    out_full = run(
        out_weight_body, [low(share, width)], (mixa, mixb, *m), flops=2 * 4 * n * share * width
    )[0]

    def attention_back(ga, gb, q, k, v, p):
        return run(
            functools.partial(attn_back_body, scale, heads),
            [low(2, n, 3 * share), shaped((2, share), f32), low(n, width), low(n, width)],
            (ga, gb, q, k, v, p, enc_qkv, enc_out_proj),
            flops=2 * 2 * n * width * 4 * share,
        )

    g3a, sa, part0, part1 = attention_back(m[0], m[1], qa, ka, va, pa)
    g3b, sb, part2, part3 = attention_back(m[2], m[3], qb, kb, vb, pb)
    grad_qkv = dp.product(x, [g3a, g3b])
    grad_tokens, last = run(
        last_body,
        [shaped((n, width), f32), shaped((8, width), f32)],
        (at, grad_middle, *scatter_blocks([part0, part1, part2, part3]), stream, enc_gain, sa, sb),
        smem=1,
    )

    def over_mp(kept, sent):
        near = swap(sent, "mp", 1).astype(f32)
        far = swap((kept[1].astype(f32) + near[1]).astype(bf16), "mp", 2)
        return kept[0].astype(f32) + near[0] + far.astype(f32)

    wide_sum = dp.whole(over_mp(wk, ws))
    thin_sum = dp.whole(over_mp(tk, ts))
    out_sum = dp.whole(out_full)
    e_down = spread(*grad_down, dp.place, [(ff, width)], [(0, None, 0, ff // 8, 0, width)])[0]
    e_up = spread(*grad_up, dp.place, [(width, ff)], [(0, None, 0, width // 8, 0, ff)])[0]
    e_out = spread(*out_sum, dp.place, [(share, width)], [(0, None, 0, share // 8, 0, width)])[0]
    e_qkv = spread(
        *grad_qkv, dp.place, [(3, width, share)],
        [(0, c, 0, width // 8, c * share, share) for c in range(3)],
    )[0]
    part = dwidth // 8
    d_up, d_down, d_out = spread(
        *wide_sum, dp.place, [(dwidth, dwidth), (dwidth, dwidth), (dshare, dwidth)],
        [(0, None, 0, part, 0, dwidth), (1, None, part, part, 0, dwidth), (2, None, 2 * part, dshare // 8, 0, dwidth)],
    )
    d_qkv, e_embed = spread(
        *thin_sum, dp.place, [(3, dwidth, dshare), (width, dshare)],
        [(0, c, c * part, part, 0, dshare) for c in range(3)] + [(1, None, 3 * part, width // 8, 0, dshare)],
    )
    pack = sum_over_all(pack)
    last = sum_over_all(last)

    def own(whole, size):
        return lax.dynamic_slice_in_dim(whole, slot * size, size, whole.ndim - 1)

    dec = pack[8:]
    return (
        output,
        grad_tokens,
        e_qkv,
        own(last[2:4], share),
        e_out,
        e_up,
        own(pack[4:8].reshape(-1), ff),
        e_down,
        jnp.concatenate([pack[0:1], dec[0:1]], axis=0),
        jnp.concatenate([last[0:1], pack[1:2]], axis=0),
        jnp.concatenate([last[1:2], pack[2:3]], axis=0),
        e_embed,
        dec[3, dwidth:],
        d_qkv,
        own(dec[4:6, dwidth:], dshare),
        d_out,
        d_up,
        own(dec[6:8].reshape(-1), dff // 4),
        d_down,
        dec[1:3, :dwidth],
        dec[1:3, dwidth:],
        dec[3:5, :dwidth],
    )


def solution(mesh):
    return jax.shard_map(
        per_device,
        mesh=mesh,
        in_specs=(
            P(("dp", "mp"), None),
            P("dp", None),
            P("dp", None),
            P(None, None, "mp"),
            P(None, "mp"),
            P("mp", None),
            P(None, "mp"),
            P("mp"),
            P("mp", None),
            P(),
            P(),
            P(),
            P(None, "mp"),
            P(),
            P(None, None, "mp"),
            P(None, "mp"),
            P("mp", None),
            P(None, "mp"),
            P("mp"),
            P("mp", None),
            P(),
            P(),
            P(),
            P(("dp", "mp"), None),
        ),
        out_specs=(
            P(("dp", "mp"), None),
            P(("dp", "mp"), None),
            P(None, None, "mp"),
            P(None, "mp"),
            P("mp", None),
            P(None, "mp"),
            P("mp"),
            P("mp", None),
            P(),
            P(),
            P(),
            P(None, "mp"),
            P(),
            P(None, None, "mp"),
            P(None, "mp"),
            P("mp", None),
            P(None, "mp"),
            P("mp"),
            P("mp", None),
            P(),
            P(),
            P(),
        ),
        check_vma=False,
    )
```

```python
import functools
import math

import jax
import jax.numpy as jnp
from jax import lax
from jax.experimental import pallas as pl
from jax.experimental.pallas import tpu as pltpu
from jax.sharding import PartitionSpec as P

HEADS = 16
DHEADS = 16
norm_eps = 1e-06
f32 = jnp.float32
bf16 = jnp.bfloat16
MIB = 1 << 20
VMEM = pl.BlockSpec(memory_space=pltpu.VMEM)
SMEM = pl.BlockSpec(memory_space=pltpu.SMEM)


def shaped(dims, kind):
    return jax.ShapeDtypeStruct(dims, kind)


class Chain:
    def __init__(self):
        self.last = None

    def __call__(self, body, outs, args, smem=0, scratch=(), limit=16, prefetch=None, grid=None, specs=None):
        args = list(args)
        extra = self.last is not None
        lead = smem if prefetch is None else 1
        inner = body
        if extra:
            count = len(args) + (prefetch is not None)

            def inner(*refs):
                return body(*refs[:count], *refs[count + 1 :])

            args.append(self.last)
        tail = [pl.BlockSpec(memory_space=pl.ANY)] * extra
        params = pltpu.CompilerParams(vmem_limit_bytes=limit * MIB)
        cost = pl.CostEstimate(flops=1, bytes_accessed=1, transcendentals=0)
        if prefetch is None:
            got = pl.pallas_call(
                inner,
                out_shape=outs,
                in_specs=[SMEM] * smem + [VMEM] * (len(args) - smem - extra) + tail,
                out_specs=[VMEM] * len(outs),
                scratch_shapes=scratch,
                compiler_params=params,
                cost_estimate=cost,
            )(*args)
        else:
            got = pl.pallas_call(
                inner,
                out_shape=outs,
                grid_spec=pltpu.PrefetchScalarGridSpec(
                    num_scalar_prefetch=1, grid=grid, in_specs=specs[0] + tail, out_specs=specs[1]
                ),
                compiler_params=params,
                cost_estimate=cost,
            )(prefetch, *args)
        self.last = min(got, key=lambda g: g.size * g.dtype.itemsize)
        return got


def nn(a, b):
    return lax.dot_general(a, b, (((1,), (0,)), ((), ())), preferred_element_type=f32)


def nt(a, b):
    return lax.dot_general(a, b, (((1,), (1,)), ((), ())), preferred_element_type=f32)


def tn(a, b):
    return lax.dot_general(a, b, (((0,), (0,)), ((), ())), preferred_element_type=f32)


def swap(value, axis, mask):
    size = lax.axis_size(axis)
    return lax.ppermute(value, axis, [(i, i ^ mask) for i in range(size)])


def norm_parts(values):
    average = jnp.mean(values, axis=-1, keepdims=True)
    centred = values - average
    variance = jnp.mean(centred * centred, axis=-1, keepdims=True)
    scale = lax.rsqrt(variance + norm_eps)
    return centred * scale, scale


def norm_back(normal, scale, gain, grad):
    wide = grad * gain
    one = jnp.mean(wide, axis=-1, keepdims=True)
    two = jnp.mean(wide * normal, axis=-1, keepdims=True)
    return scale * (wide - one - normal * two)


def gelu_both(v):
    slope = math.sqrt(2.0 / math.pi)
    square = v * v
    t = jnp.tanh(slope * v * (1.0 + 0.044715 * square))
    half = 0.5 * (1.0 + t)
    return v * half, half + 0.5 * slope * v * (1.0 - t * t) * (1.0 + 3.0 * 0.044715 * square)


def sin_cos(x):
    turn = jnp.floor(x * (2.0 / math.pi) + 0.5)
    r = ((x - turn * 1.5703125) - turn * 4.837512969970703125e-4) - turn * 7.54978995489188216e-8
    z = r * r
    s = r + r * z * (-1.6666654611e-1 + z * (8.3321608736e-3 + z * -1.9515295891e-4))
    c = 1.0 - 0.5 * z + z * z * (
        4.166664568298827e-2 + z * (-1.388731625493765e-3 + z * 2.443315711809948e-5)
    )
    quarter = turn.astype(jnp.int32)
    odd = (quarter & 1) != 0
    sine = jnp.where(odd, c, s)
    cosine = jnp.where(odd, s, c)
    sine = jnp.where((quarter & 2) != 0, -sine, sine)
    cosine = jnp.where(((quarter + 1) & 2) != 0, -cosine, cosine)
    return sine, cosine


def head_masks(heads):
    size = 256 // heads
    lane = lax.broadcasted_iota(jnp.int32, (1, 256), 1)
    return [
        jnp.where((lane >= h * size) & (lane < (h + 1) * size), 1.0, 0.0).astype(bf16)
        for h in range(heads)
    ]


def attend(q, k, v, bias, heads, scale, keep):
    size = 256 // heads
    vt = v.astype(f32).T.astype(bf16)
    mixes = []
    for h, mask in enumerate(head_masks(heads)):
        s = nt(k, q * mask) + bias
        top = jnp.max(s, axis=0, keepdims=True)
        p = jnp.exp2((s - top) * (scale * math.log2(math.e)))
        total = jnp.sum(p, axis=0, keepdims=True)
        p = (p * (1.0 / total)).astype(bf16)
        keep(h, p)
        mixes.append(nn(vt[h * size : (h + 1) * size], p))
    return jnp.concatenate(mixes, axis=0).T


def attend_back(q, k, v, gm, probs, heads, scale):
    size = 256 // heads
    kt = k.astype(f32).T.astype(bf16)
    gq, gk, gv = [], 0.0, 0.0
    for h, mask in enumerate(head_masks(heads)):
        gmh = gm * mask
        p = probs(h)
        wide = p.astype(f32)
        t = wide * nt(v, gmh)
        gs = (t - wide * jnp.sum(t, axis=0, keepdims=True)).astype(bf16)
        gk = gk + nn(gs, q * mask)
        gv = gv + nn(p, gmh)
        gq.append(nn(kt[h * size : (h + 1) * size], gs))
    return jnp.concatenate(gq, axis=0).T * scale, gk * scale, gv


def start_body(slot_ref, seg_ref, gsd_ref, tokens_ref, gain_ref, shift_ref, eb_ref, wf_ref, nf_ref,
               stream_ref, normed_ref, pos_ref, bias_a_ref, bias_b_ref):
    slot = slot_ref[0]
    n = seg_ref.shape[1]
    place = None
    for j in range(4):
        across = jnp.broadcast_to(seg_ref[pl.ds(slot ^ j, 1), :].astype(f32), (n, n))
        down = across.T
        same = across == down
        (bias_a_ref, bias_b_ref)[j // 2][j % 2] = jnp.where(same, 0.0, -1e30)
        if j == 0:
            earlier = lax.broadcasted_iota(jnp.int32, (n, n), 1) < lax.broadcasted_iota(
                jnp.int32, (n, n), 0
            )
            rank = jnp.sum(jnp.where(same & earlier, 1.0, 0.0), axis=1, keepdims=True)
            index = jnp.broadcast_to(gsd_ref[pl.ds(slot, 1), :].astype(f32), (n, n)).T[:, :1]
            place = rank * (0.5 + 0.25 * index)
    half = wf_ref.shape[1]
    sine, cosine = sin_cos(place * wf_ref[...])
    stream_ref[:, :half] = tokens_ref[:, :half].astype(f32) + sine
    stream_ref[:, half:] = tokens_ref[:, half:].astype(f32) + cosine
    normal, _ = norm_parts(stream_ref[...])
    normed_ref[...] = (normal * gain_ref[0:1] + shift_ref[0:1]).astype(bf16)
    sine, cosine = sin_cos(place * nf_ref[...])
    half = nf_ref.shape[1]
    pos_ref[:, :half] = sine + eb_ref[:, :half]
    pos_ref[:, half:] = cosine + eb_ref[:, half:]


def attn_body(scale, heads, xa_ref, xb_ref, bias_ref, w_ref, qvb_ref, o_ref,
              q_ref, k_ref, v_ref, p_ref, mix_ref, pa_ref, pb_ref):
    for r, (x_ref, part_ref) in enumerate(((xa_ref, pa_ref), (xb_ref, pb_ref))):
        x = x_ref[...]
        q = (nn(x, w_ref[0]) + qvb_ref[0:1]).astype(bf16)
        k = nn(x, w_ref[1]).astype(bf16)
        v = (nn(x, w_ref[2]) + qvb_ref[1:2]).astype(bf16)
        q_ref[r], k_ref[r], v_ref[r] = q, k, v

        def keep(h, p):
            p_ref[r, h] = p

        mix = attend(q, k, v, bias_ref[r], heads, scale, keep).astype(bf16)
        mix_ref[r] = mix
        part_ref[...] = nn(mix, o_ref[...]).astype(bf16)


def attn_back_body(scale, heads, ga_ref, gb_ref, q_ref, k_ref, v_ref, p_ref, w_ref, o_ref,
                   g3_ref, sums_ref, pa_ref, pb_ref):
    total_q, total_v = 0.0, 0.0
    for r, (g_ref, part_ref) in enumerate(((ga_ref, pa_ref), (gb_ref, pb_ref))):
        gm = nt(g_ref[...], o_ref[...]).astype(bf16)
        gq, gk, gv = attend_back(
            q_ref[r], k_ref[r], v_ref[r], gm, lambda h: p_ref[r, h], heads, scale
        )
        total_q = total_q + jnp.sum(gq, axis=0, keepdims=True)
        total_v = total_v + jnp.sum(gv, axis=0, keepdims=True)
        acc = 0.0
        for c, g in enumerate((gq, gk, gv)):
            low = g.astype(bf16)
            g3_ref[r, :, c * 256 : (c + 1) * 256] = low
            acc = acc + nt(low, w_ref[c])
        part_ref[...] = acc.astype(bf16)
    sums_ref[0:1] = total_q
    sums_ref[1:2] = total_v


def mid_body(stream_ref, p_ref, near_ref, far_ref, ob_ref, gain_ref, shift_ref, mid_ref, normed_ref):
    total = p_ref[...].astype(f32) + near_ref[...].astype(f32) + far_ref[...].astype(f32)
    middle = stream_ref[...] + total + ob_ref[0:1]
    mid_ref[...] = middle
    normal, _ = norm_parts(middle)
    normed_ref[...] = (normal * gain_ref[1:2] + shift_ref[1:2]).astype(bf16)


def mlp_body(xa_ref, xb_ref, up_ref, ub_ref, down_ref, hid_ref, dg_ref, pa_ref, pb_ref):
    width = up_ref.shape[1]
    for r, (x_ref, part_ref) in enumerate(((xa_ref, pa_ref), (xb_ref, pb_ref))):
        x = x_ref[...]
        for c in range(0, width, 256):
            cut = slice(c, c + 256)
            hidden, slope = gelu_both(nn(x, up_ref[:, cut]) + ub_ref[:, cut])
            hid_ref[r, :, cut] = hidden.astype(bf16)
            dg_ref[r, :, cut] = slope.astype(bf16)
        hidden = hid_ref[r]
        for c in range(0, down_ref.shape[1], 512):
            cut = slice(c, c + 512)
            part_ref[:, cut] = nn(hidden, down_ref[:, cut]).astype(bf16)


def mlp_back_body(ga_ref, gb_ref, dg_ref, up_ref, down_ref, gp_ref, sums_ref, pa_ref, pb_ref):
    width = up_ref.shape[1]
    for r, (g_ref, part_ref) in enumerate(((ga_ref, pa_ref), (gb_ref, pb_ref))):
        g = g_ref[...]
        for c in range(0, width, 256):
            cut = slice(c, c + 256)
            grad = nt(g, down_ref[cut]) * dg_ref[r, :, cut].astype(f32)
            gp_ref[r, :, cut] = grad.astype(bf16)
            total = jnp.sum(grad, axis=0, keepdims=True)
            sums_ref[:, cut] = total if r == 0 else sums_ref[:, cut] + total
        gp = gp_ref[r]
        for c in range(0, up_ref.shape[0], 512):
            cut = slice(c, c + 512)
            part_ref[:, cut] = nt(gp, up_ref[cut]).astype(bf16)


def mlp_end_body(slot_ref, ge_ref, p_ref, near_ref, far_ref, mid_ref, gain_ref, ua_ref, ub_ref, dec_ref,
                 gmid_ref, gm_ref, pack_ref):
    slot = slot_ref[0]
    grad = p_ref[...].astype(f32) + near_ref[...].astype(f32) + far_ref[...].astype(f32)
    normal, scale = norm_parts(mid_ref[...])
    gmid = ge_ref[...] + norm_back(normal, scale, gain_ref[1:2], grad)
    gmid_ref[...] = gmid
    gm_ref[...] = gmid.astype(bf16)
    pack_ref[...] = jnp.zeros(pack_ref.shape, f32)
    pack_ref[0:1] = jnp.sum(gmid, axis=0, keepdims=True)
    pack_ref[1:2] = jnp.sum(grad * normal, axis=0, keepdims=True)
    pack_ref[2:3] = jnp.sum(grad, axis=0, keepdims=True)
    pack_ref[pl.ds(4 + slot, 1), :] = ua_ref[...] + ub_ref[...]
    pack_ref[8:16] = dec_ref[...]


def last_body(slot_ref, gmid_ref, p_ref, near_ref, far_ref, stream_ref, gain_ref, sa_ref, sb_ref, mid_ref,
              gtok_ref, pack_ref):
    slot = slot_ref[0]
    grad = p_ref[...].astype(f32) + near_ref[...].astype(f32) + far_ref[...].astype(f32)
    normal, scale = norm_parts(stream_ref[...])
    gtok_ref[...] = gmid_ref[...] + norm_back(normal, scale, gain_ref[0:1], grad)
    pack_ref[:16] = mid_ref[...]
    pack_ref[16:] = jnp.zeros((8, pack_ref.shape[1]), f32)
    pack_ref[16:17] = jnp.sum(grad * normal, axis=0, keepdims=True)
    pack_ref[17:18] = jnp.sum(grad, axis=0, keepdims=True)
    share = sa_ref.shape[1]
    place = pl.ds(pl.multiple_of(slot * share, share), share)
    pack_ref[18:20, place] = sa_ref[...] + sb_ref[...]


def decoder_body(slot_ref, mid_ref, p_ref, near_ref, far_ref, eob_ref, own_ref, by_ref, pf_ref, pn_ref,
                 qvb_ref, upb_ref, pos_ref, bias_ref, dob_ref, dgain_ref, dnb_ref, cot_ref,
                 encl_ref, out_ref, x1_ref, x2_ref, hid_ref, mix_ref, gp_ref, gm_ref, g3_ref, gz_ref,
                 gel_ref, ge_ref, sums_ref,
                 wfar, wnear, wqkv, wout, wemb, pt, dg, qkv, wide):
    slot, home = slot_ref[0], slot_ref[1]
    wides = (own_ref, by_ref, wfar, wnear)
    width = cot_ref.shape[1]
    block = width // 4
    heads = DHEADS * 256 // width
    groups = width // 256
    scale = (width // DHEADS) ** -0.5

    def place(j, base=0):
        return pl.ds(pl.multiple_of(base + (slot ^ j) * block, block), block)

    chunk = pf_ref.shape[0] // 8
    for i in range(8):
        rows = pl.ds(pl.multiple_of((home ^ i) * chunk, chunk), chunk)
        wfar[rows] = pf_ref[i * chunk : (i + 1) * chunk]
        wnear[rows] = pn_ref[i * chunk : (i + 1) * chunk]
    for j in range(4):
        cut = slice(j * block, (j + 1) * block)
        wout[cut] = wides[j][2 * width : 2 * width + block]
        top = 2 * width + block
        for c in range(3):
            wqkv[c, :, cut] = wides[j][top : top + width, c * block : (c + 1) * block]
        wemb[:width, cut] = wides[j][top : top + width, 3 * block :]
        for c in range(4):
            wemb[width + c * block : width + (c + 1) * block, cut] = (
                wides[j][top + width : top + width + block, c * block : (c + 1) * block]
            )
    encoded = mid_ref[...] + eob_ref[1:2]
    encoded = encoded + p_ref[...].astype(f32) + near_ref[...].astype(f32) + far_ref[...].astype(f32)
    encl_ref[...] = encoded.astype(bf16)
    embedded = nn(encl_ref[...], wemb[...])
    for j in range(4):
        wide[:, place(j)] = embedded[:, j * block : (j + 1) * block]
    stream = wide[...] + pos_ref[...]
    normal1, scale1 = norm_parts(stream)
    x1_ref[...] = (normal1 * dgain_ref[0:1] + dnb_ref[0:1]).astype(bf16)
    x1 = x1_ref[...]
    qkv[0] = (nn(x1, wqkv[0]) + qvb_ref[0:1]).astype(bf16)
    qkv[1] = nn(x1, wqkv[1]).astype(bf16)
    qkv[2] = (nn(x1, wqkv[2]) + qvb_ref[1:2]).astype(bf16)
    bias = bias_ref[0]
    for g in range(groups):
        cut = slice(g * 256, (g + 1) * 256)

        def keep(h, p):
            pt[g * heads + h] = p

        mix_ref[:, cut] = attend(
            qkv[0, :, cut], qkv[1, :, cut], qkv[2, :, cut], bias, heads, scale, keep
        ).astype(bf16)
    middle = stream + nn(mix_ref[...], wout[...]) + dob_ref[0:1]
    normal2, scale2 = norm_parts(middle)
    x2_ref[...] = (normal2 * dgain_ref[1:2] + dnb_ref[1:2]).astype(bf16)
    x2 = x2_ref[...]
    result = middle + dob_ref[1:2]
    for j in range(4):
        cut = slice(j * width, (j + 1) * width)
        hidden, slope = gelu_both(nn(x2, wides[j][:width]) + upb_ref[:, cut])
        hid_ref[:, cut] = hidden.astype(bf16)
        dg[:, cut] = slope.astype(bf16)
        result = result + nn(hid_ref[:, cut], wides[j][width : 2 * width])
    out_ref[...] = result

    cot = cot_ref[...]
    grad = 0.0
    sums_ref[...] = jnp.zeros(sums_ref.shape, f32)
    for j in range(4):
        cut = slice(j * width, (j + 1) * width)
        pre = nt(cot, wides[j][width : 2 * width]) * dg[:, cut].astype(f32)
        gp_ref[:, cut] = pre.astype(bf16)
        block_sum = jnp.sum(pre, axis=0, keepdims=True)
        at = slot ^ j
        sums_ref[pl.ds(6 + (at >> 1), 1), pl.ds(pl.multiple_of((at & 1) * width, width), width)] = (
            block_sum
        )
        grad = grad + nt(gp_ref[:, cut], wides[j][:width])
    cotf = cot.astype(f32)
    gmid = cotf + norm_back(normal2, scale2, dgain_ref[1:2], grad)
    gm_ref[...] = gmid.astype(bf16)
    sums_ref[1:2, :width] = jnp.sum(gmid, axis=0, keepdims=True)
    sums_ref[2:3, :width] = jnp.sum(cotf, axis=0, keepdims=True)
    sums_ref[2:3, width:] = jnp.sum(grad * normal2, axis=0, keepdims=True)
    sums_ref[4:5, :width] = jnp.sum(grad, axis=0, keepdims=True)
    gmix = nt(gm_ref[...], wout[...]).astype(bf16)
    grad = 0.0
    for g in range(groups):
        cut = slice(g * 256, (g + 1) * 256)
        three = attend_back(
            qkv[0, :, cut], qkv[1, :, cut], qkv[2, :, cut], gmix[:, cut],
            lambda h: pt[g * heads + h], heads, scale,
        )
        for c, part in enumerate(three):
            begin = c * width + g * 256
            low = part.astype(bf16)
            g3_ref[:, begin : begin + 256] = low
            grad = grad + nt(low, wqkv[c, :, cut])
        for c, row, base in ((0, 4, width), (2, 5, width)):
            total = jnp.sum(three[c], axis=0, keepdims=True)
            for i in range(256 // block):
                sums_ref[row : row + 1, place(g * (256 // block) + i, base)] = (
                    total[:, i * block : (i + 1) * block]
                )
    gstream = gmid + norm_back(normal1, scale1, dgain_ref[0:1], grad)
    sums_ref[3:4, width:] = jnp.sum(gstream, axis=0, keepdims=True)
    sums_ref[1:2, width:] = jnp.sum(grad * normal1, axis=0, keepdims=True)
    sums_ref[3:4, :width] = jnp.sum(grad, axis=0, keepdims=True)
    wide[...] = gstream
    for j in range(4):
        gz_ref[:, j * block : (j + 1) * block] = wide[:, place(j)].astype(bf16)
    ge = nt(gz_ref[...], wemb[...])
    ge_ref[...] = ge
    gel_ref[...] = ge.astype(bf16)
    sums_ref[0:1] = jnp.sum(ge, axis=0, keepdims=True)


def decoder_weights_body(x1_ref, x2_ref, hid_ref, mix_ref, gp_ref, gm_ref, g3_ref, gz_ref, encl_ref, cot_ref,
                         ws_ref, ts_ref, wk_ref, tk_ref):
    width = cot_ref.shape[1]
    block = width // 4
    cot, gm, x2 = cot_ref[...], gm_ref[...], x2_ref[...]
    piece, thin = width // 8, block // 8
    step = 2 * piece + thin
    tall = encl_ref.shape[1] // 8
    jump = 3 * piece + tall

    def to(j):
        return (ws_ref, ts_ref) if j % 2 else (wk_ref, tk_ref)

    for j in (1, 3, 0, 2):
        w, t = to(j)
        i = j // 2
        cut = slice(j * width, (j + 1) * width)
        up = tn(x2, gp_ref[:, cut]).astype(bf16)
        down = tn(hid_ref[:, cut], cot).astype(bf16)
        out = tn(mix_ref[:, j * block : (j + 1) * block], gm).astype(bf16)
        for c in range(8):
            w[i, c * step : c * step + piece] = up[c * piece : (c + 1) * piece]
            w[i, c * step + piece : c * step + 2 * piece] = down[c * piece : (c + 1) * piece]
            w[i, c * step + 2 * piece : (c + 1) * step] = out[c * thin : (c + 1) * thin]
    x1 = x1_ref[...]
    for k in range(3):
        full = tn(x1, g3_ref[:, k * width : (k + 1) * width]).astype(bf16)
        for j in range(4):
            t = to(j)[1]
            for c in range(8):
                t[j // 2, c * jump + k * piece : c * jump + (k + 1) * piece] = (
                    full[c * piece : (c + 1) * piece, j * block : (j + 1) * block]
                )
    full = tn(encl_ref[...], gz_ref[...]).astype(bf16)
    for j in range(4):
        t = to(j)[1]
        for c in range(8):
            t[j // 2, c * jump + 3 * piece : (c + 1) * jump] = (
                full[c * tall : (c + 1) * tall, j * block : (j + 1) * block]
            )


def pack_body(home_ref, up_ref, down_ref, out_ref, qkv_ref, emb_ref, all_ref, piece_ref):
    width, block = up_ref.shape[1], out_ref.shape[0]
    all_ref[:width] = up_ref[...]
    all_ref[width : 2 * width] = down_ref[...]
    top = 2 * width + block
    all_ref[2 * width : top] = out_ref[...]
    for c in range(3):
        all_ref[top : top + width, c * block : (c + 1) * block] = qkv_ref[c]
    all_ref[top : top + width, 3 * block :] = emb_ref[:width]
    for c in range(4):
        all_ref[top + width :, c * block : (c + 1) * block] = (
            emb_ref[width + c * block : width + (c + 1) * block]
        )
    rows = piece_ref.shape[0]
    piece_ref[...] = all_ref[pl.ds(pl.multiple_of(home_ref[0] * rows, rows), rows)]


def join_body(a_ref, b_ref, out_ref):
    rows = a_ref.shape[0]
    out_ref[:rows] = a_ref[...]
    out_ref[rows:] = b_ref[...]


def add_body(a_ref, b_ref, out_ref):
    out_ref[...] = (a_ref[...].astype(f32) + b_ref[...].astype(f32)).astype(out_ref.dtype)


def halve_body(bit_ref, *refs):
    ins, (send_ref, keep_ref) = refs[:-2], refs[-2:]
    half = send_ref.shape[0]
    bit = bit_ref[0]
    for ref, which in ((send_ref, 1 - bit), (keep_ref, bit)):
        rows = pl.ds(pl.multiple_of(which * half, half), half)
        total = ins[0][rows].astype(f32)
        for other in ins[1:]:
            total = total + other[rows].astype(f32)
        ref[...] = total.astype(bf16)


def pair_add_body(kept_ref, near_ref, out_ref):
    out_ref[...] = (kept_ref[1].astype(f32) + near_ref[1].astype(f32)).astype(bf16)


def three_halve_body(bit_ref, kept_ref, near_ref, far_ref, send_ref, keep_ref):
    half = send_ref.shape[0]
    bit = bit_ref[0]
    for ref, which in ((send_ref, 1 - bit), (keep_ref, bit)):
        rows = pl.ds(pl.multiple_of(which * half, half), half)
        total = kept_ref[0, rows].astype(f32) + near_ref[0, rows].astype(f32)
        ref[...] = (total + far_ref[rows].astype(f32)).astype(bf16)


def piece_of(refs, j):
    if len(refs) == 4:
        return refs[j][...]
    return refs[j // 2][j % 2]


def first_half_body(nx, ng, pick_ref, *refs):
    xs, gs, out_ref = refs[:nx], refs[nx : nx + ng], refs[nx + ng]
    acc = 0.0
    for j in range(4):
        acc = acc + tn(piece_of(xs, j), piece_of(gs, j))
    out_ref[...] = acc.astype(bf16)


def other_half_body(nx, ng, pick_ref, *refs):
    xs, gs, add_ref, send_ref, keep_ref = refs[:nx], refs[nx : nx + ng], *refs[nx + ng :]
    acc = add_ref[...].astype(f32)
    for j in range(4):
        acc = acc + tn(piece_of(xs, j), piece_of(gs, j))
    low = acc.astype(bf16)

    @pl.when(pl.program_id(0) == 0)
    def _():
        send_ref[...] = low

    @pl.when(pl.program_id(0) == 1)
    def _():
        keep_ref[...] = low


def weight_half(chain, xs, gs, pick, add=None):
    out_cols = gs[0].shape[-1]
    tile = xs[0].shape[-1] // 4

    def column(shape):
        lead = shape[:-1]
        return pl.BlockSpec(lead + (tile,), lambda i, p: (0,) * len(lead) + (p[i],))

    def whole(shape):
        return pl.BlockSpec(shape, lambda i, p: (0,) * len(shape))

    in_specs = [column(x.shape) for x in xs] + [whole(g.shape) for g in gs]
    args = list(xs) + list(gs)
    nx, ng = len(xs), len(gs)
    if add is None:
        body = functools.partial(first_half_body, nx, ng)
        outs = [shaped((2 * tile, out_cols), bf16)]
        out_specs = [pl.BlockSpec((tile, out_cols), lambda i, p: (i, 0))]
    else:
        body = functools.partial(other_half_body, nx, ng)
        in_specs.append(pl.BlockSpec((tile, out_cols), lambda i, p: (p[2 + i], 0)))
        args.append(add)
        outs = [shaped((tile, out_cols), bf16)] * 2
        out_specs = [pl.BlockSpec((tile, out_cols), lambda i, p: (0, 0))] * 2
    return chain(body, outs, args, prefetch=pick, grid=(2,), specs=(in_specs, out_specs), limit=20)


def spread_body(writes, place_ref, near_ref, far_ref, *out_refs):
    chunk = near_ref.shape[0] // 4
    for i in range(8):
        ref = (near_ref, far_ref)[i // 4]
        at = place_ref[0] ^ i
        base = i % 4 * chunk
        for which, lead, row, rows, col, cols in writes:
            value = ref[base + row : base + row + rows, col : col + cols].astype(f32)
            to = pl.ds(pl.multiple_of(at * rows, rows), rows)
            if lead is None:
                out_refs[which][to] = value
            else:
                out_refs[which][lead, to] = value


def out_weight_body(xa_ref, xb_ref, g0, g1, g2, g3, out_ref):
    acc = 0.0
    for j, g_ref in enumerate((g0, g1, g2, g3)):
        acc = acc + tn(piece_of((xa_ref, xb_ref), j), g_ref[...])
    out_ref[...] = acc.astype(bf16)


class Across:
    def __init__(self, chain):
        self.chain = chain
        self.size = lax.axis_size("dp")
        me = lax.axis_index("dp").astype(jnp.int32)
        self.x, self.b2, self.b4 = [(me >> i) & 1 for i in range(3)]
        home = 4 * self.x + 2 * self.b2 + self.b4
        self.home = home if self.size == 8 else jnp.int32(0)
        self.place = self.home.reshape(1)
        self.there = jnp.stack([2 * (1 - self.x), 2 * (1 - self.x) + 1])
        self.mine = jnp.stack([2 * self.x + 1 - self.b2, 2 * self.x + self.b2, 1 - self.b2, self.b2])


class Sum:
    def __init__(self, across, outs, writes):
        self.across, self.chain = across, across.chain
        self.outs, self.writes = outs, writes
        self.result = None
        rest = [self.second, self.third, self.fourth, self.fifth, self.last]
        self.steps = iter(rest if across.size == 8 else [])

    def step(self):
        for todo in self.steps:
            todo()
            return

    def halve(self, bit, *terms):
        rows, cols = terms[0].shape
        half = shaped((rows // 2, cols), bf16)
        return self.chain(halve_body, [half, half], (bit.reshape(1), *terms), smem=1)

    def product(self, xs, gs):
        a = self.across
        self.xs, self.gs = xs, gs
        if a.size != 8:
            first = weight_half(self.chain, xs, gs, jnp.array([0, 1], jnp.int32))[0]
            other = weight_half(self.chain, xs, gs, jnp.array([2, 3], jnp.int32))[0]
            return self.general(jnp.concatenate([first, other], axis=0))
        self.got = swap(weight_half(self.chain, xs, gs, a.there)[0], "dp", 1)

    def array(self, value):
        self.xs = None
        if self.across.size != 8:
            return self.general(value)
        send, self.keep = self.halve(self.across.x, value)
        self.got = swap(send, "dp", 1)

    def terms(self, kept, near, far):
        self.xs = None
        if self.across.size != 8:
            total = kept[0].astype(f32) + near[0].astype(f32) + far.astype(f32)
            return self.general(total.astype(bf16))
        rows, cols = far.shape
        half = shaped((rows // 2, cols), bf16)
        send, self.keep = self.chain(
            three_halve_body, [half, half], (self.across.x.reshape(1), kept, near, far), smem=1
        )
        self.got = swap(send, "dp", 1)

    def second(self):
        if self.xs is None:
            send, self.keep = self.halve(self.across.b2, self.keep, self.got)
        else:
            send, self.keep = weight_half(self.chain, self.xs, self.gs, self.across.mine, self.got)
        self.got = swap(send, "dp", 2)

    def third(self):
        send, self.keep = self.halve(self.across.b4, self.keep, self.got)
        self.got = swap(send, "dp", 4)

    def fourth(self):
        self.keep = self.chain(add_body, [shaped(self.keep.shape, bf16)], (self.keep, self.got))[0]
        self.got = swap(self.keep, "dp", 4)

    def join(self):
        rows, cols = self.keep.shape
        self.keep = self.chain(join_body, [shaped((2 * rows, cols), bf16)], (self.keep, self.got))[0]

    def fifth(self):
        self.join()
        self.got = swap(self.keep, "dp", 2)
        self.steps = iter([self.sixth, self.last])

    def sixth(self):
        self.join()
        self.got = swap(self.keep, "dp", 1)

    def last(self):
        self.spread(self.keep, self.got)

    def spread(self, near, far):
        self.result = self.chain(
            functools.partial(spread_body, self.writes),
            [shaped(dims, f32) for dims in self.outs],
            (self.across.place, near, far),
            smem=1,
        )

    def general(self, held):
        me = lax.axis_index("dp")
        bits = [1 << i for i in range(self.across.size.bit_length() - 1)]
        for bit in bits:
            mine = (me & bit) != 0
            half = held.shape[0] // 2
            other = lax.dynamic_slice_in_dim(held, jnp.where(mine, 0, half), half, 0)
            own = lax.dynamic_slice_in_dim(held, jnp.where(mine, half, 0), half, 0)
            held = (own.astype(f32) + swap(other, "dp", bit).astype(f32)).astype(bf16)
        for bit in reversed(bits):
            mine = (me & bit) != 0
            other = swap(held, "dp", bit)
            held = jnp.where(
                mine,
                jnp.concatenate([other, held], axis=0),
                jnp.concatenate([held, other], axis=0),
            )
        half = held.shape[0] // 2
        self.spread(held[:half], held[half:])


def per_device(
    tokens, segment_ids, gsd_index, enc_qkv, enc_qv_bias, enc_out_proj, enc_up, enc_up_bias,
    enc_down, enc_out_bias, enc_gain, enc_norm_bias, embed_weight, embed_bias, dec_qkv,
    dec_qv_bias, dec_out_proj, dec_up, dec_up_bias, dec_down, dec_out_bias, dec_gain,
    dec_norm_bias, cotangent,
):
    n, width = tokens.shape
    rows, length = segment_ids.shape
    assert rows == 4 and n == length == 256 and lax.axis_size("mp") == 4
    share, ff = enc_qkv.shape[2], enc_up.shape[1]
    dwidth, dff = cotangent.shape[1], dec_up.shape[1] * 4
    dshare = dwidth // 4
    heads = share // (width // HEADS)
    scale = (width // HEADS) ** -0.5
    slot = lax.axis_index("mp").astype(jnp.int32)
    at = slot.reshape(1)
    chain = Chain()
    across = Across(chain)

    def low(*dims):
        return shaped(dims, bf16)

    def full(*dims):
        return shaped(dims, f32)

    def waves(size):
        half = size // 2
        return jnp.power(10000.0, -jnp.arange(half, dtype=f32) / half).reshape(1, half)

    def near(value):
        return swap(value, "mp", 1)

    def far(value):
        return swap(value, "mp", 2)

    stream, normed, pos, bias_a, bias_b = chain(
        start_body,
        [full(n, width), low(n, width), full(n, dwidth), full(2, n, n), full(2, n, n)],
        (at, segment_ids, gsd_index, tokens, enc_gain, enc_norm_bias, embed_bias.reshape(1, -1), waves(width), waves(dwidth)),
        smem=1,
    )
    x = [normed, near(normed), far(normed)]
    x.append(near(x[2]))
    pack_rows = 2 * dwidth + dshare + dwidth + dshare
    packed, piece = chain(
        pack_body,
        [low(pack_rows, dwidth), low(pack_rows // 8, dwidth)],
        (across.place, dec_up, dec_down, dec_out_proj, dec_qkv, embed_weight),
        smem=1,
    )
    if across.size == 8:
        got = far(piece)
        more = swap(got, "dp", 4)
    packed_near = near(packed)
    vector = jnp.concatenate([dec_qv_bias.reshape(-1), dec_up_bias]).reshape(1, -1)
    vectors = [vector, far(vector)]
    vectors = vectors + [near(jnp.concatenate(vectors, axis=0))]

    def join(a, b):
        return chain(join_body, [low(a.shape[0] + b.shape[0], a.shape[1])], (a, b))[0]

    def attention(bias, xa, xb):
        return chain(
            functools.partial(attn_body, scale, heads),
            [low(2, n, share)] * 3 + [low(2, heads, n, n), low(2, n, share)] + [low(n, width)] * 2,
            (xa, xb, bias, enc_qkv, enc_qv_bias, enc_out_proj),
        )

    def add(a, b):
        return chain(add_body, [shaped(a.shape, a.dtype)], (a, b))[0]

    qa, ka, va, pa, mixa, part0, part1 = attention(bias_a, x[0], x[1])
    part1 = near(part1)
    qb, kb, vb, pb, mixb, part2, part3 = attention(bias_b, x[2], x[3])
    part3 = near(part3)
    part2 = far(add(part2, part3))
    if across.size == 8:
        got = join(got, more)
        more = swap(got, "dp", 2)
    middle, normed2 = chain(
        mid_body,
        [full(n, width), low(n, width)],
        (stream, part0, part1, part2, enc_out_bias, enc_gain, enc_norm_bias),
    )
    y = [normed2, near(normed2), far(normed2)]
    y.append(near(y[2]))
    if across.size == 8:
        got = join(got, more)
        more = swap(got, "dp", 1)

    def feed(xa, xb):
        return chain(
            mlp_body,
            [low(2, n, ff)] * 2 + [low(n, width)] * 2,
            (xa, xb, enc_up, enc_up_bias.reshape(1, -1), enc_down),
        )

    hida, dga, part0, part1 = feed(y[0], y[1])
    part1 = near(part1)
    hidb, dgb, part2, part3 = feed(y[2], y[3])
    part3 = near(part3)
    part2 = far(add(part2, part3))
    packed_far = join(got, more) if across.size == 8 else far(packed)
    packed_far_near = near(packed_far)

    small = [vectors[0], vectors[2][:1], vectors[1], vectors[2][1:]]
    qv_full = jnp.concatenate([b[:, : 2 * dshare].reshape(2, dshare) for b in small], axis=1)
    upb_full = jnp.concatenate([b[:, 2 * dshare :] for b in small], axis=1)
    (enc_low, output, x1, x2, hid, mix, gp, gm, g3, gz, ge_low, ge, dec_sums) = chain(
        decoder_body,
        [low(n, width), full(n, dwidth), low(n, dwidth), low(n, dwidth), low(n, dff), low(n, dwidth),
         low(n, dff), low(n, dwidth), low(n, 3 * dwidth), low(n, dwidth), low(n, width), full(n, width),
         full(8, width)],
        (jnp.stack([slot, across.home]), middle, part0, part1, part2, enc_out_bias, packed, packed_near,
         packed_far, packed_far_near, qv_full, upb_full, pos, bias_a, dec_out_bias, dec_gain,
         dec_norm_bias, cotangent),
        smem=1,
        scratch=[
            pltpu.VMEM((pack_rows, dwidth), bf16), pltpu.VMEM((pack_rows, dwidth), bf16),
            pltpu.VMEM((3, dwidth, dwidth), bf16), pltpu.VMEM((dwidth, dwidth), bf16),
            pltpu.VMEM((width, dwidth), bf16), pltpu.VMEM((DHEADS, n, n), bf16),
            pltpu.VMEM((n, dff), bf16), pltpu.VMEM((3, n, dwidth), bf16), pltpu.VMEM((n, dwidth), f32),
        ],
        limit=40,
    )
    g = [ge_low, near(ge_low), far(ge_low)]
    g.append(near(g[2]))
    wide_rows, thin_rows = 9 * dwidth // 4, 3 * dwidth + width
    ws, ts, wk, tk = chain(
        decoder_weights_body,
        [low(2, wide_rows, dwidth), low(2, thin_rows, dshare)] * 2,
        (x1, x2, hid, mix, gp, gm, g3, gz, enc_low, cotangent),
        limit=24,
    )
    ws, ts = near(ws), near(ts)

    def plain(dims, cols):
        return [dims], [(0, None, 0, dims[0] // 8, 0, cols)]

    down = Sum(across, *plain((ff, width), width))
    up = Sum(across, *plain((width, ff), ff))
    out = Sum(across, *plain((share, width), width))
    qkv = Sum(across, [(3, width, share)], [(0, c, 0, width // 8, c * share, share) for c in range(3)])
    part = dwidth // 8
    wide = Sum(
        across,
        [(dwidth, dwidth), (dwidth, dwidth), (dshare, dwidth)],
        [(0, None, 0, part, 0, dwidth), (1, None, part, part, 0, dwidth), (2, None, 2 * part, dshare // 8, 0, dwidth)],
    )
    thin = Sum(
        across,
        [(3, dwidth, dshare), (width, dshare)],
        [(0, c, c * part, part, 0, dshare) for c in range(3)] + [(1, None, 3 * part, width // 8, 0, dshare)],
    )

    def feed_back(ga, gb, slope):
        return chain(
            mlp_back_body,
            [low(2, n, ff), full(1, ff), low(n, width), low(n, width)],
            (ga, gb, slope, enc_up, enc_down),
        )

    def pair_add(kept, got):
        return chain(pair_add_body, [low(*kept.shape[1:])], (kept, got))[0]

    gpa, upa, part0, part1 = feed_back(g[0], g[1], dga)
    part1 = near(part1)
    tfar = far(pair_add(tk, ts))
    down.product([hida, hidb], g)
    gpb, upb, part2, part3 = feed_back(g[2], g[3], dgb)
    part3 = near(part3)
    part2 = far(add(part2, part3))
    up.product(y, [gpa, gpb])
    grad_middle, gm_low, sums_mid = chain(
        mlp_end_body,
        [full(n, width), low(n, width), full(16, width)],
        (at, ge, part0, part1, part2, middle, enc_gain, upa, upb, dec_sums),
        smem=1,
    )
    m = [gm_low, near(gm_low), far(gm_low)]
    m.append(near(m[2]))
    wfar = far(pair_add(wk, ws))
    thin.terms(tk, ts, tfar)
    down.step()

    def attention_back(ga, gb, q, k, v, p):
        return chain(
            functools.partial(attn_back_body, scale, heads),
            [low(2, n, 3 * share), full(2, share), low(n, width), low(n, width)],
            (ga, gb, q, k, v, p, enc_qkv, enc_out_proj),
        )

    g3a, sa, part0, part1 = attention_back(m[0], m[1], qa, ka, va, pa)
    part1 = near(part1)
    g3b, sb, part2, part3 = attention_back(m[2], m[3], qb, kb, vb, pb)
    part3 = near(part3)
    part2 = far(add(part2, part3))
    up.step()
    qkv.product(x, [g3a, g3b])
    out.array(chain(out_weight_body, [low(share, width)], (mixa, mixb, *m))[0])
    down.step()
    thin.step()
    wide.terms(wk, ws, wfar)
    up.step()
    down.step()
    thin.step()
    out.step()
    grad_tokens, sums = chain(
        last_body,
        [full(n, width), full(24, width)],
        (at, grad_middle, part0, part1, part2, stream, enc_gain, sa, sb, sums_mid),
        smem=1,
    )
    hops = [("mp", 1), ("mp", 2), ("dp", 1), ("dp", 2), ("dp", 4)]
    if across.size != 8:
        hops = hops[:2] + [("dp", 1 << i) for i in range(across.size.bit_length() - 1)]
    hops = iter(hops)

    def hop():
        for axis, mask in hops:
            return add(sums, swap(sums, axis, mask))
        return sums

    up.step()
    down.step()
    qkv.step()
    thin.step()
    out.step()
    sums = hop()
    up.step()
    down.step()
    wide.step()
    qkv.step()
    thin.step()
    out.step()
    up.step()
    sums = hop()
    qkv.step()
    wide.step()
    thin.step()
    out.step()
    sums = hop()
    qkv.step()
    wide.step()
    sums = hop()
    wide.step()
    down.step()
    sums = hop()
    wide.step()
    thin.step()
    qkv.step()
    out.step()
    wide.step()
    up.step()
    for flow in (down, up, thin, out, qkv, wide):
        for _ in range(7):
            flow.step()
    for _ in range(8):
        sums = hop()
    last, mid, dec = sums[16:], sums[:8], sums[8:16]

    def own(whole, size):
        return lax.dynamic_slice_in_dim(whole, slot * size, size, whole.ndim - 1)

    return (
        output,
        grad_tokens,
        qkv.result[0],
        own(last[2:4], share),
        out.result[0],
        up.result[0],
        own(mid[4:8].reshape(-1), ff),
        down.result[0],
        jnp.concatenate([mid[0:1], dec[0:1]], axis=0),
        jnp.concatenate([last[0:1], mid[1:2]], axis=0),
        jnp.concatenate([last[1:2], mid[2:3]], axis=0),
        thin.result[1],
        dec[3, dwidth:],
        thin.result[0],
        own(dec[4:6, dwidth:], dshare),
        wide.result[2],
        wide.result[0],
        own(dec[6:8].reshape(-1), dff // 4),
        wide.result[1],
        dec[1:3, :dwidth],
        dec[1:3, dwidth:],
        dec[3:5, :dwidth],
    )


def solution(mesh):
    return jax.shard_map(
        per_device,
        mesh=mesh,
        in_specs=(
            P(("dp", "mp"), None),
            P("dp", None),
            P("dp", None),
            P(None, None, "mp"),
            P(None, "mp"),
            P("mp", None),
            P(None, "mp"),
            P("mp"),
            P("mp", None),
            P(),
            P(),
            P(),
            P(None, "mp"),
            P(),
            P(None, None, "mp"),
            P(None, "mp"),
            P("mp", None),
            P(None, "mp"),
            P("mp"),
            P("mp", None),
            P(),
            P(),
            P(),
            P(("dp", "mp"), None),
        ),
        out_specs=(
            P(("dp", "mp"), None),
            P(("dp", "mp"), None),
            P(None, None, "mp"),
            P(None, "mp"),
            P("mp", None),
            P(None, "mp"),
            P("mp"),
            P("mp", None),
            P(),
            P(),
            P(),
            P(None, "mp"),
            P(),
            P(None, None, "mp"),
            P(None, "mp"),
            P("mp", None),
            P(None, "mp"),
            P("mp"),
            P("mp", None),
            P(),
            P(),
            P(),
        ),
        check_vma=False,
    )
```

```python
import functools
import math

import jax
import jax.numpy as jnp
from jax import lax
from jax.experimental import pallas as pl
from jax.experimental.pallas import tpu as pltpu
from jax.sharding import PartitionSpec as P

HEADS = 16
DHEADS = 16
norm_eps = 1e-06
f32 = jnp.float32
bf16 = jnp.bfloat16
MIB = 1 << 20
VMEM = pl.BlockSpec(memory_space=pltpu.VMEM)
SMEM = pl.BlockSpec(memory_space=pltpu.SMEM)


def shaped(dims, kind):
    return jax.ShapeDtypeStruct(dims, kind)


def kept(shape):
    return pltpu.HBM(shape.shape, shape.dtype)


def in_hbm(value):
    return pltpu.with_memory_space_constraint(value, pltpu.HBM)


class Chain:
    def __init__(self):
        self.last = None

    def __call__(self, body, outs, args, smem=0, scratch=(), limit=16, prefetch=None, grid=None, specs=None):
        args = list(args)
        extra = self.last is not None
        lead = smem if prefetch is None else 1
        inner = body
        if extra:
            count = len(args) + (prefetch is not None)

            def inner(*refs):
                return body(*refs[:count], *refs[count + 1 :])

            args.append(self.last)
        tail = [pl.BlockSpec(memory_space=pl.ANY)] * extra
        params = pltpu.CompilerParams(vmem_limit_bytes=limit * MIB)
        cost = pl.CostEstimate(flops=1, bytes_accessed=1, transcendentals=0)
        if prefetch is None:
            got = pl.pallas_call(
                inner,
                out_shape=outs,
                in_specs=[SMEM] * smem + [VMEM] * (len(args) - smem - extra) + tail,
                out_specs=[VMEM] * len(outs),
                scratch_shapes=scratch,
                compiler_params=params,
                cost_estimate=cost,
            )(*args)
        else:
            got = pl.pallas_call(
                inner,
                out_shape=outs,
                grid_spec=pltpu.PrefetchScalarGridSpec(
                    num_scalar_prefetch=1, grid=grid, in_specs=specs[0] + tail, out_specs=specs[1]
                ),
                compiler_params=params,
                cost_estimate=cost,
            )(prefetch, *args)
        self.last = min(got, key=lambda g: g.size * g.dtype.itemsize)
        return got

    def pin(self, value):
        any_space = pl.BlockSpec(memory_space=pl.ANY)
        got = pl.pallas_call(
            lambda *refs: None,
            out_shape=shaped(value.shape, value.dtype),
            in_specs=[any_space, any_space],
            out_specs=any_space,
            input_output_aliases={0: 0},
            compiler_params=pltpu.CompilerParams(vmem_limit_bytes=MIB),
            cost_estimate=pl.CostEstimate(flops=1, bytes_accessed=1, transcendentals=0),
        )(value, self.last)
        self.last = got
        return got


def nn(a, b):
    return lax.dot_general(a, b, (((1,), (0,)), ((), ())), preferred_element_type=f32)


def nt(a, b):
    return lax.dot_general(a, b, (((1,), (1,)), ((), ())), preferred_element_type=f32)


def tn(a, b):
    return lax.dot_general(a, b, (((0,), (0,)), ((), ())), preferred_element_type=f32)


def swap(value, axis, mask):
    size = lax.axis_size(axis)
    return lax.ppermute(value, axis, [(i, i ^ mask) for i in range(size)])


def norm_parts(values):
    average = jnp.mean(values, axis=-1, keepdims=True)
    centred = values - average
    variance = jnp.mean(centred * centred, axis=-1, keepdims=True)
    scale = lax.rsqrt(variance + norm_eps)
    return centred * scale, scale


def norm_back(normal, scale, gain, grad):
    wide = grad * gain
    one = jnp.mean(wide, axis=-1, keepdims=True)
    two = jnp.mean(wide * normal, axis=-1, keepdims=True)
    return scale * (wide - one - normal * two)


def gelu_both(v):
    slope = math.sqrt(2.0 / math.pi)
    square = v * v
    t = jnp.tanh(slope * v * (1.0 + 0.044715 * square))
    half = 0.5 * (1.0 + t)
    return v * half, half + 0.5 * slope * v * (1.0 - t * t) * (1.0 + 3.0 * 0.044715 * square)


def sin_cos(x):
    turn = jnp.floor(x * (2.0 / math.pi) + 0.5)
    r = ((x - turn * 1.5703125) - turn * 4.837512969970703125e-4) - turn * 7.54978995489188216e-8
    z = r * r
    s = r + r * z * (-1.6666654611e-1 + z * (8.3321608736e-3 + z * -1.9515295891e-4))
    c = 1.0 - 0.5 * z + z * z * (
        4.166664568298827e-2 + z * (-1.388731625493765e-3 + z * 2.443315711809948e-5)
    )
    quarter = turn.astype(jnp.int32)
    odd = (quarter & 1) != 0
    sine = jnp.where(odd, c, s)
    cosine = jnp.where(odd, s, c)
    sine = jnp.where((quarter & 2) != 0, -sine, sine)
    cosine = jnp.where(((quarter + 1) & 2) != 0, -cosine, cosine)
    return sine, cosine


def head_masks(heads):
    size = 256 // heads
    lane = lax.broadcasted_iota(jnp.int32, (1, 256), 1)
    return [
        jnp.where((lane >= h * size) & (lane < (h + 1) * size), 1.0, 0.0).astype(bf16)
        for h in range(heads)
    ]


def attend(q, k, v, bias, heads, scale, keep):
    size = 256 // heads
    vt = v.astype(f32).T.astype(bf16)
    mixes = []
    for h, mask in enumerate(head_masks(heads)):
        s = nt(k, q * mask) + bias
        top = jnp.max(s, axis=0, keepdims=True)
        p = jnp.exp2((s - top) * (scale * math.log2(math.e)))
        total = jnp.sum(p, axis=0, keepdims=True)
        p = (p * (1.0 / total)).astype(bf16)
        keep(h, p)
        mixes.append(nn(vt[h * size : (h + 1) * size], p))
    return jnp.concatenate(mixes, axis=0).T


def attend_back(q, k, v, gm, probs, heads, scale):
    size = 256 // heads
    kt = k.astype(f32).T.astype(bf16)
    gq, gk, gv = [], 0.0, 0.0
    for h, mask in enumerate(head_masks(heads)):
        gmh = gm * mask
        p = probs(h)
        wide = p.astype(f32)
        t = wide * nt(v, gmh)
        gs = (t - wide * jnp.sum(t, axis=0, keepdims=True)).astype(bf16)
        gk = gk + nn(gs, q * mask)
        gv = gv + nn(p, gmh)
        gq.append(nn(kt[h * size : (h + 1) * size], gs))
    return jnp.concatenate(gq, axis=0).T * scale, gk * scale, gv


def start_body(slot_ref, seg_ref, gsd_ref, tokens_ref, gain_ref, shift_ref, eb_ref, wf_ref, nf_ref,
               stream_ref, normed_ref, pos_ref, bias_a_ref, bias_b_ref):
    slot = slot_ref[0]
    n = seg_ref.shape[1]
    place = None
    for j in range(4):
        across = jnp.broadcast_to(seg_ref[pl.ds(slot ^ j, 1), :].astype(f32), (n, n))
        down = across.T
        same = across == down
        (bias_a_ref, bias_b_ref)[j // 2][j % 2] = jnp.where(same, 0.0, -1e30)
        if j == 0:
            earlier = lax.broadcasted_iota(jnp.int32, (n, n), 1) < lax.broadcasted_iota(
                jnp.int32, (n, n), 0
            )
            rank = jnp.sum(jnp.where(same & earlier, 1.0, 0.0), axis=1, keepdims=True)
            index = jnp.broadcast_to(gsd_ref[pl.ds(slot, 1), :].astype(f32), (n, n)).T[:, :1]
            place = rank * (0.5 + 0.25 * index)
    half = wf_ref.shape[1]
    sine, cosine = sin_cos(place * wf_ref[...])
    stream_ref[:, :half] = tokens_ref[:, :half].astype(f32) + sine
    stream_ref[:, half:] = tokens_ref[:, half:].astype(f32) + cosine
    normal, _ = norm_parts(stream_ref[...])
    normed_ref[...] = (normal * gain_ref[0:1] + shift_ref[0:1]).astype(bf16)
    sine, cosine = sin_cos(place * nf_ref[...])
    half = nf_ref.shape[1]
    pos_ref[:, :half] = sine + eb_ref[:, :half]
    pos_ref[:, half:] = cosine + eb_ref[:, half:]


def attn_body(scale, heads, xa_ref, xb_ref, bias_ref, w_ref, qvb_ref, o_ref,
              q_ref, k_ref, v_ref, p_ref, mix_ref, pa_ref, pb_ref):
    for r, (x_ref, part_ref) in enumerate(((xa_ref, pa_ref), (xb_ref, pb_ref))):
        x = x_ref[...]
        q = (nn(x, w_ref[0]) + qvb_ref[0:1]).astype(bf16)
        k = nn(x, w_ref[1]).astype(bf16)
        v = (nn(x, w_ref[2]) + qvb_ref[1:2]).astype(bf16)
        q_ref[r], k_ref[r], v_ref[r] = q, k, v

        def keep(h, p):
            p_ref[r, h] = p

        mix = attend(q, k, v, bias_ref[r], heads, scale, keep).astype(bf16)
        mix_ref[r] = mix
        part_ref[...] = nn(mix, o_ref[...]).astype(bf16)


def attn_back_body(scale, heads, ga_ref, gb_ref, q_ref, k_ref, v_ref, p_ref, w_ref, o_ref,
                   g3_ref, sums_ref, pa_ref, pb_ref):
    total_q, total_v = 0.0, 0.0
    for r, (g_ref, part_ref) in enumerate(((ga_ref, pa_ref), (gb_ref, pb_ref))):
        gm = nt(g_ref[...], o_ref[...]).astype(bf16)
        gq, gk, gv = attend_back(
            q_ref[r], k_ref[r], v_ref[r], gm, lambda h: p_ref[r, h], heads, scale
        )
        total_q = total_q + jnp.sum(gq, axis=0, keepdims=True)
        total_v = total_v + jnp.sum(gv, axis=0, keepdims=True)
        acc = 0.0
        for c, g in enumerate((gq, gk, gv)):
            low = g.astype(bf16)
            g3_ref[r, :, c * 256 : (c + 1) * 256] = low
            acc = acc + nt(low, w_ref[c])
        part_ref[...] = acc.astype(bf16)
    sums_ref[0:1] = total_q
    sums_ref[1:2] = total_v


def mid_body(stream_ref, p_ref, near_ref, far_ref, ob_ref, gain_ref, shift_ref, mid_ref, normed_ref):
    total = p_ref[...].astype(f32) + near_ref[...].astype(f32) + far_ref[...].astype(f32)
    middle = stream_ref[...] + total + ob_ref[0:1]
    mid_ref[...] = middle
    normal, _ = norm_parts(middle)
    normed_ref[...] = (normal * gain_ref[1:2] + shift_ref[1:2]).astype(bf16)


def mlp_body(xa_ref, xb_ref, up_ref, ub_ref, down_ref, hid_ref, dg_ref, pa_ref, pb_ref):
    width = up_ref.shape[1]
    for r, (x_ref, part_ref) in enumerate(((xa_ref, pa_ref), (xb_ref, pb_ref))):
        x = x_ref[...]
        for c in range(0, width, 256):
            cut = slice(c, c + 256)
            hidden, slope = gelu_both(nn(x, up_ref[:, cut]) + ub_ref[:, cut])
            hid_ref[r, :, cut] = hidden.astype(bf16)
            dg_ref[r, :, cut] = slope.astype(bf16)
        hidden = hid_ref[r]
        for c in range(0, down_ref.shape[1], 512):
            cut = slice(c, c + 512)
            part_ref[:, cut] = nn(hidden, down_ref[:, cut]).astype(bf16)


def mlp_back_body(ga_ref, gb_ref, dg_ref, up_ref, down_ref, gp_ref, sums_ref, pa_ref, pb_ref):
    width = up_ref.shape[1]
    for r, (g_ref, part_ref) in enumerate(((ga_ref, pa_ref), (gb_ref, pb_ref))):
        g = g_ref[...]
        for c in range(0, width, 256):
            cut = slice(c, c + 256)
            grad = nt(g, down_ref[cut]) * dg_ref[r, :, cut].astype(f32)
            gp_ref[r, :, cut] = grad.astype(bf16)
            total = jnp.sum(grad, axis=0, keepdims=True)
            sums_ref[:, cut] = total if r == 0 else sums_ref[:, cut] + total
        gp = gp_ref[r]
        for c in range(0, up_ref.shape[0], 512):
            cut = slice(c, c + 512)
            part_ref[:, cut] = nt(gp, up_ref[cut]).astype(bf16)


def mlp_end_body(slot_ref, ge_ref, p_ref, near_ref, far_ref, mid_ref, gain_ref, ua_ref, ub_ref, dec_ref,
                 gmid_ref, gm_ref, pack_ref):
    slot = slot_ref[0]
    grad = p_ref[...].astype(f32) + near_ref[...].astype(f32) + far_ref[...].astype(f32)
    normal, scale = norm_parts(mid_ref[...])
    gmid = ge_ref[...] + norm_back(normal, scale, gain_ref[1:2], grad)
    gmid_ref[...] = gmid
    gm_ref[...] = gmid.astype(bf16)
    pack_ref[...] = jnp.zeros(pack_ref.shape, f32)
    pack_ref[0:1] = jnp.sum(gmid, axis=0, keepdims=True)
    pack_ref[1:2] = jnp.sum(grad * normal, axis=0, keepdims=True)
    pack_ref[2:3] = jnp.sum(grad, axis=0, keepdims=True)
    pack_ref[pl.ds(4 + slot, 1), :] = ua_ref[...] + ub_ref[...]
    pack_ref[8:16] = dec_ref[...]


def last_body(slot_ref, gmid_ref, p_ref, near_ref, far_ref, stream_ref, gain_ref, sa_ref, sb_ref, mid_ref,
              gtok_ref, pack_ref):
    slot = slot_ref[0]
    grad = p_ref[...].astype(f32) + near_ref[...].astype(f32) + far_ref[...].astype(f32)
    normal, scale = norm_parts(stream_ref[...])
    gtok_ref[...] = gmid_ref[...] + norm_back(normal, scale, gain_ref[0:1], grad)
    pack_ref[:16] = mid_ref[...]
    pack_ref[16:] = jnp.zeros((8, pack_ref.shape[1]), f32)
    pack_ref[16:17] = jnp.sum(grad * normal, axis=0, keepdims=True)
    pack_ref[17:18] = jnp.sum(grad, axis=0, keepdims=True)
    share = sa_ref.shape[1]
    place = pl.ds(pl.multiple_of(slot * share, share), share)
    pack_ref[18:20, place] = sa_ref[...] + sb_ref[...]


def decoder_body(slot_ref, mid_ref, p_ref, near_ref, far_ref, eob_ref, own_ref, by_ref, fa_ref, fb_ref, na_ref, nb_ref,
                 qvb_ref, upb_ref, pos_ref, bias_ref, dob_ref, dgain_ref, dnb_ref, cot_ref,
                 encl_ref, out_ref, x1_ref, x2_ref, hid_ref, mix_ref, gp_ref, gm_ref, g3_ref, gz_ref,
                 gel_ref, ge_ref, sums_ref,
                 wup, wdown, wqkv, wout, wemb, pt, dg, qkv, wide):
    slot, home = slot_ref[0], slot_ref[1]
    width = cot_ref.shape[1]
    block = width // 4
    heads = DHEADS * 256 // width
    groups = width // 256
    scale = (width // DHEADS) ** -0.5

    def place(j, base=0):
        return pl.ds(pl.multiple_of(base + (slot ^ j) * block, block), block)

    piece, thin, tall = width // 8, block // 8, 2 * width // 8
    top = 2 * piece + thin
    step = top + piece + thin
    for j, (low_ref, high_ref) in enumerate(
        ((own_ref, own_ref), (by_ref, by_ref), (fa_ref, fb_ref), (na_ref, nb_ref))
    ):
        cut = slice(j * block, (j + 1) * block)
        for i in range(8):
            ref = (low_ref, high_ref)[i // 4]
            base = (i if j < 2 else i % 4) * step
            chunk = i if j < 2 else home ^ i

            def rows(size):
                return pl.ds(pl.multiple_of(chunk * size, size), size)

            wup[j, rows(piece)] = ref[base : base + piece]
            wdown[j, rows(piece)] = ref[base + piece : base + 2 * piece]
            wout[pl.ds(pl.multiple_of(j * block + chunk * thin, thin), thin)] = (
                ref[base + 2 * piece : base + top]
            )
            for c in range(3):
                wqkv[c, rows(piece), cut] = ref[base + top : base + top + piece, c * block : (c + 1) * block]
            wemb[pl.ds(pl.multiple_of(chunk * tall, tall), piece), cut] = (
                ref[base + top : base + top + piece, 3 * block :]
            )
            for c in range(4):
                wemb[pl.ds(pl.multiple_of(chunk * tall + piece + c * thin, thin), thin), cut] = (
                    ref[base + top + piece : base + step, c * block : (c + 1) * block]
                )
    encoded = mid_ref[...] + eob_ref[1:2]
    encoded = encoded + p_ref[...].astype(f32) + near_ref[...].astype(f32) + far_ref[...].astype(f32)
    encl_ref[...] = encoded.astype(bf16)
    embedded = nn(encl_ref[...], wemb[...])
    for j in range(4):
        wide[:, place(j)] = embedded[:, j * block : (j + 1) * block]
    stream = wide[...] + pos_ref[...]
    normal1, scale1 = norm_parts(stream)
    x1_ref[...] = (normal1 * dgain_ref[0:1] + dnb_ref[0:1]).astype(bf16)
    x1 = x1_ref[...]
    qkv[0] = (nn(x1, wqkv[0]) + qvb_ref[0:1]).astype(bf16)
    qkv[1] = nn(x1, wqkv[1]).astype(bf16)
    qkv[2] = (nn(x1, wqkv[2]) + qvb_ref[1:2]).astype(bf16)
    bias = bias_ref[0]
    for g in range(groups):
        cut = slice(g * 256, (g + 1) * 256)

        def keep(h, p):
            pt[g * heads + h] = p

        mix_ref[:, cut] = attend(
            qkv[0, :, cut], qkv[1, :, cut], qkv[2, :, cut], bias, heads, scale, keep
        ).astype(bf16)
    middle = stream + nn(mix_ref[...], wout[...]) + dob_ref[0:1]
    normal2, scale2 = norm_parts(middle)
    x2_ref[...] = (normal2 * dgain_ref[1:2] + dnb_ref[1:2]).astype(bf16)
    x2 = x2_ref[...]
    result = middle + dob_ref[1:2]
    for j in range(4):
        cut = slice(j * width, (j + 1) * width)
        hidden, slope = gelu_both(nn(x2, wup[j]) + upb_ref[:, cut])
        hid_ref[:, cut] = hidden.astype(bf16)
        dg[:, cut] = slope.astype(bf16)
        result = result + nn(hid_ref[:, cut], wdown[j])
    out_ref[...] = result

    cot = cot_ref[...]
    grad = 0.0
    sums_ref[...] = jnp.zeros(sums_ref.shape, f32)
    for j in range(4):
        cut = slice(j * width, (j + 1) * width)
        pre = nt(cot, wdown[j]) * dg[:, cut].astype(f32)
        gp_ref[:, cut] = pre.astype(bf16)
        block_sum = jnp.sum(pre, axis=0, keepdims=True)
        at = slot ^ j
        sums_ref[pl.ds(6 + (at >> 1), 1), pl.ds(pl.multiple_of((at & 1) * width, width), width)] = (
            block_sum
        )
        grad = grad + nt(gp_ref[:, cut], wup[j])
    cotf = cot.astype(f32)
    gmid = cotf + norm_back(normal2, scale2, dgain_ref[1:2], grad)
    gm_ref[...] = gmid.astype(bf16)
    sums_ref[1:2, :width] = jnp.sum(gmid, axis=0, keepdims=True)
    sums_ref[2:3, :width] = jnp.sum(cotf, axis=0, keepdims=True)
    sums_ref[2:3, width:] = jnp.sum(grad * normal2, axis=0, keepdims=True)
    sums_ref[4:5, :width] = jnp.sum(grad, axis=0, keepdims=True)
    gmix = nt(gm_ref[...], wout[...]).astype(bf16)
    grad = 0.0
    for g in range(groups):
        cut = slice(g * 256, (g + 1) * 256)
        three = attend_back(
            qkv[0, :, cut], qkv[1, :, cut], qkv[2, :, cut], gmix[:, cut],
            lambda h: pt[g * heads + h], heads, scale,
        )
        for c, part in enumerate(three):
            begin = c * width + g * 256
            low = part.astype(bf16)
            g3_ref[:, begin : begin + 256] = low
            grad = grad + nt(low, wqkv[c, :, cut])
        for c, row, base in ((0, 4, width), (2, 5, width)):
            total = jnp.sum(three[c], axis=0, keepdims=True)
            for i in range(256 // block):
                sums_ref[row : row + 1, place(g * (256 // block) + i, base)] = (
                    total[:, i * block : (i + 1) * block]
                )
    gstream = gmid + norm_back(normal1, scale1, dgain_ref[0:1], grad)
    sums_ref[3:4, width:] = jnp.sum(gstream, axis=0, keepdims=True)
    sums_ref[1:2, width:] = jnp.sum(grad * normal1, axis=0, keepdims=True)
    sums_ref[3:4, :width] = jnp.sum(grad, axis=0, keepdims=True)
    wide[...] = gstream
    for j in range(4):
        gz_ref[:, j * block : (j + 1) * block] = wide[:, place(j)].astype(bf16)
    ge = nt(gz_ref[...], wemb[...])
    ge_ref[...] = ge
    gel_ref[...] = ge.astype(bf16)
    sums_ref[0:1] = jnp.sum(ge, axis=0, keepdims=True)


def decoder_weights_body(x1_ref, x2_ref, hid_ref, mix_ref, gp_ref, gm_ref, g3_ref, gz_ref, encl_ref, cot_ref,
                         sent_ref, kept_ref):
    width = cot_ref.shape[1]
    block = width // 4
    cot, gm, x2 = cot_ref[...], gm_ref[...], x2_ref[...]
    piece, thin = width // 8, block // 8
    tall = encl_ref.shape[1] // 8
    top = 2 * piece + thin
    step = top + piece + thin

    def to(j):
        return sent_ref if j % 2 else kept_ref

    for j in (1, 3, 0, 2):
        w = to(j)
        i = j // 2
        cut = slice(j * width, (j + 1) * width)
        up = tn(x2, gp_ref[:, cut]).astype(bf16)
        down = tn(hid_ref[:, cut], cot).astype(bf16)
        out = tn(mix_ref[:, j * block : (j + 1) * block], gm).astype(bf16)
        for c in range(8):
            w[i, c * step : c * step + piece] = up[c * piece : (c + 1) * piece]
            w[i, c * step + piece : c * step + 2 * piece] = down[c * piece : (c + 1) * piece]
            w[i, c * step + 2 * piece : c * step + top] = out[c * thin : (c + 1) * thin]
    x1 = x1_ref[...]
    for k in range(3):
        full = tn(x1, g3_ref[:, k * width : (k + 1) * width]).astype(bf16)
        for j in range(4):
            for c in range(8):
                to(j)[j // 2, c * step + top : c * step + top + piece, k * block : (k + 1) * block] = (
                    full[c * piece : (c + 1) * piece, j * block : (j + 1) * block]
                )
    full = tn(encl_ref[...], gz_ref[...]).astype(bf16)
    for j in range(4):
        cut = slice(j * block, (j + 1) * block)
        for c in range(8):
            base = c * tall
            to(j)[j // 2, c * step + top : c * step + top + piece, 3 * block :] = full[base : base + piece, cut]
            base = base + piece
            for k in range(4):
                to(j)[j // 2, c * step + top + piece : (c + 1) * step, k * block : (k + 1) * block] = (
                    full[base + k * thin : base + (k + 1) * thin, cut]
                )


def pack_body(pick_ref, up_ref, down_ref, out_ref, qkv_ref, emb_ref, chunk_ref):
    piece, thin, block = up_ref.shape[0], out_ref.shape[0], emb_ref.shape[1]
    chunk_ref[:piece] = up_ref[...]
    chunk_ref[piece : 2 * piece] = down_ref[...]
    top = 2 * piece + thin
    chunk_ref[2 * piece : top] = out_ref[...]
    for c in range(3):
        chunk_ref[top : top + piece, c * block : (c + 1) * block] = qkv_ref[c]
    chunk_ref[top : top + piece, 3 * block :] = emb_ref[:piece]
    for c in range(4):
        base = piece + c * thin
        chunk_ref[top + piece :, c * block : (c + 1) * block] = emb_ref[base : base + thin]


def join_body(a_ref, b_ref, out_ref):
    rows = a_ref.shape[0]
    out_ref[:rows] = a_ref[...]
    out_ref[rows:] = b_ref[...]


def add_body(a_ref, b_ref, out_ref):
    out_ref[...] = (a_ref[...].astype(f32) + b_ref[...].astype(f32)).astype(out_ref.dtype)


def halve_body(bit_ref, *refs):
    ins, (send_ref, keep_ref) = refs[:-2], refs[-2:]
    half = send_ref.shape[0]
    bit = bit_ref[0]
    for ref, which in ((send_ref, 1 - bit), (keep_ref, bit)):
        rows = pl.ds(pl.multiple_of(which * half, half), half)
        total = ins[0][rows].astype(f32)
        for other in ins[1:]:
            total = total + other[rows].astype(f32)
        ref[...] = total.astype(bf16)


def far_body(bit_ref, kept_ref, near_ref, there_ref, mine_ref):
    half = there_ref.shape[0]
    bit = bit_ref[0]
    for ref, which in ((there_ref, 1 - bit), (mine_ref, bit)):
        rows = pl.ds(pl.multiple_of(which * half, half), half)
        ref[...] = (kept_ref[1, rows].astype(f32) + near_ref[1, rows].astype(f32)).astype(bf16)


def there_body(bit_ref, kept_ref, near_ref, far_ref, send_ref):
    half = send_ref.shape[0]
    rows = pl.ds(pl.multiple_of((1 - bit_ref[0]) * half, half), half)
    total = kept_ref[0, rows].astype(f32) + near_ref[0, rows].astype(f32)
    send_ref[...] = (total + far_ref[...].astype(f32)).astype(bf16)


def mine_body(bit_ref, kept_ref, near_ref, far_ref, got_ref, send_ref, keep_ref):
    quarter = send_ref.shape[0]
    base = bit_ref[0] * 2 * quarter
    for ref, which in ((send_ref, 1 - bit_ref[1]), (keep_ref, bit_ref[1])):
        rows = pl.ds(pl.multiple_of(base + which * quarter, quarter), quarter)
        inner = pl.ds(pl.multiple_of(which * quarter, quarter), quarter)
        total = kept_ref[0, rows].astype(f32) + near_ref[0, rows].astype(f32)
        ref[...] = (total + far_ref[inner].astype(f32) + got_ref[inner].astype(f32)).astype(bf16)


def piece_of(refs, j):
    if len(refs) == 4:
        return refs[j][...]
    return refs[j // 2][j % 2]


def tile_sum(xs, gs, more):
    acc = 0.0
    for j in range(4):
        acc = acc + tn(piece_of(xs, j), piece_of(gs, j))
    if not more:
        return [(slice(None), slice(None), acc)]
    rows, cols = acc.shape
    parts = [(slice(None), slice(0, cols), acc)]
    half, quarter = rows // 2, rows // 8
    wide = more[0].shape[1] // 4
    for c in range(2):
        for k in range(4):
            parts.append((
                slice(c * half + k * quarter, c * half + (k + 1) * quarter),
                slice(cols, cols + wide),
                more[0][c * quarter : (c + 1) * quarter, k * wide : (k + 1) * wide].astype(f32),
            ))
    return parts


def first_half_body(nx, ng, nm, pick_ref, *refs):
    xs, gs, more = refs[:nx], refs[nx : nx + ng], refs[nx + ng : nx + ng + nm]
    out_ref = refs[nx + ng + nm]
    for rows, cols, value in tile_sum(xs, gs, more):
        out_ref[rows, cols] = value.astype(bf16)


def other_half_body(nx, ng, nm, pick_ref, *refs):
    xs, gs, more = refs[:nx], refs[nx : nx + ng], refs[nx + ng : nx + ng + nm]
    add_ref, send_ref, keep_ref = refs[nx + ng + nm :]
    parts = [
        (rows, cols, (value + add_ref[rows, cols].astype(f32)).astype(bf16))
        for rows, cols, value in tile_sum(xs, gs, more)
    ]

    def put(ref):
        for rows, cols, value in parts:
            ref[rows, cols] = value

    @pl.when(pl.program_id(0) == 0)
    def _():
        put(send_ref)

    @pl.when(pl.program_id(0) == 1)
    def _():
        put(keep_ref)


def weight_half(chain, xs, gs, more, pick, add=None):
    tile = xs[0].shape[-1] // 4
    out_cols = gs[0].shape[-1] + sum(m.shape[1] // 4 for m in more)

    def column(shape):
        lead = shape[:-1]
        return pl.BlockSpec(lead + (tile,), lambda i, p: (0,) * len(lead) + (p[i],))

    def whole(shape):
        return pl.BlockSpec(shape, lambda i, p: (0,) * len(shape))

    in_specs = [column(x.shape) for x in xs] + [whole(g.shape) for g in gs]
    in_specs += [pl.BlockSpec((tile // 4, m.shape[1]), lambda i, p: (p[i], 0)) for m in more]
    args = list(xs) + list(gs) + list(more)
    counts = len(xs), len(gs), len(more)
    if add is None:
        body = functools.partial(first_half_body, *counts)
        outs = [shaped((2 * tile, out_cols), bf16)]
        out_specs = [pl.BlockSpec((tile, out_cols), lambda i, p: (i, 0))]
    else:
        body = functools.partial(other_half_body, *counts)
        in_specs.append(pl.BlockSpec((tile, out_cols), lambda i, p: (p[2 + i], 0)))
        args.append(add)
        outs = [shaped((tile, out_cols), bf16)] * 2
        out_specs = [pl.BlockSpec((tile, out_cols), lambda i, p: (0, 0))] * 2
    return chain(body, outs, args, prefetch=pick, grid=(2,), specs=(in_specs, out_specs), limit=20)


def spread_body(writes, place_ref, near_ref, far_ref, *out_refs):
    chunk = near_ref.shape[0] // 4
    for i in range(8):
        ref = (near_ref, far_ref)[i // 4]
        at = place_ref[0] ^ i
        base = i % 4 * chunk
        for which, lead, first, every, row, rows, col, cols, at_col in writes:
            value = ref[base + row : base + row + rows, col : col + cols].astype(f32)
            to = pl.ds(pl.multiple_of(at * every + first, rows), rows)
            if lead is None:
                out_refs[which][to, at_col : at_col + cols] = value
            else:
                out_refs[which][lead, to] = value


def out_weight_body(xa_ref, xb_ref, g0, g1, g2, g3, out_ref):
    acc = 0.0
    for j, g_ref in enumerate((g0, g1, g2, g3)):
        acc = acc + tn(piece_of((xa_ref, xb_ref), j), g_ref[...])
    out_ref[...] = acc.astype(bf16)


class Across:
    def __init__(self, chain):
        self.chain = chain
        self.size = lax.axis_size("dp")
        me = lax.axis_index("dp").astype(jnp.int32)
        self.x, self.b2, self.b4 = [(me >> i) & 1 for i in range(3)]
        home = 4 * self.x + 2 * self.b2 + self.b4
        self.home = home if self.size == 8 else jnp.int32(0)
        self.place = self.home.reshape(1)
        self.there = jnp.stack([2 * (1 - self.x), 2 * (1 - self.x) + 1])
        self.mine = jnp.stack([2 * self.x + 1 - self.b2, 2 * self.x + self.b2, 1 - self.b2, self.b2])


class Sum:
    def __init__(self, across, outs, writes):
        self.across, self.chain = across, across.chain
        self.outs, self.writes = outs, writes
        self.result = None
        rest = [self.second, self.third, self.fourth, self.fifth, self.last]
        self.steps = iter(rest if across.size == 8 else [])

    def step(self):
        for todo in self.steps:
            todo()
            return

    def halve(self, bit, *terms):
        rows, cols = terms[0].shape
        half = shaped((rows // 2, cols), bf16)
        return self.chain(halve_body, [half, half], (bit.reshape(1), *terms), smem=1)

    def product(self, xs, gs, more=()):
        a = self.across
        self.terms = (xs, gs, more)
        if a.size != 8:
            first = weight_half(self.chain, *self.terms, jnp.array([0, 1], jnp.int32))[0]
            other = weight_half(self.chain, *self.terms, jnp.array([2, 3], jnp.int32))[0]
            return self.general(jnp.concatenate([first, other], axis=0))
        self.got = swap(weight_half(self.chain, *self.terms, a.there)[0], "dp", 1)

    def shares(self, kept, near, there, mine):
        self.terms = None
        a = self.across
        if a.size != 8:
            total = kept[0].astype(f32) + near[0].astype(f32)
            total = total + jnp.concatenate([mine, there], axis=0).astype(f32)
            return self.general(total.astype(bf16))
        self.held = (kept, near, mine)
        half = shaped(there.shape, bf16)
        send = self.chain(there_body, [half], (a.x.reshape(1), kept, near, there), smem=1)[0]
        self.got = swap(send, "dp", 1)

    def second(self):
        a = self.across
        if self.terms is None:
            rows, cols = self.got.shape
            half = shaped((rows // 2, cols), bf16)
            send, self.keep = self.chain(
                mine_body, [half, half], (jnp.stack([a.x, a.b2]), *self.held, self.got), smem=1
            )
        else:
            send, self.keep = weight_half(self.chain, *self.terms, a.mine, self.got)
        self.got = swap(send, "dp", 2)

    def third(self):
        send, self.keep = self.halve(self.across.b4, self.keep, self.got)
        self.got = swap(send, "dp", 4)

    def fourth(self):
        self.keep = self.chain(add_body, [shaped(self.keep.shape, bf16)], (self.keep, self.got))[0]
        self.got = swap(self.keep, "dp", 4)

    def join(self):
        rows, cols = self.keep.shape
        self.keep = self.chain(join_body, [shaped((2 * rows, cols), bf16)], (self.keep, self.got))[0]

    def fifth(self):
        self.join()
        self.got = swap(self.keep, "dp", 2)
        self.steps = iter([self.sixth, self.last])

    def sixth(self):
        self.join()
        self.got = swap(self.keep, "dp", 1)

    def last(self):
        self.spread(self.keep, self.got)

    def spread(self, near, far):
        self.result = self.chain(
            functools.partial(spread_body, self.writes),
            [shaped(dims, f32) for dims in self.outs],
            (self.across.place, near, far),
            smem=1,
        )

    def general(self, held):
        me = lax.axis_index("dp")
        bits = [1 << i for i in range(self.across.size.bit_length() - 1)]
        for bit in bits:
            mine = (me & bit) != 0
            half = held.shape[0] // 2
            other = lax.dynamic_slice_in_dim(held, jnp.where(mine, 0, half), half, 0)
            own = lax.dynamic_slice_in_dim(held, jnp.where(mine, half, 0), half, 0)
            held = (own.astype(f32) + swap(other, "dp", bit).astype(f32)).astype(bf16)
        for bit in reversed(bits):
            mine = (me & bit) != 0
            other = swap(held, "dp", bit)
            held = jnp.where(
                mine,
                jnp.concatenate([other, held], axis=0),
                jnp.concatenate([held, other], axis=0),
            )
        half = held.shape[0] // 2
        self.spread(held[:half], held[half:])


def per_device(
    tokens, segment_ids, gsd_index, enc_qkv, enc_qv_bias, enc_out_proj, enc_up, enc_up_bias,
    enc_down, enc_out_bias, enc_gain, enc_norm_bias, embed_weight, embed_bias, dec_qkv,
    dec_qv_bias, dec_out_proj, dec_up, dec_up_bias, dec_down, dec_out_bias, dec_gain,
    dec_norm_bias, cotangent,
):
    n, width = tokens.shape
    rows, length = segment_ids.shape
    assert rows == 4 and n == length == 256 and lax.axis_size("mp") == 4
    share, ff = enc_qkv.shape[2], enc_up.shape[1]
    dwidth, dff = cotangent.shape[1], dec_up.shape[1] * 4
    dshare = dwidth // 4
    heads = share // (width // HEADS)
    scale = (width // HEADS) ** -0.5
    slot = lax.axis_index("mp").astype(jnp.int32)
    at = slot.reshape(1)
    chain = Chain()
    across = Across(chain)

    def low(*dims):
        return shaped(dims, bf16)

    def full(*dims):
        return shaped(dims, f32)

    def waves(size):
        half = size // 2
        return jnp.power(10000.0, -jnp.arange(half, dtype=f32) / half).reshape(1, half)

    def near(value):
        return swap(value, "mp", 1)

    def far(value):
        return swap(value, "mp", 2)

    pack_rows = 3 * dwidth + 2 * dshare
    decoder_weights = (dec_up, dec_down, dec_out_proj, dec_qkv, embed_weight)

    def pack(pick, steps):
        def block(shape):
            if len(shape) == 3:
                return pl.BlockSpec((shape[0], shape[1] // 8, shape[2]), lambda i, p: (0, p[i], 0))
            return pl.BlockSpec((shape[0] // 8, shape[1]), lambda i, p: (p[i], 0))

        rows = pack_rows // 8
        return chain(
            pack_body,
            [low(steps * rows, dwidth)],
            decoder_weights,
            prefetch=pick,
            grid=(steps,),
            specs=([block(w.shape) for w in decoder_weights], [pl.BlockSpec((rows, dwidth), lambda i, p: (i, 0))]),
        )[0]

    split = across.size == 8
    got = far(pack(across.place, 1)) if split else None
    stream, normed, pos, bias_a, bias_b = chain(
        start_body,
        [kept(full(n, width)), low(n, width), kept(full(n, dwidth)), kept(full(2, n, n)), kept(full(2, n, n))],
        (at, in_hbm(segment_ids), in_hbm(gsd_index), in_hbm(tokens), in_hbm(enc_gain), in_hbm(enc_norm_bias),
         in_hbm(embed_bias.reshape(1, -1)), waves(width), waves(dwidth)),
        smem=1,
    )
    x = [normed, near(normed), far(normed)]

    def attention(bias, xa, xb):
        return chain(
            functools.partial(attn_body, scale, heads),
            [kept(low(2, n, share))] * 3 + [kept(low(2, heads, n, n)), kept(low(2, n, share))] + [low(n, width)] * 2,
            (xa, xb, bias, enc_qkv, enc_qv_bias, enc_out_proj),
        )

    def add(a, b):
        return chain(add_body, [shaped(a.shape, a.dtype)], (a, b))[0]

    def join(a, b):
        return chain(join_body, [low(a.shape[0] + b.shape[0], a.shape[1])], (a, b))[0]

    def both(blocks):
        blocks[2] = chain.pin(blocks[2])
        blocks.append(near(blocks[2]))

    qa, ka, va, pa, mixa, part0, part1 = attention(bias_a, x[0], x[1])
    part1 = near(part1)
    packed = pack(jnp.arange(8, dtype=jnp.int32), 8)
    packed_near = near(packed)
    vector = jnp.concatenate([dec_qv_bias.reshape(-1), dec_up_bias]).reshape(1, -1)
    far_vector = far(vector)
    both(x)
    if split:
        got = chain.pin(got)
        more = swap(got, "dp", 4)
    qb, kb, vb, pb, mixb, part2, part3 = attention(bias_b, x[2], x[3])
    part3 = near(part3)
    part2 = far(add(part2, part3))
    if split:
        got = join(got, more)
        more = swap(got, "dp", 2)
    else:
        got = far(packed)
    middle, normed2 = chain(
        mid_body,
        [kept(full(n, width)), low(n, width)],
        (stream, part0, part1, part2, enc_out_bias, enc_gain, enc_norm_bias),
    )
    y = [normed2, near(normed2), far(normed2)]

    def feed(xa, xb):
        return chain(
            mlp_body,
            [kept(low(2, n, ff))] * 2 + [low(n, width)] * 2,
            (xa, xb, enc_up, enc_up_bias.reshape(1, -1), enc_down),
        )

    hida, dga, part0, part1 = feed(y[0], y[1])
    part1 = near(part1)
    far_vector = chain.pin(far_vector)
    near_vectors = near(jnp.concatenate([vector, far_vector], axis=0))
    if split:
        got = join(got, more)
        more = swap(got, "dp", 1)
    else:
        more = got[pack_rows // 2 :]
        got = got[: pack_rows // 2]
    far_weights = [got, more]
    near_weights = [near(got)]
    both(y)
    hidb, dgb, part2, part3 = feed(y[2], y[3])
    part3 = near(part3)
    far_weights[1] = chain.pin(more)
    near_weights.append(near(far_weights[1]))
    part2 = far(add(part2, part3))

    small = [vector, near_vectors[:1], far_vector, near_vectors[1:]]
    qv_full = jnp.concatenate([b[:, : 2 * dshare].reshape(2, dshare) for b in small], axis=1)
    upb_full = jnp.concatenate([b[:, 2 * dshare :] for b in small], axis=1)
    (enc_low, output, x1, x2, hid, mix, gp, gm, g3, gz, ge_low, ge, dec_sums) = chain(
        decoder_body,
        [kept(o) for o in (low(n, width), full(n, dwidth), low(n, dwidth), low(n, dwidth), low(n, dff),
                           low(n, dwidth), low(n, dff), low(n, dwidth), low(n, 3 * dwidth), low(n, dwidth))]
        + [low(n, width), kept(full(n, width)), kept(full(8, width))],
        (jnp.stack([slot, across.home]), middle, part0, part1, part2, enc_out_bias, packed, packed_near,
         *far_weights, *near_weights, qv_full, upb_full, pos, bias_a, dec_out_bias, dec_gain,
         dec_norm_bias, cotangent),
        smem=1,
        scratch=[
            pltpu.VMEM((4, dwidth, dwidth), bf16), pltpu.VMEM((4, dwidth, dwidth), bf16),
            pltpu.VMEM((3, dwidth, dwidth), bf16), pltpu.VMEM((dwidth, dwidth), bf16),
            pltpu.VMEM((width, dwidth), bf16), pltpu.VMEM((DHEADS, n, n), bf16),
            pltpu.VMEM((n, dff), bf16), pltpu.VMEM((3, n, dwidth), bf16), pltpu.VMEM((n, dwidth), f32),
        ],
        limit=40,
    )
    g = [ge_low, near(ge_low), far(ge_low)]

    def feed_back(ga, gb, slope):
        return chain(
            mlp_back_body,
            [kept(low(2, n, ff)), kept(full(1, ff)), low(n, width), low(n, width)],
            (ga, gb, slope, enc_up, enc_down),
        )

    def attention_back(ga, gb, q, k, v, p):
        return chain(
            functools.partial(attn_back_body, scale, heads),
            [kept(low(2, n, 3 * share)), kept(full(2, share)), low(n, width), low(n, width)],
            (ga, gb, q, k, v, p, enc_qkv, enc_out_proj),
        )

    def plain(dims):
        return [dims], [(0, None, 0, dims[0] // 8, 0, dims[0] // 8, 0, dims[1], 0)]

    down = Sum(across, *plain((ff, width)))
    up = Sum(across, *plain((width, ff)))
    rows, fold = width // 8, share // 8
    attn = Sum(
        across,
        [(3, width, share), (share, width)],
        [(0, c, 0, rows, 0, rows, c * share, share, 0) for c in range(3)]
        + [(1, None, 0, fold, k * fold, fold, 3 * share, width // 4, k * (width // 4)) for k in range(4)],
    )
    part, thin, tall = dwidth // 8, dshare // 8, width // 8
    top = 2 * part + thin
    dec = Sum(
        across,
        [(dwidth, dwidth), (dwidth, dwidth), (dshare, dwidth), (3, dwidth, dshare), (width, dshare)],
        [
            (0, None, 0, part, 0, part, 0, dwidth, 0),
            (1, None, 0, part, part, part, 0, dwidth, 0),
            (2, None, 0, thin, 2 * part, thin, 0, dwidth, 0),
        ]
        + [(3, c, 0, part, top, part, c * dshare, dshare, 0) for c in range(3)]
        + [(4, None, 0, tall, top, part, 3 * dshare, dshare, 0)]
        + [(4, None, part + k * thin, tall, top + part, thin, k * dshare, dshare, 0) for k in range(4)],
    )

    gpa, upa, part0, part1 = feed_back(g[0], g[1], dga)
    part1 = near(part1)
    sent, kept_share = chain(
        decoder_weights_body,
        [low(2, pack_rows, dwidth), kept(low(2, pack_rows, dwidth))],
        (x1, x2, hid, mix, gp, gm, g3, gz, enc_low, cotangent),
        limit=24,
    )
    sent = near(sent)
    both(g)
    down.product([hida, hidb], g)
    gpb, upb, part2, part3 = feed_back(g[2], g[3], dgb)
    part3 = near(part3)
    there, mine = chain(
        far_body, [low(pack_rows // 2, dwidth)] * 2, (across.x.reshape(1), kept_share, sent), smem=1
    )
    part2 = far(add(part2, part3))
    there = far(there)
    grad_middle, gm_low, sums_mid = chain(
        mlp_end_body,
        [kept(full(n, width)), low(n, width), kept(full(16, width))],
        (at, ge, part0, part1, part2, middle, enc_gain, upa, upb, dec_sums),
        smem=1,
    )
    m = [gm_low, near(gm_low), far(gm_low)]
    up.product(y, [gpa, gpb])
    g3a, sa, part0, part1 = attention_back(m[0], m[1], qa, ka, va, pa)
    part1 = near(part1)
    mine = far(mine)
    down.step()
    dec.shares(kept_share, sent, there, mine)
    both(m)
    out_full = chain(out_weight_body, [low(share, width)], (mixa, mixb, *m))[0]
    g3b, sb, part2, part3 = attention_back(m[2], m[3], qb, kb, vb, pb)
    part3 = near(part3)
    down.step()
    attn.product(x, [g3a, g3b], [out_full])
    part2 = far(add(part2, part3))
    down.step()
    up.step()
    dec.step()
    up.step()
    down.step()
    grad_tokens, sums = chain(
        last_body,
        [full(n, width), full(24, width)],
        (at, grad_middle, part0, part1, part2, stream, enc_gain, sa, sb, sums_mid),
        smem=1,
    )
    up.step()
    hops = [("mp", 1), ("mp", 2)] + [("dp", 1 << i) for i in range(across.size.bit_length() - 1)]
    hops = iter(hops)

    def hop(total):
        for axis, mask in hops:
            return add(total, swap(total, axis, mask))
        return total

    dec.step()
    down.step()
    sums = hop(sums)
    attn.step()
    up.step()
    dec.step()
    sums = hop(sums)
    attn.step()
    up.step()
    dec.step()
    sums = hop(sums)
    attn.step()
    down.step()
    dec.step()
    sums = hop(sums)
    attn.step()
    up.step()
    sums = hop(sums)
    attn.step()
    dec.step()
    for _ in range(8):
        sums = hop(sums)
    for flow in (down, up, dec, attn):
        for _ in range(7):
            flow.step()
    last, mid, small = sums[16:], sums[:8], sums[8:16]

    def own(whole, size):
        return lax.dynamic_slice_in_dim(whole, slot * size, size, whole.ndim - 1)

    return (
        output,
        grad_tokens,
        attn.result[0],
        own(last[2:4], share),
        attn.result[1],
        up.result[0],
        own(mid[4:8].reshape(-1), ff),
        down.result[0],
        jnp.concatenate([mid[0:1], small[0:1]], axis=0),
        jnp.concatenate([last[0:1], mid[1:2]], axis=0),
        jnp.concatenate([last[1:2], mid[2:3]], axis=0),
        dec.result[4],
        small[3, dwidth:],
        dec.result[3],
        own(small[4:6, dwidth:], dshare),
        dec.result[2],
        dec.result[0],
        own(small[6:8].reshape(-1), dff // 4),
        dec.result[1],
        small[1:3, :dwidth],
        small[1:3, dwidth:],
        small[3:5, :dwidth],
    )


def solution(mesh):
    return jax.shard_map(
        per_device,
        mesh=mesh,
        in_specs=(
            P(("dp", "mp"), None),
            P("dp", None),
            P("dp", None),
            P(None, None, "mp"),
            P(None, "mp"),
            P("mp", None),
            P(None, "mp"),
            P("mp"),
            P("mp", None),
            P(),
            P(),
            P(),
            P(None, "mp"),
            P(),
            P(None, None, "mp"),
            P(None, "mp"),
            P("mp", None),
            P(None, "mp"),
            P("mp"),
            P("mp", None),
            P(),
            P(),
            P(),
            P(("dp", "mp"), None),
        ),
        out_specs=(
            P(("dp", "mp"), None),
            P(("dp", "mp"), None),
            P(None, None, "mp"),
            P(None, "mp"),
            P("mp", None),
            P(None, "mp"),
            P("mp"),
            P("mp", None),
            P(),
            P(),
            P(),
            P(None, "mp"),
            P(),
            P(None, None, "mp"),
            P(None, "mp"),
            P("mp", None),
            P(None, "mp"),
            P("mp"),
            P("mp", None),
            P(),
            P(),
            P(),
        ),
        check_vma=False,
    )
```

```python
import functools
import math

import jax
import jax.numpy as jnp
from jax import lax
from jax.experimental import pallas as pl
from jax.experimental.pallas import tpu as pltpu
from jax.sharding import PartitionSpec as P

HEADS = 16
DHEADS = 16
norm_eps = 1e-06
f32 = jnp.float32
bf16 = jnp.bfloat16
MIB = 1 << 20
VMEM = pl.BlockSpec(memory_space=pltpu.VMEM)
SMEM = pl.BlockSpec(memory_space=pltpu.SMEM)
COST = pl.CostEstimate(flops=10**10, bytes_accessed=10**8, transcendentals=0)


def shaped(dims, kind):
    return jax.ShapeDtypeStruct(dims, kind)


def kept(shape):
    return pltpu.HBM(shape.shape, shape.dtype)


def in_hbm(value):
    return pltpu.with_memory_space_constraint(value, pltpu.HBM)


class Chain:
    def __init__(self):
        self.last = None

    def __call__(self, body, outs, args, smem=0, scratch=(), limit=16, prefetch=None, grid=None, specs=None):
        args = list(args)
        extra = self.last is not None
        lead = smem if prefetch is None else 1
        inner = body
        if extra:
            count = len(args) + (prefetch is not None)

            def inner(*refs):
                return body(*refs[:count], *refs[count + 1 :])

            args.append(self.last)
        tail = [pl.BlockSpec(memory_space=pl.ANY)] * extra
        params = pltpu.CompilerParams(vmem_limit_bytes=limit * MIB)
        cost = COST
        if prefetch is None:
            got = pl.pallas_call(
                inner,
                out_shape=outs,
                in_specs=[SMEM] * smem + [VMEM] * (len(args) - smem - extra) + tail,
                out_specs=[VMEM] * len(outs),
                scratch_shapes=scratch,
                compiler_params=params,
                cost_estimate=cost,
            )(*args)
        else:
            got = pl.pallas_call(
                inner,
                out_shape=outs,
                grid_spec=pltpu.PrefetchScalarGridSpec(
                    num_scalar_prefetch=1, grid=grid, in_specs=specs[0] + tail, out_specs=specs[1]
                ),
                compiler_params=params,
                cost_estimate=cost,
            )(prefetch, *args)
        self.last = min(got, key=lambda g: g.size * g.dtype.itemsize)
        return got

    def pin(self, value):
        any_space = pl.BlockSpec(memory_space=pl.ANY)
        args = (value,) if value is self.last else (value, self.last)
        got = pl.pallas_call(
            lambda *refs: None,
            out_shape=shaped(value.shape, value.dtype),
            in_specs=[any_space] * len(args),
            out_specs=any_space,
            input_output_aliases={0: 0},
            compiler_params=pltpu.CompilerParams(vmem_limit_bytes=MIB),
            cost_estimate=COST,
        )(*args)
        self.last = got
        return got

    def gap(self):
        self.pin(self.last)


def nn(a, b):
    return lax.dot_general(a, b, (((1,), (0,)), ((), ())), preferred_element_type=f32)


def nt(a, b):
    return lax.dot_general(a, b, (((1,), (1,)), ((), ())), preferred_element_type=f32)


def tn(a, b):
    return lax.dot_general(a, b, (((0,), (0,)), ((), ())), preferred_element_type=f32)


def swap(value, axis, mask):
    size = lax.axis_size(axis)
    return lax.ppermute(value, axis, [(i, i ^ mask) for i in range(size)])


def norm_parts(values):
    average = jnp.mean(values, axis=-1, keepdims=True)
    centred = values - average
    variance = jnp.mean(centred * centred, axis=-1, keepdims=True)
    scale = lax.rsqrt(variance + norm_eps)
    return centred * scale, scale


def norm_back(normal, scale, gain, grad):
    wide = grad * gain
    one = jnp.mean(wide, axis=-1, keepdims=True)
    two = jnp.mean(wide * normal, axis=-1, keepdims=True)
    return scale * (wide - one - normal * two)


def gelu_both(v):
    slope = math.sqrt(2.0 / math.pi)
    square = v * v
    t = jnp.tanh(slope * v * (1.0 + 0.044715 * square))
    half = 0.5 * (1.0 + t)
    return v * half, half + 0.5 * slope * v * (1.0 - t * t) * (1.0 + 3.0 * 0.044715 * square)


def sin_cos(x):
    turn = jnp.floor(x * (2.0 / math.pi) + 0.5)
    r = ((x - turn * 1.5703125) - turn * 4.837512969970703125e-4) - turn * 7.54978995489188216e-8
    z = r * r
    s = r + r * z * (-1.6666654611e-1 + z * (8.3321608736e-3 + z * -1.9515295891e-4))
    c = 1.0 - 0.5 * z + z * z * (
        4.166664568298827e-2 + z * (-1.388731625493765e-3 + z * 2.443315711809948e-5)
    )
    quarter = turn.astype(jnp.int32)
    odd = (quarter & 1) != 0
    sine = jnp.where(odd, c, s)
    cosine = jnp.where(odd, s, c)
    sine = jnp.where((quarter & 2) != 0, -sine, sine)
    cosine = jnp.where(((quarter + 1) & 2) != 0, -cosine, cosine)
    return sine, cosine


def head_masks(heads):
    size = 256 // heads
    lane = lax.broadcasted_iota(jnp.int32, (1, 256), 1)
    return [
        jnp.where((lane >= h * size) & (lane < (h + 1) * size), 1.0, 0.0).astype(bf16)
        for h in range(heads)
    ]


def attend(q, k, v, bias, heads, scale, keep):
    size = 256 // heads
    vt = v.astype(f32).T.astype(bf16)
    mixes = []
    for h, mask in enumerate(head_masks(heads)):
        s = nt(k, q * mask) + bias
        top = jnp.max(s, axis=0, keepdims=True)
        p = jnp.exp2((s - top) * (scale * math.log2(math.e)))
        total = jnp.sum(p, axis=0, keepdims=True)
        p = (p * (1.0 / total)).astype(bf16)
        keep(h, p)
        mixes.append(nn(vt[h * size : (h + 1) * size], p))
    return jnp.concatenate(mixes, axis=0).T


def attend_back(q, k, v, gm, probs, heads, scale):
    size = 256 // heads
    kt = k.astype(f32).T.astype(bf16)
    gq, gk, gv = [], 0.0, 0.0
    for h, mask in enumerate(head_masks(heads)):
        gmh = gm * mask
        p = probs(h)
        wide = p.astype(f32)
        t = wide * nt(v, gmh)
        gs = (t - wide * jnp.sum(t, axis=0, keepdims=True)).astype(bf16)
        gk = gk + nn(gs, q * mask)
        gv = gv + nn(p, gmh)
        gq.append(nn(kt[h * size : (h + 1) * size], gs))
    return jnp.concatenate(gq, axis=0).T * scale, gk * scale, gv


def place_of(slot, seg_ref, gsd_ref):
    n = seg_ref.shape[1]
    across = jnp.broadcast_to(seg_ref[pl.ds(slot, 1), :].astype(f32), (n, n))
    earlier = lax.broadcasted_iota(jnp.int32, (n, n), 1) < lax.broadcasted_iota(jnp.int32, (n, n), 0)
    rank = jnp.sum(jnp.where((across == across.T) & earlier, 1.0, 0.0), axis=1, keepdims=True)
    index = jnp.broadcast_to(gsd_ref[pl.ds(slot, 1), :].astype(f32), (n, n)).T[:, :1]
    return rank * (0.5 + 0.25 * index)


def start_body(slot_ref, seg_ref, gsd_ref, tokens_ref, gain_ref, shift_ref, wf_ref, normed_ref, stream_ref):
    place = place_of(slot_ref[0], seg_ref, gsd_ref)
    half = wf_ref.shape[1]
    sine, cosine = sin_cos(place * wf_ref[...])
    stream_ref[:, :half] = tokens_ref[:, :half].astype(f32) + sine
    stream_ref[:, half:] = tokens_ref[:, half:].astype(f32) + cosine
    normal, _ = norm_parts(stream_ref[...])
    normed_ref[...] = (normal * gain_ref[0:1] + shift_ref[0:1]).astype(bf16)


def mask_body(slot_ref, seg_ref, gsd_ref, tokens_ref, eb_ref, wf_ref, nf_ref, bias_a_ref, bias_b_ref, pos_ref, stream_ref):
    slot = slot_ref[0]
    n = seg_ref.shape[1]
    for j in range(4):
        across = jnp.broadcast_to(seg_ref[pl.ds(slot ^ j, 1), :].astype(f32), (n, n))
        (bias_a_ref, bias_b_ref)[j // 2][j % 2] = jnp.where(across == across.T, 0.0, -1e30)
    place = place_of(slot, seg_ref, gsd_ref)
    half = wf_ref.shape[1]
    sine, cosine = sin_cos(place * wf_ref[...])
    stream_ref[:, :half] = tokens_ref[:, :half].astype(f32) + sine
    stream_ref[:, half:] = tokens_ref[:, half:].astype(f32) + cosine
    half = nf_ref.shape[1]
    sine, cosine = sin_cos(place * nf_ref[...])
    pos_ref[:, :half] = sine + eb_ref[:, :half]
    pos_ref[:, half:] = cosine + eb_ref[:, half:]


def attn_body(scale, heads, xa_ref, xb_ref, bias_ref, w_ref, qvb_ref, o_ref,
              q_ref, k_ref, v_ref, p_ref, mix_ref, pa_ref, pb_ref):
    for r, (x_ref, part_ref) in enumerate(((xa_ref, pa_ref), (xb_ref, pb_ref))):
        x = x_ref[...]
        q = (nn(x, w_ref[0]) + qvb_ref[0:1]).astype(bf16)
        k = nn(x, w_ref[1]).astype(bf16)
        v = (nn(x, w_ref[2]) + qvb_ref[1:2]).astype(bf16)
        q_ref[r], k_ref[r], v_ref[r] = q, k, v

        def keep(h, p):
            p_ref[r, h] = p

        mix = attend(q, k, v, bias_ref[r], heads, scale, keep).astype(bf16)
        mix_ref[r] = mix
        part_ref[...] = nn(mix, o_ref[...]).astype(bf16)


def attn_back_body(scale, heads, ga_ref, gb_ref, q_ref, k_ref, v_ref, p_ref, w_ref, o_ref,
                   g3_ref, sums_ref, pa_ref, pb_ref):
    total_q, total_v = 0.0, 0.0
    for r, (g_ref, part_ref) in enumerate(((ga_ref, pa_ref), (gb_ref, pb_ref))):
        gm = nt(g_ref[...], o_ref[...]).astype(bf16)
        gq, gk, gv = attend_back(
            q_ref[r], k_ref[r], v_ref[r], gm, lambda h: p_ref[r, h], heads, scale
        )
        total_q = total_q + jnp.sum(gq, axis=0, keepdims=True)
        total_v = total_v + jnp.sum(gv, axis=0, keepdims=True)
        acc = 0.0
        for c, g in enumerate((gq, gk, gv)):
            low = g.astype(bf16)
            g3_ref[r, :, c * 256 : (c + 1) * 256] = low
            acc = acc + nt(low, w_ref[c])
        part_ref[...] = acc.astype(bf16)
    sums_ref[0:1] = total_q
    sums_ref[1:2] = total_v


def mid_body(stream_ref, p_ref, near_ref, far_ref, ob_ref, gain_ref, shift_ref, mid_ref, normed_ref):
    total = p_ref[...].astype(f32) + near_ref[...].astype(f32) + far_ref[...].astype(f32)
    middle = stream_ref[...] + total + ob_ref[0:1]
    mid_ref[...] = middle
    normal, _ = norm_parts(middle)
    normed_ref[...] = (normal * gain_ref[1:2] + shift_ref[1:2]).astype(bf16)


def mlp_body(xa_ref, xb_ref, up_ref, ub_ref, down_ref, hid_ref, dg_ref, pa_ref, pb_ref):
    width = up_ref.shape[1]
    for r, (x_ref, part_ref) in enumerate(((xa_ref, pa_ref), (xb_ref, pb_ref))):
        x = x_ref[...]
        for c in range(0, width, 256):
            cut = slice(c, c + 256)
            hidden, slope = gelu_both(nn(x, up_ref[:, cut]) + ub_ref[:, cut])
            hid_ref[r, :, cut] = hidden.astype(bf16)
            dg_ref[r, :, cut] = slope.astype(bf16)
        hidden = hid_ref[r]
        for c in range(0, down_ref.shape[1], 512):
            cut = slice(c, c + 512)
            part_ref[:, cut] = nn(hidden, down_ref[:, cut]).astype(bf16)


def mlp_back_body(ga_ref, gb_ref, dg_ref, up_ref, down_ref, gp_ref, sums_ref, pa_ref, pb_ref):
    width = up_ref.shape[1]
    for r, (g_ref, part_ref) in enumerate(((ga_ref, pa_ref), (gb_ref, pb_ref))):
        g = g_ref[...]
        for c in range(0, width, 256):
            cut = slice(c, c + 256)
            grad = nt(g, down_ref[cut]) * dg_ref[r, :, cut].astype(f32)
            gp_ref[r, :, cut] = grad.astype(bf16)
            total = jnp.sum(grad, axis=0, keepdims=True)
            sums_ref[:, cut] = total if r == 0 else sums_ref[:, cut] + total
        gp = gp_ref[r]
        for c in range(0, up_ref.shape[0], 512):
            cut = slice(c, c + 512)
            part_ref[:, cut] = nt(gp, up_ref[cut]).astype(bf16)


def mlp_end_body(slot_ref, ge_ref, p_ref, near_ref, far_ref, mid_ref, gain_ref, ua_ref, ub_ref, dec_ref,
                 gmid_ref, gm_ref, pack_ref):
    slot = slot_ref[0]
    grad = p_ref[...].astype(f32) + near_ref[...].astype(f32) + far_ref[...].astype(f32)
    normal, scale = norm_parts(mid_ref[...])
    gmid = ge_ref[...] + norm_back(normal, scale, gain_ref[1:2], grad)
    gmid_ref[...] = gmid
    gm_ref[...] = gmid.astype(bf16)
    pack_ref[...] = jnp.zeros(pack_ref.shape, f32)
    pack_ref[0:1] = jnp.sum(gmid, axis=0, keepdims=True)
    pack_ref[1:2] = jnp.sum(grad * normal, axis=0, keepdims=True)
    pack_ref[2:3] = jnp.sum(grad, axis=0, keepdims=True)
    pack_ref[pl.ds(4 + slot, 1), :] = ua_ref[...] + ub_ref[...]
    pack_ref[8:16] = dec_ref[...]


def last_body(slot_ref, gmid_ref, p_ref, near_ref, far_ref, stream_ref, gain_ref, sa_ref, sb_ref, mid_ref,
              gtok_ref, pack_ref):
    slot = slot_ref[0]
    grad = p_ref[...].astype(f32) + near_ref[...].astype(f32) + far_ref[...].astype(f32)
    normal, scale = norm_parts(stream_ref[...])
    gtok_ref[...] = gmid_ref[...] + norm_back(normal, scale, gain_ref[0:1], grad)
    pack_ref[:16] = mid_ref[...]
    pack_ref[16:] = jnp.zeros((8, pack_ref.shape[1]), f32)
    pack_ref[16:17] = jnp.sum(grad * normal, axis=0, keepdims=True)
    pack_ref[17:18] = jnp.sum(grad, axis=0, keepdims=True)
    share = sa_ref.shape[1]
    place = pl.ds(pl.multiple_of(slot * share, share), share)
    pack_ref[18:20, place] = sa_ref[...] + sb_ref[...]


def decoder_body(slot_ref, mid_ref, p_ref, near_ref, far_ref, eob_ref, own_ref, by_ref, fa_ref, fb_ref, na_ref, nb_ref,
                 qvb_ref, upb_ref, pos_ref, bias_ref, dob_ref, dgain_ref, dnb_ref, cot_ref,
                 encl_ref, out_ref, x1_ref, x2_ref, hid_ref, mix_ref, gp_ref, gm_ref, g3_ref, gz_ref,
                 gel_ref, ge_ref, sums_ref,
                 wup, wdown, wqkv, wout, wemb, pt, dg, qkv, wide):
    slot, home = slot_ref[0], slot_ref[1]
    width = cot_ref.shape[1]
    block = width // 4
    heads = DHEADS * 256 // width
    groups = width // 256
    scale = (width // DHEADS) ** -0.5

    def place(j, base=0):
        return pl.ds(pl.multiple_of(base + (slot ^ j) * block, block), block)

    piece, thin, tall = width // 8, block // 8, 2 * width // 8
    top = 2 * piece + thin
    step = top + piece + thin
    for j, (low_ref, high_ref) in enumerate(
        ((own_ref, own_ref), (by_ref, by_ref), (fa_ref, fb_ref), (na_ref, nb_ref))
    ):
        cut = slice(j * block, (j + 1) * block)
        for i in range(8):
            ref = (low_ref, high_ref)[i // 4]
            base = (i if j < 2 else i % 4) * step
            chunk = i if j < 2 else home ^ i

            def rows(size):
                return pl.ds(pl.multiple_of(chunk * size, size), size)

            wup[j, rows(piece)] = ref[base : base + piece]
            wdown[j, rows(piece)] = ref[base + piece : base + 2 * piece]
            wout[pl.ds(pl.multiple_of(j * block + chunk * thin, thin), thin)] = (
                ref[base + 2 * piece : base + top]
            )
            for c in range(3):
                wqkv[c, rows(piece), cut] = ref[base + top : base + top + piece, c * block : (c + 1) * block]
            wemb[pl.ds(pl.multiple_of(chunk * tall, tall), piece), cut] = (
                ref[base + top : base + top + piece, 3 * block :]
            )
            for c in range(4):
                wemb[pl.ds(pl.multiple_of(chunk * tall + piece + c * thin, thin), thin), cut] = (
                    ref[base + top + piece : base + step, c * block : (c + 1) * block]
                )
    encoded = mid_ref[...] + eob_ref[1:2]
    encoded = encoded + p_ref[...].astype(f32) + near_ref[...].astype(f32) + far_ref[...].astype(f32)
    encl_ref[...] = encoded.astype(bf16)
    embedded = nn(encl_ref[...], wemb[...])
    for j in range(4):
        wide[:, place(j)] = embedded[:, j * block : (j + 1) * block]
    stream = wide[...] + pos_ref[...]
    normal1, scale1 = norm_parts(stream)
    x1_ref[...] = (normal1 * dgain_ref[0:1] + dnb_ref[0:1]).astype(bf16)
    x1 = x1_ref[...]
    qkv[0] = (nn(x1, wqkv[0]) + qvb_ref[0:1]).astype(bf16)
    qkv[1] = nn(x1, wqkv[1]).astype(bf16)
    qkv[2] = (nn(x1, wqkv[2]) + qvb_ref[1:2]).astype(bf16)
    bias = bias_ref[0]
    for g in range(groups):
        cut = slice(g * 256, (g + 1) * 256)

        def keep(h, p):
            pt[g * heads + h] = p

        mix_ref[:, cut] = attend(
            qkv[0, :, cut], qkv[1, :, cut], qkv[2, :, cut], bias, heads, scale, keep
        ).astype(bf16)
    middle = stream + nn(mix_ref[...], wout[...]) + dob_ref[0:1]
    normal2, scale2 = norm_parts(middle)
    x2_ref[...] = (normal2 * dgain_ref[1:2] + dnb_ref[1:2]).astype(bf16)
    x2 = x2_ref[...]
    result = middle + dob_ref[1:2]
    for j in range(4):
        cut = slice(j * width, (j + 1) * width)
        hidden, slope = gelu_both(nn(x2, wup[j]) + upb_ref[:, cut])
        hid_ref[:, cut] = hidden.astype(bf16)
        dg[:, cut] = slope.astype(bf16)
        result = result + nn(hid_ref[:, cut], wdown[j])
    out_ref[...] = result

    cot = cot_ref[...]
    grad = 0.0
    sums_ref[...] = jnp.zeros(sums_ref.shape, f32)
    for j in range(4):
        cut = slice(j * width, (j + 1) * width)
        pre = nt(cot, wdown[j]) * dg[:, cut].astype(f32)
        gp_ref[:, cut] = pre.astype(bf16)
        block_sum = jnp.sum(pre, axis=0, keepdims=True)
        at = slot ^ j
        sums_ref[pl.ds(6 + (at >> 1), 1), pl.ds(pl.multiple_of((at & 1) * width, width), width)] = (
            block_sum
        )
        grad = grad + nt(gp_ref[:, cut], wup[j])
    cotf = cot.astype(f32)
    gmid = cotf + norm_back(normal2, scale2, dgain_ref[1:2], grad)
    gm_ref[...] = gmid.astype(bf16)
    sums_ref[1:2, :width] = jnp.sum(gmid, axis=0, keepdims=True)
    sums_ref[2:3, :width] = jnp.sum(cotf, axis=0, keepdims=True)
    sums_ref[2:3, width:] = jnp.sum(grad * normal2, axis=0, keepdims=True)
    sums_ref[4:5, :width] = jnp.sum(grad, axis=0, keepdims=True)
    gmix = nt(gm_ref[...], wout[...]).astype(bf16)
    grad = 0.0
    for g in range(groups):
        cut = slice(g * 256, (g + 1) * 256)
        three = attend_back(
            qkv[0, :, cut], qkv[1, :, cut], qkv[2, :, cut], gmix[:, cut],
            lambda h: pt[g * heads + h], heads, scale,
        )
        for c, part in enumerate(three):
            begin = c * width + g * 256
            low = part.astype(bf16)
            g3_ref[:, begin : begin + 256] = low
            grad = grad + nt(low, wqkv[c, :, cut])
        for c, row, base in ((0, 4, width), (2, 5, width)):
            total = jnp.sum(three[c], axis=0, keepdims=True)
            for i in range(256 // block):
                sums_ref[row : row + 1, place(g * (256 // block) + i, base)] = (
                    total[:, i * block : (i + 1) * block]
                )
    gstream = gmid + norm_back(normal1, scale1, dgain_ref[0:1], grad)
    sums_ref[3:4, width:] = jnp.sum(gstream, axis=0, keepdims=True)
    sums_ref[1:2, width:] = jnp.sum(grad * normal1, axis=0, keepdims=True)
    sums_ref[3:4, :width] = jnp.sum(grad, axis=0, keepdims=True)
    wide[...] = gstream
    for j in range(4):
        gz_ref[:, j * block : (j + 1) * block] = wide[:, place(j)].astype(bf16)
    ge = nt(gz_ref[...], wemb[...])
    ge_ref[...] = ge
    gel_ref[...] = ge.astype(bf16)
    sums_ref[0:1] = jnp.sum(ge, axis=0, keepdims=True)


def decoder_weights_body(x1_ref, x2_ref, hid_ref, mix_ref, gp_ref, gm_ref, g3_ref, gz_ref, encl_ref, cot_ref,
                         sent_ref, kept_ref):
    width = cot_ref.shape[1]
    block = width // 4
    cot, gm, x2 = cot_ref[...], gm_ref[...], x2_ref[...]
    piece, thin = width // 8, block // 8
    tall = encl_ref.shape[1] // 8
    top = 2 * piece + thin
    step = top + piece + thin

    def to(j):
        return sent_ref if j % 2 else kept_ref

    for j in (1, 3, 0, 2):
        w = to(j)
        i = j // 2
        cut = slice(j * width, (j + 1) * width)
        up = tn(x2, gp_ref[:, cut]).astype(bf16)
        down = tn(hid_ref[:, cut], cot).astype(bf16)
        out = tn(mix_ref[:, j * block : (j + 1) * block], gm).astype(bf16)
        for c in range(8):
            w[i, c * step : c * step + piece] = up[c * piece : (c + 1) * piece]
            w[i, c * step + piece : c * step + 2 * piece] = down[c * piece : (c + 1) * piece]
            w[i, c * step + 2 * piece : c * step + top] = out[c * thin : (c + 1) * thin]
    x1 = x1_ref[...]
    for k in range(3):
        full = tn(x1, g3_ref[:, k * width : (k + 1) * width]).astype(bf16)
        for j in range(4):
            for c in range(8):
                to(j)[j // 2, c * step + top : c * step + top + piece, k * block : (k + 1) * block] = (
                    full[c * piece : (c + 1) * piece, j * block : (j + 1) * block]
                )
    full = tn(encl_ref[...], gz_ref[...]).astype(bf16)
    for j in range(4):
        cut = slice(j * block, (j + 1) * block)
        for c in range(8):
            base = c * tall
            to(j)[j // 2, c * step + top : c * step + top + piece, 3 * block :] = full[base : base + piece, cut]
            base = base + piece
            for k in range(4):
                to(j)[j // 2, c * step + top + piece : (c + 1) * step, k * block : (k + 1) * block] = (
                    full[base + k * thin : base + (k + 1) * thin, cut]
                )


def pack_body(pick_ref, up_ref, down_ref, out_ref, qkv_ref, emb_ref, chunk_ref):
    piece, thin, block = up_ref.shape[0], out_ref.shape[0], emb_ref.shape[1]
    chunk_ref[:piece] = up_ref[...]
    chunk_ref[piece : 2 * piece] = down_ref[...]
    top = 2 * piece + thin
    chunk_ref[2 * piece : top] = out_ref[...]
    for c in range(3):
        chunk_ref[top : top + piece, c * block : (c + 1) * block] = qkv_ref[c]
    chunk_ref[top : top + piece, 3 * block :] = emb_ref[:piece]
    for c in range(4):
        base = piece + c * thin
        chunk_ref[top + piece :, c * block : (c + 1) * block] = emb_ref[base : base + thin]


def join_body(a_ref, b_ref, out_ref):
    rows = a_ref.shape[0]
    out_ref[:rows] = a_ref[...]
    out_ref[rows:] = b_ref[...]


def add_body(a_ref, b_ref, out_ref):
    out_ref[...] = (a_ref[...].astype(f32) + b_ref[...].astype(f32)).astype(out_ref.dtype)


def add_all_body(*refs):
    total = refs[0][...]
    for ref in refs[1:-1]:
        total = total + ref[...]
    refs[-1][...] = total


def last_sums_body(slot_ref, *refs):
    terms, outs, total_ref = refs[:-12], refs[-12:-1], refs[-1]
    total = terms[0][...]
    for ref in terms[1:]:
        total = total + ref[...]
    total_ref[...] = total
    slot = slot_ref[0]
    e_qv, e_upb, e_ob, e_gain, e_nb, d_emb, d_qv, d_upb, d_ob, d_gain, d_nb = outs
    share, thin, width = e_qv.shape[1], d_qv.shape[1], d_emb.shape[1]
    e_qv[...] = total_ref[18:20, pl.ds(pl.multiple_of(slot * share, share), share)]
    e_upb[...] = total_ref[pl.ds(4 + slot, 1), :]
    e_ob[0:1] = total_ref[0:1]
    e_ob[1:2] = total_ref[8:9]
    e_gain[0:1] = total_ref[16:17]
    e_gain[1:2] = total_ref[1:2]
    e_nb[0:1] = total_ref[17:18]
    e_nb[1:2] = total_ref[2:3]
    d_ob[...] = total_ref[9:11, :width]
    d_gain[...] = total_ref[9:11, width:]
    d_nb[...] = total_ref[11:13, :width]
    d_emb[...] = total_ref[11:12, width:]
    d_qv[...] = total_ref[12:14, pl.ds(pl.multiple_of(width + slot * thin, thin), thin)]
    d_upb[...] = total_ref[pl.ds(14 + (slot >> 1), 1), pl.ds(pl.multiple_of((slot & 1) * width, width), width)]


def halve_body(bit_ref, *refs):
    ins, (send_ref, keep_ref) = refs[:-2], refs[-2:]
    half = send_ref.shape[0]
    bit = bit_ref[0]
    for ref, which in ((send_ref, 1 - bit), (keep_ref, bit)):
        rows = pl.ds(pl.multiple_of(which * half, half), half)
        total = ins[0][rows].astype(f32)
        for other in ins[1:]:
            total = total + other[rows].astype(f32)
        ref[...] = total.astype(bf16)


def far_body(bit_ref, kept_ref, near_ref, out_ref):
    half = out_ref.shape[0]
    rows = pl.ds(pl.multiple_of(bit_ref[0] * half, half), half)
    out_ref[...] = (kept_ref[1, rows].astype(f32) + near_ref[1, rows].astype(f32)).astype(bf16)


def there_body(bit_ref, kept_ref, near_ref, far_ref, send_ref):
    half = send_ref.shape[0]
    rows = pl.ds(pl.multiple_of((1 - bit_ref[0]) * half, half), half)
    total = kept_ref[0, rows].astype(f32) + near_ref[0, rows].astype(f32)
    send_ref[...] = (total + far_ref[...].astype(f32)).astype(bf16)


def mine_body(bit_ref, kept_ref, near_ref, far_ref, got_ref, send_ref, keep_ref):
    quarter = send_ref.shape[0]
    base = bit_ref[0] * 2 * quarter
    for ref, which in ((send_ref, 1 - bit_ref[1]), (keep_ref, bit_ref[1])):
        rows = pl.ds(pl.multiple_of(base + which * quarter, quarter), quarter)
        inner = pl.ds(pl.multiple_of(which * quarter, quarter), quarter)
        total = kept_ref[0, rows].astype(f32) + near_ref[0, rows].astype(f32)
        ref[...] = (total + far_ref[inner].astype(f32) + got_ref[inner].astype(f32)).astype(bf16)


def piece_of(refs, j):
    if len(refs) == 4:
        return refs[j][...]
    return refs[j // 2][j % 2]


def tile_sum(xs, gs, more):
    acc = 0.0
    for j in range(4):
        acc = acc + tn(piece_of(xs, j), piece_of(gs, j))
    if not more:
        return [(slice(None), slice(None), acc)]
    rows, cols = acc.shape
    parts = [(slice(None), slice(0, cols), acc)]
    half, quarter = rows // 2, rows // 8
    wide = more[0].shape[1] // 4
    for c in range(2):
        for k in range(4):
            parts.append((
                slice(c * half + k * quarter, c * half + (k + 1) * quarter),
                slice(cols, cols + wide),
                more[0][c * quarter : (c + 1) * quarter, k * wide : (k + 1) * wide].astype(f32),
            ))
    return parts


def first_half_body(nx, ng, nm, pick_ref, *refs):
    xs, gs, more = refs[:nx], refs[nx : nx + ng], refs[nx + ng : nx + ng + nm]
    out_ref = refs[nx + ng + nm]
    for rows, cols, value in tile_sum(xs, gs, more):
        out_ref[rows, cols] = value.astype(bf16)


def other_half_body(nx, ng, nm, pick_ref, *refs):
    xs, gs, more = refs[:nx], refs[nx : nx + ng], refs[nx + ng : nx + ng + nm]
    add_ref, send_ref, keep_ref = refs[nx + ng + nm :]
    parts = [
        (rows, cols, (value + add_ref[rows, cols].astype(f32)).astype(bf16))
        for rows, cols, value in tile_sum(xs, gs, more)
    ]

    def put(ref):
        for rows, cols, value in parts:
            ref[rows, cols] = value

    @pl.when(pl.program_id(0) == 0)
    def _():
        put(send_ref)

    @pl.when(pl.program_id(0) == 1)
    def _():
        put(keep_ref)


def weight_half(chain, xs, gs, more, pick, add=None):
    tile = xs[0].shape[-1] // 4
    out_cols = gs[0].shape[-1] + sum(m.shape[1] // 4 for m in more)

    def column(shape):
        lead = shape[:-1]
        return pl.BlockSpec(lead + (tile,), lambda i, p: (0,) * len(lead) + (p[i],))

    def whole(shape):
        return pl.BlockSpec(shape, lambda i, p: (0,) * len(shape))

    in_specs = [column(x.shape) for x in xs] + [whole(g.shape) for g in gs]
    in_specs += [pl.BlockSpec((tile // 4, m.shape[1]), lambda i, p: (p[i], 0)) for m in more]
    args = list(xs) + list(gs) + list(more)
    counts = len(xs), len(gs), len(more)
    if add is None:
        body = functools.partial(first_half_body, *counts)
        outs = [shaped((2 * tile, out_cols), bf16)]
        out_specs = [pl.BlockSpec((tile, out_cols), lambda i, p: (i, 0))]
    else:
        body = functools.partial(other_half_body, *counts)
        in_specs.append(pl.BlockSpec((tile, out_cols), lambda i, p: (p[2 + i], 0)))
        args.append(add)
        outs = [shaped((tile, out_cols), bf16)] * 2
        out_specs = [pl.BlockSpec((tile, out_cols), lambda i, p: (0, 0))] * 2
    return chain(body, outs, args, prefetch=pick, grid=(2,), specs=(in_specs, out_specs), limit=20)


def spread_body(writes, place_ref, near_ref, far_ref, *out_refs):
    chunk = near_ref.shape[0] // 4
    for i in range(8):
        ref = (near_ref, far_ref)[i // 4]
        at = place_ref[0] ^ i
        base = i % 4 * chunk
        for which, lead, first, every, row, rows, col, cols, at_col in writes:
            value = ref[base + row : base + row + rows, col : col + cols].astype(f32)
            to = pl.ds(pl.multiple_of(at * every + first, rows), rows)
            if lead is None:
                out_refs[which][to, at_col : at_col + cols] = value
            else:
                out_refs[which][lead, to] = value


def out_weight_body(xa_ref, xb_ref, g0, g1, g2, g3, out_ref):
    acc = 0.0
    for j, g_ref in enumerate((g0, g1, g2, g3)):
        acc = acc + tn(piece_of((xa_ref, xb_ref), j), g_ref[...])
    out_ref[...] = acc.astype(bf16)


class Across:
    def __init__(self, chain):
        self.chain = chain
        self.size = lax.axis_size("dp")
        me = lax.axis_index("dp").astype(jnp.int32)
        self.x, self.b2, self.b4 = [(me >> i) & 1 for i in range(3)]
        home = 4 * self.x + 2 * self.b2 + self.b4
        self.home = home if self.size == 8 else jnp.int32(0)
        self.place = self.home.reshape(1)
        self.there = jnp.stack([2 * (1 - self.x), 2 * (1 - self.x) + 1])
        self.mine = jnp.stack([2 * self.x + 1 - self.b2, 2 * self.x + self.b2, 1 - self.b2, self.b2])


class Sum:
    def __init__(self, across, outs, writes):
        self.across, self.chain = across, across.chain
        self.outs, self.writes = outs, writes
        self.result = None
        rest = [self.second, self.third, self.fourth, self.fifth, self.last]
        self.steps = iter(rest if across.size == 8 else [])

    def step(self):
        for todo in self.steps:
            todo()
            return

    def halve(self, bit, *terms):
        rows, cols = terms[0].shape
        half = shaped((rows // 2, cols), bf16)
        return self.chain(halve_body, [half, half], (bit.reshape(1), *terms), smem=1)

    def product(self, xs, gs, more=()):
        a = self.across
        self.terms = (xs, gs, more)
        if a.size != 8:
            first = weight_half(self.chain, *self.terms, jnp.array([0, 1], jnp.int32))[0]
            other = weight_half(self.chain, *self.terms, jnp.array([2, 3], jnp.int32))[0]
            return self.general(jnp.concatenate([first, other], axis=0))
        self.got = swap(weight_half(self.chain, *self.terms, a.there)[0], "dp", 1)

    def shares(self, kept, near, there, mine):
        self.terms = None
        a = self.across
        if a.size != 8:
            total = kept[0].astype(f32) + near[0].astype(f32)
            total = total + jnp.concatenate([swap(mine, "mp", 2), there], axis=0).astype(f32)
            return self.general(total.astype(bf16))
        self.held = (kept, near, swap(mine, "mp", 2))
        half = shaped(there.shape, bf16)
        send = self.chain(there_body, [half], (a.x.reshape(1), kept, near, there), smem=1)[0]
        self.got = swap(send, "dp", 1)

    def second(self):
        a = self.across
        if self.terms is None:
            rows, cols = self.got.shape
            half = shaped((rows // 2, cols), bf16)
            send, self.keep = self.chain(
                mine_body, [half, half], (jnp.stack([a.x, a.b2]), *self.held, self.got), smem=1
            )
        else:
            send, self.keep = weight_half(self.chain, *self.terms, a.mine, self.got)
        self.got = swap(send, "dp", 2)

    def third(self):
        send, self.keep = self.halve(self.across.b4, self.keep, self.got)
        self.got = swap(send, "dp", 4)

    def fourth(self):
        self.keep = self.chain(add_body, [shaped(self.keep.shape, bf16)], (self.keep, self.got))[0]
        self.got = swap(self.keep, "dp", 4)

    def join(self):
        rows, cols = self.keep.shape
        self.keep = self.chain(join_body, [shaped((2 * rows, cols), bf16)], (self.keep, self.got))[0]

    def fifth(self):
        self.join()
        self.got = swap(self.keep, "dp", 2)
        self.steps = iter([self.sixth, self.last])

    def sixth(self):
        self.join()
        self.got = swap(self.keep, "dp", 1)

    def last(self):
        self.spread(self.keep, self.got)

    def spread(self, near, far):
        self.result = self.chain(
            functools.partial(spread_body, self.writes),
            [kept(shaped(dims, f32)) for dims in self.outs],
            (self.across.place, near, far),
            smem=1,
        )

    def general(self, held):
        me = lax.axis_index("dp")
        bits = [1 << i for i in range(self.across.size.bit_length() - 1)]
        for bit in bits:
            mine = (me & bit) != 0
            half = held.shape[0] // 2
            other = lax.dynamic_slice_in_dim(held, jnp.where(mine, 0, half), half, 0)
            own = lax.dynamic_slice_in_dim(held, jnp.where(mine, half, 0), half, 0)
            held = (own.astype(f32) + swap(other, "dp", bit).astype(f32)).astype(bf16)
        for bit in reversed(bits):
            mine = (me & bit) != 0
            other = swap(held, "dp", bit)
            held = jnp.where(
                mine,
                jnp.concatenate([other, held], axis=0),
                jnp.concatenate([held, other], axis=0),
            )
        half = held.shape[0] // 2
        self.spread(held[:half], held[half:])


def per_device(
    tokens, segment_ids, gsd_index, enc_qkv, enc_qv_bias, enc_out_proj, enc_up, enc_up_bias,
    enc_down, enc_out_bias, enc_gain, enc_norm_bias, embed_weight, embed_bias, dec_qkv,
    dec_qv_bias, dec_out_proj, dec_up, dec_up_bias, dec_down, dec_out_bias, dec_gain,
    dec_norm_bias, cotangent,
):
    n, width = tokens.shape
    rows, length = segment_ids.shape
    assert rows == 4 and n == length == 256 and lax.axis_size("mp") == 4
    share, ff = enc_qkv.shape[2], enc_up.shape[1]
    dwidth, dff = cotangent.shape[1], dec_up.shape[1] * 4
    dshare = dwidth // 4
    heads = share // (width // HEADS)
    scale = (width // HEADS) ** -0.5
    slot = lax.axis_index("mp").astype(jnp.int32)
    at = slot.reshape(1)
    chain = Chain()
    across = Across(chain)

    def low(*dims):
        return shaped(dims, bf16)

    def full(*dims):
        return shaped(dims, f32)

    def waves(size):
        half = size // 2
        return jnp.power(10000.0, -jnp.arange(half, dtype=f32) / half).reshape(1, half)

    def near(value):
        return swap(value, "mp", 1)

    def far(value):
        return swap(value, "mp", 2)

    pack_rows = 3 * dwidth + 2 * dshare
    decoder_weights = [in_hbm(w) for w in (dec_up, dec_down, dec_out_proj, dec_qkv, embed_weight)]

    def pack(pick, steps):
        def block(shape):
            if len(shape) == 3:
                return pl.BlockSpec((shape[0], shape[1] // 8, shape[2]), lambda i, p: (0, p[i], 0))
            return pl.BlockSpec((shape[0] // 8, shape[1]), lambda i, p: (p[i], 0))

        rows = pack_rows // 8
        return chain(
            pack_body,
            [low(steps * rows, dwidth)],
            decoder_weights,
            prefetch=pick,
            grid=(steps,),
            specs=([block(w.shape) for w in decoder_weights], [pl.BlockSpec((rows, dwidth), lambda i, p: (i, 0))]),
        )[0]

    split = across.size == 8
    got = far(pack(across.place, 1)) if split else None
    normed = chain(
        start_body,
        [low(n, width)],
        (at, in_hbm(segment_ids), in_hbm(gsd_index), in_hbm(tokens), in_hbm(enc_gain), in_hbm(enc_norm_bias), waves(width)),
        smem=1,
        scratch=[pltpu.VMEM((n, width), f32)],
    )[0]
    x = [normed, near(normed), far(normed)]
    bias_a, bias_b, pos, stream = chain(
        mask_body,
        [full(2, n, n), kept(full(2, n, n)), kept(full(n, dwidth)), kept(full(n, width))],
        (at, in_hbm(segment_ids), in_hbm(gsd_index), in_hbm(tokens), in_hbm(embed_bias.reshape(1, -1)), waves(width), waves(dwidth)),
        smem=1,
    )

    def attention(bias, xa, xb):
        return chain(
            functools.partial(attn_body, scale, heads),
            [kept(low(2, n, share))] * 3 + [kept(low(2, heads, n, n)), kept(low(2, n, share))] + [low(n, width)] * 2,
            (xa, xb, bias, enc_qkv, enc_qv_bias, enc_out_proj),
        )

    def add(a, b):
        return chain(add_body, [shaped(a.shape, a.dtype)], (a, b))[0]

    def join(a, b):
        return chain(join_body, [low(a.shape[0] + b.shape[0], a.shape[1])], (a, b))[0]

    def both(blocks):
        blocks[2] = chain.pin(blocks[2])
        blocks.append(near(blocks[2]))

    qa, ka, va, pa, mixa, part0, part1 = attention(bias_a, x[0], x[1])
    part1 = near(part1)
    packed = pack(jnp.arange(8, dtype=jnp.int32), 8)
    packed_near = near(packed)
    vector = jnp.concatenate([dec_qv_bias.reshape(-1), dec_up_bias]).reshape(1, -1)
    far_vector = far(vector)
    if split:
        got = chain.pin(got)
        more = swap(got, "dp", 4)
    both(x)
    chain.gap()
    qb, kb, vb, pb, mixb, part2, part3 = attention(bias_b, x[2], x[3])
    part3 = near(part3)
    chain.gap()
    part2 = far(add(part2, part3))
    if split:
        got = join(got, more)
        more = swap(got, "dp", 2)
    else:
        got = far(packed)
    packed_near = chain.pin(packed_near)
    middle, normed2 = chain(
        mid_body,
        [kept(full(n, width)), low(n, width)],
        (stream, part0, part1, part2, enc_out_bias, enc_gain, enc_norm_bias),
    )
    y = [normed2, near(normed2), far(normed2)]

    def feed(xa, xb):
        return chain(
            mlp_body,
            [kept(low(2, n, ff))] * 2 + [low(n, width)] * 2,
            (xa, xb, enc_up, enc_up_bias.reshape(1, -1), enc_down),
        )

    if split:
        got = join(got, more)
        more = swap(got, "dp", 1)
    else:
        more = got[pack_rows // 2 :]
        got = got[: pack_rows // 2]
    hida, dga, part0, part1 = feed(y[0], y[1])
    part1 = near(part1)
    far_vector = chain.pin(far_vector)
    near_vectors = near(jnp.concatenate([vector, far_vector], axis=0))
    far_weights = [got, more]
    near_weights = [near(got)]
    both(y)
    chain.gap()
    hidb, dgb, part2, part3 = feed(y[2], y[3])
    part3 = near(part3)
    chain.gap()
    part2 = far(add(part2, part3))
    far_weights[1] = chain.pin(more)
    near_weights.append(near(far_weights[1]))
    part2 = chain.pin(part2)

    small = [vector, near_vectors[:1], far_vector, near_vectors[1:]]
    qv_full = jnp.concatenate([b[:, : 2 * dshare].reshape(2, dshare) for b in small], axis=1)
    upb_full = jnp.concatenate([b[:, 2 * dshare :] for b in small], axis=1)
    (enc_low, output, x1, x2, hid, mix, gp, gm, g3, gz, ge_low, ge, dec_sums) = chain(
        decoder_body,
        [kept(o) for o in (low(n, width), full(n, dwidth), low(n, dwidth), low(n, dwidth), low(n, dff),
                           low(n, dwidth), low(n, dff), low(n, dwidth), low(n, 3 * dwidth), low(n, dwidth))]
        + [low(n, width), kept(full(n, width)), kept(full(8, width))],
        (jnp.stack([slot, across.home]), middle, part0, part1, part2, enc_out_bias, packed, packed_near,
         *far_weights, *near_weights, qv_full, upb_full, pos, bias_a, dec_out_bias, dec_gain,
         dec_norm_bias, cotangent),
        smem=1,
        scratch=[
            pltpu.VMEM((4, dwidth, dwidth), bf16), pltpu.VMEM((4, dwidth, dwidth), bf16),
            pltpu.VMEM((3, dwidth, dwidth), bf16), pltpu.VMEM((dwidth, dwidth), bf16),
            pltpu.VMEM((width, dwidth), bf16), pltpu.VMEM((DHEADS, n, n), bf16),
            pltpu.VMEM((n, dff), bf16), pltpu.VMEM((3, n, dwidth), bf16), pltpu.VMEM((n, dwidth), f32),
        ],
        limit=40,
    )
    g = [ge_low, near(ge_low), far(ge_low)]

    def feed_back(ga, gb, slope):
        return chain(
            mlp_back_body,
            [kept(low(2, n, ff)), kept(full(1, ff)), low(n, width), low(n, width)],
            (ga, gb, slope, enc_up, enc_down),
        )

    def attention_back(ga, gb, q, k, v, p):
        return chain(
            functools.partial(attn_back_body, scale, heads),
            [kept(low(2, n, 3 * share)), kept(full(2, share)), low(n, width), low(n, width)],
            (ga, gb, q, k, v, p, enc_qkv, enc_out_proj),
        )

    def plain(dims):
        return [dims], [(0, None, 0, dims[0] // 8, 0, dims[0] // 8, 0, dims[1], 0)]

    down = Sum(across, *plain((ff, width)))
    up = Sum(across, *plain((width, ff)))
    rows, fold = width // 8, share // 8
    attn = Sum(
        across,
        [(3, width, share), (share, width)],
        [(0, c, 0, rows, 0, rows, c * share, share, 0) for c in range(3)]
        + [(1, None, 0, fold, k * fold, fold, 3 * share, width // 4, k * (width // 4)) for k in range(4)],
    )
    part, thin, tall = dwidth // 8, dshare // 8, width // 8
    top = 2 * part + thin
    dec = Sum(
        across,
        [(dwidth, dwidth), (dwidth, dwidth), (dshare, dwidth), (3, dwidth, dshare), (width, dshare)],
        [
            (0, None, 0, part, 0, part, 0, dwidth, 0),
            (1, None, 0, part, part, part, 0, dwidth, 0),
            (2, None, 0, thin, 2 * part, thin, 0, dwidth, 0),
        ]
        + [(3, c, 0, part, top, part, c * dshare, dshare, 0) for c in range(3)]
        + [(4, None, 0, tall, top, part, 3 * dshare, dshare, 0)]
        + [(4, None, part + k * thin, tall, top + part, thin, k * dshare, dshare, 0) for k in range(4)],
    )

    chain.gap()
    gpa, upa, part0, part1 = feed_back(g[0], g[1], dga)
    part1 = near(part1)
    sent, kept_share = chain(
        decoder_weights_body,
        [low(2, pack_rows, dwidth), kept(low(2, pack_rows, dwidth))],
        (x1, x2, hid, mix, gp, gm, g3, gz, enc_low, cotangent),
        limit=24,
    )
    sent = near(sent)
    both(g)
    chain.gap()
    gpb, upb, part2, part3 = feed_back(g[2], g[3], dgb)
    part3 = near(part3)
    down.product([in_hbm(hida), in_hbm(hidb)], g)
    part2 = far(add(part2, part3))

    def far_share(bit):
        return chain(far_body, [low(pack_rows // 2, dwidth)], (bit.reshape(1), kept_share, sent), smem=1)[0]

    there = far(far_share(1 - across.x))
    grad_middle, gm_low, sums_mid = chain(
        mlp_end_body,
        [kept(full(n, width)), low(n, width), kept(full(16, width))],
        (at, ge, part0, part1, part2, middle, enc_gain, upa, upb, dec_sums),
        smem=1,
    )
    m = [gm_low, near(gm_low), far(gm_low)]
    up.product([in_hbm(b) for b in y], [in_hbm(gpa), in_hbm(gpb)])
    g3a, sa, part0, part1 = attention_back(m[0], m[1], qa, ka, va, pa)
    part1 = near(part1)
    down.step()
    both(m)
    mine = far_share(across.x)
    dec.shares(kept_share, sent, there, mine)
    out_full = chain(out_weight_body, [low(share, width)], (mixa, mixb, *m))[0]
    g3b, sb, part2, part3 = attention_back(m[2], m[3], qb, kb, vb, pb)
    part3 = near(part3)
    down.step()
    attn.product([in_hbm(b) for b in x], [in_hbm(g3a), in_hbm(g3b)], [out_full])
    part2 = far(add(part2, part3))
    up.step()
    down.step()
    dec.step()
    up.step()
    grad_tokens, sums = chain(
        last_body,
        [kept(full(n, width)), full(24, width)],
        (at, grad_middle, part0, part1, part2, stream, enc_gain, sa, sb, sums_mid),
        smem=1,
    )
    down.step()
    dec.step()
    up.step()
    stages = [("mp", [1, 2, 3])]
    bit = 1
    while bit < across.size:
        pair = [bit] if bit == 1 or 2 * bit >= across.size else [bit, 2 * bit, 3 * bit]
        stages.append(("dp", pair))
        bit *= 4 if len(pair) == 3 else 2

    def add_all(*terms):
        return chain(add_all_body, [shaped(terms[0].shape, f32)], terms)[0]

    def spread_sums(terms):
        axis, masks = stages.pop(0)
        terms = terms if len(terms) == 1 else [add_all(*terms)]
        return terms + [swap(terms[0], axis, mask) for mask in masks]

    sums = spread_sums([sums])
    attn.step()
    down.step()
    dec.step()
    up.step()
    sums = spread_sums(sums)
    attn.step()
    dec.step()
    up.step()
    attn.step()
    down.step()
    dec.step()
    sums = spread_sums(sums)
    attn.step()
    up.step()
    attn.step()
    while stages:
        sums = spread_sums(sums)
    vectors = chain(
        last_sums_body,
        [full(2, share), full(1, ff), full(2, width), full(2, width), full(2, width), full(1, dwidth),
         full(2, dshare), full(1, dff // 4), full(2, dwidth), full(2, dwidth), full(2, dwidth)],
        (at, *sums),
        smem=1,
        scratch=[pltpu.VMEM((24, width), f32)],
    )
    dec.step()
    for flow in (down, up, dec, attn):
        for _ in range(7):
            flow.step()
    e_qv, e_upb, e_ob, e_gain, e_nb, d_emb, d_qv, d_upb, d_ob, d_gain, d_nb = vectors

    return (
        output,
        grad_tokens,
        attn.result[0],
        e_qv,
        attn.result[1],
        up.result[0],
        e_upb.reshape(-1),
        down.result[0],
        e_ob,
        e_gain,
        e_nb,
        dec.result[4],
        d_emb.reshape(-1),
        dec.result[3],
        d_qv,
        dec.result[2],
        dec.result[0],
        d_upb.reshape(-1),
        dec.result[1],
        d_ob,
        d_gain,
        d_nb,
    )


def solution(mesh):
    return jax.shard_map(
        per_device,
        mesh=mesh,
        in_specs=(
            P(("dp", "mp"), None),
            P("dp", None),
            P("dp", None),
            P(None, None, "mp"),
            P(None, "mp"),
            P("mp", None),
            P(None, "mp"),
            P("mp"),
            P("mp", None),
            P(),
            P(),
            P(),
            P(None, "mp"),
            P(),
            P(None, None, "mp"),
            P(None, "mp"),
            P("mp", None),
            P(None, "mp"),
            P("mp"),
            P("mp", None),
            P(),
            P(),
            P(),
            P(("dp", "mp"), None),
        ),
        out_specs=(
            P(("dp", "mp"), None),
            P(("dp", "mp"), None),
            P(None, None, "mp"),
            P(None, "mp"),
            P("mp", None),
            P(None, "mp"),
            P("mp"),
            P("mp", None),
            P(),
            P(),
            P(),
            P(None, "mp"),
            P(),
            P(None, None, "mp"),
            P(None, "mp"),
            P("mp", None),
            P(None, "mp"),
            P("mp"),
            P("mp", None),
            P(),
            P(),
            P(),
        ),
        check_vma=False,
    )
```

```python
import functools
import math

import jax
import jax.numpy as jnp
from jax import lax
from jax.experimental import pallas as pl
from jax.experimental.pallas import tpu as pltpu
from jax.sharding import PartitionSpec as P

HEADS = 16
DHEADS = 16
norm_eps = 1e-06
f32 = jnp.float32
bf16 = jnp.bfloat16
MIB = 1 << 20
VMEM = pl.BlockSpec(memory_space=pltpu.VMEM)
SMEM = pl.BlockSpec(memory_space=pltpu.SMEM)
COST = pl.CostEstimate(flops=10**10, bytes_accessed=10**8, transcendentals=0)


def shaped(dims, kind):
    return jax.ShapeDtypeStruct(dims, kind)


def kept(shape):
    return pltpu.HBM(shape.shape, shape.dtype)


def in_hbm(value):
    return pltpu.with_memory_space_constraint(value, pltpu.HBM)


class Chain:
    def __init__(self):
        self.last = None

    def __call__(self, body, outs, args, smem=0, scratch=(), limit=16, prefetch=None, grid=None, specs=None):
        args = list(args)
        extra = self.last is not None
        lead = smem if prefetch is None else 1
        inner = body
        if extra:
            count = len(args) + (prefetch is not None)

            def inner(*refs):
                return body(*refs[:count], *refs[count + 1 :])

            args.append(self.last)
        tail = [pl.BlockSpec(memory_space=pl.ANY)] * extra
        params = pltpu.CompilerParams(vmem_limit_bytes=limit * MIB)
        cost = COST
        if prefetch is None:
            got = pl.pallas_call(
                inner,
                out_shape=outs,
                in_specs=[SMEM] * smem + [VMEM] * (len(args) - smem - extra) + tail,
                out_specs=[VMEM] * len(outs),
                scratch_shapes=scratch,
                compiler_params=params,
                cost_estimate=cost,
            )(*args)
        else:
            got = pl.pallas_call(
                inner,
                out_shape=outs,
                grid_spec=pltpu.PrefetchScalarGridSpec(
                    num_scalar_prefetch=1, grid=grid, in_specs=specs[0] + tail, out_specs=specs[1]
                ),
                compiler_params=params,
                cost_estimate=cost,
            )(prefetch, *args)
        self.last = min(got, key=lambda g: g.size * g.dtype.itemsize)
        return got

    def pin(self, value):
        any_space = pl.BlockSpec(memory_space=pl.ANY)
        args = (value,) if value is self.last else (value, self.last)
        got = pl.pallas_call(
            lambda *refs: None,
            out_shape=shaped(value.shape, value.dtype),
            in_specs=[any_space] * len(args),
            out_specs=any_space,
            input_output_aliases={0: 0},
            compiler_params=pltpu.CompilerParams(vmem_limit_bytes=MIB),
            cost_estimate=COST,
        )(*args)
        self.last = got
        return got

    def gap(self):
        def body(last_ref, out_ref):
            out_ref[...] = jnp.zeros(out_ref.shape, f32)

        self.last = pl.pallas_call(
            body,
            out_shape=shaped((8, 128), f32),
            in_specs=[pl.BlockSpec(memory_space=pl.ANY)],
            out_specs=VMEM,
            compiler_params=pltpu.CompilerParams(vmem_limit_bytes=MIB),
            cost_estimate=COST,
        )(self.last)


def nn(a, b):
    return lax.dot_general(a, b, (((1,), (0,)), ((), ())), preferred_element_type=f32)


def nt(a, b):
    return lax.dot_general(a, b, (((1,), (1,)), ((), ())), preferred_element_type=f32)


def tn(a, b):
    return lax.dot_general(a, b, (((0,), (0,)), ((), ())), preferred_element_type=f32)


def swap(value, axis, mask):
    size = lax.axis_size(axis)
    return lax.ppermute(value, axis, [(i, i ^ mask) for i in range(size)])


def norm_parts(values):
    average = jnp.mean(values, axis=-1, keepdims=True)
    centred = values - average
    variance = jnp.mean(centred * centred, axis=-1, keepdims=True)
    scale = lax.rsqrt(variance + norm_eps)
    return centred * scale, scale


def norm_back(normal, scale, gain, grad):
    wide = grad * gain
    one = jnp.mean(wide, axis=-1, keepdims=True)
    two = jnp.mean(wide * normal, axis=-1, keepdims=True)
    return scale * (wide - one - normal * two)


def gelu_both(v):
    slope = math.sqrt(2.0 / math.pi)
    square = v * v
    t = jnp.tanh(slope * v * (1.0 + 0.044715 * square))
    half = 0.5 * (1.0 + t)
    return v * half, half + 0.5 * slope * v * (1.0 - t * t) * (1.0 + 3.0 * 0.044715 * square)


def sin_cos(x):
    turn = jnp.floor(x * (2.0 / math.pi) + 0.5)
    r = ((x - turn * 1.5703125) - turn * 4.837512969970703125e-4) - turn * 7.54978995489188216e-8
    z = r * r
    s = r + r * z * (-1.6666654611e-1 + z * (8.3321608736e-3 + z * -1.9515295891e-4))
    c = 1.0 - 0.5 * z + z * z * (
        4.166664568298827e-2 + z * (-1.388731625493765e-3 + z * 2.443315711809948e-5)
    )
    quarter = turn.astype(jnp.int32)
    odd = (quarter & 1) != 0
    sine = jnp.where(odd, c, s)
    cosine = jnp.where(odd, s, c)
    sine = jnp.where((quarter & 2) != 0, -sine, sine)
    cosine = jnp.where(((quarter + 1) & 2) != 0, -cosine, cosine)
    return sine, cosine


def head_masks(heads):
    size = 256 // heads
    lane = lax.broadcasted_iota(jnp.int32, (1, 256), 1)
    return [
        jnp.where((lane >= h * size) & (lane < (h + 1) * size), 1.0, 0.0).astype(bf16)
        for h in range(heads)
    ]


def attend(q, k, v, bias, heads, scale, keep):
    size = 256 // heads
    vt = v.astype(f32).T.astype(bf16)
    mixes = []
    for h, mask in enumerate(head_masks(heads)):
        s = nt(k, q * mask) + bias
        top = jnp.max(s, axis=0, keepdims=True)
        p = jnp.exp2((s - top) * (scale * math.log2(math.e)))
        total = jnp.sum(p, axis=0, keepdims=True)
        p = (p * (1.0 / total)).astype(bf16)
        keep(h, p)
        mixes.append(nn(vt[h * size : (h + 1) * size], p))
    return jnp.concatenate(mixes, axis=0).T


def attend_back(q, k, v, gm, probs, heads, scale):
    size = 256 // heads
    kt = k.astype(f32).T.astype(bf16)
    gq, gk, gv = [], 0.0, 0.0
    for h, mask in enumerate(head_masks(heads)):
        gmh = gm * mask
        p = probs(h)
        wide = p.astype(f32)
        t = wide * nt(v, gmh)
        gs = (t - wide * jnp.sum(t, axis=0, keepdims=True)).astype(bf16)
        gk = gk + nn(gs, q * mask)
        gv = gv + nn(p, gmh)
        gq.append(nn(kt[h * size : (h + 1) * size], gs))
    return jnp.concatenate(gq, axis=0).T * scale, gk * scale, gv


def place_of(slot, seg_ref, gsd_ref):
    n = seg_ref.shape[1]
    across = jnp.broadcast_to(seg_ref[pl.ds(slot, 1), :].astype(f32), (n, n))
    earlier = lax.broadcasted_iota(jnp.int32, (n, n), 1) < lax.broadcasted_iota(jnp.int32, (n, n), 0)
    rank = jnp.sum(jnp.where((across == across.T) & earlier, 1.0, 0.0), axis=1, keepdims=True)
    index = jnp.broadcast_to(gsd_ref[pl.ds(slot, 1), :].astype(f32), (n, n)).T[:, :1]
    return rank * (0.5 + 0.25 * index)


def start_body(slot_ref, seg_ref, gsd_ref, tokens_ref, gain_ref, shift_ref, wf_ref, normed_ref, stream_ref):
    place = place_of(slot_ref[0], seg_ref, gsd_ref)
    half = wf_ref.shape[1]
    sine, cosine = sin_cos(place * wf_ref[...])
    stream_ref[:, :half] = tokens_ref[:, :half].astype(f32) + sine
    stream_ref[:, half:] = tokens_ref[:, half:].astype(f32) + cosine
    normal, _ = norm_parts(stream_ref[...])
    normed_ref[...] = (normal * gain_ref[0:1] + shift_ref[0:1]).astype(bf16)


def mask_body(slot_ref, seg_ref, bias_a_ref, bias_b_ref):
    slot = slot_ref[0]
    n = seg_ref.shape[1]
    for j in range(4):
        across = jnp.broadcast_to(seg_ref[pl.ds(slot ^ j, 1), :].astype(f32), (n, n))
        (bias_a_ref, bias_b_ref)[j // 2][j % 2] = jnp.where(across == across.T, 0.0, -1e30)


def stream_body(slot_ref, seg_ref, gsd_ref, tokens_ref, eb_ref, wf_ref, nf_ref, pos_ref, stream_ref):
    place = place_of(slot_ref[0], seg_ref, gsd_ref)
    half = wf_ref.shape[1]
    sine, cosine = sin_cos(place * wf_ref[...])
    stream_ref[:, :half] = tokens_ref[:, :half].astype(f32) + sine
    stream_ref[:, half:] = tokens_ref[:, half:].astype(f32) + cosine
    half = nf_ref.shape[1]
    sine, cosine = sin_cos(place * nf_ref[...])
    pos_ref[:, :half] = sine + eb_ref[:, :half]
    pos_ref[:, half:] = cosine + eb_ref[:, half:]


def attn_body(scale, heads, first, *refs):
    count = (len(refs) - 9) // 2
    xs, rest = refs[:count], refs[count:]
    bias_ref, w_ref, qvb_ref, o_ref, q_ref, k_ref, v_ref, p_ref, mix_ref = rest[:9]
    for r, (x_ref, part_ref) in enumerate(zip(xs, rest[9:])):
        x = x_ref[...]
        q = (nn(x, w_ref[0]) + qvb_ref[0:1]).astype(bf16)
        k = nn(x, w_ref[1]).astype(bf16)
        v = (nn(x, w_ref[2]) + qvb_ref[1:2]).astype(bf16)
        q_ref[r], k_ref[r], v_ref[r] = q, k, v

        def keep(h, p):
            p_ref[r, h] = p

        mix = attend(q, k, v, bias_ref[first + r], heads, scale, keep).astype(bf16)
        mix_ref[r] = mix
        part_ref[...] = nn(mix, o_ref[...]).astype(bf16)


def attn_back_body(scale, heads, *refs):
    count = (len(refs) - 8) // 2
    gs, rest = refs[:count], refs[count:]
    q_ref, k_ref, v_ref, p_ref, w_ref, o_ref, g3_ref, sums_ref = rest[:8]
    total_q, total_v = 0.0, 0.0
    for r, (g_ref, part_ref) in enumerate(zip(gs, rest[8:])):
        gm = nt(g_ref[...], o_ref[...]).astype(bf16)
        gq, gk, gv = attend_back(
            q_ref[r], k_ref[r], v_ref[r], gm, lambda h: p_ref[r, h], heads, scale
        )
        total_q = total_q + jnp.sum(gq, axis=0, keepdims=True)
        total_v = total_v + jnp.sum(gv, axis=0, keepdims=True)
        acc = 0.0
        for c, g in enumerate((gq, gk, gv)):
            low = g.astype(bf16)
            g3_ref[r, :, c * 256 : (c + 1) * 256] = low
            acc = acc + nt(low, w_ref[c])
        part_ref[...] = acc.astype(bf16)
    sums_ref[0:1] = total_q
    sums_ref[1:2] = total_v


def mid_body(stream_ref, p_ref, near_ref, far_ref, ob_ref, gain_ref, shift_ref, mid_ref, normed_ref):
    total = p_ref[...].astype(f32) + near_ref[...].astype(f32) + far_ref[...].astype(f32)
    middle = stream_ref[...] + total + ob_ref[0:1]
    mid_ref[...] = middle
    normal, _ = norm_parts(middle)
    normed_ref[...] = (normal * gain_ref[1:2] + shift_ref[1:2]).astype(bf16)


def mlp_body(*refs):
    count = (len(refs) - 5) // 2
    xs, rest = refs[:count], refs[count:]
    up_ref, ub_ref, down_ref, hid_ref, dg_ref = rest[:5]
    width = up_ref.shape[1]
    for r, (x_ref, part_ref) in enumerate(zip(xs, rest[5:])):
        x = x_ref[...]
        for c in range(0, width, 256):
            cut = slice(c, c + 256)
            hidden, slope = gelu_both(nn(x, up_ref[:, cut]) + ub_ref[:, cut])
            hid_ref[r, :, cut] = hidden.astype(bf16)
            dg_ref[r, :, cut] = slope.astype(bf16)
        hidden = hid_ref[r]
        for c in range(0, down_ref.shape[1], 512):
            cut = slice(c, c + 512)
            part_ref[:, cut] = nn(hidden, down_ref[:, cut]).astype(bf16)


def mlp_back_body(*refs):
    count = (len(refs) - 5) // 2
    gs, rest = refs[:count], refs[count:]
    dg_ref, up_ref, down_ref, gp_ref, sums_ref = rest[:5]
    width = up_ref.shape[1]
    for r, (g_ref, part_ref) in enumerate(zip(gs, rest[5:])):
        g = g_ref[...]
        for c in range(0, width, 256):
            cut = slice(c, c + 256)
            grad = nt(g, down_ref[cut]) * dg_ref[r, :, cut].astype(f32)
            gp_ref[r, :, cut] = grad.astype(bf16)
            total = jnp.sum(grad, axis=0, keepdims=True)
            sums_ref[:, cut] = total if r == 0 else sums_ref[:, cut] + total
        gp = gp_ref[r]
        for c in range(0, up_ref.shape[0], 512):
            cut = slice(c, c + 512)
            part_ref[:, cut] = nt(gp, up_ref[cut]).astype(bf16)


def mlp_end_body(slot_ref, ge_ref, p_ref, near_ref, far_ref, mid_ref, gain_ref, ua_ref, ub_ref, uc_ref, dec_ref,
                 gmid_ref, gm_ref, pack_ref):
    slot = slot_ref[0]
    grad = p_ref[...].astype(f32) + near_ref[...].astype(f32) + far_ref[...].astype(f32)
    normal, scale = norm_parts(mid_ref[...])
    gmid = ge_ref[...] + norm_back(normal, scale, gain_ref[1:2], grad)
    gmid_ref[...] = gmid
    gm_ref[...] = gmid.astype(bf16)
    pack_ref[...] = jnp.zeros(pack_ref.shape, f32)
    pack_ref[0:1] = jnp.sum(gmid, axis=0, keepdims=True)
    pack_ref[1:2] = jnp.sum(grad * normal, axis=0, keepdims=True)
    pack_ref[2:3] = jnp.sum(grad, axis=0, keepdims=True)
    pack_ref[pl.ds(4 + slot, 1), :] = ua_ref[...] + ub_ref[...] + uc_ref[...]
    pack_ref[8:16] = dec_ref[...]


def last_body(slot_ref, gmid_ref, p_ref, near_ref, far_ref, stream_ref, gain_ref, sa_ref, sb_ref, sc_ref, mid_ref,
              gtok_ref, pack_ref):
    slot = slot_ref[0]
    grad = p_ref[...].astype(f32) + near_ref[...].astype(f32) + far_ref[...].astype(f32)
    normal, scale = norm_parts(stream_ref[...])
    gtok_ref[...] = gmid_ref[...] + norm_back(normal, scale, gain_ref[0:1], grad)
    pack_ref[:16] = mid_ref[...]
    pack_ref[16:] = jnp.zeros((8, pack_ref.shape[1]), f32)
    pack_ref[16:17] = jnp.sum(grad * normal, axis=0, keepdims=True)
    pack_ref[17:18] = jnp.sum(grad, axis=0, keepdims=True)
    share = sa_ref.shape[1]
    place = pl.ds(pl.multiple_of(slot * share, share), share)
    pack_ref[18:20, place] = sa_ref[...] + sb_ref[...] + sc_ref[...]


def decoder_body(slot_ref, mid_ref, p_ref, near_ref, far_ref, eob_ref, own_ref, by_ref, fa_ref, fb_ref, na_ref, nb_ref,
                 qvb_ref, upb_ref, pos_ref, bias_ref, dob_ref, dgain_ref, dnb_ref, cot_ref,
                 encl_ref, out_ref, x1_ref, x2_ref, hid_ref, mix_ref, gp_ref, gm_ref, g3_ref, gz_ref,
                 gel_ref, ge_ref, sums_ref,
                 wup, wdown, wqkv, wout, wemb, pt, dg, qkv, wide):
    slot, home = slot_ref[0], slot_ref[1]
    width = cot_ref.shape[1]
    block = width // 4
    heads = DHEADS * 256 // width
    groups = width // 256
    scale = (width // DHEADS) ** -0.5

    def place(j, base=0):
        return pl.ds(pl.multiple_of(base + (slot ^ j) * block, block), block)

    piece, thin, tall = width // 8, block // 8, 2 * width // 8
    top = 2 * piece + thin
    step = top + piece + thin
    for j, (low_ref, high_ref) in enumerate(
        ((own_ref, own_ref), (by_ref, by_ref), (fa_ref, fb_ref), (na_ref, nb_ref))
    ):
        cut = slice(j * block, (j + 1) * block)
        for i in range(8):
            ref = (low_ref, high_ref)[i // 4]
            base = (i if j < 2 else i % 4) * step
            chunk = i if j < 2 else home ^ i

            def rows(size):
                return pl.ds(pl.multiple_of(chunk * size, size), size)

            wup[j, rows(piece)] = ref[base : base + piece]
            wdown[j, rows(piece)] = ref[base + piece : base + 2 * piece]
            wout[pl.ds(pl.multiple_of(j * block + chunk * thin, thin), thin)] = (
                ref[base + 2 * piece : base + top]
            )
            for c in range(3):
                wqkv[c, rows(piece), cut] = ref[base + top : base + top + piece, c * block : (c + 1) * block]
            wemb[pl.ds(pl.multiple_of(chunk * tall, tall), piece), cut] = (
                ref[base + top : base + top + piece, 3 * block :]
            )
            for c in range(4):
                wemb[pl.ds(pl.multiple_of(chunk * tall + piece + c * thin, thin), thin), cut] = (
                    ref[base + top + piece : base + step, c * block : (c + 1) * block]
                )
    encoded = mid_ref[...] + eob_ref[1:2]
    encoded = encoded + p_ref[...].astype(f32) + near_ref[...].astype(f32) + far_ref[...].astype(f32)
    encl_ref[...] = encoded.astype(bf16)
    embedded = nn(encl_ref[...], wemb[...])
    for j in range(4):
        wide[:, place(j)] = embedded[:, j * block : (j + 1) * block]
    stream = wide[...] + pos_ref[...]
    normal1, scale1 = norm_parts(stream)
    x1_ref[...] = (normal1 * dgain_ref[0:1] + dnb_ref[0:1]).astype(bf16)
    x1 = x1_ref[...]
    qkv[0] = (nn(x1, wqkv[0]) + qvb_ref[0:1]).astype(bf16)
    qkv[1] = nn(x1, wqkv[1]).astype(bf16)
    qkv[2] = (nn(x1, wqkv[2]) + qvb_ref[1:2]).astype(bf16)
    bias = bias_ref[0]
    for g in range(groups):
        cut = slice(g * 256, (g + 1) * 256)

        def keep(h, p):
            pt[g * heads + h] = p

        mix_ref[:, cut] = attend(
            qkv[0, :, cut], qkv[1, :, cut], qkv[2, :, cut], bias, heads, scale, keep
        ).astype(bf16)
    middle = stream + nn(mix_ref[...], wout[...]) + dob_ref[0:1]
    normal2, scale2 = norm_parts(middle)
    x2_ref[...] = (normal2 * dgain_ref[1:2] + dnb_ref[1:2]).astype(bf16)
    x2 = x2_ref[...]
    result = middle + dob_ref[1:2]
    for j in range(4):
        cut = slice(j * width, (j + 1) * width)
        hidden, slope = gelu_both(nn(x2, wup[j]) + upb_ref[:, cut])
        hid_ref[:, cut] = hidden.astype(bf16)
        dg[:, cut] = slope.astype(bf16)
        result = result + nn(hid_ref[:, cut], wdown[j])
    out_ref[...] = result

    cot = cot_ref[...]
    grad = 0.0
    sums_ref[...] = jnp.zeros(sums_ref.shape, f32)
    for j in range(4):
        cut = slice(j * width, (j + 1) * width)
        pre = nt(cot, wdown[j]) * dg[:, cut].astype(f32)
        gp_ref[:, cut] = pre.astype(bf16)
        block_sum = jnp.sum(pre, axis=0, keepdims=True)
        at = slot ^ j
        sums_ref[pl.ds(6 + (at >> 1), 1), pl.ds(pl.multiple_of((at & 1) * width, width), width)] = (
            block_sum
        )
        grad = grad + nt(gp_ref[:, cut], wup[j])
    cotf = cot.astype(f32)
    gmid = cotf + norm_back(normal2, scale2, dgain_ref[1:2], grad)
    gm_ref[...] = gmid.astype(bf16)
    sums_ref[1:2, :width] = jnp.sum(gmid, axis=0, keepdims=True)
    sums_ref[2:3, :width] = jnp.sum(cotf, axis=0, keepdims=True)
    sums_ref[2:3, width:] = jnp.sum(grad * normal2, axis=0, keepdims=True)
    sums_ref[4:5, :width] = jnp.sum(grad, axis=0, keepdims=True)
    gmix = nt(gm_ref[...], wout[...]).astype(bf16)
    grad = 0.0
    for g in range(groups):
        cut = slice(g * 256, (g + 1) * 256)
        three = attend_back(
            qkv[0, :, cut], qkv[1, :, cut], qkv[2, :, cut], gmix[:, cut],
            lambda h: pt[g * heads + h], heads, scale,
        )
        for c, part in enumerate(three):
            begin = c * width + g * 256
            low = part.astype(bf16)
            g3_ref[:, begin : begin + 256] = low
            grad = grad + nt(low, wqkv[c, :, cut])
        for c, row, base in ((0, 4, width), (2, 5, width)):
            total = jnp.sum(three[c], axis=0, keepdims=True)
            for i in range(256 // block):
                sums_ref[row : row + 1, place(g * (256 // block) + i, base)] = (
                    total[:, i * block : (i + 1) * block]
                )
    gstream = gmid + norm_back(normal1, scale1, dgain_ref[0:1], grad)
    sums_ref[3:4, width:] = jnp.sum(gstream, axis=0, keepdims=True)
    sums_ref[1:2, width:] = jnp.sum(grad * normal1, axis=0, keepdims=True)
    sums_ref[3:4, :width] = jnp.sum(grad, axis=0, keepdims=True)
    wide[...] = gstream
    for j in range(4):
        gz_ref[:, j * block : (j + 1) * block] = wide[:, place(j)].astype(bf16)
    ge = nt(gz_ref[...], wemb[...])
    ge_ref[...] = ge
    gel_ref[...] = ge.astype(bf16)
    sums_ref[0:1] = jnp.sum(ge, axis=0, keepdims=True)


def decoder_weights_body(x1_ref, x2_ref, hid_ref, mix_ref, gp_ref, gm_ref, g3_ref, gz_ref, encl_ref, cot_ref,
                         sent_ref, kept_ref):
    width = cot_ref.shape[1]
    block = width // 4
    cot, gm, x2 = cot_ref[...], gm_ref[...], x2_ref[...]
    piece, thin = width // 8, block // 8
    tall = encl_ref.shape[1] // 8
    top = 2 * piece + thin
    step = top + piece + thin

    def to(j):
        return sent_ref if j % 2 else kept_ref

    for j in (1, 3, 0, 2):
        w = to(j)
        i = j // 2
        cut = slice(j * width, (j + 1) * width)
        up = tn(x2, gp_ref[:, cut]).astype(bf16)
        down = tn(hid_ref[:, cut], cot).astype(bf16)
        out = tn(mix_ref[:, j * block : (j + 1) * block], gm).astype(bf16)
        for c in range(8):
            w[i, c * step : c * step + piece] = up[c * piece : (c + 1) * piece]
            w[i, c * step + piece : c * step + 2 * piece] = down[c * piece : (c + 1) * piece]
            w[i, c * step + 2 * piece : c * step + top] = out[c * thin : (c + 1) * thin]
    x1 = x1_ref[...]
    for k in range(3):
        full = tn(x1, g3_ref[:, k * width : (k + 1) * width]).astype(bf16)
        for j in range(4):
            for c in range(8):
                to(j)[j // 2, c * step + top : c * step + top + piece, k * block : (k + 1) * block] = (
                    full[c * piece : (c + 1) * piece, j * block : (j + 1) * block]
                )
    full = tn(encl_ref[...], gz_ref[...]).astype(bf16)
    for j in range(4):
        cut = slice(j * block, (j + 1) * block)
        for c in range(8):
            base = c * tall
            to(j)[j // 2, c * step + top : c * step + top + piece, 3 * block :] = full[base : base + piece, cut]
            base = base + piece
            for k in range(4):
                to(j)[j // 2, c * step + top + piece : (c + 1) * step, k * block : (k + 1) * block] = (
                    full[base + k * thin : base + (k + 1) * thin, cut]
                )


def pack_body(pick_ref, up_ref, down_ref, out_ref, qkv_ref, emb_ref, chunk_ref):
    piece, thin, block = up_ref.shape[0], out_ref.shape[0], emb_ref.shape[1]
    chunk_ref[:piece] = up_ref[...]
    chunk_ref[piece : 2 * piece] = down_ref[...]
    top = 2 * piece + thin
    chunk_ref[2 * piece : top] = out_ref[...]
    for c in range(3):
        chunk_ref[top : top + piece, c * block : (c + 1) * block] = qkv_ref[c]
    chunk_ref[top : top + piece, 3 * block :] = emb_ref[:piece]
    for c in range(4):
        base = piece + c * thin
        chunk_ref[top + piece :, c * block : (c + 1) * block] = emb_ref[base : base + thin]


def join_body(a_ref, b_ref, out_ref):
    rows = a_ref.shape[0]
    out_ref[:rows] = a_ref[...]
    out_ref[rows:] = b_ref[...]


def add_body(a_ref, b_ref, out_ref):
    out_ref[...] = (a_ref[...].astype(f32) + b_ref[...].astype(f32)).astype(out_ref.dtype)


def add_all_body(*refs):
    total = refs[0][...]
    for ref in refs[1:-1]:
        total = total + ref[...]
    refs[-1][...] = total


def last_sums_body(slot_ref, *refs):
    terms, outs, total_ref = refs[:-12], refs[-12:-1], refs[-1]
    total = terms[0][...]
    for ref in terms[1:]:
        total = total + ref[...]
    total_ref[...] = total
    slot = slot_ref[0]
    e_qv, e_upb, e_ob, e_gain, e_nb, d_emb, d_qv, d_upb, d_ob, d_gain, d_nb = outs
    share, thin, width = e_qv.shape[1], d_qv.shape[1], d_emb.shape[1]
    e_qv[...] = total_ref[18:20, pl.ds(pl.multiple_of(slot * share, share), share)]
    e_upb[...] = total_ref[pl.ds(4 + slot, 1), :]
    e_ob[0:1] = total_ref[0:1]
    e_ob[1:2] = total_ref[8:9]
    e_gain[0:1] = total_ref[16:17]
    e_gain[1:2] = total_ref[1:2]
    e_nb[0:1] = total_ref[17:18]
    e_nb[1:2] = total_ref[2:3]
    d_ob[...] = total_ref[9:11, :width]
    d_gain[...] = total_ref[9:11, width:]
    d_nb[...] = total_ref[11:13, :width]
    d_emb[...] = total_ref[11:12, width:]
    d_qv[...] = total_ref[12:14, pl.ds(pl.multiple_of(width + slot * thin, thin), thin)]
    d_upb[...] = total_ref[pl.ds(14 + (slot >> 1), 1), pl.ds(pl.multiple_of((slot & 1) * width, width), width)]


def halve_body(bit_ref, *refs):
    ins, (send_ref, keep_ref) = refs[:-2], refs[-2:]
    half = send_ref.shape[0]
    bit = bit_ref[0]
    for ref, which in ((send_ref, 1 - bit), (keep_ref, bit)):
        rows = pl.ds(pl.multiple_of(which * half, half), half)
        total = ins[0][rows].astype(f32)
        for other in ins[1:]:
            total = total + other[rows].astype(f32)
        ref[...] = total.astype(bf16)


def far_body(bit_ref, kept_ref, near_ref, out_ref):
    half = out_ref.shape[0]
    rows = pl.ds(pl.multiple_of(bit_ref[0] * half, half), half)
    out_ref[...] = (kept_ref[1, rows].astype(f32) + near_ref[1, rows].astype(f32)).astype(bf16)


def there_body(bit_ref, kept_ref, near_ref, far_ref, send_ref):
    half = send_ref.shape[0]
    rows = pl.ds(pl.multiple_of((1 - bit_ref[0]) * half, half), half)
    total = kept_ref[0, rows].astype(f32) + near_ref[0, rows].astype(f32)
    send_ref[...] = (total + far_ref[...].astype(f32)).astype(bf16)


def mine_body(bit_ref, kept_ref, near_ref, far_ref, got_ref, send_ref, keep_ref):
    quarter = send_ref.shape[0]
    base = bit_ref[0] * 2 * quarter
    for ref, which in ((send_ref, 1 - bit_ref[1]), (keep_ref, bit_ref[1])):
        rows = pl.ds(pl.multiple_of(base + which * quarter, quarter), quarter)
        inner = pl.ds(pl.multiple_of(which * quarter, quarter), quarter)
        total = kept_ref[0, rows].astype(f32) + near_ref[0, rows].astype(f32)
        ref[...] = (total + far_ref[inner].astype(f32) + got_ref[inner].astype(f32)).astype(bf16)


def piece_of(refs, j):
    for ref in refs:
        if len(ref.shape) == 2:
            if j == 0:
                return ref[...]
            j -= 1
        elif j < ref.shape[0]:
            return ref[j]
        else:
            j -= ref.shape[0]


def tile_sum(xs, gs, more):
    acc = 0.0
    for j in range(4):
        acc = acc + tn(piece_of(xs, j), piece_of(gs, j))
    if not more:
        return [(slice(None), slice(None), acc)]
    rows, cols = acc.shape
    parts = [(slice(None), slice(0, cols), acc)]
    half, quarter = rows // 2, rows // 8
    wide = more[0].shape[1] // 4
    for c in range(2):
        for k in range(4):
            parts.append((
                slice(c * half + k * quarter, c * half + (k + 1) * quarter),
                slice(cols, cols + wide),
                more[0][c * quarter : (c + 1) * quarter, k * wide : (k + 1) * wide].astype(f32),
            ))
    return parts


def first_half_body(nx, ng, nm, pick_ref, *refs):
    xs, gs, more = refs[:nx], refs[nx : nx + ng], refs[nx + ng : nx + ng + nm]
    out_ref = refs[nx + ng + nm]
    for rows, cols, value in tile_sum(xs, gs, more):
        out_ref[rows, cols] = value.astype(bf16)


def other_half_body(nx, ng, nm, pick_ref, *refs):
    xs, gs, more = refs[:nx], refs[nx : nx + ng], refs[nx + ng : nx + ng + nm]
    add_ref, send_ref, keep_ref = refs[nx + ng + nm :]
    parts = [
        (rows, cols, (value + add_ref[rows, cols].astype(f32)).astype(bf16))
        for rows, cols, value in tile_sum(xs, gs, more)
    ]

    def put(ref):
        for rows, cols, value in parts:
            ref[rows, cols] = value

    @pl.when(pl.program_id(0) == 0)
    def _():
        put(send_ref)

    @pl.when(pl.program_id(0) == 1)
    def _():
        put(keep_ref)


def weight_half(chain, xs, gs, more, cut, pick, add=None):
    tile = xs[0].shape[-1] // 4
    begin, cols = cut
    out_cols = cols + sum(m.shape[1] // 4 for m in more)

    def column(shape):
        lead = shape[:-1]
        return pl.BlockSpec(lead + (tile,), lambda i, p: (0,) * len(lead) + (p[i],))

    def whole(shape):
        lead = shape[:-1]
        return pl.BlockSpec(lead + (cols,), lambda i, p: (0,) * len(lead) + (begin // cols,))

    in_specs = [column(x.shape) for x in xs] + [whole(g.shape) for g in gs]
    in_specs += [pl.BlockSpec((tile // 4, m.shape[1]), lambda i, p: (p[i], 0)) for m in more]
    args = list(xs) + list(gs) + list(more)
    counts = len(xs), len(gs), len(more)
    if add is None:
        body = functools.partial(first_half_body, *counts)
        outs = [shaped((2 * tile, out_cols), bf16)]
        out_specs = [pl.BlockSpec((tile, out_cols), lambda i, p: (i, 0))]
    else:
        body = functools.partial(other_half_body, *counts)
        in_specs.append(pl.BlockSpec((tile, out_cols), lambda i, p: (p[2 + i], 0)))
        args.append(add)
        outs = [shaped((tile, out_cols), bf16)] * 2
        out_specs = [pl.BlockSpec((tile, out_cols), lambda i, p: (0, 0))] * 2
    return chain(body, outs, args, prefetch=pick, grid=(2,), specs=(in_specs, out_specs), limit=20)


def spread_body(writes, place_ref, *refs):
    sums = max(write[0] for write in writes) + 1
    out_refs = refs[2 * sums :]
    for i in range(8):
        for source, which, lead, first, every, row, rows, col, cols, at_col in writes:
            ref = refs[2 * source + i // 4]
            base = i % 4 * (ref.shape[0] // 4)
            at = place_ref[source] ^ i
            value = ref[base + row : base + row + rows, col : col + cols].astype(f32)
            to = pl.ds(pl.multiple_of(at * every + first, rows), rows)
            if lead is None:
                out_refs[which][to, at_col : at_col + cols] = value
            else:
                out_refs[which][lead, to] = value


def out_weight_body(*refs):
    mixes, gs, out_ref = refs[:3], refs[3:7], refs[7]
    acc = 0.0
    for j in range(4):
        acc = acc + tn(piece_of(mixes, j), piece_of(gs, j))
    out_ref[...] = acc.astype(bf16)


class Sum:
    def __init__(self, chain, masks=(1, 2, 4)):
        self.chain, self.masks = chain, masks
        self.size = lax.axis_size("dp")
        me = lax.axis_index("dp").astype(jnp.int32)
        b1, b2, b3 = self.bits = [jnp.where((me & mask) != 0, 1, 0).astype(jnp.int32) for mask in masks]
        self.place = 4 * b1 + 2 * b2 + b3 if self.size == 8 else jnp.int32(0)
        self.there = jnp.stack([2 * (1 - b1), 2 * (1 - b1) + 1])
        self.mine = jnp.stack([2 * b1 + 1 - b2, 2 * b1 + b2, 1 - b2, b2])
        steps = [self.second, self.third, self.fourth, self.fifth, self.sixth]
        self.steps = iter(steps if self.size == 8 else [])

    def step(self):
        for todo in self.steps:
            todo()
            return

    def product(self, xs, gs, more=(), cut=None):
        self.terms = (xs, gs, more, cut or (0, gs[0].shape[-1]))
        if self.size != 8:
            first = weight_half(self.chain, *self.terms, jnp.array([0, 1], jnp.int32))[0]
            other = weight_half(self.chain, *self.terms, jnp.array([2, 3], jnp.int32))[0]
            return self.general(jnp.concatenate([first, other], axis=0))
        self.got = swap(weight_half(self.chain, *self.terms, self.there)[0], "dp", self.masks[0])

    def shares(self, kept, near, there, mine):
        self.terms = None
        if self.size != 8:
            total = kept[0].astype(f32) + near[0].astype(f32)
            total = total + jnp.concatenate([mine, there], axis=0).astype(f32)
            return self.general(total.astype(bf16))
        self.held = (kept, near, mine)
        half = shaped(there.shape, bf16)
        send = self.chain(there_body, [half], (self.bits[0].reshape(1), kept, near, there), smem=1)[0]
        self.got = swap(send, "dp", self.masks[0])

    def second(self):
        if self.terms is None:
            rows, cols = self.got.shape
            half = shaped((rows // 2, cols), bf16)
            send, self.keep = self.chain(
                mine_body, [half, half], (jnp.stack(self.bits[:2]), *self.held, self.got), smem=1
            )
        else:
            send, self.keep = weight_half(self.chain, *self.terms, self.mine, self.got)
        self.got = swap(send, "dp", self.masks[1])

    def third(self):
        rows, cols = self.keep.shape
        half = shaped((rows // 2, cols), bf16)
        send, self.keep = self.chain(
            halve_body, [half, half], (self.bits[2].reshape(1), self.keep, self.got), smem=1
        )
        self.got = swap(send, "dp", self.masks[2])

    def fourth(self):
        self.keep = self.chain(add_body, [shaped(self.keep.shape, bf16)], (self.keep, self.got))[0]
        self.got = swap(self.keep, "dp", self.masks[2])

    def join(self):
        rows, cols = self.keep.shape
        self.keep = self.chain(join_body, [shaped((2 * rows, cols), bf16)], (self.keep, self.got))[0]

    def fifth(self):
        self.join()
        self.got = swap(self.keep, "dp", self.masks[1])

    def sixth(self):
        self.join()
        self.got = swap(self.keep, "dp", self.masks[0])

    def general(self, held):
        me = lax.axis_index("dp")
        bits = [1 << i for i in range(self.size.bit_length() - 1)]
        for bit in bits:
            mine = (me & bit) != 0
            half = held.shape[0] // 2
            other = lax.dynamic_slice_in_dim(held, jnp.where(mine, 0, half), half, 0)
            own = lax.dynamic_slice_in_dim(held, jnp.where(mine, half, 0), half, 0)
            held = (own.astype(f32) + swap(other, "dp", bit).astype(f32)).astype(bf16)
        for bit in reversed(bits):
            mine = (me & bit) != 0
            other = swap(held, "dp", bit)
            held = jnp.where(
                mine,
                jnp.concatenate([other, held], axis=0),
                jnp.concatenate([held, other], axis=0),
            )
        half = held.shape[0] // 2
        self.keep, self.got = held[:half], held[half:]


def per_device(
    tokens, segment_ids, gsd_index, enc_qkv, enc_qv_bias, enc_out_proj, enc_up, enc_up_bias,
    enc_down, enc_out_bias, enc_gain, enc_norm_bias, embed_weight, embed_bias, dec_qkv,
    dec_qv_bias, dec_out_proj, dec_up, dec_up_bias, dec_down, dec_out_bias, dec_gain,
    dec_norm_bias, cotangent,
):
    n, width = tokens.shape
    rows, length = segment_ids.shape
    assert rows == 4 and n == length == 256 and lax.axis_size("mp") == 4
    share, ff = enc_qkv.shape[2], enc_up.shape[1]
    dwidth, dff = cotangent.shape[1], dec_up.shape[1] * 4
    dshare = dwidth // 4
    heads = share // (width // HEADS)
    scale = (width // HEADS) ** -0.5
    slot = lax.axis_index("mp").astype(jnp.int32)
    at = slot.reshape(1)
    chain = Chain()
    dec = Sum(chain)
    home = dec.place

    def low(*dims):
        return shaped(dims, bf16)

    def full(*dims):
        return shaped(dims, f32)

    def waves(size):
        half = size // 2
        return jnp.power(10000.0, -jnp.arange(half, dtype=f32) / half).reshape(1, half)

    def near(value):
        return swap(value, "mp", 1)

    def far(value):
        return swap(value, "mp", 2)

    pack_rows = 3 * dwidth + 2 * dshare
    decoder_weights = [in_hbm(w) for w in (dec_up, dec_down, dec_out_proj, dec_qkv, embed_weight)]

    def pack(pick, steps):
        def block(shape):
            if len(shape) == 3:
                return pl.BlockSpec((shape[0], shape[1] // 8, shape[2]), lambda i, p: (0, p[i], 0))
            return pl.BlockSpec((shape[0] // 8, shape[1]), lambda i, p: (p[i], 0))

        rows = pack_rows // 8
        return chain(
            pack_body,
            [low(steps * rows, dwidth)],
            decoder_weights,
            prefetch=pick,
            grid=(steps,),
            specs=([block(w.shape) for w in decoder_weights], [pl.BlockSpec((rows, dwidth), lambda i, p: (i, 0))]),
        )[0]

    split = dec.size == 8
    got = far(pack(home.reshape(1), 1)) if split else None
    normed = chain(
        start_body,
        [low(n, width)],
        (at, in_hbm(segment_ids), in_hbm(gsd_index), in_hbm(tokens), in_hbm(enc_gain), in_hbm(enc_norm_bias), waves(width)),
        smem=1,
        scratch=[pltpu.VMEM((n, width), f32)],
    )[0]
    x = [normed, near(normed), far(normed)]
    bias_a, bias_b = chain(mask_body, [full(2, n, n), full(2, n, n)], (at, in_hbm(segment_ids)), smem=1)

    def attention(bias, first, *blocks):
        count = len(blocks)
        return chain(
            functools.partial(attn_body, scale, heads, first),
            [kept(low(count, n, share))] * 3
            + [kept(low(count, heads, n, n)), kept(low(count, n, share))]
            + [low(n, width)] * count,
            (*blocks, bias, enc_qkv, enc_qv_bias, enc_out_proj),
        )

    def add(a, b):
        return chain(add_body, [shaped(a.shape, a.dtype)], (a, b))[0]

    def join(a, b):
        return chain(join_body, [low(a.shape[0] + b.shape[0], a.shape[1])], (a, b))[0]

    def both(blocks):
        blocks[2] = chain.pin(blocks[2])
        blocks.append(near(blocks[2]))

    *saved_a, mixa, part0, part1 = attention(bias_a, 0, x[0], x[1])
    part1 = near(part1)
    if split:
        got = chain.pin(got)
        more = swap(got, "dp", 4)
    vector = jnp.concatenate([dec_qv_bias.reshape(-1), dec_up_bias]).reshape(1, -1)
    far_vector = far(vector)
    both(x)
    chain.gap()
    *saved_d, mixd, part3 = attention(bias_b, 1, x[3])
    part3 = near(part3)
    *saved_c, mixc, part2 = attention(bias_b, 0, x[2])
    part2 = far(add(part2, part3))
    packed = pack(jnp.arange(8, dtype=jnp.int32), 8)
    packed_near = near(packed)
    pos, stream = chain(
        stream_body,
        [kept(full(n, dwidth)), full(n, width)],
        (at, in_hbm(segment_ids), in_hbm(gsd_index), in_hbm(tokens), in_hbm(embed_bias.reshape(1, -1)), waves(width), waves(dwidth)),
        smem=1,
    )
    if split:
        got = join(got, more)
        more = swap(got, "dp", 2)
    else:
        got = far(packed)
    middle, normed2 = chain(
        mid_body,
        [kept(full(n, width)), low(n, width)],
        (stream, part0, part1, part2, enc_out_bias, enc_gain, enc_norm_bias),
    )
    y = [normed2, near(normed2), far(normed2)]
    packed_near = chain.pin(packed_near)
    if split:
        got = join(got, more)
        more = swap(got, "dp", 1)
    else:
        more = got[pack_rows // 2 :]
        got = got[: pack_rows // 2]

    def feed(*blocks):
        count = len(blocks)
        return chain(
            mlp_body,
            [kept(low(count, n, ff))] * 2 + [low(n, width)] * count,
            (*blocks, enc_up, enc_up_bias.reshape(1, -1), enc_down),
        )

    hida, dga, part0, part1 = feed(y[0], y[1])
    part1 = near(part1)
    far_vector = chain.pin(far_vector)
    near_vectors = near(jnp.concatenate([vector, far_vector], axis=0))
    far_weights = [got, more]
    near_weights = [near(got)]
    both(y)
    chain.gap()
    hidd, dgd, part3 = feed(y[3])
    part3 = near(part3)
    hidc, dgc, part2 = feed(y[2])
    part2 = far(add(part2, part3))
    far_weights[1] = chain.pin(more)
    near_weights.append(near(far_weights[1]))
    part2 = chain.pin(part2)

    small = [vector, near_vectors[:1], far_vector, near_vectors[1:]]
    qv_full = jnp.concatenate([b[:, : 2 * dshare].reshape(2, dshare) for b in small], axis=1)
    upb_full = jnp.concatenate([b[:, 2 * dshare :] for b in small], axis=1)
    (enc_low, output, x1, x2, hid, mix, gp, gm, g3, gz, ge_low, ge, dec_sums) = chain(
        decoder_body,
        [kept(o) for o in (low(n, width), full(n, dwidth), low(n, dwidth), low(n, dwidth), low(n, dff),
                           low(n, dwidth), low(n, dff), low(n, dwidth), low(n, 3 * dwidth), low(n, dwidth))]
        + [low(n, width), kept(full(n, width)), kept(full(8, width))],
        (jnp.stack([slot, home]), middle, part0, part1, part2, enc_out_bias, packed, packed_near,
         *far_weights, *near_weights, qv_full, upb_full, pos, bias_a, dec_out_bias, dec_gain,
         dec_norm_bias, cotangent),
        smem=1,
        scratch=[
            pltpu.VMEM((4, dwidth, dwidth), bf16), pltpu.VMEM((4, dwidth, dwidth), bf16),
            pltpu.VMEM((3, dwidth, dwidth), bf16), pltpu.VMEM((dwidth, dwidth), bf16),
            pltpu.VMEM((width, dwidth), bf16), pltpu.VMEM((DHEADS, n, n), bf16),
            pltpu.VMEM((n, dff), bf16), pltpu.VMEM((3, n, dwidth), bf16), pltpu.VMEM((n, dwidth), f32),
        ],
        limit=40,
    )
    g = [ge_low, near(ge_low), far(ge_low)]

    def feed_back(slope, *blocks):
        count = len(blocks)
        return chain(
            mlp_back_body,
            [kept(low(count, n, ff)), kept(full(1, ff))] + [low(n, width)] * count,
            (*blocks, slope, enc_up, enc_down),
        )

    def attention_back(saved, *blocks):
        count = len(blocks)
        return chain(
            functools.partial(attn_back_body, scale, heads),
            [kept(low(count, n, 3 * share)), kept(full(2, share))] + [low(n, width)] * count,
            (*blocks, *saved, enc_qkv, enc_out_proj),
        )

    def far_share(bit):
        return far(chain(far_body, [low(pack_rows // 2, dwidth)], (bit.reshape(1), kept_share, sent), smem=1)[0])

    def hbm(*values):
        return [in_hbm(v) for v in values]

    down = Sum(chain)
    up0, up1 = Sum(chain), Sum(chain, (2, 1, 4))
    qk, vo = Sum(chain), Sum(chain, (2, 1, 4))

    def finish(sums, outs, writes):
        return chain(
            functools.partial(spread_body, writes),
            [kept(full(*dims)) for dims in outs],
            (jnp.stack([f.place for f in sums]), *[v for f in sums for v in (f.keep, f.got)]),
            smem=1,
            limit=24,
        )

    chain.gap()
    gpa, upa, part0, part1 = feed_back(dga, g[0], g[1])
    part1 = near(part1)
    sent, kept_share = chain(
        decoder_weights_body,
        [low(2, pack_rows, dwidth), kept(low(2, pack_rows, dwidth))],
        (x1, x2, hid, mix, gp, gm, g3, gz, enc_low, cotangent),
        limit=24,
    )
    sent = near(sent)
    both(g)
    gpc, upc, part2 = feed_back(dgc, g[2])
    gpd, upd, part3 = feed_back(dgd, g[3])
    part3 = near(part3)
    gps = hbm(gpa, gpc, gpd)
    ys = hbm(*y)
    up0.product(ys, gps, cut=(0, ff // 2))
    part2 = far(add(part2, part3))
    up1.product(ys, gps, cut=(ff // 2, ff // 2))
    down.product(hbm(hida, hidc, hidd), g)
    up0.step()
    grad_middle, gm_low, sums_mid = chain(
        mlp_end_body,
        [kept(full(n, width)), low(n, width), kept(full(16, width))],
        (at, ge, part0, part1, part2, middle, enc_gain, upa, upc, upd, dec_sums),
        smem=1,
    )
    m = [gm_low, near(gm_low), far(gm_low)]
    up1.step()
    g3a, sa, part0, part1 = attention_back(saved_a, m[0], m[1])
    part1 = near(part1)
    up0.step()
    there = far_share(1 - dec.bits[0])
    both(m)
    g3c, sc, part2 = attention_back(saved_c, m[2])
    out_full = chain(out_weight_body, [low(share, width)], (mixa, mixc, mixd, *m))[0]
    down.step()
    up0.step()
    g3d, sd, part3 = attention_back(saved_d, m[3])
    part3 = near(part3)
    g3s = hbm(g3a, g3c, g3d)
    xs = hbm(*x)
    qk.product(xs, g3s, cut=(0, 2 * share))
    mine = far_share(dec.bits[0])
    dec.shares(kept_share, sent, there, mine)
    up0.step()
    down.step()
    vo.product(xs, g3s, [out_full], cut=(2 * share, share))
    part2 = far(add(part2, part3))
    up1.step()
    up0.step()
    qk.step()
    down.step()
    up1.step()
    grad_tokens, sums = chain(
        last_body,
        [kept(full(n, width)), full(24, width)],
        (at, grad_middle, part0, part1, part2, stream, enc_gain, sa, sc, sd, sums_mid),
        smem=1,
    )
    stages = [("mp", [1, 2, 3])]
    bit = 1
    while bit < dec.size:
        pair = [bit] if bit == 1 or 2 * bit >= dec.size else [bit, 2 * bit, 3 * bit]
        stages.append(("dp", pair))
        bit *= 4 if len(pair) == 3 else 2

    def add_all(*terms):
        return chain(add_all_body, [shaped(terms[0].shape, f32)], terms)[0]

    def spread_sums(terms):
        axis, masks = stages.pop(0)
        terms = terms if len(terms) == 1 else [add_all(*terms)]
        return terms + [swap(terms[0], axis, mask) for mask in masks]

    sums = spread_sums([sums])
    dec.step()
    qk.step()
    down.step()
    vo.step()
    up1.step()
    sums = spread_sums(sums)
    qk.step()
    dec.step()
    vo.step()
    qk.step()
    up1.step()
    down.step()
    sums = spread_sums(sums)
    vo.step()
    dec.step()
    qk.step()
    vo.step()
    dec.step()
    e_up = finish(
        (up0, up1),
        [(width, ff)],
        [(h, 0, None, 0, width // 8, 0, width // 8, 0, ff // 2, h * (ff // 2)) for h in range(2)],
    )[0]
    while stages:
        sums = spread_sums(sums)
    vectors = chain(
        last_sums_body,
        [full(2, share), full(1, ff), full(2, width), full(2, width), full(2, width), full(1, dwidth),
         full(2, dshare), full(1, dff // 4), full(2, dwidth), full(2, dwidth), full(2, dwidth)],
        (at, *sums),
        smem=1,
        scratch=[pltpu.VMEM((24, width), f32)],
    )
    dec.step()
    vo.step()
    e_down = finish((down,), [(ff, width)], [(0, 0, None, 0, ff // 8, 0, ff // 8, 0, width, 0)])[0]
    rows, fold = width // 8, share // 8
    e_qkv, e_out = finish(
        (qk, vo),
        [(3, width, share), (share, width)],
        [(0, 0, c, 0, rows, 0, rows, c * share, share, 0) for c in range(2)]
        + [(1, 0, 2, 0, rows, 0, rows, 0, share, 0)]
        + [(1, 1, None, 0, fold, k * fold, fold, share, width // 4, k * (width // 4)) for k in range(4)],
    )
    part, thin, tall = dwidth // 8, dshare // 8, width // 8
    top = 2 * part + thin
    d_up, d_down, d_out, d_qkv, e_embed = finish(
        (dec,),
        [(dwidth, dwidth), (dwidth, dwidth), (dshare, dwidth), (3, dwidth, dshare), (width, dshare)],
        [
            (0, 0, None, 0, part, 0, part, 0, dwidth, 0),
            (0, 1, None, 0, part, part, part, 0, dwidth, 0),
            (0, 2, None, 0, thin, 2 * part, thin, 0, dwidth, 0),
        ]
        + [(0, 3, c, 0, part, top, part, c * dshare, dshare, 0) for c in range(3)]
        + [(0, 4, None, 0, tall, top, part, 3 * dshare, dshare, 0)]
        + [(0, 4, None, part + k * thin, tall, top + part, thin, k * dshare, dshare, 0) for k in range(4)],
    )
    e_qv, e_upb, e_ob, e_gain, e_nb, d_emb, d_qv, d_upb, d_ob, d_gain, d_nb = vectors

    return (
        output,
        grad_tokens,
        e_qkv,
        e_qv,
        e_out,
        e_up,
        e_upb.reshape(-1),
        e_down,
        e_ob,
        e_gain,
        e_nb,
        e_embed,
        d_emb.reshape(-1),
        d_qkv,
        d_qv,
        d_out,
        d_up,
        d_upb.reshape(-1),
        d_down,
        d_ob,
        d_gain,
        d_nb,
    )


def solution(mesh):
    return jax.shard_map(
        per_device,
        mesh=mesh,
        in_specs=(
            P(("dp", "mp"), None),
            P("dp", None),
            P("dp", None),
            P(None, None, "mp"),
            P(None, "mp"),
            P("mp", None),
            P(None, "mp"),
            P("mp"),
            P("mp", None),
            P(),
            P(),
            P(),
            P(None, "mp"),
            P(),
            P(None, None, "mp"),
            P(None, "mp"),
            P("mp", None),
            P(None, "mp"),
            P("mp"),
            P("mp", None),
            P(),
            P(),
            P(),
            P(("dp", "mp"), None),
        ),
        out_specs=(
            P(("dp", "mp"), None),
            P(("dp", "mp"), None),
            P(None, None, "mp"),
            P(None, "mp"),
            P("mp", None),
            P(None, "mp"),
            P("mp"),
            P("mp", None),
            P(),
            P(),
            P(),
            P(None, "mp"),
            P(),
            P(None, None, "mp"),
            P(None, "mp"),
            P("mp", None),
            P(None, "mp"),
            P("mp"),
            P("mp", None),
            P(),
            P(),
            P(),
        ),
        check_vma=False,
    )
```

```python
import functools
import math

import jax
import jax.numpy as jnp
from jax import lax
from jax.experimental import pallas as pl
from jax.experimental.pallas import tpu as pltpu
from jax.sharding import PartitionSpec as P

HEADS = 16
DHEADS = 16
norm_eps = 1e-06
f32 = jnp.float32
bf16 = jnp.bfloat16
MIB = 1 << 20
VMEM = pl.BlockSpec(memory_space=pltpu.VMEM)
SMEM = pl.BlockSpec(memory_space=pltpu.SMEM)
COST = pl.CostEstimate(flops=10**10, bytes_accessed=10**8, transcendentals=0)


def shaped(dims, kind):
    return jax.ShapeDtypeStruct(dims, kind)


def kept(shape):
    return pltpu.HBM(shape.shape, shape.dtype)


def in_hbm(value):
    return pltpu.with_memory_space_constraint(value, pltpu.HBM)


class Chain:
    token = jax.ShapeDtypeStruct((8, 128), jnp.float32)

    def __init__(self):
        self.last = None

    def __call__(self, body, outs, args, smem=0, scratch=(), limit=16, prefetch=None, grid=None, specs=None):
        args, outs = list(args), list(outs)
        extra = self.last is not None
        ins = len(args) + (prefetch is not None)
        many = len(outs)

        def inner(*refs):
            out_refs = refs[ins + extra :]
            out_refs[many][...] = jnp.zeros((8, 128), f32)
            return body(*refs[:ins], *out_refs[:many], *out_refs[many + 1 :])

        if extra:
            args.append(self.last)
        tail = [pl.BlockSpec(memory_space=pl.ANY)] * extra
        params = pltpu.CompilerParams(vmem_limit_bytes=limit * MIB)
        if prefetch is None:
            got = pl.pallas_call(
                inner,
                out_shape=outs + [self.token],
                in_specs=[SMEM] * smem + [VMEM] * (len(args) - smem - extra) + tail,
                out_specs=[VMEM] * (many + 1),
                scratch_shapes=scratch,
                compiler_params=params,
                cost_estimate=COST,
            )(*args)
        else:
            got = pl.pallas_call(
                inner,
                out_shape=outs + [self.token],
                grid_spec=pltpu.PrefetchScalarGridSpec(
                    num_scalar_prefetch=1,
                    grid=grid,
                    in_specs=specs[0] + tail,
                    out_specs=specs[1] + [pl.BlockSpec((8, 128), lambda i, p: (0, 0))],
                ),
                compiler_params=params,
                cost_estimate=COST,
            )(prefetch, *args)
        *got, self.last = got
        return got

    def pin(self, value):
        def body(value_ref, last_ref, out_ref, token_ref):
            token_ref[...] = jnp.zeros((8, 128), f32)

        any_space = pl.BlockSpec(memory_space=pl.ANY)
        got, self.last = pl.pallas_call(
            body,
            out_shape=[shaped(value.shape, value.dtype), self.token],
            in_specs=[any_space, any_space],
            out_specs=[any_space, VMEM],
            input_output_aliases={0: 0},
            compiler_params=pltpu.CompilerParams(vmem_limit_bytes=MIB),
            cost_estimate=COST,
        )(value, self.last)
        return got

    def gap(self):
        self(lambda: None, [], [], limit=1)


def nn(a, b):
    return lax.dot_general(a, b, (((1,), (0,)), ((), ())), preferred_element_type=f32)


def nt(a, b):
    return lax.dot_general(a, b, (((1,), (1,)), ((), ())), preferred_element_type=f32)


def tn(a, b):
    return lax.dot_general(a, b, (((0,), (0,)), ((), ())), preferred_element_type=f32)


def swap(value, axis, mask):
    size = lax.axis_size(axis)
    return lax.ppermute(value, axis, [(i, i ^ mask) for i in range(size)])


def norm_parts(values):
    average = jnp.mean(values, axis=-1, keepdims=True)
    centred = values - average
    variance = jnp.mean(centred * centred, axis=-1, keepdims=True)
    scale = lax.rsqrt(variance + norm_eps)
    return centred * scale, scale


def norm_back(normal, scale, gain, grad):
    wide = grad * gain
    one = jnp.mean(wide, axis=-1, keepdims=True)
    two = jnp.mean(wide * normal, axis=-1, keepdims=True)
    return scale * (wide - one - normal * two)


def gelu_both(v):
    slope = math.sqrt(2.0 / math.pi)
    square = v * v
    t = jnp.tanh(slope * v * (1.0 + 0.044715 * square))
    half = 0.5 * (1.0 + t)
    return v * half, half + 0.5 * slope * v * (1.0 - t * t) * (1.0 + 3.0 * 0.044715 * square)


def sin_cos(x):
    turn = jnp.floor(x * (2.0 / math.pi) + 0.5)
    r = ((x - turn * 1.5703125) - turn * 4.837512969970703125e-4) - turn * 7.54978995489188216e-8
    z = r * r
    s = r + r * z * (-1.6666654611e-1 + z * (8.3321608736e-3 + z * -1.9515295891e-4))
    c = 1.0 - 0.5 * z + z * z * (
        4.166664568298827e-2 + z * (-1.388731625493765e-3 + z * 2.443315711809948e-5)
    )
    quarter = turn.astype(jnp.int32)
    odd = (quarter & 1) != 0
    sine = jnp.where(odd, c, s)
    cosine = jnp.where(odd, s, c)
    sine = jnp.where((quarter & 2) != 0, -sine, sine)
    cosine = jnp.where(((quarter + 1) & 2) != 0, -cosine, cosine)
    return sine, cosine


def head_masks(heads):
    size = 256 // heads
    lane = lax.broadcasted_iota(jnp.int32, (1, 256), 1)
    return [
        jnp.where((lane >= h * size) & (lane < (h + 1) * size), 1.0, 0.0).astype(bf16)
        for h in range(heads)
    ]


def attend(q, k, v, bias, heads, scale, keep):
    size = 256 // heads
    vt = v.astype(f32).T.astype(bf16)
    mixes = []
    for h, mask in enumerate(head_masks(heads)):
        s = nt(k, q * mask) + bias
        top = jnp.max(s, axis=0, keepdims=True)
        p = jnp.exp2((s - top) * (scale * math.log2(math.e)))
        total = jnp.sum(p, axis=0, keepdims=True)
        p = (p * (1.0 / total)).astype(bf16)
        keep(h, p)
        mixes.append(nn(vt[h * size : (h + 1) * size], p))
    return jnp.concatenate(mixes, axis=0).T


def attend_back(q, k, v, gm, probs, heads, scale):
    size = 256 // heads
    kt = k.astype(f32).T.astype(bf16)
    gq, gk, gv = [], 0.0, 0.0
    for h, mask in enumerate(head_masks(heads)):
        gmh = gm * mask
        p = probs(h)
        wide = p.astype(f32)
        t = wide * nt(v, gmh)
        gs = (t - wide * jnp.sum(t, axis=0, keepdims=True)).astype(bf16)
        gk = gk + nn(gs, q * mask)
        gv = gv + nn(p, gmh)
        gq.append(nn(kt[h * size : (h + 1) * size], gs))
    return jnp.concatenate(gq, axis=0).T * scale, gk * scale, gv


def place_of(slot, seg_ref, gsd_ref):
    n = seg_ref.shape[1]
    across = jnp.broadcast_to(seg_ref[pl.ds(slot, 1), :].astype(f32), (n, n))
    earlier = lax.broadcasted_iota(jnp.int32, (n, n), 1) < lax.broadcasted_iota(jnp.int32, (n, n), 0)
    rank = jnp.sum(jnp.where((across == across.T) & earlier, 1.0, 0.0), axis=1, keepdims=True)
    index = jnp.broadcast_to(gsd_ref[pl.ds(slot, 1), :].astype(f32), (n, n)).T[:, :1]
    return rank * (0.5 + 0.25 * index)


def start_body(slot_ref, seg_ref, gsd_ref, tokens_ref, gain_ref, shift_ref, wf_ref, normed_ref, stream_ref):
    place = place_of(slot_ref[0], seg_ref, gsd_ref)
    half = wf_ref.shape[1]
    sine, cosine = sin_cos(place * wf_ref[...])
    stream_ref[:, :half] = tokens_ref[:, :half].astype(f32) + sine
    stream_ref[:, half:] = tokens_ref[:, half:].astype(f32) + cosine
    normal, _ = norm_parts(stream_ref[...])
    normed_ref[...] = (normal * gain_ref[0:1] + shift_ref[0:1]).astype(bf16)


def mask_body(slot_ref, seg_ref, bias_a_ref, bias_b_ref):
    slot = slot_ref[0]
    n = seg_ref.shape[1]
    for j in range(4):
        across = jnp.broadcast_to(seg_ref[pl.ds(slot ^ j, 1), :].astype(f32), (n, n))
        (bias_a_ref, bias_b_ref)[j // 2][j % 2] = jnp.where(across == across.T, 0.0, -1e30)


def stream_body(slot_ref, seg_ref, gsd_ref, tokens_ref, eb_ref, wf_ref, nf_ref, pos_ref, stream_ref):
    place = place_of(slot_ref[0], seg_ref, gsd_ref)
    half = wf_ref.shape[1]
    sine, cosine = sin_cos(place * wf_ref[...])
    stream_ref[:, :half] = tokens_ref[:, :half].astype(f32) + sine
    stream_ref[:, half:] = tokens_ref[:, half:].astype(f32) + cosine
    half = nf_ref.shape[1]
    sine, cosine = sin_cos(place * nf_ref[...])
    pos_ref[:, :half] = sine + eb_ref[:, :half]
    pos_ref[:, half:] = cosine + eb_ref[:, half:]


def attn_body(scale, heads, first, *refs):
    count = (len(refs) - 9) // 2
    xs, rest = refs[:count], refs[count:]
    bias_ref, w_ref, qvb_ref, o_ref, q_ref, k_ref, v_ref, p_ref, mix_ref = rest[:9]
    for r, (x_ref, part_ref) in enumerate(zip(xs, rest[9:])):
        x = x_ref[...]
        q = (nn(x, w_ref[0]) + qvb_ref[0:1]).astype(bf16)
        k = nn(x, w_ref[1]).astype(bf16)
        v = (nn(x, w_ref[2]) + qvb_ref[1:2]).astype(bf16)
        q_ref[r], k_ref[r], v_ref[r] = q, k, v

        def keep(h, p):
            p_ref[r, h] = p

        mix = attend(q, k, v, bias_ref[first + r], heads, scale, keep).astype(bf16)
        mix_ref[r] = mix
        part_ref[...] = nn(mix, o_ref[...]).astype(bf16)


def attn_back_body(scale, heads, *refs):
    count = (len(refs) - 8) // 2
    gs, rest = refs[:count], refs[count:]
    q_ref, k_ref, v_ref, p_ref, w_ref, o_ref, g3_ref, sums_ref = rest[:8]
    total_q, total_v = 0.0, 0.0
    for r, (g_ref, part_ref) in enumerate(zip(gs, rest[8:])):
        gm = nt(g_ref[...], o_ref[...]).astype(bf16)
        gq, gk, gv = attend_back(
            q_ref[r], k_ref[r], v_ref[r], gm, lambda h: p_ref[r, h], heads, scale
        )
        total_q = total_q + jnp.sum(gq, axis=0, keepdims=True)
        total_v = total_v + jnp.sum(gv, axis=0, keepdims=True)
        acc = 0.0
        for c, g in enumerate((gq, gk, gv)):
            low = g.astype(bf16)
            g3_ref[r, :, c * 256 : (c + 1) * 256] = low
            acc = acc + nt(low, w_ref[c])
        part_ref[...] = acc.astype(bf16)
    sums_ref[0:1] = total_q
    sums_ref[1:2] = total_v


def mid_body(stream_ref, p_ref, near_ref, far_ref, ob_ref, gain_ref, shift_ref, mid_ref, normed_ref):
    total = p_ref[...].astype(f32) + near_ref[...].astype(f32) + far_ref[...].astype(f32)
    middle = stream_ref[...] + total + ob_ref[0:1]
    mid_ref[...] = middle
    normal, _ = norm_parts(middle)
    normed_ref[...] = (normal * gain_ref[1:2] + shift_ref[1:2]).astype(bf16)


def mlp_body(*refs):
    count = (len(refs) - 5) // 2
    xs, rest = refs[:count], refs[count:]
    up_ref, ub_ref, down_ref, hid_ref, dg_ref = rest[:5]
    width = up_ref.shape[1]
    for r, (x_ref, part_ref) in enumerate(zip(xs, rest[5:])):
        x = x_ref[...]
        for c in range(0, width, 256):
            cut = slice(c, c + 256)
            hidden, slope = gelu_both(nn(x, up_ref[:, cut]) + ub_ref[:, cut])
            hid_ref[r, :, cut] = hidden.astype(bf16)
            dg_ref[r, :, cut] = slope.astype(bf16)
        hidden = hid_ref[r]
        for c in range(0, down_ref.shape[1], 512):
            cut = slice(c, c + 512)
            part_ref[:, cut] = nn(hidden, down_ref[:, cut]).astype(bf16)


def mlp_back_body(*refs):
    count = (len(refs) - 5) // 2
    gs, rest = refs[:count], refs[count:]
    dg_ref, up_ref, down_ref, gp_ref, sums_ref = rest[:5]
    width = up_ref.shape[1]
    for r, (g_ref, part_ref) in enumerate(zip(gs, rest[5:])):
        g = g_ref[...]
        for c in range(0, width, 256):
            cut = slice(c, c + 256)
            grad = nt(g, down_ref[cut]) * dg_ref[r, :, cut].astype(f32)
            gp_ref[r, :, cut] = grad.astype(bf16)
            total = jnp.sum(grad, axis=0, keepdims=True)
            sums_ref[:, cut] = total if r == 0 else sums_ref[:, cut] + total
        gp = gp_ref[r]
        for c in range(0, up_ref.shape[0], 512):
            cut = slice(c, c + 512)
            part_ref[:, cut] = nt(gp, up_ref[cut]).astype(bf16)


def mlp_end_body(slot_ref, ge_ref, p_ref, near_ref, far_ref, mid_ref, gain_ref, ua_ref, ub_ref, uc_ref, dec_ref,
                 gmid_ref, gm_ref, pack_ref):
    slot = slot_ref[0]
    grad = p_ref[...].astype(f32) + near_ref[...].astype(f32) + far_ref[...].astype(f32)
    normal, scale = norm_parts(mid_ref[...])
    gmid = ge_ref[...] + norm_back(normal, scale, gain_ref[1:2], grad)
    gmid_ref[...] = gmid
    gm_ref[...] = gmid.astype(bf16)
    pack_ref[...] = jnp.zeros(pack_ref.shape, f32)
    pack_ref[0:1] = jnp.sum(gmid, axis=0, keepdims=True)
    pack_ref[1:2] = jnp.sum(grad * normal, axis=0, keepdims=True)
    pack_ref[2:3] = jnp.sum(grad, axis=0, keepdims=True)
    pack_ref[pl.ds(4 + slot, 1), :] = ua_ref[...] + ub_ref[...] + uc_ref[...]
    pack_ref[8:16] = dec_ref[...]


def last_body(slot_ref, gmid_ref, p_ref, near_ref, far_ref, stream_ref, gain_ref, sa_ref, sb_ref, sc_ref, mid_ref,
              gtok_ref, pack_ref):
    slot = slot_ref[0]
    grad = p_ref[...].astype(f32) + near_ref[...].astype(f32) + far_ref[...].astype(f32)
    normal, scale = norm_parts(stream_ref[...])
    gtok_ref[...] = gmid_ref[...] + norm_back(normal, scale, gain_ref[0:1], grad)
    pack_ref[:16] = mid_ref[...]
    pack_ref[16:] = jnp.zeros((8, pack_ref.shape[1]), f32)
    pack_ref[16:17] = jnp.sum(grad * normal, axis=0, keepdims=True)
    pack_ref[17:18] = jnp.sum(grad, axis=0, keepdims=True)
    share = sa_ref.shape[1]
    place = pl.ds(pl.multiple_of(slot * share, share), share)
    pack_ref[18:20, place] = sa_ref[...] + sb_ref[...] + sc_ref[...]


def decoder_body(slot_ref, mid_ref, p_ref, near_ref, far_ref, eob_ref, own_ref, by_ref, fa_ref, fb_ref, na_ref, nb_ref,
                 b0_ref, b1_ref, b2_ref, b3_ref, pos_ref, bias_ref, dob_ref, dgain_ref, dnb_ref, cot_ref,
                 encl_ref, out_ref, x1_ref, x2_ref, hid_ref, mix_ref, gp_ref, gm_ref, g3_ref, gz_ref,
                 gel_ref, ge_ref, sums_ref,
                 wup, wdown, wqkv, wout, wemb, pt, dg, qkv, wide, qvb_ref, upb_ref):
    slot, home = slot_ref[0], slot_ref[1]
    width = cot_ref.shape[1]
    block = width // 4
    heads = DHEADS * 256 // width
    groups = width // 256
    scale = (width // DHEADS) ** -0.5

    def place(j, base=0):
        return pl.ds(pl.multiple_of(base + (slot ^ j) * block, block), block)

    for j, ref in enumerate((b0_ref, b1_ref, b2_ref, b3_ref)):
        for c in range(2):
            qvb_ref[c : c + 1, j * block : (j + 1) * block] = ref[:, c * block : (c + 1) * block]
        upb_ref[:, j * width : (j + 1) * width] = ref[:, 2 * block :]
    piece, thin, tall = width // 8, block // 8, 2 * width // 8
    top = 2 * piece + thin
    step = top + piece + thin
    for j, (low_ref, high_ref) in enumerate(
        ((own_ref, own_ref), (by_ref, by_ref), (fa_ref, fb_ref), (na_ref, nb_ref))
    ):
        cut = slice(j * block, (j + 1) * block)
        for i in range(8):
            ref = (low_ref, high_ref)[i // 4]
            base = (i if j < 2 else i % 4) * step
            chunk = i if j < 2 else home ^ i

            def rows(size):
                return pl.ds(pl.multiple_of(chunk * size, size), size)

            wup[j, rows(piece)] = ref[base : base + piece]
            wdown[j, rows(piece)] = ref[base + piece : base + 2 * piece]
            wout[pl.ds(pl.multiple_of(j * block + chunk * thin, thin), thin)] = (
                ref[base + 2 * piece : base + top]
            )
            for c in range(3):
                wqkv[c, rows(piece), cut] = ref[base + top : base + top + piece, c * block : (c + 1) * block]
            wemb[pl.ds(pl.multiple_of(chunk * tall, tall), piece), cut] = (
                ref[base + top : base + top + piece, 3 * block :]
            )
            for c in range(4):
                wemb[pl.ds(pl.multiple_of(chunk * tall + piece + c * thin, thin), thin), cut] = (
                    ref[base + top + piece : base + step, c * block : (c + 1) * block]
                )
    encoded = mid_ref[...] + eob_ref[1:2]
    encoded = encoded + p_ref[...].astype(f32) + near_ref[...].astype(f32) + far_ref[...].astype(f32)
    encl_ref[...] = encoded.astype(bf16)
    embedded = nn(encl_ref[...], wemb[...])
    for j in range(4):
        wide[:, place(j)] = embedded[:, j * block : (j + 1) * block]
    stream = wide[...] + pos_ref[...]
    normal1, scale1 = norm_parts(stream)
    x1_ref[...] = (normal1 * dgain_ref[0:1] + dnb_ref[0:1]).astype(bf16)
    x1 = x1_ref[...]
    qkv[0] = (nn(x1, wqkv[0]) + qvb_ref[0:1]).astype(bf16)
    qkv[1] = nn(x1, wqkv[1]).astype(bf16)
    qkv[2] = (nn(x1, wqkv[2]) + qvb_ref[1:2]).astype(bf16)
    bias = bias_ref[0]
    for g in range(groups):
        cut = slice(g * 256, (g + 1) * 256)

        def keep(h, p):
            pt[g * heads + h] = p

        mix_ref[:, cut] = attend(
            qkv[0, :, cut], qkv[1, :, cut], qkv[2, :, cut], bias, heads, scale, keep
        ).astype(bf16)
    middle = stream + nn(mix_ref[...], wout[...]) + dob_ref[0:1]
    normal2, scale2 = norm_parts(middle)
    x2_ref[...] = (normal2 * dgain_ref[1:2] + dnb_ref[1:2]).astype(bf16)
    x2 = x2_ref[...]
    result = middle + dob_ref[1:2]
    for j in range(4):
        cut = slice(j * width, (j + 1) * width)
        hidden, slope = gelu_both(nn(x2, wup[j]) + upb_ref[:, cut])
        hid_ref[:, cut] = hidden.astype(bf16)
        dg[:, cut] = slope.astype(bf16)
        result = result + nn(hid_ref[:, cut], wdown[j])
    out_ref[...] = result

    cot = cot_ref[...]
    grad = 0.0
    sums_ref[...] = jnp.zeros(sums_ref.shape, f32)
    for j in range(4):
        cut = slice(j * width, (j + 1) * width)
        pre = nt(cot, wdown[j]) * dg[:, cut].astype(f32)
        gp_ref[:, cut] = pre.astype(bf16)
        block_sum = jnp.sum(pre, axis=0, keepdims=True)
        at = slot ^ j
        sums_ref[pl.ds(6 + (at >> 1), 1), pl.ds(pl.multiple_of((at & 1) * width, width), width)] = (
            block_sum
        )
        grad = grad + nt(gp_ref[:, cut], wup[j])
    cotf = cot.astype(f32)
    gmid = cotf + norm_back(normal2, scale2, dgain_ref[1:2], grad)
    gm_ref[...] = gmid.astype(bf16)
    sums_ref[1:2, :width] = jnp.sum(gmid, axis=0, keepdims=True)
    sums_ref[2:3, :width] = jnp.sum(cotf, axis=0, keepdims=True)
    sums_ref[2:3, width:] = jnp.sum(grad * normal2, axis=0, keepdims=True)
    sums_ref[4:5, :width] = jnp.sum(grad, axis=0, keepdims=True)
    gmix = nt(gm_ref[...], wout[...]).astype(bf16)
    grad = 0.0
    for g in range(groups):
        cut = slice(g * 256, (g + 1) * 256)
        three = attend_back(
            qkv[0, :, cut], qkv[1, :, cut], qkv[2, :, cut], gmix[:, cut],
            lambda h: pt[g * heads + h], heads, scale,
        )
        for c, part in enumerate(three):
            begin = c * width + g * 256
            low = part.astype(bf16)
            g3_ref[:, begin : begin + 256] = low
            grad = grad + nt(low, wqkv[c, :, cut])
        for c, row, base in ((0, 4, width), (2, 5, width)):
            total = jnp.sum(three[c], axis=0, keepdims=True)
            for i in range(256 // block):
                sums_ref[row : row + 1, place(g * (256 // block) + i, base)] = (
                    total[:, i * block : (i + 1) * block]
                )
    gstream = gmid + norm_back(normal1, scale1, dgain_ref[0:1], grad)
    sums_ref[3:4, width:] = jnp.sum(gstream, axis=0, keepdims=True)
    sums_ref[1:2, width:] = jnp.sum(grad * normal1, axis=0, keepdims=True)
    sums_ref[3:4, :width] = jnp.sum(grad, axis=0, keepdims=True)
    wide[...] = gstream
    for j in range(4):
        gz_ref[:, j * block : (j + 1) * block] = wide[:, place(j)].astype(bf16)
    ge = nt(gz_ref[...], wemb[...])
    ge_ref[...] = ge
    gel_ref[...] = ge.astype(bf16)
    sums_ref[0:1] = jnp.sum(ge, axis=0, keepdims=True)


def decoder_weights_body(x1_ref, x2_ref, hid_ref, mix_ref, gp_ref, gm_ref, g3_ref, gz_ref, encl_ref, cot_ref,
                         sent_ref, kept_ref):
    width = cot_ref.shape[1]
    block = width // 4
    cot, gm, x2 = cot_ref[...], gm_ref[...], x2_ref[...]
    piece, thin = width // 8, block // 8
    tall = encl_ref.shape[1] // 8
    top = 2 * piece + thin
    step = top + piece + thin

    def to(j):
        return sent_ref if j % 2 else kept_ref

    for j in (1, 3, 0, 2):
        w = to(j)
        i = j // 2
        cut = slice(j * width, (j + 1) * width)
        up = tn(x2, gp_ref[:, cut]).astype(bf16)
        down = tn(hid_ref[:, cut], cot).astype(bf16)
        out = tn(mix_ref[:, j * block : (j + 1) * block], gm).astype(bf16)
        for c in range(8):
            w[i, c * step : c * step + piece] = up[c * piece : (c + 1) * piece]
            w[i, c * step + piece : c * step + 2 * piece] = down[c * piece : (c + 1) * piece]
            w[i, c * step + 2 * piece : c * step + top] = out[c * thin : (c + 1) * thin]
    x1 = x1_ref[...]
    for k in range(3):
        full = tn(x1, g3_ref[:, k * width : (k + 1) * width]).astype(bf16)
        for j in range(4):
            for c in range(8):
                to(j)[j // 2, c * step + top : c * step + top + piece, k * block : (k + 1) * block] = (
                    full[c * piece : (c + 1) * piece, j * block : (j + 1) * block]
                )
    full = tn(encl_ref[...], gz_ref[...]).astype(bf16)
    for j in range(4):
        cut = slice(j * block, (j + 1) * block)
        for c in range(8):
            base = c * tall
            to(j)[j // 2, c * step + top : c * step + top + piece, 3 * block :] = full[base : base + piece, cut]
            base = base + piece
            for k in range(4):
                to(j)[j // 2, c * step + top + piece : (c + 1) * step, k * block : (k + 1) * block] = (
                    full[base + k * thin : base + (k + 1) * thin, cut]
                )


def pack_body(pick_ref, up_ref, down_ref, out_ref, qkv_ref, emb_ref, chunk_ref):
    piece, thin, block = up_ref.shape[0], out_ref.shape[0], emb_ref.shape[1]
    chunk_ref[:piece] = up_ref[...]
    chunk_ref[piece : 2 * piece] = down_ref[...]
    top = 2 * piece + thin
    chunk_ref[2 * piece : top] = out_ref[...]
    for c in range(3):
        chunk_ref[top : top + piece, c * block : (c + 1) * block] = qkv_ref[c]
    chunk_ref[top : top + piece, 3 * block :] = emb_ref[:piece]
    for c in range(4):
        base = piece + c * thin
        chunk_ref[top + piece :, c * block : (c + 1) * block] = emb_ref[base : base + thin]


def join_body(a_ref, b_ref, out_ref):
    rows = a_ref.shape[0]
    out_ref[:rows] = a_ref[...]
    out_ref[rows:] = b_ref[...]


def add_body(a_ref, b_ref, out_ref):
    out_ref[...] = (a_ref[...].astype(f32) + b_ref[...].astype(f32)).astype(out_ref.dtype)


def add_all_body(*refs):
    total = refs[0][...]
    for ref in refs[1:-1]:
        total = total + ref[...]
    refs[-1][...] = total


def last_sums_body(slot_ref, *refs):
    terms, outs, total_ref = refs[:-12], refs[-12:-1], refs[-1]
    total = terms[0][...]
    for ref in terms[1:]:
        total = total + ref[...]
    total_ref[...] = total
    slot = slot_ref[0]
    e_qv, e_upb, e_ob, e_gain, e_nb, d_emb, d_qv, d_upb, d_ob, d_gain, d_nb = outs
    share, thin, width = e_qv.shape[1], d_qv.shape[1], d_emb.shape[1]
    e_qv[...] = total_ref[18:20, pl.ds(pl.multiple_of(slot * share, share), share)]
    e_upb[...] = total_ref[pl.ds(4 + slot, 1), :]
    e_ob[0:1] = total_ref[0:1]
    e_ob[1:2] = total_ref[8:9]
    e_gain[0:1] = total_ref[16:17]
    e_gain[1:2] = total_ref[1:2]
    e_nb[0:1] = total_ref[17:18]
    e_nb[1:2] = total_ref[2:3]
    d_ob[...] = total_ref[9:11, :width]
    d_gain[...] = total_ref[9:11, width:]
    d_nb[...] = total_ref[11:13, :width]
    d_emb[...] = total_ref[11:12, width:]
    d_qv[...] = total_ref[12:14, pl.ds(pl.multiple_of(width + slot * thin, thin), thin)]
    d_upb[...] = total_ref[pl.ds(14 + (slot >> 1), 1), pl.ds(pl.multiple_of((slot & 1) * width, width), width)]


def halve_body(bit_ref, *refs):
    ins, (send_ref, keep_ref) = refs[:-2], refs[-2:]
    half = send_ref.shape[0]
    bit = bit_ref[0]
    for ref, which in ((send_ref, 1 - bit), (keep_ref, bit)):
        rows = pl.ds(pl.multiple_of(which * half, half), half)
        total = ins[0][rows].astype(f32)
        for other in ins[1:]:
            total = total + other[rows].astype(f32)
        ref[...] = total.astype(bf16)


def far_body(bit_ref, kept_ref, near_ref, out_ref):
    half = out_ref.shape[0]
    rows = pl.ds(pl.multiple_of(bit_ref[0] * half, half), half)
    out_ref[...] = (kept_ref[1, rows].astype(f32) + near_ref[1, rows].astype(f32)).astype(bf16)


def there_body(bit_ref, kept_ref, near_ref, far_ref, send_ref):
    half = send_ref.shape[0]
    rows = pl.ds(pl.multiple_of((1 - bit_ref[0]) * half, half), half)
    total = kept_ref[0, rows].astype(f32) + near_ref[0, rows].astype(f32)
    send_ref[...] = (total + far_ref[...].astype(f32)).astype(bf16)


def mine_body(bit_ref, kept_ref, near_ref, far_ref, got_ref, send_ref, keep_ref):
    quarter = send_ref.shape[0]
    base = bit_ref[0] * 2 * quarter
    for ref, which in ((send_ref, 1 - bit_ref[1]), (keep_ref, bit_ref[1])):
        rows = pl.ds(pl.multiple_of(base + which * quarter, quarter), quarter)
        inner = pl.ds(pl.multiple_of(which * quarter, quarter), quarter)
        total = kept_ref[0, rows].astype(f32) + near_ref[0, rows].astype(f32)
        ref[...] = (total + far_ref[inner].astype(f32) + got_ref[inner].astype(f32)).astype(bf16)


def piece_of(refs, j):
    for ref in refs:
        if len(ref.shape) == 2:
            if j == 0:
                return ref[...]
            j -= 1
        elif j < ref.shape[0]:
            return ref[j]
        else:
            j -= ref.shape[0]


def tile_sum(xs, gs, more):
    acc = 0.0
    for j in range(4):
        acc = acc + tn(piece_of(xs, j), piece_of(gs, j))
    if not more:
        return [(slice(None), slice(None), acc)]
    rows, cols = acc.shape
    parts = [(slice(None), slice(0, cols), acc)]
    half, quarter = rows // 2, rows // 8
    wide = more[0].shape[1] // 4
    for c in range(2):
        for k in range(4):
            parts.append((
                slice(c * half + k * quarter, c * half + (k + 1) * quarter),
                slice(cols, cols + wide),
                more[0][c * quarter : (c + 1) * quarter, k * wide : (k + 1) * wide].astype(f32),
            ))
    return parts


def first_half_body(nx, ng, nm, pick_ref, *refs):
    xs, gs, more = refs[:nx], refs[nx : nx + ng], refs[nx + ng : nx + ng + nm]
    out_ref = refs[nx + ng + nm]
    for rows, cols, value in tile_sum(xs, gs, more):
        out_ref[rows, cols] = value.astype(bf16)


def other_half_body(nx, ng, nm, pick_ref, *refs):
    xs, gs, more = refs[:nx], refs[nx : nx + ng], refs[nx + ng : nx + ng + nm]
    add_ref, send_ref, keep_ref = refs[nx + ng + nm :]
    parts = [
        (rows, cols, (value + add_ref[rows, cols].astype(f32)).astype(bf16))
        for rows, cols, value in tile_sum(xs, gs, more)
    ]

    def put(ref):
        for rows, cols, value in parts:
            ref[rows, cols] = value

    @pl.when(pl.program_id(0) == 0)
    def _():
        put(send_ref)

    @pl.when(pl.program_id(0) == 1)
    def _():
        put(keep_ref)


def weight_half(chain, xs, gs, more, cut, pick, add=None):
    tile = xs[0].shape[-1] // 4
    begin, cols = cut
    out_cols = cols + sum(m.shape[1] // 4 for m in more)

    def column(shape):
        lead = shape[:-1]
        return pl.BlockSpec(lead + (tile,), lambda i, p: (0,) * len(lead) + (p[i],))

    def whole(shape):
        lead = shape[:-1]
        return pl.BlockSpec(lead + (cols,), lambda i, p: (0,) * len(lead) + (begin // cols,))

    in_specs = [column(x.shape) for x in xs] + [whole(g.shape) for g in gs]
    in_specs += [pl.BlockSpec((tile // 4, m.shape[1]), lambda i, p: (p[i], 0)) for m in more]
    args = list(xs) + list(gs) + list(more)
    counts = len(xs), len(gs), len(more)
    if add is None:
        body = functools.partial(first_half_body, *counts)
        outs = [shaped((2 * tile, out_cols), bf16)]
        out_specs = [pl.BlockSpec((tile, out_cols), lambda i, p: (i, 0))]
    else:
        body = functools.partial(other_half_body, *counts)
        in_specs.append(pl.BlockSpec((tile, out_cols), lambda i, p: (p[2 + i], 0)))
        args.append(add)
        outs = [shaped((tile, out_cols), bf16)] * 2
        out_specs = [pl.BlockSpec((tile, out_cols), lambda i, p: (0, 0))] * 2
    return chain(body, outs, args, prefetch=pick, grid=(2,), specs=(in_specs, out_specs), limit=20)


def spread_body(writes, place_ref, *refs):
    sums = max(write[0] for write in writes) + 1
    out_refs = refs[2 * sums :]
    for i in range(8):
        for source, which, lead, first, every, row, rows, col, cols, at_col in writes:
            ref = refs[2 * source + i // 4]
            base = i % 4 * (ref.shape[0] // 4)
            at = place_ref[source] ^ i
            value = ref[base + row : base + row + rows, col : col + cols].astype(f32)
            to = pl.ds(pl.multiple_of(at * every + first, rows), rows)
            if lead is None:
                out_refs[which][to, at_col : at_col + cols] = value
            else:
                out_refs[which][lead, to] = value


def out_weight_body(*refs):
    mixes, gs, out_ref = refs[:3], refs[3:7], refs[7]
    acc = 0.0
    for j in range(4):
        acc = acc + tn(piece_of(mixes, j), piece_of(gs, j))
    out_ref[...] = acc.astype(bf16)


class Sum:
    def __init__(self, chain, masks=(1, 2, 4)):
        self.chain, self.masks = chain, masks
        self.size = lax.axis_size("dp")
        me = lax.axis_index("dp").astype(jnp.int32)
        b1, b2, b3 = self.bits = [jnp.where((me & mask) != 0, 1, 0).astype(jnp.int32) for mask in masks]
        self.place = 4 * b1 + 2 * b2 + b3 if self.size == 8 else jnp.int32(0)
        self.there = jnp.stack([2 * (1 - b1), 2 * (1 - b1) + 1])
        self.mine = jnp.stack([2 * b1 + 1 - b2, 2 * b1 + b2, 1 - b2, b2])
        steps = [self.second, self.third, self.fourth, self.fifth, self.sixth]
        self.steps = iter(steps if self.size == 8 else [])

    def step(self):
        for todo in self.steps:
            todo()
            return

    def product(self, xs, gs, more=(), cut=None):
        self.terms = (xs, gs, more, cut or (0, gs[0].shape[-1]))
        if self.size != 8:
            first = weight_half(self.chain, *self.terms, jnp.array([0, 1], jnp.int32))[0]
            other = weight_half(self.chain, *self.terms, jnp.array([2, 3], jnp.int32))[0]
            return self.general(jnp.concatenate([first, other], axis=0))
        self.got = swap(weight_half(self.chain, *self.terms, self.there)[0], "dp", self.masks[0])

    def shares(self, kept, near, there):
        self.terms = None
        self.held = (kept, near, there)
        if self.size == 8:
            half = shaped(there.shape, bf16)
            send = self.chain(there_body, [half], (self.bits[0].reshape(1), kept, near, there), smem=1)[0]
            self.got = swap(send, "dp", self.masks[0])

    def other(self, mine):
        kept, near, there = self.held
        self.held = (kept, near, mine)
        if self.size != 8:
            total = kept[0].astype(f32) + near[0].astype(f32)
            total = total + jnp.concatenate([mine, there], axis=0).astype(f32)
            self.general(total.astype(bf16))

    def second(self):
        if self.terms is None:
            rows, cols = self.got.shape
            half = shaped((rows // 2, cols), bf16)
            send, self.keep = self.chain(
                mine_body, [half, half], (jnp.stack(self.bits[:2]), *self.held, self.got), smem=1
            )
        else:
            send, self.keep = weight_half(self.chain, *self.terms, self.mine, self.got)
        self.got = swap(send, "dp", self.masks[1])

    def third(self):
        rows, cols = self.keep.shape
        half = shaped((rows // 2, cols), bf16)
        send, self.keep = self.chain(
            halve_body, [half, half], (self.bits[2].reshape(1), self.keep, self.got), smem=1
        )
        self.got = swap(send, "dp", self.masks[2])

    def fourth(self):
        self.keep = self.chain(add_body, [shaped(self.keep.shape, bf16)], (self.keep, self.got))[0]
        self.got = swap(self.keep, "dp", self.masks[2])

    def join(self):
        rows, cols = self.keep.shape
        self.keep = self.chain(join_body, [shaped((2 * rows, cols), bf16)], (self.keep, self.got))[0]

    def fifth(self):
        self.join()
        self.got = swap(self.keep, "dp", self.masks[1])

    def sixth(self):
        self.join()
        self.got = swap(self.keep, "dp", self.masks[0])

    def general(self, held):
        me = lax.axis_index("dp")
        bits = [1 << i for i in range(self.size.bit_length() - 1)]
        for bit in bits:
            mine = (me & bit) != 0
            half = held.shape[0] // 2
            other = lax.dynamic_slice_in_dim(held, jnp.where(mine, 0, half), half, 0)
            own = lax.dynamic_slice_in_dim(held, jnp.where(mine, half, 0), half, 0)
            held = (own.astype(f32) + swap(other, "dp", bit).astype(f32)).astype(bf16)
        for bit in reversed(bits):
            mine = (me & bit) != 0
            other = swap(held, "dp", bit)
            held = jnp.where(
                mine,
                jnp.concatenate([other, held], axis=0),
                jnp.concatenate([held, other], axis=0),
            )
        half = held.shape[0] // 2
        self.keep, self.got = held[:half], held[half:]


def per_device(
    tokens, segment_ids, gsd_index, enc_qkv, enc_qv_bias, enc_out_proj, enc_up, enc_up_bias,
    enc_down, enc_out_bias, enc_gain, enc_norm_bias, embed_weight, embed_bias, dec_qkv,
    dec_qv_bias, dec_out_proj, dec_up, dec_up_bias, dec_down, dec_out_bias, dec_gain,
    dec_norm_bias, cotangent,
):
    n, width = tokens.shape
    rows, length = segment_ids.shape
    assert rows == 4 and n == length == 256 and lax.axis_size("mp") == 4
    share, ff = enc_qkv.shape[2], enc_up.shape[1]
    dwidth, dff = cotangent.shape[1], dec_up.shape[1] * 4
    dshare = dwidth // 4
    heads = share // (width // HEADS)
    scale = (width // HEADS) ** -0.5
    slot = lax.axis_index("mp").astype(jnp.int32)
    at = slot.reshape(1)
    chain = Chain()
    dec = Sum(chain)
    home = dec.place

    def low(*dims):
        return shaped(dims, bf16)

    def full(*dims):
        return shaped(dims, f32)

    def waves(size):
        half = size // 2
        return jnp.power(10000.0, -jnp.arange(half, dtype=f32) / half).reshape(1, half)

    def near(value):
        return swap(value, "mp", 1)

    def far(value):
        return swap(value, "mp", 2)

    pack_rows = 3 * dwidth + 2 * dshare
    decoder_weights = [in_hbm(w) for w in (dec_up, dec_down, dec_out_proj, dec_qkv, embed_weight)]

    def pack(pick, steps):
        def block(shape):
            if len(shape) == 3:
                return pl.BlockSpec((shape[0], shape[1] // 8, shape[2]), lambda i, p: (0, p[i], 0))
            return pl.BlockSpec((shape[0] // 8, shape[1]), lambda i, p: (p[i], 0))

        rows = pack_rows // 8
        return chain(
            pack_body,
            [low(steps * rows, dwidth)],
            decoder_weights,
            prefetch=pick,
            grid=(steps,),
            specs=([block(w.shape) for w in decoder_weights], [pl.BlockSpec((rows, dwidth), lambda i, p: (i, 0))]),
        )[0]

    split = dec.size == 8
    got = far(pack(home.reshape(1), 1)) if split else None
    normed = chain(
        start_body,
        [low(n, width)],
        (at, in_hbm(segment_ids), in_hbm(gsd_index), in_hbm(tokens), in_hbm(enc_gain), in_hbm(enc_norm_bias), waves(width)),
        smem=1,
        scratch=[pltpu.VMEM((n, width), f32)],
    )[0]
    x = [normed, near(normed), far(normed)]
    bias_a, bias_b = chain(mask_body, [kept(full(2, n, n)), kept(full(2, n, n))], (at, in_hbm(segment_ids)), smem=1)

    def attention(bias, first, *blocks):
        count = len(blocks)
        return chain(
            functools.partial(attn_body, scale, heads, first),
            [kept(low(count, n, share))] * 3
            + [kept(low(count, heads, n, n)), kept(low(count, n, share))]
            + [low(n, width)] * count,
            (*blocks, bias, enc_qkv, enc_qv_bias, enc_out_proj),
        )

    def add(a, b):
        return chain(add_body, [shaped(a.shape, a.dtype)], (a, b))[0]

    def join(a, b):
        return chain(join_body, [low(a.shape[0] + b.shape[0], a.shape[1])], (a, b))[0]

    def both(blocks):
        blocks[2] = chain.pin(blocks[2])
        blocks.append(near(blocks[2]))

    *saved_a, mixa, part0, part1 = attention(bias_a, 0, x[0], x[1])
    part1 = near(part1)
    vector = jnp.concatenate([dec_qv_bias.reshape(-1), dec_up_bias]).reshape(1, -1)
    vectors = [vector, chain.pin(near(vector)), far(vector)]
    both(vectors)
    part1 = chain.pin(part1)
    if split:
        got = chain.pin(got)
        more = swap(got, "dp", 4)
    both(x)
    vectors[3] = chain.pin(vectors[3])
    chain.gap()
    *saved_d, mixd, part3 = attention(bias_b, 1, x[3])
    part3 = near(part3)
    *saved_c, mixc, part2 = attention(bias_b, 0, x[2])
    part2 = far(add(part2, part3))
    packed = pack(jnp.arange(8, dtype=jnp.int32), 8)
    packed_near = near(packed)
    pos, stream = chain(
        stream_body,
        [kept(full(n, dwidth)), full(n, width)],
        (at, in_hbm(segment_ids), in_hbm(gsd_index), in_hbm(tokens), in_hbm(embed_bias.reshape(1, -1)), waves(width), waves(dwidth)),
        smem=1,
    )
    if split:
        got = join(got, more)
        more = swap(got, "dp", 2)
    else:
        got = far(packed)
    middle, normed2 = chain(
        mid_body,
        [kept(full(n, width)), low(n, width)],
        (stream, part0, part1, part2, enc_out_bias, enc_gain, enc_norm_bias),
    )
    y = [normed2, near(normed2), far(normed2)]
    packed_near = chain.pin(packed_near)
    if split:
        got = join(got, more)
        more = swap(got, "dp", 1)
    else:
        more = got[pack_rows // 2 :]
        got = got[: pack_rows // 2]

    def feed(*blocks):
        count = len(blocks)
        return chain(
            mlp_body,
            [kept(low(count, n, ff))] * 2 + [low(n, width)] * count,
            (*blocks, enc_up, enc_up_bias.reshape(1, -1), enc_down),
        )

    hida, dga, part0, part1 = feed(y[0], y[1])
    part1 = near(part1)
    far_weights = [got, more]
    near_weights = [near(got)]
    part1 = chain.pin(part1)
    both(y)
    near_weights[0] = chain.pin(near_weights[0])
    hidd, dgd, part3 = feed(y[3])
    part3 = near(part3)
    hidc, dgc, part2 = feed(y[2])
    part2 = far(add(part2, part3))
    far_weights[1] = chain.pin(more)
    near_weights.append(near(far_weights[1]))
    part2 = chain.pin(part2)

    (enc_low, output, x1, x2, hid, mix, gp, gm, g3, gz, ge_low, ge, dec_sums) = chain(
        decoder_body,
        [kept(o) for o in (low(n, width), full(n, dwidth), low(n, dwidth), low(n, dwidth), low(n, dff),
                           low(n, dwidth), low(n, dff), low(n, dwidth), low(n, 3 * dwidth), low(n, dwidth))]
        + [low(n, width), kept(full(n, width)), kept(full(8, width))],
        (jnp.stack([slot, home]), middle, part0, part1, part2, enc_out_bias, packed, packed_near,
         *far_weights, *near_weights, *vectors, pos, bias_a, dec_out_bias, dec_gain,
         dec_norm_bias, cotangent),
        smem=1,
        scratch=[
            pltpu.VMEM((4, dwidth, dwidth), bf16), pltpu.VMEM((4, dwidth, dwidth), bf16),
            pltpu.VMEM((3, dwidth, dwidth), bf16), pltpu.VMEM((dwidth, dwidth), bf16),
            pltpu.VMEM((width, dwidth), bf16), pltpu.VMEM((DHEADS, n, n), bf16),
            pltpu.VMEM((n, dff), bf16), pltpu.VMEM((3, n, dwidth), bf16), pltpu.VMEM((n, dwidth), f32),
            pltpu.VMEM((2, dwidth), f32), pltpu.VMEM((1, dff), f32),
        ],
        limit=40,
    )
    g = [ge_low, near(ge_low), far(ge_low)]

    def feed_back(slope, *blocks):
        count = len(blocks)
        return chain(
            mlp_back_body,
            [kept(low(count, n, ff)), kept(full(1, ff))] + [low(n, width)] * count,
            (*blocks, slope, enc_up, enc_down),
        )

    def attention_back(saved, *blocks):
        count = len(blocks)
        return chain(
            functools.partial(attn_back_body, scale, heads),
            [kept(low(count, n, 3 * share)), kept(full(2, share))] + [low(n, width)] * count,
            (*blocks, *saved, enc_qkv, enc_out_proj),
        )

    def far_share(bit):
        return far(chain(far_body, [low(pack_rows // 2, dwidth)], (bit.reshape(1), kept_share, sent), smem=1)[0])

    def hbm(*values):
        return [in_hbm(v) for v in values]

    down, up, attn = Sum(chain), Sum(chain), Sum(chain)

    def finish(sums, outs, writes):
        return chain(
            functools.partial(spread_body, writes),
            [kept(full(*dims)) for dims in outs],
            (jnp.stack([f.place for f in sums]), *[v for f in sums for v in (f.keep, f.got)]),
            smem=1,
            limit=24,
        )

    chain.gap()
    gpa, upa, part0, part1 = feed_back(dga, g[0], g[1])
    part1 = near(part1)
    sent, kept_share = chain(
        decoder_weights_body,
        [low(2, pack_rows, dwidth), kept(low(2, pack_rows, dwidth))],
        (x1, x2, hid, mix, gp, gm, g3, gz, enc_low, cotangent),
        limit=24,
    )
    sent = near(sent)
    part1 = chain.pin(part1)
    both(g)
    gpc, upc, part2 = feed_back(dgc, g[2])
    gpd, upd, part3 = feed_back(dgd, g[3])
    part3 = near(part3)
    down.product(hbm(hida, hidc, hidd), g)
    part2 = far(add(part2, part3))
    there = far_share(1 - dec.bits[0])
    grad_middle, gm_low, sums_mid = chain(
        mlp_end_body,
        [kept(full(n, width)), low(n, width), kept(full(16, width))],
        (at, ge, part0, part1, part2, middle, enc_gain, upa, upc, upd, dec_sums),
        smem=1,
    )
    m = [gm_low, near(gm_low), far(gm_low)]
    up.product(hbm(*y), hbm(gpa, gpc, gpd))
    down.step()
    g3a, sa, part0, part1 = attention_back(saved_a, m[0], m[1])
    part1 = near(part1)
    chain.gap()
    part1 = chain.pin(part1)
    both(m)
    g3c, sc, part2 = attention_back(saved_c, m[2])
    out_full = chain(out_weight_body, [low(share, width)], (mixa, mixc, mixd, *m))[0]
    g3d, sd, part3 = attention_back(saved_d, m[3])
    part3 = near(part3)
    down.step()
    attn.product(hbm(*x), hbm(g3a, g3c, g3d), [out_full])
    part2 = far(add(part2, part3))
    up.step()
    down.step()
    dec.shares(kept_share, sent, there)
    up.step()
    grad_tokens, sums = chain(
        last_body,
        [kept(full(n, width)), full(24, width)],
        (at, grad_middle, part0, part1, part2, stream, enc_gain, sa, sc, sd, sums_mid),
        smem=1,
    )
    hops = [("mp", 1), ("mp", 2)] + [("dp", 1 << i) for i in range(dec.size.bit_length() - 1)]
    hops = iter(hops)

    def hop(total, got=None):
        if got is not None:
            total = add(total, got)
        for axis, mask in hops:
            return total, swap(total, axis, mask)
        return total, None

    dec.other(far_share(dec.bits[0]))
    attn.step()
    down.step()
    up.step()
    attn.step()
    dec.step()
    small = hop(sums)
    down.step()
    up.step()
    small = hop(*small)
    attn.step()
    dec.step()
    small = hop(*small)
    up.step()
    attn.step()
    small = hop(*small)
    e_down = finish((down,), [(ff, width)], [(0, 0, None, 0, ff // 8, 0, ff // 8, 0, width, 0)])[0]
    dec.step()
    small = hop(*small)
    attn.step()
    e_up = finish((up,), [(width, ff)], [(0, 0, None, 0, width // 8, 0, width // 8, 0, ff, 0)])[0]
    dec.step()
    while small[1] is not None:
        sums = small
        small = hop(*small)
    vectors = chain(
        last_sums_body,
        [full(2, share), full(1, ff), full(2, width), full(2, width), full(2, width), full(1, dwidth),
         full(2, dshare), full(1, dff // 4), full(2, dwidth), full(2, dwidth), full(2, dwidth)],
        (at, *sums),
        smem=1,
        scratch=[pltpu.VMEM((24, width), f32)],
    )
    dec.step()
    rows, fold = width // 8, share // 8
    e_qkv, e_out = finish(
        (attn,),
        [(3, width, share), (share, width)],
        [(0, 0, c, 0, rows, 0, rows, c * share, share, 0) for c in range(3)]
        + [(0, 1, None, 0, fold, k * fold, fold, 3 * share, width // 4, k * (width // 4)) for k in range(4)],
    )
    part, thin, tall = dwidth // 8, dshare // 8, width // 8
    top = 2 * part + thin
    d_up, d_down, d_out, d_qkv, e_embed = finish(
        (dec,),
        [(dwidth, dwidth), (dwidth, dwidth), (dshare, dwidth), (3, dwidth, dshare), (width, dshare)],
        [
            (0, 0, None, 0, part, 0, part, 0, dwidth, 0),
            (0, 1, None, 0, part, part, part, 0, dwidth, 0),
            (0, 2, None, 0, thin, 2 * part, thin, 0, dwidth, 0),
        ]
        + [(0, 3, c, 0, part, top, part, c * dshare, dshare, 0) for c in range(3)]
        + [(0, 4, None, 0, tall, top, part, 3 * dshare, dshare, 0)]
        + [(0, 4, None, part + k * thin, tall, top + part, thin, k * dshare, dshare, 0) for k in range(4)],
    )
    e_qv, e_upb, e_ob, e_gain, e_nb, d_emb, d_qv, d_upb, d_ob, d_gain, d_nb = vectors

    return (
        output,
        grad_tokens,
        e_qkv,
        e_qv,
        e_out,
        e_up,
        e_upb.reshape(-1),
        e_down,
        e_ob,
        e_gain,
        e_nb,
        e_embed,
        d_emb.reshape(-1),
        d_qkv,
        d_qv,
        d_out,
        d_up,
        d_upb.reshape(-1),
        d_down,
        d_ob,
        d_gain,
        d_nb,
    )


def solution(mesh):
    return jax.shard_map(
        per_device,
        mesh=mesh,
        in_specs=(
            P(("dp", "mp"), None),
            P("dp", None),
            P("dp", None),
            P(None, None, "mp"),
            P(None, "mp"),
            P("mp", None),
            P(None, "mp"),
            P("mp"),
            P("mp", None),
            P(),
            P(),
            P(),
            P(None, "mp"),
            P(),
            P(None, None, "mp"),
            P(None, "mp"),
            P("mp", None),
            P(None, "mp"),
            P("mp"),
            P("mp", None),
            P(),
            P(),
            P(),
            P(("dp", "mp"), None),
        ),
        out_specs=(
            P(("dp", "mp"), None),
            P(("dp", "mp"), None),
            P(None, None, "mp"),
            P(None, "mp"),
            P("mp", None),
            P(None, "mp"),
            P("mp"),
            P("mp", None),
            P(),
            P(),
            P(),
            P(None, "mp"),
            P(),
            P(None, None, "mp"),
            P(None, "mp"),
            P("mp", None),
            P(None, "mp"),
            P("mp"),
            P("mp", None),
            P(),
            P(),
            P(),
        ),
        check_vma=False,
    )
```

```python
import functools
import math

import jax
import jax.numpy as jnp
from jax import lax
from jax.experimental import pallas as pl
from jax.experimental.pallas import tpu as pltpu
from jax.sharding import PartitionSpec as P

HEADS = 16
DHEADS = 16
norm_eps = 1e-06
f32 = jnp.float32
bf16 = jnp.bfloat16
MIB = 1 << 20
VMEM = pl.BlockSpec(memory_space=pltpu.VMEM)
SMEM = pl.BlockSpec(memory_space=pltpu.SMEM)
COST = pl.CostEstimate(flops=10**10, bytes_accessed=10**8, transcendentals=0)


def shaped(dims, kind):
    return jax.ShapeDtypeStruct(dims, kind)


def kept(shape):
    return pltpu.HBM(shape.shape, shape.dtype)


def in_hbm(value):
    return pltpu.with_memory_space_constraint(value, pltpu.HBM)


class Chain:
    token = jax.ShapeDtypeStruct((8, 128), jnp.float32)

    def __init__(self):
        self.last = None

    def __call__(self, body, outs, args, smem=0, scratch=(), limit=16, prefetch=None, grid=None, specs=None):
        args, outs = list(args), list(outs)
        extra = self.last is not None
        ins = len(args) + (prefetch is not None)
        many = len(outs)

        def inner(*refs):
            out_refs = refs[ins + extra :]
            out_refs[many][...] = jnp.zeros((8, 128), f32)
            return body(*refs[:ins], *out_refs[:many], *out_refs[many + 1 :])

        if extra:
            args.append(self.last)
        tail = [pl.BlockSpec(memory_space=pl.ANY)] * extra
        params = pltpu.CompilerParams(vmem_limit_bytes=limit * MIB)
        if prefetch is None:
            got = pl.pallas_call(
                inner,
                out_shape=outs + [self.token],
                in_specs=[SMEM] * smem + [VMEM] * (len(args) - smem - extra) + tail,
                out_specs=[VMEM] * (many + 1),
                scratch_shapes=scratch,
                compiler_params=params,
                cost_estimate=COST,
            )(*args)
        else:
            got = pl.pallas_call(
                inner,
                out_shape=outs + [self.token],
                grid_spec=pltpu.PrefetchScalarGridSpec(
                    num_scalar_prefetch=1,
                    grid=grid,
                    in_specs=specs[0] + tail,
                    out_specs=specs[1] + [pl.BlockSpec((8, 128), lambda i, p: (0, 0))],
                ),
                compiler_params=params,
                cost_estimate=COST,
            )(prefetch, *args)
        *got, self.last = got
        return got

    def pin(self, value):
        def body(value_ref, last_ref, out_ref, token_ref):
            token_ref[...] = jnp.zeros((8, 128), f32)

        any_space = pl.BlockSpec(memory_space=pl.ANY)
        got, self.last = pl.pallas_call(
            body,
            out_shape=[shaped(value.shape, value.dtype), self.token],
            in_specs=[any_space, any_space],
            out_specs=[any_space, VMEM],
            input_output_aliases={0: 0},
            compiler_params=pltpu.CompilerParams(vmem_limit_bytes=MIB),
            cost_estimate=COST,
        )(value, self.last)
        return got

    def gap(self):
        self(lambda: None, [], [], limit=1)


def nn(a, b):
    return lax.dot_general(a, b, (((1,), (0,)), ((), ())), preferred_element_type=f32)


def nt(a, b):
    return lax.dot_general(a, b, (((1,), (1,)), ((), ())), preferred_element_type=f32)


def tn(a, b):
    return lax.dot_general(a, b, (((0,), (0,)), ((), ())), preferred_element_type=f32)


def swap(value, axis, mask):
    size = lax.axis_size(axis)
    return lax.ppermute(value, axis, [(i, i ^ mask) for i in range(size)])


def norm_parts(values):
    average = jnp.mean(values, axis=-1, keepdims=True)
    centred = values - average
    variance = jnp.mean(centred * centred, axis=-1, keepdims=True)
    scale = lax.rsqrt(variance + norm_eps)
    return centred * scale, scale


def norm_back(normal, scale, gain, grad):
    wide = grad * gain
    one = jnp.mean(wide, axis=-1, keepdims=True)
    two = jnp.mean(wide * normal, axis=-1, keepdims=True)
    return scale * (wide - one - normal * two)


def gelu_both(v):
    slope = math.sqrt(2.0 / math.pi)
    square = v * v
    t = jnp.tanh(slope * v * (1.0 + 0.044715 * square))
    half = 0.5 * (1.0 + t)
    return v * half, half + 0.5 * slope * v * (1.0 - t * t) * (1.0 + 3.0 * 0.044715 * square)


def sin_cos(x):
    turn = jnp.floor(x * (2.0 / math.pi) + 0.5)
    r = ((x - turn * 1.5703125) - turn * 4.837512969970703125e-4) - turn * 7.54978995489188216e-8
    z = r * r
    s = r + r * z * (-1.6666654611e-1 + z * (8.3321608736e-3 + z * -1.9515295891e-4))
    c = 1.0 - 0.5 * z + z * z * (
        4.166664568298827e-2 + z * (-1.388731625493765e-3 + z * 2.443315711809948e-5)
    )
    quarter = turn.astype(jnp.int32)
    odd = (quarter & 1) != 0
    sine = jnp.where(odd, c, s)
    cosine = jnp.where(odd, s, c)
    sine = jnp.where((quarter & 2) != 0, -sine, sine)
    cosine = jnp.where(((quarter + 1) & 2) != 0, -cosine, cosine)
    return sine, cosine


def head_masks(heads):
    size = 256 // heads
    lane = lax.broadcasted_iota(jnp.int32, (1, 256), 1)
    return [
        jnp.where((lane >= h * size) & (lane < (h + 1) * size), 1.0, 0.0).astype(bf16)
        for h in range(heads)
    ]


def attend(q, k, v, bias, heads, scale, keep):
    size = 256 // heads
    vt = v.astype(f32).T.astype(bf16)
    mixes = []
    for h, mask in enumerate(head_masks(heads)):
        s = nt(k, q * mask) + bias
        top = jnp.max(s, axis=0, keepdims=True)
        p = jnp.exp2((s - top) * (scale * math.log2(math.e)))
        total = jnp.sum(p, axis=0, keepdims=True)
        p = (p * (1.0 / total)).astype(bf16)
        keep(h, p)
        mixes.append(nn(vt[h * size : (h + 1) * size], p))
    return jnp.concatenate(mixes, axis=0).T


def attend_back(q, k, v, gm, probs, heads, scale):
    size = 256 // heads
    kt = k.astype(f32).T.astype(bf16)
    gq, gk, gv = [], 0.0, 0.0
    for h, mask in enumerate(head_masks(heads)):
        gmh = gm * mask
        p = probs(h)
        wide = p.astype(f32)
        t = wide * nt(v, gmh)
        gs = (t - wide * jnp.sum(t, axis=0, keepdims=True)).astype(bf16)
        gk = gk + nn(gs, q * mask)
        gv = gv + nn(p, gmh)
        gq.append(nn(kt[h * size : (h + 1) * size], gs))
    return jnp.concatenate(gq, axis=0).T * scale, gk * scale, gv


def place_of(slot, seg_ref, gsd_ref):
    n = seg_ref.shape[1]
    across = jnp.broadcast_to(seg_ref[pl.ds(slot, 1), :].astype(f32), (n, n))
    earlier = lax.broadcasted_iota(jnp.int32, (n, n), 1) < lax.broadcasted_iota(jnp.int32, (n, n), 0)
    rank = jnp.sum(jnp.where((across == across.T) & earlier, 1.0, 0.0), axis=1, keepdims=True)
    index = jnp.broadcast_to(gsd_ref[pl.ds(slot, 1), :].astype(f32), (n, n)).T[:, :1]
    return rank * (0.5 + 0.25 * index)


def start_body(slot_ref, seg_ref, gsd_ref, tokens_ref, gain_ref, shift_ref, wf_ref, normed_ref, stream_ref):
    place = place_of(slot_ref[0], seg_ref, gsd_ref)
    half = wf_ref.shape[1]
    sine, cosine = sin_cos(place * wf_ref[...])
    stream_ref[:, :half] = tokens_ref[:, :half].astype(f32) + sine
    stream_ref[:, half:] = tokens_ref[:, half:].astype(f32) + cosine
    normal, _ = norm_parts(stream_ref[...])
    normed_ref[...] = (normal * gain_ref[0:1] + shift_ref[0:1]).astype(bf16)


def mask_body(slot_ref, seg_ref, bias_a_ref, bias_b_ref):
    slot = slot_ref[0]
    n = seg_ref.shape[1]
    for j in range(4):
        across = jnp.broadcast_to(seg_ref[pl.ds(slot ^ j, 1), :].astype(f32), (n, n))
        (bias_a_ref, bias_b_ref)[j // 2][j % 2] = jnp.where(across == across.T, 0.0, -1e30)


def stream_body(slot_ref, seg_ref, gsd_ref, tokens_ref, eb_ref, wf_ref, nf_ref, pos_ref, stream_ref):
    place = place_of(slot_ref[0], seg_ref, gsd_ref)
    half = wf_ref.shape[1]
    sine, cosine = sin_cos(place * wf_ref[...])
    stream_ref[:, :half] = tokens_ref[:, :half].astype(f32) + sine
    stream_ref[:, half:] = tokens_ref[:, half:].astype(f32) + cosine
    half = nf_ref.shape[1]
    sine, cosine = sin_cos(place * nf_ref[...])
    pos_ref[:, :half] = sine + eb_ref[:, :half]
    pos_ref[:, half:] = cosine + eb_ref[:, half:]


def attn_body(scale, heads, first, *refs):
    count = (len(refs) - 9) // 2
    xs, rest = refs[:count], refs[count:]
    bias_ref, w_ref, qvb_ref, o_ref, q_ref, k_ref, v_ref, p_ref, mix_ref = rest[:9]
    for r, (x_ref, part_ref) in enumerate(zip(xs, rest[9:])):
        x = x_ref[...]
        q = (nn(x, w_ref[0]) + qvb_ref[0:1]).astype(bf16)
        k = nn(x, w_ref[1]).astype(bf16)
        v = (nn(x, w_ref[2]) + qvb_ref[1:2]).astype(bf16)
        q_ref[r], k_ref[r], v_ref[r] = q, k, v

        def keep(h, p):
            p_ref[r, h] = p

        mix = attend(q, k, v, bias_ref[first + r], heads, scale, keep).astype(bf16)
        mix_ref[r] = mix
        part_ref[...] = nn(mix, o_ref[...]).astype(bf16)


def attn_back_body(scale, heads, *refs):
    count = (len(refs) - 8) // 2
    gs, rest = refs[:count], refs[count:]
    q_ref, k_ref, v_ref, p_ref, w_ref, o_ref, g3_ref, sums_ref = rest[:8]
    total_q, total_v = 0.0, 0.0
    for r, (g_ref, part_ref) in enumerate(zip(gs, rest[8:])):
        gm = nt(g_ref[...], o_ref[...]).astype(bf16)
        gq, gk, gv = attend_back(
            q_ref[r], k_ref[r], v_ref[r], gm, lambda h: p_ref[r, h], heads, scale
        )
        total_q = total_q + jnp.sum(gq, axis=0, keepdims=True)
        total_v = total_v + jnp.sum(gv, axis=0, keepdims=True)
        acc = 0.0
        for c, g in enumerate((gq, gk, gv)):
            low = g.astype(bf16)
            g3_ref[r, :, c * 256 : (c + 1) * 256] = low
            acc = acc + nt(low, w_ref[c])
        part_ref[...] = acc.astype(bf16)
    sums_ref[0:1] = total_q
    sums_ref[1:2] = total_v


def mid_body(stream_ref, p_ref, near_ref, far_ref, ob_ref, gain_ref, shift_ref, mid_ref, normed_ref):
    total = p_ref[...].astype(f32) + near_ref[...].astype(f32) + far_ref[...].astype(f32)
    middle = stream_ref[...] + total + ob_ref[0:1]
    mid_ref[...] = middle
    normal, _ = norm_parts(middle)
    normed_ref[...] = (normal * gain_ref[1:2] + shift_ref[1:2]).astype(bf16)


def mlp_body(*refs):
    count = (len(refs) - 5) // 2
    xs, rest = refs[:count], refs[count:]
    up_ref, ub_ref, down_ref, hid_ref, dg_ref = rest[:5]
    width = up_ref.shape[1]
    for r, (x_ref, part_ref) in enumerate(zip(xs, rest[5:])):
        x = x_ref[...]
        for c in range(0, width, 256):
            cut = slice(c, c + 256)
            hidden, slope = gelu_both(nn(x, up_ref[:, cut]) + ub_ref[:, cut])
            hid_ref[r, :, cut] = hidden.astype(bf16)
            dg_ref[r, :, cut] = slope.astype(bf16)
        hidden = hid_ref[r]
        for c in range(0, down_ref.shape[1], 512):
            cut = slice(c, c + 512)
            part_ref[:, cut] = nn(hidden, down_ref[:, cut]).astype(bf16)


def mlp_back_body(*refs):
    count = (len(refs) - 5) // 2
    gs, rest = refs[:count], refs[count:]
    dg_ref, up_ref, down_ref, gp_ref, sums_ref = rest[:5]
    width = up_ref.shape[1]
    for r, (g_ref, part_ref) in enumerate(zip(gs, rest[5:])):
        g = g_ref[...]
        for c in range(0, width, 256):
            cut = slice(c, c + 256)
            grad = nt(g, down_ref[cut]) * dg_ref[r, :, cut].astype(f32)
            gp_ref[r, :, cut] = grad.astype(bf16)
            total = jnp.sum(grad, axis=0, keepdims=True)
            sums_ref[:, cut] = total if r == 0 else sums_ref[:, cut] + total
        gp = gp_ref[r]
        for c in range(0, up_ref.shape[0], 512):
            cut = slice(c, c + 512)
            part_ref[:, cut] = nt(gp, up_ref[cut]).astype(bf16)


def mlp_end_body(slot_ref, ge_ref, p_ref, near_ref, far_ref, mid_ref, gain_ref, ua_ref, ub_ref, uc_ref, dec_ref,
                 gmid_ref, gm_ref, pack_ref):
    slot = slot_ref[0]
    grad = p_ref[...].astype(f32) + near_ref[...].astype(f32) + far_ref[...].astype(f32)
    normal, scale = norm_parts(mid_ref[...])
    gmid = ge_ref[...] + norm_back(normal, scale, gain_ref[1:2], grad)
    gmid_ref[...] = gmid
    gm_ref[...] = gmid.astype(bf16)
    pack_ref[...] = jnp.zeros(pack_ref.shape, f32)
    pack_ref[0:1] = jnp.sum(gmid, axis=0, keepdims=True)
    pack_ref[1:2] = jnp.sum(grad * normal, axis=0, keepdims=True)
    pack_ref[2:3] = jnp.sum(grad, axis=0, keepdims=True)
    pack_ref[pl.ds(4 + slot, 1), :] = ua_ref[...] + ub_ref[...] + uc_ref[...]
    pack_ref[8:16] = dec_ref[...]


def last_body(slot_ref, gmid_ref, p_ref, near_ref, far_ref, stream_ref, gain_ref, sa_ref, sb_ref, sc_ref, mid_ref,
              gtok_ref, pack_ref):
    slot = slot_ref[0]
    grad = p_ref[...].astype(f32) + near_ref[...].astype(f32) + far_ref[...].astype(f32)
    normal, scale = norm_parts(stream_ref[...])
    gtok_ref[...] = gmid_ref[...] + norm_back(normal, scale, gain_ref[0:1], grad)
    pack_ref[:16] = mid_ref[...]
    pack_ref[16:] = jnp.zeros((8, pack_ref.shape[1]), f32)
    pack_ref[16:17] = jnp.sum(grad * normal, axis=0, keepdims=True)
    pack_ref[17:18] = jnp.sum(grad, axis=0, keepdims=True)
    share = sa_ref.shape[1]
    place = pl.ds(pl.multiple_of(slot * share, share), share)
    pack_ref[18:20, place] = sa_ref[...] + sb_ref[...] + sc_ref[...]


def decoder_body(slot_ref, mid_ref, p_ref, near_ref, far_ref, eob_ref, own_ref, by_ref, fa_ref, fb_ref, na_ref, nb_ref,
                 b0_ref, b1_ref, b2_ref, b3_ref, pos_ref, bias_ref, dob_ref, dgain_ref, dnb_ref, cot_ref,
                 encl_ref, out_ref, x1_ref, x2_ref, hid_ref, mix_ref, gp_ref, gm_ref, g3_ref, gz_ref,
                 gel_ref, ge_ref, sums_ref,
                 wup, wdown, wqkv, wout, wemb, pt, dg, qkv, wide, qvb_ref, upb_ref):
    slot, home = slot_ref[0], slot_ref[1]
    width = cot_ref.shape[1]
    block = width // 4
    heads = DHEADS * 256 // width
    groups = width // 256
    scale = (width // DHEADS) ** -0.5

    def place(j, base=0):
        return pl.ds(pl.multiple_of(base + (slot ^ j) * block, block), block)

    for j, ref in enumerate((b0_ref, b1_ref, b2_ref, b3_ref)):
        for c in range(2):
            qvb_ref[c : c + 1, j * block : (j + 1) * block] = ref[:, c * block : (c + 1) * block]
        upb_ref[:, j * width : (j + 1) * width] = ref[:, 2 * block :]
    piece, thin, tall = width // 8, block // 8, 2 * width // 8
    top = 2 * piece + thin
    step = top + piece + thin
    for j, (low_ref, high_ref) in enumerate(
        ((own_ref, own_ref), (by_ref, by_ref), (fa_ref, fb_ref), (na_ref, nb_ref))
    ):
        cut = slice(j * block, (j + 1) * block)
        for i in range(8):
            ref = (low_ref, high_ref)[i // 4]
            base = (i if j < 2 else i % 4) * step
            chunk = i if j < 2 else home ^ i

            def rows(size):
                return pl.ds(pl.multiple_of(chunk * size, size), size)

            wup[j, rows(piece)] = ref[base : base + piece]
            wdown[j, rows(piece)] = ref[base + piece : base + 2 * piece]
            wout[pl.ds(pl.multiple_of(j * block + chunk * thin, thin), thin)] = (
                ref[base + 2 * piece : base + top]
            )
            for c in range(3):
                wqkv[c, rows(piece), cut] = ref[base + top : base + top + piece, c * block : (c + 1) * block]
            wemb[pl.ds(pl.multiple_of(chunk * tall, tall), piece), cut] = (
                ref[base + top : base + top + piece, 3 * block :]
            )
            for c in range(4):
                wemb[pl.ds(pl.multiple_of(chunk * tall + piece + c * thin, thin), thin), cut] = (
                    ref[base + top + piece : base + step, c * block : (c + 1) * block]
                )
    encoded = mid_ref[...] + eob_ref[1:2]
    encoded = encoded + p_ref[...].astype(f32) + near_ref[...].astype(f32) + far_ref[...].astype(f32)
    encl_ref[...] = encoded.astype(bf16)
    embedded = nn(encl_ref[...], wemb[...])
    for j in range(4):
        wide[:, place(j)] = embedded[:, j * block : (j + 1) * block]
    stream = wide[...] + pos_ref[...]
    normal1, scale1 = norm_parts(stream)
    x1_ref[...] = (normal1 * dgain_ref[0:1] + dnb_ref[0:1]).astype(bf16)
    x1 = x1_ref[...]
    qkv[0] = (nn(x1, wqkv[0]) + qvb_ref[0:1]).astype(bf16)
    qkv[1] = nn(x1, wqkv[1]).astype(bf16)
    qkv[2] = (nn(x1, wqkv[2]) + qvb_ref[1:2]).astype(bf16)
    bias = bias_ref[0]
    for g in range(groups):
        cut = slice(g * 256, (g + 1) * 256)

        def keep(h, p):
            pt[g * heads + h] = p

        mix_ref[:, cut] = attend(
            qkv[0, :, cut], qkv[1, :, cut], qkv[2, :, cut], bias, heads, scale, keep
        ).astype(bf16)
    middle = stream + nn(mix_ref[...], wout[...]) + dob_ref[0:1]
    normal2, scale2 = norm_parts(middle)
    x2_ref[...] = (normal2 * dgain_ref[1:2] + dnb_ref[1:2]).astype(bf16)
    x2 = x2_ref[...]
    result = middle + dob_ref[1:2]
    for j in range(4):
        cut = slice(j * width, (j + 1) * width)
        hidden, slope = gelu_both(nn(x2, wup[j]) + upb_ref[:, cut])
        hid_ref[:, cut] = hidden.astype(bf16)
        dg[:, cut] = slope.astype(bf16)
        result = result + nn(hid_ref[:, cut], wdown[j])
    out_ref[...] = result

    cot = cot_ref[...]
    grad = 0.0
    sums_ref[...] = jnp.zeros(sums_ref.shape, f32)
    for j in range(4):
        cut = slice(j * width, (j + 1) * width)
        pre = nt(cot, wdown[j]) * dg[:, cut].astype(f32)
        gp_ref[:, cut] = pre.astype(bf16)
        block_sum = jnp.sum(pre, axis=0, keepdims=True)
        at = slot ^ j
        sums_ref[pl.ds(6 + (at >> 1), 1), pl.ds(pl.multiple_of((at & 1) * width, width), width)] = (
            block_sum
        )
        grad = grad + nt(gp_ref[:, cut], wup[j])
    cotf = cot.astype(f32)
    gmid = cotf + norm_back(normal2, scale2, dgain_ref[1:2], grad)
    gm_ref[...] = gmid.astype(bf16)
    sums_ref[1:2, :width] = jnp.sum(gmid, axis=0, keepdims=True)
    sums_ref[2:3, :width] = jnp.sum(cotf, axis=0, keepdims=True)
    sums_ref[2:3, width:] = jnp.sum(grad * normal2, axis=0, keepdims=True)
    sums_ref[4:5, :width] = jnp.sum(grad, axis=0, keepdims=True)
    gmix = nt(gm_ref[...], wout[...]).astype(bf16)
    grad = 0.0
    for g in range(groups):
        cut = slice(g * 256, (g + 1) * 256)
        three = attend_back(
            qkv[0, :, cut], qkv[1, :, cut], qkv[2, :, cut], gmix[:, cut],
            lambda h: pt[g * heads + h], heads, scale,
        )
        for c, part in enumerate(three):
            begin = c * width + g * 256
            low = part.astype(bf16)
            g3_ref[:, begin : begin + 256] = low
            grad = grad + nt(low, wqkv[c, :, cut])
        for c, row, base in ((0, 4, width), (2, 5, width)):
            total = jnp.sum(three[c], axis=0, keepdims=True)
            for i in range(256 // block):
                sums_ref[row : row + 1, place(g * (256 // block) + i, base)] = (
                    total[:, i * block : (i + 1) * block]
                )
    gstream = gmid + norm_back(normal1, scale1, dgain_ref[0:1], grad)
    sums_ref[3:4, width:] = jnp.sum(gstream, axis=0, keepdims=True)
    sums_ref[1:2, width:] = jnp.sum(grad * normal1, axis=0, keepdims=True)
    sums_ref[3:4, :width] = jnp.sum(grad, axis=0, keepdims=True)
    wide[...] = gstream
    for j in range(4):
        gz_ref[:, j * block : (j + 1) * block] = wide[:, place(j)].astype(bf16)
    ge = nt(gz_ref[...], wemb[...])
    ge_ref[...] = ge
    gel_ref[...] = ge.astype(bf16)
    sums_ref[0:1] = jnp.sum(ge, axis=0, keepdims=True)


def decoder_weights_body(x1_ref, x2_ref, hid_ref, mix_ref, gp_ref, gm_ref, g3_ref, gz_ref, encl_ref, cot_ref,
                         sent_ref, kept_ref):
    width = cot_ref.shape[1]
    block = width // 4
    cot, gm, x2 = cot_ref[...], gm_ref[...], x2_ref[...]
    piece, thin = width // 8, block // 8
    tall = encl_ref.shape[1] // 8
    top = 2 * piece + thin
    step = top + piece + thin

    def to(j):
        return sent_ref if j % 2 else kept_ref

    for j in (1, 3, 0, 2):
        w = to(j)
        i = j // 2
        cut = slice(j * width, (j + 1) * width)
        up = tn(x2, gp_ref[:, cut]).astype(bf16)
        down = tn(hid_ref[:, cut], cot).astype(bf16)
        out = tn(mix_ref[:, j * block : (j + 1) * block], gm).astype(bf16)
        for c in range(8):
            w[i, c * step : c * step + piece] = up[c * piece : (c + 1) * piece]
            w[i, c * step + piece : c * step + 2 * piece] = down[c * piece : (c + 1) * piece]
            w[i, c * step + 2 * piece : c * step + top] = out[c * thin : (c + 1) * thin]
    x1 = x1_ref[...]
    for k in range(3):
        full = tn(x1, g3_ref[:, k * width : (k + 1) * width]).astype(bf16)
        for j in range(4):
            for c in range(8):
                to(j)[j // 2, c * step + top : c * step + top + piece, k * block : (k + 1) * block] = (
                    full[c * piece : (c + 1) * piece, j * block : (j + 1) * block]
                )
    full = tn(encl_ref[...], gz_ref[...]).astype(bf16)
    for j in range(4):
        cut = slice(j * block, (j + 1) * block)
        for c in range(8):
            base = c * tall
            to(j)[j // 2, c * step + top : c * step + top + piece, 3 * block :] = full[base : base + piece, cut]
            base = base + piece
            for k in range(4):
                to(j)[j // 2, c * step + top + piece : (c + 1) * step, k * block : (k + 1) * block] = (
                    full[base + k * thin : base + (k + 1) * thin, cut]
                )


def pack_body(pick_ref, up_ref, down_ref, out_ref, qkv_ref, emb_ref, chunk_ref):
    piece, thin, block = up_ref.shape[0], out_ref.shape[0], emb_ref.shape[1]
    chunk_ref[:piece] = up_ref[...]
    chunk_ref[piece : 2 * piece] = down_ref[...]
    top = 2 * piece + thin
    chunk_ref[2 * piece : top] = out_ref[...]
    for c in range(3):
        chunk_ref[top : top + piece, c * block : (c + 1) * block] = qkv_ref[c]
    chunk_ref[top : top + piece, 3 * block :] = emb_ref[:piece]
    for c in range(4):
        base = piece + c * thin
        chunk_ref[top + piece :, c * block : (c + 1) * block] = emb_ref[base : base + thin]


def join_body(a_ref, b_ref, out_ref):
    rows = a_ref.shape[0]
    out_ref[:rows] = a_ref[...]
    out_ref[rows:] = b_ref[...]


def add_body(a_ref, b_ref, out_ref):
    out_ref[...] = (a_ref[...].astype(f32) + b_ref[...].astype(f32)).astype(out_ref.dtype)


def add_all_body(*refs):
    total = refs[0][...]
    for ref in refs[1:-1]:
        total = total + ref[...]
    refs[-1][...] = total


def last_sums_body(slot_ref, *refs):
    terms, outs, total_ref = refs[:-12], refs[-12:-1], refs[-1]
    total = terms[0][...]
    for ref in terms[1:]:
        total = total + ref[...]
    total_ref[...] = total
    slot = slot_ref[0]
    e_qv, e_upb, e_ob, e_gain, e_nb, d_emb, d_qv, d_upb, d_ob, d_gain, d_nb = outs
    share, thin, width = e_qv.shape[1], d_qv.shape[1], d_emb.shape[1]
    e_qv[...] = total_ref[18:20, pl.ds(pl.multiple_of(slot * share, share), share)]
    e_upb[...] = total_ref[pl.ds(4 + slot, 1), :]
    e_ob[0:1] = total_ref[0:1]
    e_ob[1:2] = total_ref[8:9]
    e_gain[0:1] = total_ref[16:17]
    e_gain[1:2] = total_ref[1:2]
    e_nb[0:1] = total_ref[17:18]
    e_nb[1:2] = total_ref[2:3]
    d_ob[...] = total_ref[9:11, :width]
    d_gain[...] = total_ref[9:11, width:]
    d_nb[...] = total_ref[11:13, :width]
    d_emb[...] = total_ref[11:12, width:]
    d_qv[...] = total_ref[12:14, pl.ds(pl.multiple_of(width + slot * thin, thin), thin)]
    d_upb[...] = total_ref[pl.ds(14 + (slot >> 1), 1), pl.ds(pl.multiple_of((slot & 1) * width, width), width)]


def halve_body(bit_ref, *refs):
    ins, (send_ref, keep_ref) = refs[:-2], refs[-2:]
    half = send_ref.shape[0]
    bit = bit_ref[0]
    for ref, which in ((send_ref, 1 - bit), (keep_ref, bit)):
        rows = pl.ds(pl.multiple_of(which * half, half), half)
        total = ins[0][rows].astype(f32)
        for other in ins[1:]:
            total = total + other[rows].astype(f32)
        ref[...] = total.astype(bf16)


def far_body(bit_ref, kept_ref, near_ref, out_ref):
    half = out_ref.shape[0]
    rows = pl.ds(pl.multiple_of(bit_ref[0] * half, half), half)
    out_ref[...] = (kept_ref[1, rows].astype(f32) + near_ref[1, rows].astype(f32)).astype(bf16)


def there_body(bit_ref, kept_ref, near_ref, far_ref, send_ref):
    half = send_ref.shape[0]
    rows = pl.ds(pl.multiple_of((1 - bit_ref[0]) * half, half), half)
    total = kept_ref[0, rows].astype(f32) + near_ref[0, rows].astype(f32)
    send_ref[...] = (total + far_ref[...].astype(f32)).astype(bf16)


def mine_body(bit_ref, kept_ref, near_ref, far_ref, got_ref, send_ref, keep_ref):
    quarter = send_ref.shape[0]
    base = bit_ref[0] * 2 * quarter
    for ref, which in ((send_ref, 1 - bit_ref[1]), (keep_ref, bit_ref[1])):
        rows = pl.ds(pl.multiple_of(base + which * quarter, quarter), quarter)
        inner = pl.ds(pl.multiple_of(which * quarter, quarter), quarter)
        total = kept_ref[0, rows].astype(f32) + near_ref[0, rows].astype(f32)
        ref[...] = (total + far_ref[inner].astype(f32) + got_ref[inner].astype(f32)).astype(bf16)


def piece_of(refs, j):
    for ref in refs:
        if len(ref.shape) == 2:
            if j == 0:
                return ref[...]
            j -= 1
        elif j < ref.shape[0]:
            return ref[j]
        else:
            j -= ref.shape[0]


def tile_sum(xs, gs, more):
    acc = 0.0
    for j in range(4):
        acc = acc + tn(piece_of(xs, j), piece_of(gs, j))
    if not more:
        return [(slice(None), slice(None), acc)]
    rows, cols = acc.shape
    parts = [(slice(None), slice(0, cols), acc)]
    half, quarter = rows // 2, rows // 8
    wide = more[0].shape[1] // 4
    for c in range(2):
        for k in range(4):
            parts.append((
                slice(c * half + k * quarter, c * half + (k + 1) * quarter),
                slice(cols, cols + wide),
                more[0][c * quarter : (c + 1) * quarter, k * wide : (k + 1) * wide].astype(f32),
            ))
    return parts


def first_half_body(nx, ng, nm, pick_ref, *refs):
    xs, gs, more = refs[:nx], refs[nx : nx + ng], refs[nx + ng : nx + ng + nm]
    out_ref = refs[nx + ng + nm]
    for rows, cols, value in tile_sum(xs, gs, more):
        out_ref[rows, cols] = value.astype(bf16)


def other_half_body(nx, ng, nm, pick_ref, *refs):
    xs, gs, more = refs[:nx], refs[nx : nx + ng], refs[nx + ng : nx + ng + nm]
    add_ref, send_ref, keep_ref = refs[nx + ng + nm :]
    parts = [
        (rows, cols, (value + add_ref[rows, cols].astype(f32)).astype(bf16))
        for rows, cols, value in tile_sum(xs, gs, more)
    ]

    def put(ref):
        for rows, cols, value in parts:
            ref[rows, cols] = value

    @pl.when(pl.program_id(0) == 0)
    def _():
        put(send_ref)

    @pl.when(pl.program_id(0) == 1)
    def _():
        put(keep_ref)


def weight_half(chain, xs, gs, more, cut, pick, add=None):
    tile = xs[0].shape[-1] // 4
    begin, cols = cut
    out_cols = cols + sum(m.shape[1] // 4 for m in more)

    def column(shape):
        lead = shape[:-1]
        return pl.BlockSpec(lead + (tile,), lambda i, p: (0,) * len(lead) + (p[i],))

    def whole(shape):
        lead = shape[:-1]
        return pl.BlockSpec(lead + (cols,), lambda i, p: (0,) * len(lead) + (begin // cols,))

    in_specs = [column(x.shape) for x in xs] + [whole(g.shape) for g in gs]
    in_specs += [pl.BlockSpec((tile // 4, m.shape[1]), lambda i, p: (p[i], 0)) for m in more]
    args = list(xs) + list(gs) + list(more)
    counts = len(xs), len(gs), len(more)
    if add is None:
        body = functools.partial(first_half_body, *counts)
        outs = [shaped((2 * tile, out_cols), bf16)]
        out_specs = [pl.BlockSpec((tile, out_cols), lambda i, p: (i, 0))]
    else:
        body = functools.partial(other_half_body, *counts)
        in_specs.append(pl.BlockSpec((tile, out_cols), lambda i, p: (p[2 + i], 0)))
        args.append(add)
        outs = [shaped((tile, out_cols), bf16)] * 2
        out_specs = [pl.BlockSpec((tile, out_cols), lambda i, p: (0, 0))] * 2
    return chain(body, outs, args, prefetch=pick, grid=(2,), specs=(in_specs, out_specs), limit=20)


def spread_body(writes, place_ref, *refs):
    sums = max(write[0] for write in writes) + 1
    out_refs = refs[2 * sums :]
    for i in range(8):
        for source, which, lead, first, every, row, rows, col, cols, at_col in writes:
            ref = refs[2 * source + i // 4]
            base = i % 4 * (ref.shape[0] // 4)
            at = place_ref[source] ^ i
            value = ref[base + row : base + row + rows, col : col + cols].astype(f32)
            to = pl.ds(pl.multiple_of(at * every + first, rows), rows)
            if lead is None:
                out_refs[which][to, at_col : at_col + cols] = value
            else:
                out_refs[which][lead, to] = value


def out_weight_body(*refs):
    mixes, gs, out_ref = refs[:3], refs[3:7], refs[7]
    acc = 0.0
    for j in range(4):
        acc = acc + tn(piece_of(mixes, j), piece_of(gs, j))
    out_ref[...] = acc.astype(bf16)


class Sum:
    def __init__(self, chain, masks=(1, 2, 4)):
        self.chain, self.masks = chain, masks
        self.size = lax.axis_size("dp")
        me = lax.axis_index("dp").astype(jnp.int32)
        b1, b2, b3 = self.bits = [jnp.where((me & mask) != 0, 1, 0).astype(jnp.int32) for mask in masks]
        self.place = 4 * b1 + 2 * b2 + b3 if self.size == 8 else jnp.int32(0)
        self.there = jnp.stack([2 * (1 - b1), 2 * (1 - b1) + 1])
        self.mine = jnp.stack([2 * b1 + 1 - b2, 2 * b1 + b2, 1 - b2, b2])
        steps = [self.second, self.third, self.fourth, self.fifth, self.sixth]
        self.steps = iter(steps if self.size == 8 else [])

    def step(self):
        for todo in self.steps:
            todo()
            return

    def product(self, xs, gs, more=(), cut=None):
        self.terms = (xs, gs, more, cut or (0, gs[0].shape[-1]))
        if self.size != 8:
            first = weight_half(self.chain, *self.terms, jnp.array([0, 1], jnp.int32))[0]
            other = weight_half(self.chain, *self.terms, jnp.array([2, 3], jnp.int32))[0]
            return self.general(jnp.concatenate([first, other], axis=0))
        self.got = swap(weight_half(self.chain, *self.terms, self.there)[0], "dp", self.masks[0])

    def shares(self, kept, near, there):
        self.terms = None
        self.held = (kept, near, there)
        if self.size == 8:
            half = shaped(there.shape, bf16)
            send = self.chain(there_body, [half], (self.bits[0].reshape(1), kept, near, there), smem=1)[0]
            self.got = swap(send, "dp", self.masks[0])

    def other(self, mine):
        kept, near, there = self.held
        self.held = (kept, near, mine)
        if self.size != 8:
            total = kept[0].astype(f32) + near[0].astype(f32)
            total = total + jnp.concatenate([mine, there], axis=0).astype(f32)
            self.general(total.astype(bf16))

    def second(self):
        if self.terms is None:
            rows, cols = self.got.shape
            half = shaped((rows // 2, cols), bf16)
            send, self.keep = self.chain(
                mine_body, [half, half], (jnp.stack(self.bits[:2]), *self.held, self.got), smem=1
            )
        else:
            send, self.keep = weight_half(self.chain, *self.terms, self.mine, self.got)
        self.got = swap(send, "dp", self.masks[1])

    def third(self):
        rows, cols = self.keep.shape
        half = shaped((rows // 2, cols), bf16)
        send, self.keep = self.chain(
            halve_body, [half, half], (self.bits[2].reshape(1), self.keep, self.got), smem=1
        )
        self.got = swap(send, "dp", self.masks[2])

    def fourth(self):
        self.keep = self.chain(add_body, [shaped(self.keep.shape, bf16)], (self.keep, self.got))[0]
        self.got = swap(self.keep, "dp", self.masks[2])

    def join(self):
        rows, cols = self.keep.shape
        self.keep = self.chain(join_body, [shaped((2 * rows, cols), bf16)], (self.keep, self.got))[0]

    def fifth(self):
        self.join()
        self.got = swap(self.keep, "dp", self.masks[1])

    def sixth(self):
        self.join()
        self.got = swap(self.keep, "dp", self.masks[0])

    def general(self, held):
        me = lax.axis_index("dp")
        bits = [1 << i for i in range(self.size.bit_length() - 1)]
        for bit in bits:
            mine = (me & bit) != 0
            half = held.shape[0] // 2
            other = lax.dynamic_slice_in_dim(held, jnp.where(mine, 0, half), half, 0)
            own = lax.dynamic_slice_in_dim(held, jnp.where(mine, half, 0), half, 0)
            held = (own.astype(f32) + swap(other, "dp", bit).astype(f32)).astype(bf16)
        for bit in reversed(bits):
            mine = (me & bit) != 0
            other = swap(held, "dp", bit)
            held = jnp.where(
                mine,
                jnp.concatenate([other, held], axis=0),
                jnp.concatenate([held, other], axis=0),
            )
        half = held.shape[0] // 2
        self.keep, self.got = held[:half], held[half:]


def per_device(
    tokens, segment_ids, gsd_index, enc_qkv, enc_qv_bias, enc_out_proj, enc_up, enc_up_bias,
    enc_down, enc_out_bias, enc_gain, enc_norm_bias, embed_weight, embed_bias, dec_qkv,
    dec_qv_bias, dec_out_proj, dec_up, dec_up_bias, dec_down, dec_out_bias, dec_gain,
    dec_norm_bias, cotangent,
):
    n, width = tokens.shape
    rows, length = segment_ids.shape
    assert rows == 4 and n == length == 256 and lax.axis_size("mp") == 4
    share, ff = enc_qkv.shape[2], enc_up.shape[1]
    dwidth, dff = cotangent.shape[1], dec_up.shape[1] * 4
    dshare = dwidth // 4
    heads = share // (width // HEADS)
    scale = (width // HEADS) ** -0.5
    slot = lax.axis_index("mp").astype(jnp.int32)
    at = slot.reshape(1)
    chain = Chain()
    dec = Sum(chain)
    home = dec.place

    def low(*dims):
        return shaped(dims, bf16)

    def full(*dims):
        return shaped(dims, f32)

    def waves(size):
        half = size // 2
        return jnp.power(10000.0, -jnp.arange(half, dtype=f32) / half).reshape(1, half)

    def near(value):
        return swap(value, "mp", 1)

    def far(value):
        return swap(value, "mp", 2)

    pack_rows = 3 * dwidth + 2 * dshare
    decoder_weights = [in_hbm(w) for w in (dec_up, dec_down, dec_out_proj, dec_qkv, embed_weight)]

    def pack(pick, steps):
        def block(shape):
            if len(shape) == 3:
                return pl.BlockSpec((shape[0], shape[1] // 8, shape[2]), lambda i, p: (0, p[i], 0))
            return pl.BlockSpec((shape[0] // 8, shape[1]), lambda i, p: (p[i], 0))

        rows = pack_rows // 8
        return chain(
            pack_body,
            [low(steps * rows, dwidth)],
            decoder_weights,
            prefetch=pick,
            grid=(steps,),
            specs=([block(w.shape) for w in decoder_weights], [pl.BlockSpec((rows, dwidth), lambda i, p: (i, 0))]),
        )[0]

    split = dec.size == 8
    got = far(pack(home.reshape(1), 1)) if split else None
    normed = chain(
        start_body,
        [low(n, width)],
        (at, in_hbm(segment_ids), in_hbm(gsd_index), in_hbm(tokens), in_hbm(enc_gain), in_hbm(enc_norm_bias), waves(width)),
        smem=1,
        scratch=[pltpu.VMEM((n, width), f32)],
    )[0]
    x = [normed, near(normed), far(normed)]
    bias_a, bias_b = chain(mask_body, [kept(full(2, n, n)), kept(full(2, n, n))], (at, in_hbm(segment_ids)), smem=1)

    def attention(bias, first, *blocks):
        count = len(blocks)
        return chain(
            functools.partial(attn_body, scale, heads, first),
            [kept(low(count, n, share))] * 3
            + [kept(low(count, heads, n, n)), kept(low(count, n, share))]
            + [low(n, width)] * count,
            (*blocks, bias, enc_qkv, enc_qv_bias, enc_out_proj),
        )

    def add(a, b):
        return chain(add_body, [shaped(a.shape, a.dtype)], (a, b))[0]

    def join(a, b):
        return chain(join_body, [low(a.shape[0] + b.shape[0], a.shape[1])], (a, b))[0]

    def both(blocks):
        blocks[2] = chain.pin(blocks[2])
        blocks.append(near(blocks[2]))

    *saved_a, mixa, part0, part1 = attention(bias_a, 0, x[0], x[1])
    part1 = near(part1)
    vector = jnp.concatenate([dec_qv_bias.reshape(-1), dec_up_bias]).reshape(1, -1)
    vectors = [vector, chain.pin(near(vector)), far(vector)]
    both(vectors)
    part1 = chain.pin(part1)
    if split:
        got = chain.pin(got)
        more = swap(got, "dp", 4)
    both(x)
    vectors[3] = chain.pin(vectors[3])
    chain.gap()
    *saved_d, mixd, part3 = attention(bias_b, 1, x[3])
    part3 = near(part3)
    *saved_c, mixc, part2 = attention(bias_b, 0, x[2])
    part2 = far(add(part2, part3))
    packed = pack(jnp.arange(8, dtype=jnp.int32), 8)
    packed_near = near(packed)
    pos, stream = chain(
        stream_body,
        [kept(full(n, dwidth)), full(n, width)],
        (at, in_hbm(segment_ids), in_hbm(gsd_index), in_hbm(tokens), in_hbm(embed_bias.reshape(1, -1)), waves(width), waves(dwidth)),
        smem=1,
    )
    if split:
        got = join(got, more)
        more = swap(got, "dp", 2)
    else:
        got = far(packed)
    middle, normed2 = chain(
        mid_body,
        [kept(full(n, width)), low(n, width)],
        (stream, part0, part1, part2, enc_out_bias, enc_gain, enc_norm_bias),
    )
    y = [normed2, near(normed2), far(normed2)]
    packed_near = chain.pin(packed_near)
    if split:
        got = join(got, more)
        more = swap(got, "dp", 1)
    else:
        more = got[pack_rows // 2 :]
        got = got[: pack_rows // 2]

    def feed(*blocks):
        count = len(blocks)
        return chain(
            mlp_body,
            [kept(low(count, n, ff))] * 2 + [low(n, width)] * count,
            (*blocks, enc_up, enc_up_bias.reshape(1, -1), enc_down),
        )

    hida, dga, part0, part1 = feed(y[0], y[1])
    part1 = near(part1)
    far_weights = [got, more]
    near_weights = [near(got)]
    both(y)
    part1 = chain.pin(part1)
    near_weights[0] = chain.pin(near_weights[0])
    hidd, dgd, part3 = feed(y[3])
    part3 = near(part3)
    hidc, dgc, part2 = feed(y[2])
    part2 = far(add(part2, part3))
    far_weights[1] = chain.pin(more)
    near_weights.append(near(far_weights[1]))
    part2 = chain.pin(part2)

    (enc_low, output, x1, x2, hid, mix, gp, gm, g3, gz, ge_low, ge, dec_sums) = chain(
        decoder_body,
        [kept(o) for o in (low(n, width), full(n, dwidth), low(n, dwidth), low(n, dwidth), low(n, dff),
                           low(n, dwidth), low(n, dff), low(n, dwidth), low(n, 3 * dwidth), low(n, dwidth))]
        + [low(n, width), kept(full(n, width)), kept(full(8, width))],
        (jnp.stack([slot, home]), middle, part0, part1, part2, enc_out_bias, packed, packed_near,
         *far_weights, *near_weights, *vectors, pos, bias_a, dec_out_bias, dec_gain,
         dec_norm_bias, cotangent),
        smem=1,
        scratch=[
            pltpu.VMEM((4, dwidth, dwidth), bf16), pltpu.VMEM((4, dwidth, dwidth), bf16),
            pltpu.VMEM((3, dwidth, dwidth), bf16), pltpu.VMEM((dwidth, dwidth), bf16),
            pltpu.VMEM((width, dwidth), bf16), pltpu.VMEM((DHEADS, n, n), bf16),
            pltpu.VMEM((n, dff), bf16), pltpu.VMEM((3, n, dwidth), bf16), pltpu.VMEM((n, dwidth), f32),
            pltpu.VMEM((2, dwidth), f32), pltpu.VMEM((1, dff), f32),
        ],
        limit=40,
    )
    g = [ge_low, near(ge_low), far(ge_low)]

    def feed_back(slope, *blocks):
        count = len(blocks)
        return chain(
            mlp_back_body,
            [kept(low(count, n, ff)), kept(full(1, ff))] + [low(n, width)] * count,
            (*blocks, slope, enc_up, enc_down),
        )

    def attention_back(saved, *blocks):
        count = len(blocks)
        return chain(
            functools.partial(attn_back_body, scale, heads),
            [kept(low(count, n, 3 * share)), kept(full(2, share))] + [low(n, width)] * count,
            (*blocks, *saved, enc_qkv, enc_out_proj),
        )

    def far_share(bit):
        return far(chain(far_body, [low(pack_rows // 2, dwidth)], (bit.reshape(1), kept_share, sent), smem=1)[0])

    def hbm(*values):
        return [in_hbm(v) for v in values]

    down, up, attn = Sum(chain), Sum(chain), Sum(chain)

    def finish(sums, outs, writes):
        return chain(
            functools.partial(spread_body, writes),
            [kept(full(*dims)) for dims in outs],
            (jnp.stack([f.place for f in sums]), *[v for f in sums for v in (f.keep, f.got)]),
            smem=1,
            limit=24,
        )

    chain.gap()
    gpa, upa, part0, part1 = feed_back(dga, g[0], g[1])
    part1 = near(part1)
    sent, kept_share = chain(
        decoder_weights_body,
        [low(2, pack_rows, dwidth), kept(low(2, pack_rows, dwidth))],
        (x1, x2, hid, mix, gp, gm, g3, gz, enc_low, cotangent),
        limit=24,
    )
    sent = near(sent)
    part1 = chain.pin(part1)
    both(g)
    gpc, upc, part2 = feed_back(dgc, g[2])
    gpd, upd, part3 = feed_back(dgd, g[3])
    part3 = near(part3)
    down.product(hbm(hida, hidc, hidd), g)
    part2 = far(add(part2, part3))
    chain.gap()
    grad_middle, gm_low, sums_mid = chain(
        mlp_end_body,
        [kept(full(n, width)), low(n, width), kept(full(16, width))],
        (at, ge, part0, part1, part2, middle, enc_gain, upa, upc, upd, dec_sums),
        smem=1,
    )
    m = [gm_low, near(gm_low), far(gm_low)]
    up.product(hbm(*y), hbm(gpa, gpc, gpd))
    g3a, sa, part0, part1 = attention_back(saved_a, m[0], m[1])
    part1 = near(part1)
    down.step()
    part1 = chain.pin(part1)
    there = far_share(1 - dec.bits[0])
    both(m)
    g3c, sc, part2 = attention_back(saved_c, m[2])
    out_full = chain(out_weight_body, [low(share, width)], (mixa, mixc, mixd, *m))[0]
    g3d, sd, part3 = attention_back(saved_d, m[3])
    part3 = near(part3)
    attn.product(hbm(*x), hbm(g3a, g3c, g3d), [out_full])
    part2 = far(add(part2, part3))
    down.step()
    up.step()
    dec.shares(kept_share, sent, there)
    down.step()
    grad_tokens, sums = chain(
        last_body,
        [kept(full(n, width)), full(24, width)],
        (at, grad_middle, part0, part1, part2, stream, enc_gain, sa, sc, sd, sums_mid),
        smem=1,
    )
    dec.other(far_share(dec.bits[0]))
    up.step()
    attn.step()
    down.step()
    up.step()
    attn.step()
    dec.step()
    hops = [("mp", 1), ("mp", 2)] + [("dp", 1 << i) for i in range(dec.size.bit_length() - 1)]
    hops = iter(hops)

    def hop(total, got=None):
        if got is not None:
            total = add(total, got)
        for axis, mask in hops:
            return total, swap(total, axis, mask)
        return total, None

    small = hop(sums)
    down.step()
    up.step()
    small = hop(*small)
    attn.step()
    dec.step()
    small = hop(*small)
    up.step()
    attn.step()
    dec.step()
    small = hop(*small)
    e_down = finish((down,), [(ff, width)], [(0, 0, None, 0, ff // 8, 0, ff // 8, 0, width, 0)])[0]
    attn.step()
    dec.step()
    small = hop(*small)
    e_up = finish((up,), [(width, ff)], [(0, 0, None, 0, width // 8, 0, width // 8, 0, ff, 0)])[0]
    while small[1] is not None:
        sums = small
        small = hop(*small)
    vectors = chain(
        last_sums_body,
        [full(2, share), full(1, ff), full(2, width), full(2, width), full(2, width), full(1, dwidth),
         full(2, dshare), full(1, dff // 4), full(2, dwidth), full(2, dwidth), full(2, dwidth)],
        (at, *sums),
        smem=1,
        scratch=[pltpu.VMEM((24, width), f32)],
    )
    dec.step()
    rows, fold = width // 8, share // 8
    e_qkv, e_out = finish(
        (attn,),
        [(3, width, share), (share, width)],
        [(0, 0, c, 0, rows, 0, rows, c * share, share, 0) for c in range(3)]
        + [(0, 1, None, 0, fold, k * fold, fold, 3 * share, width // 4, k * (width // 4)) for k in range(4)],
    )
    part, thin, tall = dwidth // 8, dshare // 8, width // 8
    top = 2 * part + thin
    d_up, d_down, d_out, d_qkv, e_embed = finish(
        (dec,),
        [(dwidth, dwidth), (dwidth, dwidth), (dshare, dwidth), (3, dwidth, dshare), (width, dshare)],
        [
            (0, 0, None, 0, part, 0, part, 0, dwidth, 0),
            (0, 1, None, 0, part, part, part, 0, dwidth, 0),
            (0, 2, None, 0, thin, 2 * part, thin, 0, dwidth, 0),
        ]
        + [(0, 3, c, 0, part, top, part, c * dshare, dshare, 0) for c in range(3)]
        + [(0, 4, None, 0, tall, top, part, 3 * dshare, dshare, 0)]
        + [(0, 4, None, part + k * thin, tall, top + part, thin, k * dshare, dshare, 0) for k in range(4)],
    )
    e_qv, e_upb, e_ob, e_gain, e_nb, d_emb, d_qv, d_upb, d_ob, d_gain, d_nb = vectors

    return (
        output,
        grad_tokens,
        e_qkv,
        e_qv,
        e_out,
        e_up,
        e_upb.reshape(-1),
        e_down,
        e_ob,
        e_gain,
        e_nb,
        e_embed,
        d_emb.reshape(-1),
        d_qkv,
        d_qv,
        d_out,
        d_up,
        d_upb.reshape(-1),
        d_down,
        d_ob,
        d_gain,
        d_nb,
    )


def solution(mesh):
    return jax.shard_map(
        per_device,
        mesh=mesh,
        in_specs=(
            P(("dp", "mp"), None),
            P("dp", None),
            P("dp", None),
            P(None, None, "mp"),
            P(None, "mp"),
            P("mp", None),
            P(None, "mp"),
            P("mp"),
            P("mp", None),
            P(),
            P(),
            P(),
            P(None, "mp"),
            P(),
            P(None, None, "mp"),
            P(None, "mp"),
            P("mp", None),
            P(None, "mp"),
            P("mp"),
            P("mp", None),
            P(),
            P(),
            P(),
            P(("dp", "mp"), None),
        ),
        out_specs=(
            P(("dp", "mp"), None),
            P(("dp", "mp"), None),
            P(None, None, "mp"),
            P(None, "mp"),
            P("mp", None),
            P(None, "mp"),
            P("mp"),
            P("mp", None),
            P(),
            P(),
            P(),
            P(None, "mp"),
            P(),
            P(None, None, "mp"),
            P(None, "mp"),
            P("mp", None),
            P(None, "mp"),
            P("mp"),
            P("mp", None),
            P(),
            P(),
            P(),
        ),
        check_vma=False,
    )
```

```python
import functools
import math

import jax
import jax.numpy as jnp
from jax import lax
from jax.experimental import pallas as pl
from jax.experimental.pallas import tpu as pltpu
from jax.sharding import PartitionSpec as P

HEADS = 16
DHEADS = 16
norm_eps = 1e-06
f32 = jnp.float32
bf16 = jnp.bfloat16
MIB = 1 << 20
VMEM = pl.BlockSpec(memory_space=pltpu.VMEM)
SMEM = pl.BlockSpec(memory_space=pltpu.SMEM)
COST = pl.CostEstimate(flops=10**10, bytes_accessed=10**8, transcendentals=0)


def shaped(dims, kind):
    return jax.ShapeDtypeStruct(dims, kind)


def kept(shape):
    return pltpu.HBM(shape.shape, shape.dtype)


def in_hbm(value):
    return pltpu.with_memory_space_constraint(value, pltpu.HBM)


class Chain:
    token = jax.ShapeDtypeStruct((8, 128), jnp.float32)

    def __init__(self):
        self.last = None

    def __call__(self, body, outs, args, smem=0, scratch=(), limit=16, prefetch=None, grid=None, specs=None):
        args, outs = list(args), list(outs)
        extra = self.last is not None
        ins = len(args) + (prefetch is not None)
        many = len(outs)

        def inner(*refs):
            out_refs = refs[ins + extra :]
            out_refs[many][...] = jnp.zeros((8, 128), f32)
            return body(*refs[:ins], *out_refs[:many], *out_refs[many + 1 :])

        if extra:
            args.append(self.last)
        tail = [pl.BlockSpec(memory_space=pl.ANY)] * extra
        params = pltpu.CompilerParams(vmem_limit_bytes=limit * MIB)
        if prefetch is None:
            got = pl.pallas_call(
                inner,
                out_shape=outs + [self.token],
                in_specs=[SMEM] * smem + [VMEM] * (len(args) - smem - extra) + tail,
                out_specs=[VMEM] * (many + 1),
                scratch_shapes=scratch,
                compiler_params=params,
                cost_estimate=COST,
            )(*args)
        else:
            got = pl.pallas_call(
                inner,
                out_shape=outs + [self.token],
                grid_spec=pltpu.PrefetchScalarGridSpec(
                    num_scalar_prefetch=1,
                    grid=grid,
                    in_specs=specs[0] + tail,
                    out_specs=specs[1] + [pl.BlockSpec((8, 128), lambda i, p: (0, 0))],
                ),
                compiler_params=params,
                cost_estimate=COST,
            )(prefetch, *args)
        *got, self.last = got
        return got

    def pin(self, value):
        def body(value_ref, last_ref, out_ref, token_ref):
            token_ref[...] = jnp.zeros((8, 128), f32)

        any_space = pl.BlockSpec(memory_space=pl.ANY)
        got, self.last = pl.pallas_call(
            body,
            out_shape=[shaped(value.shape, value.dtype), self.token],
            in_specs=[any_space, any_space],
            out_specs=[any_space, VMEM],
            input_output_aliases={0: 0},
            compiler_params=pltpu.CompilerParams(vmem_limit_bytes=MIB),
            cost_estimate=COST,
        )(value, self.last)
        return got

    def gap(self):
        self(lambda: None, [], [], limit=1)


def nn(a, b):
    return lax.dot_general(a, b, (((1,), (0,)), ((), ())), preferred_element_type=f32)


def nt(a, b):
    return lax.dot_general(a, b, (((1,), (1,)), ((), ())), preferred_element_type=f32)


def tn(a, b):
    return lax.dot_general(a, b, (((0,), (0,)), ((), ())), preferred_element_type=f32)


def swap(value, axis, mask):
    size = lax.axis_size(axis)
    return lax.ppermute(value, axis, [(i, i ^ mask) for i in range(size)])


def norm_parts(values):
    average = jnp.mean(values, axis=-1, keepdims=True)
    centred = values - average
    variance = jnp.mean(centred * centred, axis=-1, keepdims=True)
    scale = lax.rsqrt(variance + norm_eps)
    return centred * scale, scale


def norm_back(normal, scale, gain, grad):
    wide = grad * gain
    one = jnp.mean(wide, axis=-1, keepdims=True)
    two = jnp.mean(wide * normal, axis=-1, keepdims=True)
    return scale * (wide - one - normal * two)


def gelu_both(v):
    slope = math.sqrt(2.0 / math.pi)
    square = v * v
    t = jnp.tanh(slope * v * (1.0 + 0.044715 * square))
    half = 0.5 * (1.0 + t)
    return v * half, half + 0.5 * slope * v * (1.0 - t * t) * (1.0 + 3.0 * 0.044715 * square)


def sin_cos(x):
    turn = jnp.floor(x * (2.0 / math.pi) + 0.5)
    r = ((x - turn * 1.5703125) - turn * 4.837512969970703125e-4) - turn * 7.54978995489188216e-8
    z = r * r
    s = r + r * z * (-1.6666654611e-1 + z * (8.3321608736e-3 + z * -1.9515295891e-4))
    c = 1.0 - 0.5 * z + z * z * (
        4.166664568298827e-2 + z * (-1.388731625493765e-3 + z * 2.443315711809948e-5)
    )
    quarter = turn.astype(jnp.int32)
    odd = (quarter & 1) != 0
    sine = jnp.where(odd, c, s)
    cosine = jnp.where(odd, s, c)
    sine = jnp.where((quarter & 2) != 0, -sine, sine)
    cosine = jnp.where(((quarter + 1) & 2) != 0, -cosine, cosine)
    return sine, cosine


def head_masks(heads):
    size = 256 // heads
    lane = lax.broadcasted_iota(jnp.int32, (1, 256), 1)
    return [
        jnp.where((lane >= h * size) & (lane < (h + 1) * size), 1.0, 0.0).astype(bf16)
        for h in range(heads)
    ]


def attend(q, k, v, bias, heads, scale, keep):
    size = 256 // heads
    vt = v.astype(f32).T.astype(bf16)
    mixes = []
    for h, mask in enumerate(head_masks(heads)):
        s = nt(k, q * mask) + bias
        top = jnp.max(s, axis=0, keepdims=True)
        p = jnp.exp2((s - top) * (scale * math.log2(math.e)))
        total = jnp.sum(p, axis=0, keepdims=True)
        p = (p * (1.0 / total)).astype(bf16)
        keep(h, p)
        mixes.append(nn(vt[h * size : (h + 1) * size], p))
    return jnp.concatenate(mixes, axis=0).T


def attend_back(q, k, v, gm, probs, heads, scale):
    size = 256 // heads
    kt = k.astype(f32).T.astype(bf16)
    gq, gk, gv = [], 0.0, 0.0
    for h, mask in enumerate(head_masks(heads)):
        gmh = gm * mask
        p = probs(h)
        wide = p.astype(f32)
        t = wide * nt(v, gmh)
        gs = (t - wide * jnp.sum(t, axis=0, keepdims=True)).astype(bf16)
        gk = gk + nn(gs, q * mask)
        gv = gv + nn(p, gmh)
        gq.append(nn(kt[h * size : (h + 1) * size], gs))
    return jnp.concatenate(gq, axis=0).T * scale, gk * scale, gv


def place_of(slot, seg_ref, gsd_ref):
    n = seg_ref.shape[1]
    across = jnp.broadcast_to(seg_ref[pl.ds(slot, 1), :].astype(f32), (n, n))
    earlier = lax.broadcasted_iota(jnp.int32, (n, n), 1) < lax.broadcasted_iota(jnp.int32, (n, n), 0)
    rank = jnp.sum(jnp.where((across == across.T) & earlier, 1.0, 0.0), axis=1, keepdims=True)
    index = jnp.broadcast_to(gsd_ref[pl.ds(slot, 1), :].astype(f32), (n, n)).T[:, :1]
    return rank * (0.5 + 0.25 * index)


def start_body(slot_ref, seg_ref, gsd_ref, tokens_ref, gain_ref, shift_ref, wf_ref, normed_ref, stream_ref):
    place = place_of(slot_ref[0], seg_ref, gsd_ref)
    half = wf_ref.shape[1]
    sine, cosine = sin_cos(place * wf_ref[...])
    stream_ref[:, :half] = tokens_ref[:, :half].astype(f32) + sine
    stream_ref[:, half:] = tokens_ref[:, half:].astype(f32) + cosine
    normal, _ = norm_parts(stream_ref[...])
    normed_ref[...] = (normal * gain_ref[0:1] + shift_ref[0:1]).astype(bf16)


def mask_body(slot_ref, seg_ref, bias_a_ref, bias_b_ref):
    slot = slot_ref[0]
    n = seg_ref.shape[1]
    for j in range(4):
        across = jnp.broadcast_to(seg_ref[pl.ds(slot ^ j, 1), :].astype(f32), (n, n))
        (bias_a_ref, bias_b_ref)[j // 2][j % 2] = jnp.where(across == across.T, 0.0, -1e30)


def stream_body(slot_ref, seg_ref, gsd_ref, tokens_ref, eb_ref, wf_ref, nf_ref, pos_ref, stream_ref):
    place = place_of(slot_ref[0], seg_ref, gsd_ref)
    half = wf_ref.shape[1]
    sine, cosine = sin_cos(place * wf_ref[...])
    stream_ref[:, :half] = tokens_ref[:, :half].astype(f32) + sine
    stream_ref[:, half:] = tokens_ref[:, half:].astype(f32) + cosine
    half = nf_ref.shape[1]
    sine, cosine = sin_cos(place * nf_ref[...])
    pos_ref[:, :half] = sine + eb_ref[:, :half]
    pos_ref[:, half:] = cosine + eb_ref[:, half:]


def attn_body(scale, heads, first, *refs):
    count = (len(refs) - 9) // 2
    xs, rest = refs[:count], refs[count:]
    bias_ref, w_ref, qvb_ref, o_ref, q_ref, k_ref, v_ref, p_ref, mix_ref = rest[:9]
    for r, (x_ref, part_ref) in enumerate(zip(xs, rest[9:])):
        x = x_ref[...]
        q = (nn(x, w_ref[0]) + qvb_ref[0:1]).astype(bf16)
        k = nn(x, w_ref[1]).astype(bf16)
        v = (nn(x, w_ref[2]) + qvb_ref[1:2]).astype(bf16)
        q_ref[r], k_ref[r], v_ref[r] = q, k, v

        def keep(h, p):
            p_ref[r, h] = p

        mix = attend(q, k, v, bias_ref[first + r], heads, scale, keep).astype(bf16)
        mix_ref[r] = mix
        part_ref[...] = nn(mix, o_ref[...]).astype(bf16)


def attn_back_body(scale, heads, *refs):
    count = (len(refs) - 8) // 2
    gs, rest = refs[:count], refs[count:]
    q_ref, k_ref, v_ref, p_ref, w_ref, o_ref, g3_ref, sums_ref = rest[:8]
    total_q, total_v = 0.0, 0.0
    for r, (g_ref, part_ref) in enumerate(zip(gs, rest[8:])):
        gm = nt(g_ref[...], o_ref[...]).astype(bf16)
        gq, gk, gv = attend_back(
            q_ref[r], k_ref[r], v_ref[r], gm, lambda h: p_ref[r, h], heads, scale
        )
        total_q = total_q + jnp.sum(gq, axis=0, keepdims=True)
        total_v = total_v + jnp.sum(gv, axis=0, keepdims=True)
        acc = 0.0
        for c, g in enumerate((gq, gk, gv)):
            low = g.astype(bf16)
            g3_ref[r, :, c * 256 : (c + 1) * 256] = low
            acc = acc + nt(low, w_ref[c])
        part_ref[...] = acc.astype(bf16)
    sums_ref[0:1] = total_q
    sums_ref[1:2] = total_v


def mid_body(stream_ref, p_ref, near_ref, far_ref, ob_ref, gain_ref, shift_ref, mid_ref, normed_ref):
    total = p_ref[...].astype(f32) + near_ref[...].astype(f32) + far_ref[...].astype(f32)
    middle = stream_ref[...] + total + ob_ref[0:1]
    mid_ref[...] = middle
    normal, _ = norm_parts(middle)
    normed_ref[...] = (normal * gain_ref[1:2] + shift_ref[1:2]).astype(bf16)


def mlp_body(*refs):
    count = (len(refs) - 5) // 2
    xs, rest = refs[:count], refs[count:]
    up_ref, ub_ref, down_ref, hid_ref, dg_ref = rest[:5]
    width = up_ref.shape[1]
    for r, (x_ref, part_ref) in enumerate(zip(xs, rest[5:])):
        x = x_ref[...]
        for c in range(0, width, 256):
            cut = slice(c, c + 256)
            hidden, slope = gelu_both(nn(x, up_ref[:, cut]) + ub_ref[:, cut])
            hid_ref[r, :, cut] = hidden.astype(bf16)
            dg_ref[r, :, cut] = slope.astype(bf16)
        hidden = hid_ref[r]
        for c in range(0, down_ref.shape[1], 512):
            cut = slice(c, c + 512)
            part_ref[:, cut] = nn(hidden, down_ref[:, cut]).astype(bf16)


def mlp_back_body(*refs):
    count = (len(refs) - 5) // 2
    gs, rest = refs[:count], refs[count:]
    dg_ref, up_ref, down_ref, gp_ref, sums_ref = rest[:5]
    width = up_ref.shape[1]
    for r, (g_ref, part_ref) in enumerate(zip(gs, rest[5:])):
        g = g_ref[...]
        for c in range(0, width, 256):
            cut = slice(c, c + 256)
            grad = nt(g, down_ref[cut]) * dg_ref[r, :, cut].astype(f32)
            gp_ref[r, :, cut] = grad.astype(bf16)
            total = jnp.sum(grad, axis=0, keepdims=True)
            sums_ref[:, cut] = total if r == 0 else sums_ref[:, cut] + total
        gp = gp_ref[r]
        for c in range(0, up_ref.shape[0], 512):
            cut = slice(c, c + 512)
            part_ref[:, cut] = nt(gp, up_ref[cut]).astype(bf16)


def mlp_end_body(slot_ref, ge_ref, p_ref, near_ref, far_ref, mid_ref, gain_ref, ua_ref, ub_ref, uc_ref, dec_ref,
                 gmid_ref, gm_ref, pack_ref):
    slot = slot_ref[0]
    grad = p_ref[...].astype(f32) + near_ref[...].astype(f32) + far_ref[...].astype(f32)
    normal, scale = norm_parts(mid_ref[...])
    gmid = ge_ref[...] + norm_back(normal, scale, gain_ref[1:2], grad)
    gmid_ref[...] = gmid
    gm_ref[...] = gmid.astype(bf16)
    pack_ref[...] = jnp.zeros(pack_ref.shape, f32)
    pack_ref[0:1] = jnp.sum(gmid, axis=0, keepdims=True)
    pack_ref[1:2] = jnp.sum(grad * normal, axis=0, keepdims=True)
    pack_ref[2:3] = jnp.sum(grad, axis=0, keepdims=True)
    pack_ref[pl.ds(4 + slot, 1), :] = ua_ref[...] + ub_ref[...] + uc_ref[...]
    pack_ref[8:16] = dec_ref[...]


def last_body(slot_ref, gmid_ref, p_ref, near_ref, far_ref, stream_ref, gain_ref, sa_ref, sb_ref, sc_ref, mid_ref,
              gtok_ref, pack_ref):
    slot = slot_ref[0]
    grad = p_ref[...].astype(f32) + near_ref[...].astype(f32) + far_ref[...].astype(f32)
    normal, scale = norm_parts(stream_ref[...])
    gtok_ref[...] = gmid_ref[...] + norm_back(normal, scale, gain_ref[0:1], grad)
    pack_ref[:16] = mid_ref[...]
    pack_ref[16:] = jnp.zeros((8, pack_ref.shape[1]), f32)
    pack_ref[16:17] = jnp.sum(grad * normal, axis=0, keepdims=True)
    pack_ref[17:18] = jnp.sum(grad, axis=0, keepdims=True)
    share = sa_ref.shape[1]
    place = pl.ds(pl.multiple_of(slot * share, share), share)
    pack_ref[18:20, place] = sa_ref[...] + sb_ref[...] + sc_ref[...]


def decoder_body(slot_ref, mid_ref, p_ref, near_ref, far_ref, eob_ref, own_ref, by_ref, fa_ref, fb_ref, na_ref, nb_ref,
                 b0_ref, b1_ref, b2_ref, b3_ref, pos_ref, bias_ref, dob_ref, dgain_ref, dnb_ref, cot_ref,
                 encl_ref, out_ref, x1_ref, x2_ref, hid_ref, mix_ref, gp_ref, gm_ref, g3_ref, gz_ref,
                 gel_ref, ge_ref, sums_ref,
                 wup, wdown, wqkv, wout, wemb, pt, dg, qkv, wide, qvb_ref, upb_ref):
    slot, home = slot_ref[0], slot_ref[1]
    width = cot_ref.shape[1]
    block = width // 4
    heads = DHEADS * 256 // width
    groups = width // 256
    scale = (width // DHEADS) ** -0.5

    def place(j, base=0):
        return pl.ds(pl.multiple_of(base + (slot ^ j) * block, block), block)

    for j, ref in enumerate((b0_ref, b1_ref, b2_ref, b3_ref)):
        for c in range(2):
            qvb_ref[c : c + 1, j * block : (j + 1) * block] = ref[:, c * block : (c + 1) * block]
        upb_ref[:, j * width : (j + 1) * width] = ref[:, 2 * block :]
    piece, thin, tall = width // 8, block // 8, 2 * width // 8
    top = 2 * piece + thin
    step = top + piece + thin
    for j, (low_ref, high_ref) in enumerate(
        ((own_ref, own_ref), (by_ref, by_ref), (fa_ref, fb_ref), (na_ref, nb_ref))
    ):
        cut = slice(j * block, (j + 1) * block)
        for i in range(8):
            ref = (low_ref, high_ref)[i // 4]
            base = (i if j < 2 else i % 4) * step
            chunk = i if j < 2 else home ^ i

            def rows(size):
                return pl.ds(pl.multiple_of(chunk * size, size), size)

            wup[j, rows(piece)] = ref[base : base + piece]
            wdown[j, rows(piece)] = ref[base + piece : base + 2 * piece]
            wout[pl.ds(pl.multiple_of(j * block + chunk * thin, thin), thin)] = (
                ref[base + 2 * piece : base + top]
            )
            for c in range(3):
                wqkv[c, rows(piece), cut] = ref[base + top : base + top + piece, c * block : (c + 1) * block]
            wemb[pl.ds(pl.multiple_of(chunk * tall, tall), piece), cut] = (
                ref[base + top : base + top + piece, 3 * block :]
            )
            for c in range(4):
                wemb[pl.ds(pl.multiple_of(chunk * tall + piece + c * thin, thin), thin), cut] = (
                    ref[base + top + piece : base + step, c * block : (c + 1) * block]
                )
    encoded = mid_ref[...] + eob_ref[1:2]
    encoded = encoded + p_ref[...].astype(f32) + near_ref[...].astype(f32) + far_ref[...].astype(f32)
    encl_ref[...] = encoded.astype(bf16)
    embedded = nn(encl_ref[...], wemb[...])
    for j in range(4):
        wide[:, place(j)] = embedded[:, j * block : (j + 1) * block]
    stream = wide[...] + pos_ref[...]
    normal1, scale1 = norm_parts(stream)
    x1_ref[...] = (normal1 * dgain_ref[0:1] + dnb_ref[0:1]).astype(bf16)
    x1 = x1_ref[...]
    qkv[0] = (nn(x1, wqkv[0]) + qvb_ref[0:1]).astype(bf16)
    qkv[1] = nn(x1, wqkv[1]).astype(bf16)
    qkv[2] = (nn(x1, wqkv[2]) + qvb_ref[1:2]).astype(bf16)
    bias = bias_ref[0]
    for g in range(groups):
        cut = slice(g * 256, (g + 1) * 256)

        def keep(h, p):
            pt[g * heads + h] = p

        mix_ref[:, cut] = attend(
            qkv[0, :, cut], qkv[1, :, cut], qkv[2, :, cut], bias, heads, scale, keep
        ).astype(bf16)
    middle = stream + nn(mix_ref[...], wout[...]) + dob_ref[0:1]
    normal2, scale2 = norm_parts(middle)
    x2_ref[...] = (normal2 * dgain_ref[1:2] + dnb_ref[1:2]).astype(bf16)
    x2 = x2_ref[...]
    result = middle + dob_ref[1:2]
    for j in range(4):
        cut = slice(j * width, (j + 1) * width)
        hidden, slope = gelu_both(nn(x2, wup[j]) + upb_ref[:, cut])
        hid_ref[:, cut] = hidden.astype(bf16)
        dg[:, cut] = slope.astype(bf16)
        result = result + nn(hid_ref[:, cut], wdown[j])
    out_ref[...] = result

    cot = cot_ref[...]
    grad = 0.0
    sums_ref[...] = jnp.zeros(sums_ref.shape, f32)
    for j in range(4):
        cut = slice(j * width, (j + 1) * width)
        pre = nt(cot, wdown[j]) * dg[:, cut].astype(f32)
        gp_ref[:, cut] = pre.astype(bf16)
        block_sum = jnp.sum(pre, axis=0, keepdims=True)
        at = slot ^ j
        sums_ref[pl.ds(6 + (at >> 1), 1), pl.ds(pl.multiple_of((at & 1) * width, width), width)] = (
            block_sum
        )
        grad = grad + nt(gp_ref[:, cut], wup[j])
    cotf = cot.astype(f32)
    gmid = cotf + norm_back(normal2, scale2, dgain_ref[1:2], grad)
    gm_ref[...] = gmid.astype(bf16)
    sums_ref[1:2, :width] = jnp.sum(gmid, axis=0, keepdims=True)
    sums_ref[2:3, :width] = jnp.sum(cotf, axis=0, keepdims=True)
    sums_ref[2:3, width:] = jnp.sum(grad * normal2, axis=0, keepdims=True)
    sums_ref[4:5, :width] = jnp.sum(grad, axis=0, keepdims=True)
    gmix = nt(gm_ref[...], wout[...]).astype(bf16)
    grad = 0.0
    for g in range(groups):
        cut = slice(g * 256, (g + 1) * 256)
        three = attend_back(
            qkv[0, :, cut], qkv[1, :, cut], qkv[2, :, cut], gmix[:, cut],
            lambda h: pt[g * heads + h], heads, scale,
        )
        for c, part in enumerate(three):
            begin = c * width + g * 256
            low = part.astype(bf16)
            g3_ref[:, begin : begin + 256] = low
            grad = grad + nt(low, wqkv[c, :, cut])
        for c, row, base in ((0, 4, width), (2, 5, width)):
            total = jnp.sum(three[c], axis=0, keepdims=True)
            for i in range(256 // block):
                sums_ref[row : row + 1, place(g * (256 // block) + i, base)] = (
                    total[:, i * block : (i + 1) * block]
                )
    gstream = gmid + norm_back(normal1, scale1, dgain_ref[0:1], grad)
    sums_ref[3:4, width:] = jnp.sum(gstream, axis=0, keepdims=True)
    sums_ref[1:2, width:] = jnp.sum(grad * normal1, axis=0, keepdims=True)
    sums_ref[3:4, :width] = jnp.sum(grad, axis=0, keepdims=True)
    wide[...] = gstream
    for j in range(4):
        gz_ref[:, j * block : (j + 1) * block] = wide[:, place(j)].astype(bf16)
    ge = nt(gz_ref[...], wemb[...])
    ge_ref[...] = ge
    gel_ref[...] = ge.astype(bf16)
    sums_ref[0:1] = jnp.sum(ge, axis=0, keepdims=True)


def decoder_weights_body(x1_ref, x2_ref, hid_ref, mix_ref, gp_ref, gm_ref, g3_ref, gz_ref, encl_ref, cot_ref,
                         sent_ref, kept_ref):
    width = cot_ref.shape[1]
    block = width // 4
    cot, gm, x2 = cot_ref[...], gm_ref[...], x2_ref[...]
    piece, thin = width // 8, block // 8
    tall = encl_ref.shape[1] // 8
    top = 2 * piece + thin
    step = top + piece + thin

    def to(j):
        return sent_ref if j % 2 else kept_ref

    for j in (1, 3, 0, 2):
        w = to(j)
        i = j // 2
        cut = slice(j * width, (j + 1) * width)
        up = tn(x2, gp_ref[:, cut]).astype(bf16)
        down = tn(hid_ref[:, cut], cot).astype(bf16)
        out = tn(mix_ref[:, j * block : (j + 1) * block], gm).astype(bf16)
        for c in range(8):
            w[i, c * step : c * step + piece] = up[c * piece : (c + 1) * piece]
            w[i, c * step + piece : c * step + 2 * piece] = down[c * piece : (c + 1) * piece]
            w[i, c * step + 2 * piece : c * step + top] = out[c * thin : (c + 1) * thin]
    x1 = x1_ref[...]
    for k in range(3):
        full = tn(x1, g3_ref[:, k * width : (k + 1) * width]).astype(bf16)
        for j in range(4):
            for c in range(8):
                to(j)[j // 2, c * step + top : c * step + top + piece, k * block : (k + 1) * block] = (
                    full[c * piece : (c + 1) * piece, j * block : (j + 1) * block]
                )
    full = tn(encl_ref[...], gz_ref[...]).astype(bf16)
    for j in range(4):
        cut = slice(j * block, (j + 1) * block)
        for c in range(8):
            base = c * tall
            to(j)[j // 2, c * step + top : c * step + top + piece, 3 * block :] = full[base : base + piece, cut]
            base = base + piece
            for k in range(4):
                to(j)[j // 2, c * step + top + piece : (c + 1) * step, k * block : (k + 1) * block] = (
                    full[base + k * thin : base + (k + 1) * thin, cut]
                )


def pack_body(pick_ref, up_ref, down_ref, out_ref, qkv_ref, emb_ref, chunk_ref):
    piece, thin, block = up_ref.shape[0], out_ref.shape[0], emb_ref.shape[1]
    chunk_ref[:piece] = up_ref[...]
    chunk_ref[piece : 2 * piece] = down_ref[...]
    top = 2 * piece + thin
    chunk_ref[2 * piece : top] = out_ref[...]
    for c in range(3):
        chunk_ref[top : top + piece, c * block : (c + 1) * block] = qkv_ref[c]
    chunk_ref[top : top + piece, 3 * block :] = emb_ref[:piece]
    for c in range(4):
        base = piece + c * thin
        chunk_ref[top + piece :, c * block : (c + 1) * block] = emb_ref[base : base + thin]


def join_body(a_ref, b_ref, out_ref):
    rows = a_ref.shape[0]
    out_ref[:rows] = a_ref[...]
    out_ref[rows:] = b_ref[...]


def add_body(a_ref, b_ref, out_ref):
    out_ref[...] = (a_ref[...].astype(f32) + b_ref[...].astype(f32)).astype(out_ref.dtype)


def add_all_body(*refs):
    total = refs[0][...]
    for ref in refs[1:-1]:
        total = total + ref[...]
    refs[-1][...] = total


def last_sums_body(slot_ref, *refs):
    terms, outs, total_ref = refs[:-12], refs[-12:-1], refs[-1]
    total = terms[0][...]
    for ref in terms[1:]:
        total = total + ref[...]
    total_ref[...] = total
    slot = slot_ref[0]
    e_qv, e_upb, e_ob, e_gain, e_nb, d_emb, d_qv, d_upb, d_ob, d_gain, d_nb = outs
    share, thin, width = e_qv.shape[1], d_qv.shape[1], d_emb.shape[1]
    e_qv[...] = total_ref[18:20, pl.ds(pl.multiple_of(slot * share, share), share)]
    e_upb[...] = total_ref[pl.ds(4 + slot, 1), :]
    e_ob[0:1] = total_ref[0:1]
    e_ob[1:2] = total_ref[8:9]
    e_gain[0:1] = total_ref[16:17]
    e_gain[1:2] = total_ref[1:2]
    e_nb[0:1] = total_ref[17:18]
    e_nb[1:2] = total_ref[2:3]
    d_ob[...] = total_ref[9:11, :width]
    d_gain[...] = total_ref[9:11, width:]
    d_nb[...] = total_ref[11:13, :width]
    d_emb[...] = total_ref[11:12, width:]
    d_qv[...] = total_ref[12:14, pl.ds(pl.multiple_of(width + slot * thin, thin), thin)]
    d_upb[...] = total_ref[pl.ds(14 + (slot >> 1), 1), pl.ds(pl.multiple_of((slot & 1) * width, width), width)]


def halve_body(bit_ref, *refs):
    ins, (send_ref, keep_ref) = refs[:-2], refs[-2:]
    half = send_ref.shape[0]
    bit = bit_ref[0]
    for ref, which in ((send_ref, 1 - bit), (keep_ref, bit)):
        rows = pl.ds(pl.multiple_of(which * half, half), half)
        total = ins[0][rows].astype(f32)
        for other in ins[1:]:
            total = total + other[rows].astype(f32)
        ref[...] = total.astype(bf16)


def far_body(bit_ref, kept_ref, near_ref, out_ref):
    half = out_ref.shape[0]
    rows = pl.ds(pl.multiple_of(bit_ref[0] * half, half), half)
    out_ref[...] = (kept_ref[1, rows].astype(f32) + near_ref[1, rows].astype(f32)).astype(bf16)


def there_body(bit_ref, kept_ref, near_ref, far_ref, send_ref):
    half = send_ref.shape[0]
    rows = pl.ds(pl.multiple_of((1 - bit_ref[0]) * half, half), half)
    total = kept_ref[0, rows].astype(f32) + near_ref[0, rows].astype(f32)
    send_ref[...] = (total + far_ref[...].astype(f32)).astype(bf16)


def mine_body(bit_ref, kept_ref, near_ref, far_ref, got_ref, send_ref, keep_ref):
    quarter = send_ref.shape[0]
    base = bit_ref[0] * 2 * quarter
    for ref, which in ((send_ref, 1 - bit_ref[1]), (keep_ref, bit_ref[1])):
        rows = pl.ds(pl.multiple_of(base + which * quarter, quarter), quarter)
        inner = pl.ds(pl.multiple_of(which * quarter, quarter), quarter)
        total = kept_ref[0, rows].astype(f32) + near_ref[0, rows].astype(f32)
        ref[...] = (total + far_ref[inner].astype(f32) + got_ref[inner].astype(f32)).astype(bf16)


def piece_of(refs, j):
    for ref in refs:
        if len(ref.shape) == 2:
            if j == 0:
                return ref[...]
            j -= 1
        elif j < ref.shape[0]:
            return ref[j]
        else:
            j -= ref.shape[0]


def tile_sum(xs, gs, more):
    acc = 0.0
    for j in range(4):
        acc = acc + tn(piece_of(xs, j), piece_of(gs, j))
    if not more:
        return [(slice(None), slice(None), acc)]
    rows, cols = acc.shape
    parts = [(slice(None), slice(0, cols), acc)]
    half, quarter = rows // 2, rows // 8
    wide = more[0].shape[1] // 4
    for c in range(2):
        for k in range(4):
            parts.append((
                slice(c * half + k * quarter, c * half + (k + 1) * quarter),
                slice(cols, cols + wide),
                more[0][c * quarter : (c + 1) * quarter, k * wide : (k + 1) * wide].astype(f32),
            ))
    return parts


def first_half_body(nx, ng, nm, pick_ref, *refs):
    xs, gs, more = refs[:nx], refs[nx : nx + ng], refs[nx + ng : nx + ng + nm]
    out_ref = refs[nx + ng + nm]
    for rows, cols, value in tile_sum(xs, gs, more):
        out_ref[rows, cols] = value.astype(bf16)


def other_half_body(nx, ng, nm, pick_ref, *refs):
    xs, gs, more = refs[:nx], refs[nx : nx + ng], refs[nx + ng : nx + ng + nm]
    add_ref, send_ref, keep_ref = refs[nx + ng + nm :]
    parts = [
        (rows, cols, (value + add_ref[rows, cols].astype(f32)).astype(bf16))
        for rows, cols, value in tile_sum(xs, gs, more)
    ]

    def put(ref):
        for rows, cols, value in parts:
            ref[rows, cols] = value

    @pl.when(pl.program_id(0) == 0)
    def _():
        put(send_ref)

    @pl.when(pl.program_id(0) == 1)
    def _():
        put(keep_ref)


def weight_half(chain, xs, gs, more, cut, pick, add=None):
    tile = xs[0].shape[-1] // 4
    begin, cols = cut
    out_cols = cols + sum(m.shape[1] // 4 for m in more)

    def column(shape):
        lead = shape[:-1]
        return pl.BlockSpec(lead + (tile,), lambda i, p: (0,) * len(lead) + (p[i],))

    def whole(shape):
        lead = shape[:-1]
        return pl.BlockSpec(lead + (cols,), lambda i, p: (0,) * len(lead) + (begin // cols,))

    in_specs = [column(x.shape) for x in xs] + [whole(g.shape) for g in gs]
    in_specs += [pl.BlockSpec((tile // 4, m.shape[1]), lambda i, p: (p[i], 0)) for m in more]
    args = list(xs) + list(gs) + list(more)
    counts = len(xs), len(gs), len(more)
    if add is None:
        body = functools.partial(first_half_body, *counts)
        outs = [shaped((2 * tile, out_cols), bf16)]
        out_specs = [pl.BlockSpec((tile, out_cols), lambda i, p: (i, 0))]
    else:
        body = functools.partial(other_half_body, *counts)
        in_specs.append(pl.BlockSpec((tile, out_cols), lambda i, p: (p[2 + i], 0)))
        args.append(add)
        outs = [shaped((tile, out_cols), bf16)] * 2
        out_specs = [pl.BlockSpec((tile, out_cols), lambda i, p: (0, 0))] * 2
    return chain(body, outs, args, prefetch=pick, grid=(2,), specs=(in_specs, out_specs), limit=20)


def spread_body(writes, place_ref, *refs):
    sums = max(write[0] for write in writes) + 1
    out_refs = refs[2 * sums :]
    for i in range(8):
        for source, which, lead, first, every, row, rows, col, cols, at_col in writes:
            ref = refs[2 * source + i // 4]
            base = i % 4 * (ref.shape[0] // 4)
            at = place_ref[source] ^ i
            value = ref[base + row : base + row + rows, col : col + cols].astype(f32)
            to = pl.ds(pl.multiple_of(at * every + first, rows), rows)
            if lead is None:
                out_refs[which][to, at_col : at_col + cols] = value
            else:
                out_refs[which][lead, to] = value


def out_weight_body(*refs):
    mixes, gs, out_ref = refs[:3], refs[3:7], refs[7]
    acc = 0.0
    for j in range(4):
        acc = acc + tn(piece_of(mixes, j), piece_of(gs, j))
    out_ref[...] = acc.astype(bf16)


class Sum:
    def __init__(self, chain, masks=(1, 2, 4)):
        self.chain, self.masks = chain, masks
        self.size = lax.axis_size("dp")
        me = lax.axis_index("dp").astype(jnp.int32)
        b1, b2, b3 = self.bits = [jnp.where((me & mask) != 0, 1, 0).astype(jnp.int32) for mask in masks]
        self.place = 4 * b1 + 2 * b2 + b3 if self.size == 8 else jnp.int32(0)
        self.there = jnp.stack([2 * (1 - b1), 2 * (1 - b1) + 1])
        self.mine = jnp.stack([2 * b1 + 1 - b2, 2 * b1 + b2, 1 - b2, b2])
        steps = [self.second, self.third, self.fourth, self.fifth, self.sixth]
        self.steps = iter(steps if self.size == 8 else [])

    def step(self):
        for todo in self.steps:
            todo()
            return

    def product(self, xs, gs, more=(), cut=None):
        self.terms = (xs, gs, more, cut or (0, gs[0].shape[-1]))
        if self.size != 8:
            first = weight_half(self.chain, *self.terms, jnp.array([0, 1], jnp.int32))[0]
            other = weight_half(self.chain, *self.terms, jnp.array([2, 3], jnp.int32))[0]
            return self.general(jnp.concatenate([first, other], axis=0))
        self.got = swap(weight_half(self.chain, *self.terms, self.there)[0], "dp", self.masks[0])

    def shares(self, kept, near, there):
        self.terms = None
        self.held = (kept, near, there)
        if self.size == 8:
            half = shaped(there.shape, bf16)
            send = self.chain(there_body, [half], (self.bits[0].reshape(1), kept, near, there), smem=1)[0]
            self.got = swap(send, "dp", self.masks[0])

    def other(self, mine):
        kept, near, there = self.held
        self.held = (kept, near, mine)
        if self.size != 8:
            total = kept[0].astype(f32) + near[0].astype(f32)
            total = total + jnp.concatenate([mine, there], axis=0).astype(f32)
            self.general(total.astype(bf16))

    def second(self):
        if self.terms is None:
            rows, cols = self.got.shape
            half = shaped((rows // 2, cols), bf16)
            send, self.keep = self.chain(
                mine_body, [half, half], (jnp.stack(self.bits[:2]), *self.held, self.got), smem=1
            )
        else:
            send, self.keep = weight_half(self.chain, *self.terms, self.mine, self.got)
        self.got = swap(send, "dp", self.masks[1])

    def third(self):
        rows, cols = self.keep.shape
        half = shaped((rows // 2, cols), bf16)
        send, self.keep = self.chain(
            halve_body, [half, half], (self.bits[2].reshape(1), self.keep, self.got), smem=1
        )
        self.got = swap(send, "dp", self.masks[2])

    def fourth(self):
        self.keep = self.chain(add_body, [shaped(self.keep.shape, bf16)], (self.keep, self.got))[0]
        self.got = swap(self.keep, "dp", self.masks[2])

    def join(self):
        rows, cols = self.keep.shape
        self.keep = self.chain(join_body, [shaped((2 * rows, cols), bf16)], (self.keep, self.got))[0]

    def fifth(self):
        self.join()
        self.got = swap(self.keep, "dp", self.masks[1])

    def sixth(self):
        self.join()
        self.got = swap(self.keep, "dp", self.masks[0])

    def general(self, held):
        me = lax.axis_index("dp")
        bits = [1 << i for i in range(self.size.bit_length() - 1)]
        for bit in bits:
            mine = (me & bit) != 0
            half = held.shape[0] // 2
            other = lax.dynamic_slice_in_dim(held, jnp.where(mine, 0, half), half, 0)
            own = lax.dynamic_slice_in_dim(held, jnp.where(mine, half, 0), half, 0)
            held = (own.astype(f32) + swap(other, "dp", bit).astype(f32)).astype(bf16)
        for bit in reversed(bits):
            mine = (me & bit) != 0
            other = swap(held, "dp", bit)
            held = jnp.where(
                mine,
                jnp.concatenate([other, held], axis=0),
                jnp.concatenate([held, other], axis=0),
            )
        half = held.shape[0] // 2
        self.keep, self.got = held[:half], held[half:]


def per_device(
    tokens, segment_ids, gsd_index, enc_qkv, enc_qv_bias, enc_out_proj, enc_up, enc_up_bias,
    enc_down, enc_out_bias, enc_gain, enc_norm_bias, embed_weight, embed_bias, dec_qkv,
    dec_qv_bias, dec_out_proj, dec_up, dec_up_bias, dec_down, dec_out_bias, dec_gain,
    dec_norm_bias, cotangent,
):
    n, width = tokens.shape
    rows, length = segment_ids.shape
    assert rows == 4 and n == length == 256 and lax.axis_size("mp") == 4
    share, ff = enc_qkv.shape[2], enc_up.shape[1]
    dwidth, dff = cotangent.shape[1], dec_up.shape[1] * 4
    dshare = dwidth // 4
    heads = share // (width // HEADS)
    scale = (width // HEADS) ** -0.5
    slot = lax.axis_index("mp").astype(jnp.int32)
    at = slot.reshape(1)
    chain = Chain()
    dec = Sum(chain)
    home = dec.place

    def low(*dims):
        return shaped(dims, bf16)

    def full(*dims):
        return shaped(dims, f32)

    def waves(size):
        half = size // 2
        return jnp.power(10000.0, -jnp.arange(half, dtype=f32) / half).reshape(1, half)

    def near(value):
        return swap(value, "mp", 1)

    def far(value):
        return swap(value, "mp", 2)

    pack_rows = 3 * dwidth + 2 * dshare
    decoder_weights = [in_hbm(w) for w in (dec_up, dec_down, dec_out_proj, dec_qkv, embed_weight)]

    def pack(pick, steps):
        def block(shape):
            if len(shape) == 3:
                return pl.BlockSpec((shape[0], shape[1] // 8, shape[2]), lambda i, p: (0, p[i], 0))
            return pl.BlockSpec((shape[0] // 8, shape[1]), lambda i, p: (p[i], 0))

        rows = pack_rows // 8
        return chain(
            pack_body,
            [low(steps * rows, dwidth)],
            decoder_weights,
            prefetch=pick,
            grid=(steps,),
            specs=([block(w.shape) for w in decoder_weights], [pl.BlockSpec((rows, dwidth), lambda i, p: (i, 0))]),
        )[0]

    split = dec.size == 8
    got = far(pack(home.reshape(1), 1)) if split else None
    normed = chain(
        start_body,
        [low(n, width)],
        (at, in_hbm(segment_ids), in_hbm(gsd_index), in_hbm(tokens), in_hbm(enc_gain), in_hbm(enc_norm_bias), waves(width)),
        smem=1,
        scratch=[pltpu.VMEM((n, width), f32)],
    )[0]
    x = [normed, near(normed), far(normed)]
    bias_a, bias_b = chain(mask_body, [kept(full(2, n, n)), kept(full(2, n, n))], (at, in_hbm(segment_ids)), smem=1)

    def attention(bias, first, *blocks):
        count = len(blocks)
        return chain(
            functools.partial(attn_body, scale, heads, first),
            [kept(low(count, n, share))] * 3
            + [kept(low(count, heads, n, n)), kept(low(count, n, share))]
            + [low(n, width)] * count,
            (*blocks, bias, enc_qkv, enc_qv_bias, enc_out_proj),
        )

    def add(a, b):
        return chain(add_body, [shaped(a.shape, a.dtype)], (a, b))[0]

    def join(a, b):
        return chain(join_body, [low(a.shape[0] + b.shape[0], a.shape[1])], (a, b))[0]

    def both(blocks):
        blocks[2] = chain.pin(blocks[2])
        blocks.append(near(blocks[2]))

    *saved_a, mixa, part0, part1 = attention(bias_a, 0, x[0], x[1])
    part1 = near(part1)
    vector = jnp.concatenate([dec_qv_bias.reshape(-1), dec_up_bias]).reshape(1, -1)
    vector = chain.pin(vector)
    vectors = [vector, near(vector), far(vector)]
    part1 = chain.pin(part1)
    both(x)
    chain.gap()
    chain.gap()
    *saved_d, mixd, part3 = attention(bias_b, 1, x[3])
    part3 = near(part3)
    *saved_c, mixc, part2 = attention(bias_b, 0, x[2])
    if split:
        got = chain.pin(got)
        more = swap(got, "dp", 4)
    part2 = far(add(part2, part3))
    vectors[1] = chain.pin(vectors[1])
    both(vectors)
    packed = pack(jnp.arange(8, dtype=jnp.int32), 8)
    packed_near = near(packed)
    pos, stream = chain(
        stream_body,
        [kept(full(n, dwidth)), full(n, width)],
        (at, in_hbm(segment_ids), in_hbm(gsd_index), in_hbm(tokens), in_hbm(embed_bias.reshape(1, -1)), waves(width), waves(dwidth)),
        smem=1,
    )
    if split:
        got = join(got, more)
        more = swap(got, "dp", 2)
    else:
        got = far(packed)
    middle, normed2 = chain(
        mid_body,
        [kept(full(n, width)), low(n, width)],
        (stream, part0, part1, part2, enc_out_bias, enc_gain, enc_norm_bias),
    )
    y = [normed2, near(normed2), far(normed2)]
    packed_near = chain.pin(packed_near)
    vectors[3] = chain.pin(vectors[3])
    if split:
        got = join(got, more)
        more = swap(got, "dp", 1)
    else:
        more = got[pack_rows // 2 :]
        got = got[: pack_rows // 2]

    def feed(*blocks):
        count = len(blocks)
        return chain(
            mlp_body,
            [kept(low(count, n, ff))] * 2 + [low(n, width)] * count,
            (*blocks, enc_up, enc_up_bias.reshape(1, -1), enc_down),
        )

    hida, dga, part0, part1 = feed(y[0], y[1])
    part1 = near(part1)
    far_weights = [got, more]
    near_weights = [near(got)]
    both(y)
    part1 = chain.pin(part1)
    near_weights[0] = chain.pin(near_weights[0])
    hidd, dgd, part3 = feed(y[3])
    part3 = near(part3)
    hidc, dgc, part2 = feed(y[2])
    part2 = far(add(part2, part3))
    far_weights[1] = chain.pin(more)
    near_weights.append(near(far_weights[1]))
    part2 = chain.pin(part2)

    (enc_low, output, x1, x2, hid, mix, gp, gm, g3, gz, ge_low, ge, dec_sums) = chain(
        decoder_body,
        [kept(o) for o in (low(n, width), full(n, dwidth), low(n, dwidth), low(n, dwidth), low(n, dff),
                           low(n, dwidth), low(n, dff), low(n, dwidth), low(n, 3 * dwidth), low(n, dwidth))]
        + [low(n, width), kept(full(n, width)), kept(full(8, width))],
        (jnp.stack([slot, home]), middle, part0, part1, part2, enc_out_bias, packed, packed_near,
         *far_weights, *near_weights, *vectors, pos, bias_a, dec_out_bias, dec_gain,
         dec_norm_bias, cotangent),
        smem=1,
        scratch=[
            pltpu.VMEM((4, dwidth, dwidth), bf16), pltpu.VMEM((4, dwidth, dwidth), bf16),
            pltpu.VMEM((3, dwidth, dwidth), bf16), pltpu.VMEM((dwidth, dwidth), bf16),
            pltpu.VMEM((width, dwidth), bf16), pltpu.VMEM((DHEADS, n, n), bf16),
            pltpu.VMEM((n, dff), bf16), pltpu.VMEM((3, n, dwidth), bf16), pltpu.VMEM((n, dwidth), f32),
            pltpu.VMEM((2, dwidth), f32), pltpu.VMEM((1, dff), f32),
        ],
        limit=40,
    )
    g = [ge_low, near(ge_low), far(ge_low)]

    def feed_back(slope, *blocks):
        count = len(blocks)
        return chain(
            mlp_back_body,
            [kept(low(count, n, ff)), kept(full(1, ff))] + [low(n, width)] * count,
            (*blocks, slope, enc_up, enc_down),
        )

    def attention_back(saved, *blocks):
        count = len(blocks)
        return chain(
            functools.partial(attn_back_body, scale, heads),
            [kept(low(count, n, 3 * share)), kept(full(2, share))] + [low(n, width)] * count,
            (*blocks, *saved, enc_qkv, enc_out_proj),
        )

    def far_share(bit):
        return far(chain(far_body, [low(pack_rows // 2, dwidth)], (bit.reshape(1), kept_share, sent), smem=1)[0])

    def hbm(*values):
        return [in_hbm(v) for v in values]

    down, up, attn = Sum(chain), Sum(chain), Sum(chain)

    def finish(sums, outs, writes):
        return chain(
            functools.partial(spread_body, writes),
            [kept(full(*dims)) for dims in outs],
            (jnp.stack([f.place for f in sums]), *[v for f in sums for v in (f.keep, f.got)]),
            smem=1,
            limit=24,
        )

    chain.gap()
    gpa, upa, part0, part1 = feed_back(dga, g[0], g[1])
    part1 = near(part1)
    sent, kept_share = chain(
        decoder_weights_body,
        [low(2, pack_rows, dwidth), kept(low(2, pack_rows, dwidth))],
        (x1, x2, hid, mix, gp, gm, g3, gz, enc_low, cotangent),
        limit=24,
    )
    sent = near(sent)
    part1 = chain.pin(part1)
    both(g)
    gpc, upc, part2 = feed_back(dgc, g[2])
    down.product(hbm(hida, hidc, hidd), g)
    gpd, upd, part3 = feed_back(dgd, g[3])
    part3 = near(part3)
    chain.gap()
    part2 = far(add(part2, part3))
    chain.gap()
    grad_middle, gm_low, sums_mid = chain(
        mlp_end_body,
        [kept(full(n, width)), low(n, width), kept(full(16, width))],
        (at, ge, part0, part1, part2, middle, enc_gain, upa, upc, upd, dec_sums),
        smem=1,
    )
    m = [gm_low, near(gm_low), far(gm_low)]
    up.product(hbm(*y), hbm(gpa, gpc, gpd))
    down.step()
    g3a, sa, part0, part1 = attention_back(saved_a, m[0], m[1])
    part1 = near(part1)
    chain.gap()
    part1 = chain.pin(part1)
    there = far_share(1 - dec.bits[0])
    both(m)
    g3c, sc, part2 = attention_back(saved_c, m[2])
    out_full = chain(out_weight_body, [low(share, width)], (mixa, mixc, mixd, *m))[0]
    g3d, sd, part3 = attention_back(saved_d, m[3])
    part3 = near(part3)
    down.step()
    attn.product(hbm(*x), hbm(g3a, g3c, g3d), [out_full])
    part2 = far(add(part2, part3))
    up.step()
    down.step()
    up.step()
    grad_tokens, sums = chain(
        last_body,
        [kept(full(n, width)), full(24, width)],
        (at, grad_middle, part0, part1, part2, stream, enc_gain, sa, sc, sd, sums_mid),
        smem=1,
    )
    dec.shares(kept_share, sent, there)
    dec.other(far_share(dec.bits[0]))
    down.step()
    attn.step()
    up.step()
    down.step()
    dec.step()
    hops = [("mp", 1), ("mp", 2)] + [("dp", 1 << i) for i in range(dec.size.bit_length() - 1)]
    hops = iter(hops)

    def hop(total, got=None):
        if got is not None:
            total = add(total, got)
        for axis, mask in hops:
            return total, swap(total, axis, mask)
        return total, None

    small = hop(sums)
    attn.step()
    up.step()
    small = hop(*small)
    dec.step()
    attn.step()
    up.step()
    e_down = finish((down,), [(ff, width)], [(0, 0, None, 0, ff // 8, 0, ff // 8, 0, width, 0)])[0]
    small = hop(*small)
    attn.step()
    dec.step()
    small = hop(*small)
    attn.step()
    e_up = finish((up,), [(width, ff)], [(0, 0, None, 0, width // 8, 0, width // 8, 0, ff, 0)])[0]
    dec.step()
    small = hop(*small)
    while small[1] is not None:
        sums = small
        small = hop(*small)
    vectors = chain(
        last_sums_body,
        [full(2, share), full(1, ff), full(2, width), full(2, width), full(2, width), full(1, dwidth),
         full(2, dshare), full(1, dff // 4), full(2, dwidth), full(2, dwidth), full(2, dwidth)],
        (at, *sums),
        smem=1,
        scratch=[pltpu.VMEM((24, width), f32)],
    )
    dec.step()
    rows, fold = width // 8, share // 8
    e_qkv, e_out = finish(
        (attn,),
        [(3, width, share), (share, width)],
        [(0, 0, c, 0, rows, 0, rows, c * share, share, 0) for c in range(3)]
        + [(0, 1, None, 0, fold, k * fold, fold, 3 * share, width // 4, k * (width // 4)) for k in range(4)],
    )
    part, thin, tall = dwidth // 8, dshare // 8, width // 8
    top = 2 * part + thin
    d_up, d_down, d_out, d_qkv, e_embed = finish(
        (dec,),
        [(dwidth, dwidth), (dwidth, dwidth), (dshare, dwidth), (3, dwidth, dshare), (width, dshare)],
        [
            (0, 0, None, 0, part, 0, part, 0, dwidth, 0),
            (0, 1, None, 0, part, part, part, 0, dwidth, 0),
            (0, 2, None, 0, thin, 2 * part, thin, 0, dwidth, 0),
        ]
        + [(0, 3, c, 0, part, top, part, c * dshare, dshare, 0) for c in range(3)]
        + [(0, 4, None, 0, tall, top, part, 3 * dshare, dshare, 0)]
        + [(0, 4, None, part + k * thin, tall, top + part, thin, k * dshare, dshare, 0) for k in range(4)],
    )
    e_qv, e_upb, e_ob, e_gain, e_nb, d_emb, d_qv, d_upb, d_ob, d_gain, d_nb = vectors

    return (
        output,
        grad_tokens,
        e_qkv,
        e_qv,
        e_out,
        e_up,
        e_upb.reshape(-1),
        e_down,
        e_ob,
        e_gain,
        e_nb,
        e_embed,
        d_emb.reshape(-1),
        d_qkv,
        d_qv,
        d_out,
        d_up,
        d_upb.reshape(-1),
        d_down,
        d_ob,
        d_gain,
        d_nb,
    )


def solution(mesh):
    return jax.shard_map(
        per_device,
        mesh=mesh,
        in_specs=(
            P(("dp", "mp"), None),
            P("dp", None),
            P("dp", None),
            P(None, None, "mp"),
            P(None, "mp"),
            P("mp", None),
            P(None, "mp"),
            P("mp"),
            P("mp", None),
            P(),
            P(),
            P(),
            P(None, "mp"),
            P(),
            P(None, None, "mp"),
            P(None, "mp"),
            P("mp", None),
            P(None, "mp"),
            P("mp"),
            P("mp", None),
            P(),
            P(),
            P(),
            P(("dp", "mp"), None),
        ),
        out_specs=(
            P(("dp", "mp"), None),
            P(("dp", "mp"), None),
            P(None, None, "mp"),
            P(None, "mp"),
            P("mp", None),
            P(None, "mp"),
            P("mp"),
            P("mp", None),
            P(),
            P(),
            P(),
            P(None, "mp"),
            P(),
            P(None, None, "mp"),
            P(None, "mp"),
            P("mp", None),
            P(None, "mp"),
            P("mp"),
            P("mp", None),
            P(),
            P(),
            P(),
        ),
        check_vma=False,
    )
```

```python
import functools
import math

import jax
import jax.numpy as jnp
from jax import lax
from jax.experimental import pallas as pl
from jax.experimental.pallas import tpu as pltpu
from jax.sharding import PartitionSpec as P

HEADS = 16
DHEADS = 16
norm_eps = 1e-06
f32 = jnp.float32
bf16 = jnp.bfloat16
MIB = 1 << 20
VMEM = pl.BlockSpec(memory_space=pltpu.VMEM)
SMEM = pl.BlockSpec(memory_space=pltpu.SMEM)
COST = pl.CostEstimate(flops=10**10, bytes_accessed=10**8, transcendentals=0)


def shaped(dims, kind):
    return jax.ShapeDtypeStruct(dims, kind)


def kept(shape):
    return pltpu.HBM(shape.shape, shape.dtype)


def in_hbm(value):
    return pltpu.with_memory_space_constraint(value, pltpu.HBM)


class Chain:
    token = jax.ShapeDtypeStruct((8, 128), jnp.float32)

    def __init__(self):
        self.last = None

    def __call__(self, body, outs, args, smem=0, scratch=(), limit=16, prefetch=None, grid=None, specs=None):
        args, outs = list(args), list(outs)
        extra = self.last is not None
        ins = len(args) + (prefetch is not None)
        many = len(outs)

        def inner(*refs):
            out_refs = refs[ins + extra :]
            out_refs[many][...] = jnp.zeros((8, 128), f32)
            return body(*refs[:ins], *out_refs[:many], *out_refs[many + 1 :])

        if extra:
            args.append(self.last)
        tail = [pl.BlockSpec(memory_space=pl.ANY)] * extra
        params = pltpu.CompilerParams(vmem_limit_bytes=limit * MIB)
        if prefetch is None:
            got = pl.pallas_call(
                inner,
                out_shape=outs + [self.token],
                in_specs=[SMEM] * smem + [VMEM] * (len(args) - smem - extra) + tail,
                out_specs=[VMEM] * (many + 1),
                scratch_shapes=scratch,
                compiler_params=params,
                cost_estimate=COST,
            )(*args)
        else:
            got = pl.pallas_call(
                inner,
                out_shape=outs + [self.token],
                grid_spec=pltpu.PrefetchScalarGridSpec(
                    num_scalar_prefetch=1,
                    grid=grid,
                    in_specs=specs[0] + tail,
                    out_specs=specs[1] + [pl.BlockSpec((8, 128), lambda i, p: (0, 0))],
                ),
                compiler_params=params,
                cost_estimate=COST,
            )(prefetch, *args)
        *got, self.last = got
        return got

    def pin(self, value):
        def body(value_ref, last_ref, out_ref, token_ref):
            token_ref[...] = jnp.zeros((8, 128), f32)

        any_space = pl.BlockSpec(memory_space=pl.ANY)
        got, self.last = pl.pallas_call(
            body,
            out_shape=[shaped(value.shape, value.dtype), self.token],
            in_specs=[any_space, any_space],
            out_specs=[any_space, VMEM],
            input_output_aliases={0: 0},
            compiler_params=pltpu.CompilerParams(vmem_limit_bytes=MIB),
            cost_estimate=COST,
        )(value, self.last)
        return got

    def gap(self):
        self(lambda: None, [], [], limit=1)


def nn(a, b):
    return lax.dot_general(a, b, (((1,), (0,)), ((), ())), preferred_element_type=f32)


def nt(a, b):
    return lax.dot_general(a, b, (((1,), (1,)), ((), ())), preferred_element_type=f32)


def tn(a, b):
    return lax.dot_general(a, b, (((0,), (0,)), ((), ())), preferred_element_type=f32)


def send(value, axis, pairs):
    return lax.ppermute(value, axis, pairs)


def swap(value, axis, mask):
    size = lax.axis_size(axis)
    return lax.ppermute(value, axis, [(i, i ^ mask) for i in range(size)])


def norm_parts(values):
    average = jnp.mean(values, axis=-1, keepdims=True)
    centred = values - average
    variance = jnp.mean(centred * centred, axis=-1, keepdims=True)
    scale = lax.rsqrt(variance + norm_eps)
    return centred * scale, scale


def norm_back(normal, scale, gain, grad):
    wide = grad * gain
    one = jnp.mean(wide, axis=-1, keepdims=True)
    two = jnp.mean(wide * normal, axis=-1, keepdims=True)
    return scale * (wide - one - normal * two)


def gelu_both(v):
    slope = math.sqrt(2.0 / math.pi)
    square = v * v
    t = jnp.tanh(slope * v * (1.0 + 0.044715 * square))
    half = 0.5 * (1.0 + t)
    return v * half, half + 0.5 * slope * v * (1.0 - t * t) * (1.0 + 3.0 * 0.044715 * square)


def sin_cos(x):
    turn = jnp.floor(x * (2.0 / math.pi) + 0.5)
    r = ((x - turn * 1.5703125) - turn * 4.837512969970703125e-4) - turn * 7.54978995489188216e-8
    z = r * r
    s = r + r * z * (-1.6666654611e-1 + z * (8.3321608736e-3 + z * -1.9515295891e-4))
    c = 1.0 - 0.5 * z + z * z * (
        4.166664568298827e-2 + z * (-1.388731625493765e-3 + z * 2.443315711809948e-5)
    )
    quarter = turn.astype(jnp.int32)
    odd = (quarter & 1) != 0
    sine = jnp.where(odd, c, s)
    cosine = jnp.where(odd, s, c)
    sine = jnp.where((quarter & 2) != 0, -sine, sine)
    cosine = jnp.where(((quarter + 1) & 2) != 0, -cosine, cosine)
    return sine, cosine


def head_masks(heads):
    size = 256 // heads
    lane = lax.broadcasted_iota(jnp.int32, (1, 256), 1)
    return [
        jnp.where((lane >= h * size) & (lane < (h + 1) * size), 1.0, 0.0).astype(bf16)
        for h in range(heads)
    ]


def attend(q, k, v, bias, heads, scale, keep):
    size = 256 // heads
    vt = v.astype(f32).T.astype(bf16)
    mixes = []
    for h, mask in enumerate(head_masks(heads)):
        s = nt(k, q * mask) + bias
        top = jnp.max(s, axis=0, keepdims=True)
        p = jnp.exp2((s - top) * (scale * math.log2(math.e)))
        total = jnp.sum(p, axis=0, keepdims=True)
        p = (p * (1.0 / total)).astype(bf16)
        keep(h, p)
        mixes.append(nn(vt[h * size : (h + 1) * size], p))
    return jnp.concatenate(mixes, axis=0).T


def attend_back(q, k, v, gm, probs, heads, scale):
    size = 256 // heads
    kt = k.astype(f32).T.astype(bf16)
    gq, gk, gv = [], 0.0, 0.0
    for h, mask in enumerate(head_masks(heads)):
        gmh = gm * mask
        p = probs(h)
        wide = p.astype(f32)
        t = wide * nt(v, gmh)
        gs = (t - wide * jnp.sum(t, axis=0, keepdims=True)).astype(bf16)
        gk = gk + nn(gs, q * mask)
        gv = gv + nn(p, gmh)
        gq.append(nn(kt[h * size : (h + 1) * size], gs))
    return jnp.concatenate(gq, axis=0).T * scale, gk * scale, gv


def place_of(slot, seg_ref, gsd_ref):
    n = seg_ref.shape[1]
    across = jnp.broadcast_to(seg_ref[pl.ds(slot, 1), :].astype(f32), (n, n))
    earlier = lax.broadcasted_iota(jnp.int32, (n, n), 1) < lax.broadcasted_iota(jnp.int32, (n, n), 0)
    rank = jnp.sum(jnp.where((across == across.T) & earlier, 1.0, 0.0), axis=1, keepdims=True)
    index = jnp.broadcast_to(gsd_ref[pl.ds(slot, 1), :].astype(f32), (n, n)).T[:, :1]
    return rank * (0.5 + 0.25 * index)


def start_body(slot_ref, seg_ref, gsd_ref, tokens_ref, gain_ref, shift_ref, wf_ref, normed_ref, stream_ref):
    place = place_of(slot_ref[0], seg_ref, gsd_ref)
    half = wf_ref.shape[1]
    sine, cosine = sin_cos(place * wf_ref[...])
    stream_ref[:, :half] = tokens_ref[:, :half].astype(f32) + sine
    stream_ref[:, half:] = tokens_ref[:, half:].astype(f32) + cosine
    normal, _ = norm_parts(stream_ref[...])
    normed_ref[...] = (normal * gain_ref[0:1] + shift_ref[0:1]).astype(bf16)


def mask_body(slot_ref, seg_ref, bias_a_ref, bias_b_ref):
    slot = slot_ref[0]
    n = seg_ref.shape[1]
    for j in range(4):
        across = jnp.broadcast_to(seg_ref[pl.ds(slot ^ j, 1), :].astype(f32), (n, n))
        (bias_a_ref, bias_b_ref)[j // 2][j % 2] = jnp.where(across == across.T, 0.0, -1e30)


def stream_body(slot_ref, seg_ref, gsd_ref, tokens_ref, eb_ref, wf_ref, nf_ref, pos_ref, stream_ref):
    place = place_of(slot_ref[0], seg_ref, gsd_ref)
    half = wf_ref.shape[1]
    sine, cosine = sin_cos(place * wf_ref[...])
    stream_ref[:, :half] = tokens_ref[:, :half].astype(f32) + sine
    stream_ref[:, half:] = tokens_ref[:, half:].astype(f32) + cosine
    half = nf_ref.shape[1]
    sine, cosine = sin_cos(place * nf_ref[...])
    pos_ref[:, :half] = sine + eb_ref[:, :half]
    pos_ref[:, half:] = cosine + eb_ref[:, half:]


def attn_body(scale, heads, first, *refs):
    count = (len(refs) - 9) // 2
    xs, rest = refs[:count], refs[count:]
    bias_ref, w_ref, qvb_ref, o_ref, q_ref, k_ref, v_ref, p_ref, mix_ref = rest[:9]
    for r, (x_ref, part_ref) in enumerate(zip(xs, rest[9:])):
        x = x_ref[...]
        q = (nn(x, w_ref[0]) + qvb_ref[0:1]).astype(bf16)
        k = nn(x, w_ref[1]).astype(bf16)
        v = (nn(x, w_ref[2]) + qvb_ref[1:2]).astype(bf16)
        q_ref[r], k_ref[r], v_ref[r] = q, k, v

        def keep(h, p):
            p_ref[r, h] = p

        mix = attend(q, k, v, bias_ref[first + r], heads, scale, keep).astype(bf16)
        mix_ref[r] = mix
        part_ref[...] = nn(mix, o_ref[...]).astype(bf16)


def attn_back_body(scale, heads, *refs):
    count = (len(refs) - 8) // 2
    gs, rest = refs[:count], refs[count:]
    q_ref, k_ref, v_ref, p_ref, w_ref, o_ref, g3_ref, sums_ref = rest[:8]
    total_q, total_v = 0.0, 0.0
    for r, (g_ref, part_ref) in enumerate(zip(gs, rest[8:])):
        gm = nt(g_ref[...], o_ref[...]).astype(bf16)
        gq, gk, gv = attend_back(
            q_ref[r], k_ref[r], v_ref[r], gm, lambda h: p_ref[r, h], heads, scale
        )
        total_q = total_q + jnp.sum(gq, axis=0, keepdims=True)
        total_v = total_v + jnp.sum(gv, axis=0, keepdims=True)
        acc = 0.0
        for c, g in enumerate((gq, gk, gv)):
            low = g.astype(bf16)
            g3_ref[r, :, c * 256 : (c + 1) * 256] = low
            acc = acc + nt(low, w_ref[c])
        part_ref[...] = acc.astype(bf16)
    sums_ref[0:1] = total_q
    sums_ref[1:2] = total_v


def mid_body(stream_ref, p_ref, near_ref, far_ref, ob_ref, gain_ref, shift_ref, mid_ref, normed_ref):
    total = p_ref[...].astype(f32) + near_ref[...].astype(f32) + far_ref[...].astype(f32)
    middle = stream_ref[...] + total + ob_ref[0:1]
    mid_ref[...] = middle
    normal, _ = norm_parts(middle)
    normed_ref[...] = (normal * gain_ref[1:2] + shift_ref[1:2]).astype(bf16)


def mlp_body(*refs):
    count = (len(refs) - 5) // 2
    xs, rest = refs[:count], refs[count:]
    up_ref, ub_ref, down_ref, hid_ref, dg_ref = rest[:5]
    width = up_ref.shape[1]
    for r, (x_ref, part_ref) in enumerate(zip(xs, rest[5:])):
        x = x_ref[...]
        for c in range(0, width, 256):
            cut = slice(c, c + 256)
            hidden, slope = gelu_both(nn(x, up_ref[:, cut]) + ub_ref[:, cut])
            hid_ref[r, :, cut] = hidden.astype(bf16)
            dg_ref[r, :, cut] = slope.astype(bf16)
        hidden = hid_ref[r]
        for c in range(0, down_ref.shape[1], 512):
            cut = slice(c, c + 512)
            part_ref[:, cut] = nn(hidden, down_ref[:, cut]).astype(bf16)


def mlp_back_body(*refs):
    count = (len(refs) - 5) // 2
    gs, rest = refs[:count], refs[count:]
    dg_ref, up_ref, down_ref, gp_ref, sums_ref = rest[:5]
    width = up_ref.shape[1]
    for r, (g_ref, part_ref) in enumerate(zip(gs, rest[5:])):
        g = g_ref[...]
        for c in range(0, width, 256):
            cut = slice(c, c + 256)
            grad = nt(g, down_ref[cut]) * dg_ref[r, :, cut].astype(f32)
            gp_ref[r, :, cut] = grad.astype(bf16)
            total = jnp.sum(grad, axis=0, keepdims=True)
            sums_ref[:, cut] = total if r == 0 else sums_ref[:, cut] + total
        gp = gp_ref[r]
        for c in range(0, up_ref.shape[0], 512):
            cut = slice(c, c + 512)
            part_ref[:, cut] = nt(gp, up_ref[cut]).astype(bf16)


def mlp_end_body(slot_ref, ge_ref, p_ref, near_ref, far_ref, mid_ref, gain_ref, ua_ref, ub_ref, uc_ref, dec_ref,
                 gmid_ref, gm_ref, pack_ref):
    slot = slot_ref[0]
    grad = p_ref[...].astype(f32) + near_ref[...].astype(f32) + far_ref[...].astype(f32)
    normal, scale = norm_parts(mid_ref[...])
    gmid = ge_ref[...] + norm_back(normal, scale, gain_ref[1:2], grad)
    gmid_ref[...] = gmid
    gm_ref[...] = gmid.astype(bf16)
    pack_ref[...] = jnp.zeros(pack_ref.shape, f32)
    pack_ref[0:1] = jnp.sum(gmid, axis=0, keepdims=True)
    pack_ref[1:2] = jnp.sum(grad * normal, axis=0, keepdims=True)
    pack_ref[2:3] = jnp.sum(grad, axis=0, keepdims=True)
    pack_ref[pl.ds(4 + slot, 1), :] = ua_ref[...] + ub_ref[...] + uc_ref[...]
    pack_ref[8:16] = dec_ref[...]


def last_body(slot_ref, gmid_ref, p_ref, near_ref, far_ref, stream_ref, gain_ref, sa_ref, sb_ref, sc_ref, mid_ref,
              gtok_ref, pack_ref):
    slot = slot_ref[0]
    grad = p_ref[...].astype(f32) + near_ref[...].astype(f32) + far_ref[...].astype(f32)
    normal, scale = norm_parts(stream_ref[...])
    gtok_ref[...] = gmid_ref[...] + norm_back(normal, scale, gain_ref[0:1], grad)
    pack_ref[:16] = mid_ref[...]
    pack_ref[16:] = jnp.zeros((8, pack_ref.shape[1]), f32)
    pack_ref[16:17] = jnp.sum(grad * normal, axis=0, keepdims=True)
    pack_ref[17:18] = jnp.sum(grad, axis=0, keepdims=True)
    share = sa_ref.shape[1]
    place = pl.ds(pl.multiple_of(slot * share, share), share)
    pack_ref[18:20, place] = sa_ref[...] + sb_ref[...] + sc_ref[...]


def decoder_body(slot_ref, mid_ref, p_ref, near_ref, far_ref, eob_ref, own_ref, by_ref, fa_ref, fb_ref, na_ref, nb_ref,
                 b0_ref, b1_ref, b2_ref, b3_ref, pos_ref, bias_ref, dob_ref, dgain_ref, dnb_ref, cot_ref,
                 encl_ref, out_ref, x1_ref, x2_ref, hid_ref, mix_ref, gp_ref, gm_ref, g3_ref, gz_ref,
                 gel_ref, ge_ref, sums_ref,
                 wup, wdown, wqkv, wout, wemb, pt, dg, qkv, wide, qvb_ref, upb_ref):
    slot, home = slot_ref[0], slot_ref[1]
    width = cot_ref.shape[1]
    block = width // 4
    heads = DHEADS * 256 // width
    groups = width // 256
    scale = (width // DHEADS) ** -0.5

    def place(j, base=0):
        return pl.ds(pl.multiple_of(base + (slot ^ j) * block, block), block)

    for j, ref in enumerate((b0_ref, b1_ref, b2_ref, b3_ref)):
        for c in range(2):
            qvb_ref[c : c + 1, j * block : (j + 1) * block] = ref[:, c * block : (c + 1) * block]
        upb_ref[:, j * width : (j + 1) * width] = ref[:, 2 * block :]
    piece, thin, tall = width // 8, block // 8, 2 * width // 8
    top = 2 * piece + thin
    step = top + piece + thin
    for j, (low_ref, high_ref) in enumerate(
        ((own_ref, own_ref), (by_ref, by_ref), (fa_ref, fb_ref), (na_ref, nb_ref))
    ):
        cut = slice(j * block, (j + 1) * block)
        for i in range(8):
            ref = (low_ref, high_ref)[i // 4]
            base = (i if j < 2 else i % 4) * step
            chunk = i if j < 2 else home ^ i

            def rows(size):
                return pl.ds(pl.multiple_of(chunk * size, size), size)

            wup[j, rows(piece)] = ref[base : base + piece]
            wdown[j, rows(piece)] = ref[base + piece : base + 2 * piece]
            wout[pl.ds(pl.multiple_of(j * block + chunk * thin, thin), thin)] = (
                ref[base + 2 * piece : base + top]
            )
            for c in range(3):
                wqkv[c, rows(piece), cut] = ref[base + top : base + top + piece, c * block : (c + 1) * block]
            wemb[pl.ds(pl.multiple_of(chunk * tall, tall), piece), cut] = (
                ref[base + top : base + top + piece, 3 * block :]
            )
            for c in range(4):
                wemb[pl.ds(pl.multiple_of(chunk * tall + piece + c * thin, thin), thin), cut] = (
                    ref[base + top + piece : base + step, c * block : (c + 1) * block]
                )
    encoded = mid_ref[...] + eob_ref[1:2]
    encoded = encoded + p_ref[...].astype(f32) + near_ref[...].astype(f32) + far_ref[...].astype(f32)
    encl_ref[...] = encoded.astype(bf16)
    embedded = nn(encl_ref[...], wemb[...])
    for j in range(4):
        wide[:, place(j)] = embedded[:, j * block : (j + 1) * block]
    stream = wide[...] + pos_ref[...]
    normal1, scale1 = norm_parts(stream)
    x1_ref[...] = (normal1 * dgain_ref[0:1] + dnb_ref[0:1]).astype(bf16)
    x1 = x1_ref[...]
    qkv[0] = (nn(x1, wqkv[0]) + qvb_ref[0:1]).astype(bf16)
    qkv[1] = nn(x1, wqkv[1]).astype(bf16)
    qkv[2] = (nn(x1, wqkv[2]) + qvb_ref[1:2]).astype(bf16)
    bias = bias_ref[0]
    for g in range(groups):
        cut = slice(g * 256, (g + 1) * 256)

        def keep(h, p):
            pt[g * heads + h] = p

        mix_ref[:, cut] = attend(
            qkv[0, :, cut], qkv[1, :, cut], qkv[2, :, cut], bias, heads, scale, keep
        ).astype(bf16)
    middle = stream + nn(mix_ref[...], wout[...]) + dob_ref[0:1]
    normal2, scale2 = norm_parts(middle)
    x2_ref[...] = (normal2 * dgain_ref[1:2] + dnb_ref[1:2]).astype(bf16)
    x2 = x2_ref[...]
    result = middle + dob_ref[1:2]
    for j in range(4):
        cut = slice(j * width, (j + 1) * width)
        hidden, slope = gelu_both(nn(x2, wup[j]) + upb_ref[:, cut])
        hid_ref[:, cut] = hidden.astype(bf16)
        dg[:, cut] = slope.astype(bf16)
        result = result + nn(hid_ref[:, cut], wdown[j])
    out_ref[...] = result

    cot = cot_ref[...]
    grad = 0.0
    sums_ref[...] = jnp.zeros(sums_ref.shape, f32)
    for j in range(4):
        cut = slice(j * width, (j + 1) * width)
        pre = nt(cot, wdown[j]) * dg[:, cut].astype(f32)
        gp_ref[:, cut] = pre.astype(bf16)
        block_sum = jnp.sum(pre, axis=0, keepdims=True)
        at = slot ^ j
        sums_ref[pl.ds(6 + (at >> 1), 1), pl.ds(pl.multiple_of((at & 1) * width, width), width)] = (
            block_sum
        )
        grad = grad + nt(gp_ref[:, cut], wup[j])
    cotf = cot.astype(f32)
    gmid = cotf + norm_back(normal2, scale2, dgain_ref[1:2], grad)
    gm_ref[...] = gmid.astype(bf16)
    sums_ref[1:2, :width] = jnp.sum(gmid, axis=0, keepdims=True)
    sums_ref[2:3, :width] = jnp.sum(cotf, axis=0, keepdims=True)
    sums_ref[2:3, width:] = jnp.sum(grad * normal2, axis=0, keepdims=True)
    sums_ref[4:5, :width] = jnp.sum(grad, axis=0, keepdims=True)
    gmix = nt(gm_ref[...], wout[...]).astype(bf16)
    grad = 0.0
    for g in range(groups):
        cut = slice(g * 256, (g + 1) * 256)
        three = attend_back(
            qkv[0, :, cut], qkv[1, :, cut], qkv[2, :, cut], gmix[:, cut],
            lambda h: pt[g * heads + h], heads, scale,
        )
        for c, part in enumerate(three):
            begin = c * width + g * 256
            low = part.astype(bf16)
            g3_ref[:, begin : begin + 256] = low
            grad = grad + nt(low, wqkv[c, :, cut])
        for c, row, base in ((0, 4, width), (2, 5, width)):
            total = jnp.sum(three[c], axis=0, keepdims=True)
            for i in range(256 // block):
                sums_ref[row : row + 1, place(g * (256 // block) + i, base)] = (
                    total[:, i * block : (i + 1) * block]
                )
    gstream = gmid + norm_back(normal1, scale1, dgain_ref[0:1], grad)
    sums_ref[3:4, width:] = jnp.sum(gstream, axis=0, keepdims=True)
    sums_ref[1:2, width:] = jnp.sum(grad * normal1, axis=0, keepdims=True)
    sums_ref[3:4, :width] = jnp.sum(grad, axis=0, keepdims=True)
    wide[...] = gstream
    for j in range(4):
        gz_ref[:, j * block : (j + 1) * block] = wide[:, place(j)].astype(bf16)
    ge = nt(gz_ref[...], wemb[...])
    ge_ref[...] = ge
    gel_ref[...] = ge.astype(bf16)
    sums_ref[0:1] = jnp.sum(ge, axis=0, keepdims=True)


def decoder_weights_body(x1_ref, x2_ref, hid_ref, mix_ref, gp_ref, gm_ref, g3_ref, gz_ref, encl_ref, cot_ref,
                         sent_ref, kept_ref):
    width = cot_ref.shape[1]
    block = width // 4
    cot, gm, x2 = cot_ref[...], gm_ref[...], x2_ref[...]
    piece, thin = width // 8, block // 8
    tall = encl_ref.shape[1] // 8
    top = 2 * piece + thin
    step = top + piece + thin

    def to(j):
        return sent_ref if j % 2 else kept_ref

    for j in (1, 3, 0, 2):
        w = to(j)
        i = j // 2
        cut = slice(j * width, (j + 1) * width)
        up = tn(x2, gp_ref[:, cut]).astype(bf16)
        down = tn(hid_ref[:, cut], cot).astype(bf16)
        out = tn(mix_ref[:, j * block : (j + 1) * block], gm).astype(bf16)
        for c in range(8):
            w[i, c * step : c * step + piece] = up[c * piece : (c + 1) * piece]
            w[i, c * step + piece : c * step + 2 * piece] = down[c * piece : (c + 1) * piece]
            w[i, c * step + 2 * piece : c * step + top] = out[c * thin : (c + 1) * thin]
    x1 = x1_ref[...]
    for k in range(3):
        full = tn(x1, g3_ref[:, k * width : (k + 1) * width]).astype(bf16)
        for j in range(4):
            for c in range(8):
                to(j)[j // 2, c * step + top : c * step + top + piece, k * block : (k + 1) * block] = (
                    full[c * piece : (c + 1) * piece, j * block : (j + 1) * block]
                )
    full = tn(encl_ref[...], gz_ref[...]).astype(bf16)
    for j in range(4):
        cut = slice(j * block, (j + 1) * block)
        for c in range(8):
            base = c * tall
            to(j)[j // 2, c * step + top : c * step + top + piece, 3 * block :] = full[base : base + piece, cut]
            base = base + piece
            for k in range(4):
                to(j)[j // 2, c * step + top + piece : (c + 1) * step, k * block : (k + 1) * block] = (
                    full[base + k * thin : base + (k + 1) * thin, cut]
                )


def pack_body(pick_ref, up_ref, down_ref, out_ref, qkv_ref, emb_ref, chunk_ref):
    piece, thin, block = up_ref.shape[0], out_ref.shape[0], emb_ref.shape[1]
    chunk_ref[:piece] = up_ref[...]
    chunk_ref[piece : 2 * piece] = down_ref[...]
    top = 2 * piece + thin
    chunk_ref[2 * piece : top] = out_ref[...]
    for c in range(3):
        chunk_ref[top : top + piece, c * block : (c + 1) * block] = qkv_ref[c]
    chunk_ref[top : top + piece, 3 * block :] = emb_ref[:piece]
    for c in range(4):
        base = piece + c * thin
        chunk_ref[top + piece :, c * block : (c + 1) * block] = emb_ref[base : base + thin]


def join_body(a_ref, b_ref, out_ref):
    rows = a_ref.shape[0]
    out_ref[:rows] = a_ref[...]
    out_ref[rows:] = b_ref[...]


def add_body(a_ref, b_ref, out_ref):
    out_ref[...] = (a_ref[...].astype(f32) + b_ref[...].astype(f32)).astype(out_ref.dtype)


def last_sums_body(slot_ref, *refs):
    terms, outs, total_ref = refs[:-12], refs[-12:-1], refs[-1]
    total = terms[0][...]
    for ref in terms[1:]:
        total = total + ref[...]
    total_ref[...] = total
    slot = slot_ref[0]
    e_qv, e_upb, e_ob, e_gain, e_nb, d_emb, d_qv, d_upb, d_ob, d_gain, d_nb = outs
    share, thin, width = e_qv.shape[1], d_qv.shape[1], d_emb.shape[1]
    e_qv[...] = total_ref[18:20, pl.ds(pl.multiple_of(slot * share, share), share)]
    e_upb[...] = total_ref[pl.ds(4 + slot, 1), :]
    e_ob[0:1] = total_ref[0:1]
    e_ob[1:2] = total_ref[8:9]
    e_gain[0:1] = total_ref[16:17]
    e_gain[1:2] = total_ref[1:2]
    e_nb[0:1] = total_ref[17:18]
    e_nb[1:2] = total_ref[2:3]
    d_ob[...] = total_ref[9:11, :width]
    d_gain[...] = total_ref[9:11, width:]
    d_nb[...] = total_ref[11:13, :width]
    d_emb[...] = total_ref[11:12, width:]
    d_qv[...] = total_ref[12:14, pl.ds(pl.multiple_of(width + slot * thin, thin), thin)]
    d_upb[...] = total_ref[pl.ds(14 + (slot >> 1), 1), pl.ds(pl.multiple_of((slot & 1) * width, width), width)]


def far_body(bit_ref, kept_ref, near_ref, out_ref):
    half = out_ref.shape[0]
    rows = pl.ds(pl.multiple_of(bit_ref[0] * half, half), half)
    out_ref[...] = (kept_ref[1, rows].astype(f32) + near_ref[1, rows].astype(f32)).astype(bf16)


def there_body(bit_ref, kept_ref, near_ref, *refs):
    *terms, out_ref = refs
    half = out_ref.shape[0]
    rows = pl.ds(pl.multiple_of(bit_ref[0] * half, half), half)
    total = kept_ref[0, rows].astype(f32) + near_ref[0, rows].astype(f32)
    for ref in terms:
        total = total + ref[...].astype(f32)
    out_ref[...] = total.astype(bf16)


def choose_body(bit_ref, keep_ref, got_ref, out_ref):
    @pl.when(bit_ref[0] == 0)
    def _():
        out_ref[...] = keep_ref[...]

    @pl.when(bit_ref[0] != 0)
    def _():
        out_ref[...] = got_ref[...]


def piece_of(refs, j):
    for ref in refs:
        if len(ref.shape) == 2:
            if j == 0:
                return ref[...]
            j -= 1
        elif j < ref.shape[0]:
            return ref[j]
        else:
            j -= ref.shape[0]


def tile_sum(xs, gs, more):
    acc = 0.0
    for j in range(4):
        acc = acc + tn(piece_of(xs, j), piece_of(gs, j))
    if not more:
        return [(slice(None), slice(None), acc)]
    rows, cols = acc.shape
    parts = [(slice(None), slice(0, cols), acc)]
    half, quarter = rows // 2, rows // 8
    wide = more[0].shape[1] // 4
    for c in range(2):
        for k in range(4):
            parts.append((
                slice(c * half + k * quarter, c * half + (k + 1) * quarter),
                slice(cols, cols + wide),
                more[0][c * quarter : (c + 1) * quarter, k * wide : (k + 1) * wide].astype(f32),
            ))
    return parts


def half_body(nx, ng, nm, pick_ref, *refs):
    xs, gs, more = refs[:nx], refs[nx : nx + ng], refs[nx + ng : nx + ng + nm]
    *add_ref, out_ref = refs[nx + ng + nm :]
    for rows, cols, value in tile_sum(xs, gs, more):
        if add_ref:
            value = value + add_ref[0][rows, cols].astype(f32)
        out_ref[rows, cols] = value.astype(bf16)


def weight_half(chain, xs, gs, more, pick, add=None):
    tile = xs[0].shape[-1] // 4
    out_cols = gs[0].shape[-1] + sum(m.shape[1] // 4 for m in more)

    def column(shape):
        lead = shape[:-1]
        return pl.BlockSpec(lead + (tile,), lambda i, p: (0,) * len(lead) + (p[i],))

    def whole(shape):
        return pl.BlockSpec(shape, lambda i, p: (0,) * len(shape))

    in_specs = [column(x.shape) for x in xs] + [whole(g.shape) for g in gs]
    in_specs += [pl.BlockSpec((tile // 4, m.shape[1]), lambda i, p: (p[i], 0)) for m in more]
    args = list(xs) + list(gs) + list(more)
    out_spec = pl.BlockSpec((tile, out_cols), lambda i, p: (i, 0))
    if add is not None:
        in_specs.append(out_spec)
        args.append(add)
    return chain(
        functools.partial(half_body, len(xs), len(gs), len(more)),
        [shaped((2 * tile, out_cols), bf16)],
        args,
        prefetch=pick,
        grid=(2,),
        specs=(in_specs, [out_spec]),
        limit=20,
    )[0]


def spread_body(writes, place_ref, *refs):
    sums = max(write[0] for write in writes) + 1
    out_refs = refs[2 * sums :]
    for i in range(8):
        for source, which, lead, first, every, row, rows, col, cols, at_col in writes:
            ref = refs[2 * source + i // 4]
            base = i % 4 * (ref.shape[0] // 4)
            at = place_ref[source] ^ i
            value = ref[base + row : base + row + rows, col : col + cols].astype(f32)
            to = pl.ds(pl.multiple_of(at * every + first, rows), rows)
            if lead is None:
                out_refs[which][to, at_col : at_col + cols] = value
            else:
                out_refs[which][lead, to] = value


def out_weight_body(*refs):
    mixes, gs, out_ref = refs[:3], refs[3:7], refs[7]
    acc = 0.0
    for j in range(4):
        acc = acc + tn(piece_of(mixes, j), piece_of(gs, j))
    out_ref[...] = acc.astype(bf16)


class Sum:
    def __init__(self, chain):
        self.chain = chain
        self.size = lax.axis_size("dp")
        me = lax.axis_index("dp").astype(jnp.int32)
        self.x, z = me & 1, me >> 1
        self.outer = jnp.where((z == 0) | (z == 3), 1, 0).astype(jnp.int32).reshape(1)
        self.place = 4 * self.x if self.size == 8 else jnp.int32(0)
        inward = [(0, 1), (3, 2)]
        self.inward = [(2 * a + x, 2 * b + x) for a, b in inward for x in range(2)]
        self.outward = [(b, a) for a, b in self.inward]
        self.middle = [(2 * a + x, 2 * b + x) for a, b in ((1, 2), (2, 1)) for x in range(2)]
        steps = [self.second, self.third, self.fourth, self.fifth]
        self.steps = iter(steps if self.size == 8 else [])

    def step(self):
        for todo in self.steps:
            todo()
            return

    def product(self, xs, gs, more=()):
        self.terms = (xs, gs, more)
        if self.size != 8:
            first = weight_half(self.chain, *self.terms, jnp.array([0, 1], jnp.int32))
            other = weight_half(self.chain, *self.terms, jnp.array([2, 3], jnp.int32))
            return self.general(jnp.concatenate([first, other], axis=0))
        there = 2 * (1 - self.x)
        self.got = swap(weight_half(self.chain, *self.terms, jnp.stack([there, there + 1])), "dp", 1)

    def shares(self, kept, near, there):
        self.terms = None
        self.held = (kept, near, there)
        if self.size == 8:
            half = shaped(there.shape, bf16)
            out = self.chain(there_body, [half], ((1 - self.x).reshape(1), kept, near, there), smem=1)[0]
            self.got = swap(out, "dp", 1)

    def other(self, mine):
        kept, near, there = self.held
        self.held = (kept, near, mine)
        if self.size != 8:
            total = kept[0].astype(f32) + near[0].astype(f32)
            total = total + jnp.concatenate([mine, there], axis=0).astype(f32)
            self.general(total.astype(bf16))

    def second(self):
        if self.terms is None:
            half = shaped(self.got.shape, bf16)
            self.keep = self.chain(there_body, [half], (self.x.reshape(1), *self.held, self.got), smem=1)[0]
        else:
            mine = 2 * self.x
            self.keep = weight_half(self.chain, *self.terms, jnp.stack([mine, mine + 1]), self.got)
        self.got = send(self.keep, "dp", self.inward)

    def plus(self):
        self.keep = self.chain(add_body, [shaped(self.keep.shape, bf16)], (self.keep, self.got))[0]

    def third(self):
        self.plus()
        self.got = send(self.keep, "dp", self.middle)

    def fourth(self):
        self.plus()
        self.got = send(self.keep, "dp", self.outward)

    def fifth(self):
        self.keep = self.chain(
            choose_body, [shaped(self.keep.shape, bf16)], (self.outer, self.keep, self.got), smem=1
        )[0]
        self.got = swap(self.keep, "dp", 1)

    def general(self, held):
        me = lax.axis_index("dp")
        bits = [1 << i for i in range(self.size.bit_length() - 1)]
        for bit in bits:
            mine = (me & bit) != 0
            half = held.shape[0] // 2
            other = lax.dynamic_slice_in_dim(held, jnp.where(mine, 0, half), half, 0)
            own = lax.dynamic_slice_in_dim(held, jnp.where(mine, half, 0), half, 0)
            held = (own.astype(f32) + swap(other, "dp", bit).astype(f32)).astype(bf16)
        for bit in reversed(bits):
            mine = (me & bit) != 0
            other = swap(held, "dp", bit)
            held = jnp.where(
                mine,
                jnp.concatenate([other, held], axis=0),
                jnp.concatenate([held, other], axis=0),
            )
        half = held.shape[0] // 2
        self.keep, self.got = held[:half], held[half:]


def per_device(
    tokens, segment_ids, gsd_index, enc_qkv, enc_qv_bias, enc_out_proj, enc_up, enc_up_bias,
    enc_down, enc_out_bias, enc_gain, enc_norm_bias, embed_weight, embed_bias, dec_qkv,
    dec_qv_bias, dec_out_proj, dec_up, dec_up_bias, dec_down, dec_out_bias, dec_gain,
    dec_norm_bias, cotangent,
):
    n, width = tokens.shape
    rows, length = segment_ids.shape
    assert rows == 4 and n == length == 256 and lax.axis_size("mp") == 4
    share, ff = enc_qkv.shape[2], enc_up.shape[1]
    dwidth, dff = cotangent.shape[1], dec_up.shape[1] * 4
    dshare = dwidth // 4
    heads = share // (width // HEADS)
    scale = (width // HEADS) ** -0.5
    slot = lax.axis_index("mp").astype(jnp.int32)
    at = slot.reshape(1)
    chain = Chain()
    dec = Sum(chain)
    group = lax.axis_index("dp").astype(jnp.int32)
    home = 4 * (group & 1) + (group & 2) + ((group >> 2) & 1) if dec.size == 8 else jnp.int32(0)

    def low(*dims):
        return shaped(dims, bf16)

    def full(*dims):
        return shaped(dims, f32)

    def waves(size):
        half = size // 2
        return jnp.power(10000.0, -jnp.arange(half, dtype=f32) / half).reshape(1, half)

    def near(value):
        return swap(value, "mp", 1)

    def far(value):
        return swap(value, "mp", 2)

    pack_rows = 3 * dwidth + 2 * dshare
    decoder_weights = [in_hbm(w) for w in (dec_up, dec_down, dec_out_proj, dec_qkv, embed_weight)]

    def pack(pick, steps):
        def block(shape):
            if len(shape) == 3:
                return pl.BlockSpec((shape[0], shape[1] // 8, shape[2]), lambda i, p: (0, p[i], 0))
            return pl.BlockSpec((shape[0] // 8, shape[1]), lambda i, p: (p[i], 0))

        rows = pack_rows // 8
        return chain(
            pack_body,
            [low(steps * rows, dwidth)],
            decoder_weights,
            prefetch=pick,
            grid=(steps,),
            specs=([block(w.shape) for w in decoder_weights], [pl.BlockSpec((rows, dwidth), lambda i, p: (i, 0))]),
        )[0]

    split = dec.size == 8
    got = far(pack(home.reshape(1), 1)) if split else None
    normed = chain(
        start_body,
        [low(n, width)],
        (at, in_hbm(segment_ids), in_hbm(gsd_index), in_hbm(tokens), in_hbm(enc_gain), in_hbm(enc_norm_bias), waves(width)),
        smem=1,
        scratch=[pltpu.VMEM((n, width), f32)],
    )[0]
    x = [normed, near(normed), far(normed)]
    bias_a, bias_b = chain(mask_body, [kept(full(2, n, n)), kept(full(2, n, n))], (at, in_hbm(segment_ids)), smem=1)

    def attention(bias, first, *blocks):
        count = len(blocks)
        return chain(
            functools.partial(attn_body, scale, heads, first),
            [kept(low(count, n, share))] * 3
            + [kept(low(count, heads, n, n)), kept(low(count, n, share))]
            + [low(n, width)] * count,
            (*blocks, bias, enc_qkv, enc_qv_bias, enc_out_proj),
        )

    def add(a, b):
        return chain(add_body, [shaped(a.shape, a.dtype)], (a, b))[0]

    def join(a, b):
        return chain(join_body, [low(a.shape[0] + b.shape[0], a.shape[1])], (a, b))[0]

    def both(blocks):
        blocks[2] = chain.pin(blocks[2])
        blocks.append(near(blocks[2]))

    *saved_a, mixa, part0, part1 = attention(bias_a, 0, x[0], x[1])
    part1 = near(part1)
    vector = jnp.concatenate([dec_qv_bias.reshape(-1), dec_up_bias]).reshape(1, -1)
    vector = chain.pin(vector)
    vectors = [vector, near(vector), far(vector)]
    part1 = chain.pin(part1)
    both(x)
    chain.gap()
    chain.gap()
    *saved_d, mixd, part3 = attention(bias_b, 1, x[3])
    part3 = near(part3)
    *saved_c, mixc, part2 = attention(bias_b, 0, x[2])
    if split:
        got = chain.pin(got)
        more = swap(got, "dp", 4)
    part2 = far(add(part2, part3))
    vectors[1] = chain.pin(vectors[1])
    both(vectors)
    packed = pack(jnp.arange(8, dtype=jnp.int32), 8)
    packed_near = near(packed)
    pos, stream = chain(
        stream_body,
        [kept(full(n, dwidth)), full(n, width)],
        (at, in_hbm(segment_ids), in_hbm(gsd_index), in_hbm(tokens), in_hbm(embed_bias.reshape(1, -1)), waves(width), waves(dwidth)),
        smem=1,
    )
    if split:
        got = join(got, more)
        more = swap(got, "dp", 2)
    else:
        got = far(packed)
    middle, normed2 = chain(
        mid_body,
        [kept(full(n, width)), low(n, width)],
        (stream, part0, part1, part2, enc_out_bias, enc_gain, enc_norm_bias),
    )
    y = [normed2, near(normed2), far(normed2)]
    packed_near = chain.pin(packed_near)
    vectors[3] = chain.pin(vectors[3])
    if split:
        got = join(got, more)
        more = swap(got, "dp", 1)
    else:
        more = got[pack_rows // 2 :]
        got = got[: pack_rows // 2]

    def feed(*blocks):
        count = len(blocks)
        return chain(
            mlp_body,
            [kept(low(count, n, ff))] * 2 + [low(n, width)] * count,
            (*blocks, enc_up, enc_up_bias.reshape(1, -1), enc_down),
        )

    hida, dga, part0, part1 = feed(y[0], y[1])
    part1 = near(part1)
    far_weights = [got, more]
    near_weights = [near(got)]
    both(y)
    part1 = chain.pin(part1)
    near_weights[0] = chain.pin(near_weights[0])
    hidd, dgd, part3 = feed(y[3])
    part3 = near(part3)
    hidc, dgc, part2 = feed(y[2])
    part2 = far(add(part2, part3))
    far_weights[1] = chain.pin(more)
    near_weights.append(near(far_weights[1]))
    part2 = chain.pin(part2)

    (enc_low, output, x1, x2, hid, mix, gp, gm, g3, gz, ge_low, ge, dec_sums) = chain(
        decoder_body,
        [kept(o) for o in (low(n, width), full(n, dwidth), low(n, dwidth), low(n, dwidth), low(n, dff),
                           low(n, dwidth), low(n, dff), low(n, dwidth), low(n, 3 * dwidth), low(n, dwidth))]
        + [low(n, width), kept(full(n, width)), kept(full(8, width))],
        (jnp.stack([slot, home]), middle, part0, part1, part2, enc_out_bias, packed, packed_near,
         *far_weights, *near_weights, *vectors, pos, bias_a, dec_out_bias, dec_gain,
         dec_norm_bias, cotangent),
        smem=1,
        scratch=[
            pltpu.VMEM((4, dwidth, dwidth), bf16), pltpu.VMEM((4, dwidth, dwidth), bf16),
            pltpu.VMEM((3, dwidth, dwidth), bf16), pltpu.VMEM((dwidth, dwidth), bf16),
            pltpu.VMEM((width, dwidth), bf16), pltpu.VMEM((DHEADS, n, n), bf16),
            pltpu.VMEM((n, dff), bf16), pltpu.VMEM((3, n, dwidth), bf16), pltpu.VMEM((n, dwidth), f32),
            pltpu.VMEM((2, dwidth), f32), pltpu.VMEM((1, dff), f32),
        ],
        limit=40,
    )
    g = [ge_low, near(ge_low), far(ge_low)]

    def feed_back(slope, *blocks):
        count = len(blocks)
        return chain(
            mlp_back_body,
            [kept(low(count, n, ff)), kept(full(1, ff))] + [low(n, width)] * count,
            (*blocks, slope, enc_up, enc_down),
        )

    def attention_back(saved, *blocks):
        count = len(blocks)
        return chain(
            functools.partial(attn_back_body, scale, heads),
            [kept(low(count, n, 3 * share)), kept(full(2, share))] + [low(n, width)] * count,
            (*blocks, *saved, enc_qkv, enc_out_proj),
        )

    def far_share(bit):
        return far(chain(far_body, [low(pack_rows // 2, dwidth)], (bit.reshape(1), kept_share, sent), smem=1)[0])

    def hbm(*values):
        return [in_hbm(v) for v in values]

    down, up, attn = Sum(chain), Sum(chain), Sum(chain)

    def finish(sums, outs, writes):
        return chain(
            functools.partial(spread_body, writes),
            [kept(full(*dims)) for dims in outs],
            (jnp.stack([f.place for f in sums]), *[v for f in sums for v in (f.keep, f.got)]),
            smem=1,
            limit=24,
        )

    chain.gap()
    gpa, upa, part0, part1 = feed_back(dga, g[0], g[1])
    part1 = near(part1)
    sent, kept_share = chain(
        decoder_weights_body,
        [low(2, pack_rows, dwidth), kept(low(2, pack_rows, dwidth))],
        (x1, x2, hid, mix, gp, gm, g3, gz, enc_low, cotangent),
        limit=24,
    )
    sent = near(sent)
    part1 = chain.pin(part1)
    both(g)
    gpc, upc, part2 = feed_back(dgc, g[2])
    down.product(hbm(hida, hidc, hidd), g)
    gpd, upd, part3 = feed_back(dgd, g[3])
    part3 = near(part3)
    chain.gap()
    part2 = far(add(part2, part3))
    chain.gap()
    grad_middle, gm_low, sums_mid = chain(
        mlp_end_body,
        [kept(full(n, width)), low(n, width), kept(full(16, width))],
        (at, ge, part0, part1, part2, middle, enc_gain, upa, upc, upd, dec_sums),
        smem=1,
    )
    m = [gm_low, near(gm_low), far(gm_low)]
    up.product(hbm(*y), hbm(gpa, gpc, gpd))
    down.step()
    g3a, sa, part0, part1 = attention_back(saved_a, m[0], m[1])
    part1 = near(part1)
    chain.gap()
    part1 = chain.pin(part1)
    there = far_share(1 - dec.x)
    both(m)
    g3c, sc, part2 = attention_back(saved_c, m[2])
    out_full = chain(out_weight_body, [low(share, width)], (mixa, mixc, mixd, *m))[0]
    g3d, sd, part3 = attention_back(saved_d, m[3])
    part3 = near(part3)
    attn.product(hbm(*x), hbm(g3a, g3c, g3d), [out_full])
    part2 = far(add(part2, part3))
    down.step()
    up.step()
    grad_tokens, sums = chain(
        last_body,
        [kept(full(n, width)), full(24, width)],
        (at, grad_middle, part0, part1, part2, stream, enc_gain, sa, sc, sd, sums_mid),
        smem=1,
    )
    dec.shares(kept_share, sent, there)
    dec.other(far_share(dec.x))
    down.step()
    attn.step()
    up.step()
    hops = [("mp", 1), ("mp", 2)] + [("dp", 1 << i) for i in range(dec.size.bit_length() - 1)]
    hops = iter(hops)

    def hop(total, got=None):
        if got is not None:
            total = add(total, got)
        for axis, mask in hops:
            return total, swap(total, axis, mask)
        return total, None

    small = hop(sums)
    dec.step()
    down.step()
    small = hop(*small)
    up.step()
    attn.step()
    small = hop(*small)
    e_down = finish((down,), [(ff, width)], [(0, 0, None, 0, ff // 8, 0, ff // 8, 0, width, 0)])[0]
    dec.step()
    up.step()
    attn.step()
    small = hop(*small)
    dec.step()
    e_up = finish((up,), [(width, ff)], [(0, 0, None, 0, width // 8, 0, width // 8, 0, ff, 0)])[0]
    attn.step()
    small = hop(*small)
    while small[1] is not None:
        sums = small
        small = hop(*small)
    vectors = chain(
        last_sums_body,
        [full(2, share), full(1, ff), full(2, width), full(2, width), full(2, width), full(1, dwidth),
         full(2, dshare), full(1, dff // 4), full(2, dwidth), full(2, dwidth), full(2, dwidth)],
        (at, *sums),
        smem=1,
        scratch=[pltpu.VMEM((24, width), f32)],
    )
    dec.step()
    rows, fold = width // 8, share // 8
    e_qkv, e_out = finish(
        (attn,),
        [(3, width, share), (share, width)],
        [(0, 0, c, 0, rows, 0, rows, c * share, share, 0) for c in range(3)]
        + [(0, 1, None, 0, fold, k * fold, fold, 3 * share, width // 4, k * (width // 4)) for k in range(4)],
    )
    part, thin, tall = dwidth // 8, dshare // 8, width // 8
    top = 2 * part + thin
    d_up, d_down, d_out, d_qkv, e_embed = finish(
        (dec,),
        [(dwidth, dwidth), (dwidth, dwidth), (dshare, dwidth), (3, dwidth, dshare), (width, dshare)],
        [
            (0, 0, None, 0, part, 0, part, 0, dwidth, 0),
            (0, 1, None, 0, part, part, part, 0, dwidth, 0),
            (0, 2, None, 0, thin, 2 * part, thin, 0, dwidth, 0),
        ]
        + [(0, 3, c, 0, part, top, part, c * dshare, dshare, 0) for c in range(3)]
        + [(0, 4, None, 0, tall, top, part, 3 * dshare, dshare, 0)]
        + [(0, 4, None, part + k * thin, tall, top + part, thin, k * dshare, dshare, 0) for k in range(4)],
    )
    e_qv, e_upb, e_ob, e_gain, e_nb, d_emb, d_qv, d_upb, d_ob, d_gain, d_nb = vectors

    return (
        output,
        grad_tokens,
        e_qkv,
        e_qv,
        e_out,
        e_up,
        e_upb.reshape(-1),
        e_down,
        e_ob,
        e_gain,
        e_nb,
        e_embed,
        d_emb.reshape(-1),
        d_qkv,
        d_qv,
        d_out,
        d_up,
        d_upb.reshape(-1),
        d_down,
        d_ob,
        d_gain,
        d_nb,
    )


def solution(mesh):
    return jax.shard_map(
        per_device,
        mesh=mesh,
        in_specs=(
            P(("dp", "mp"), None),
            P("dp", None),
            P("dp", None),
            P(None, None, "mp"),
            P(None, "mp"),
            P("mp", None),
            P(None, "mp"),
            P("mp"),
            P("mp", None),
            P(),
            P(),
            P(),
            P(None, "mp"),
            P(),
            P(None, None, "mp"),
            P(None, "mp"),
            P("mp", None),
            P(None, "mp"),
            P("mp"),
            P("mp", None),
            P(),
            P(),
            P(),
            P(("dp", "mp"), None),
        ),
        out_specs=(
            P(("dp", "mp"), None),
            P(("dp", "mp"), None),
            P(None, None, "mp"),
            P(None, "mp"),
            P("mp", None),
            P(None, "mp"),
            P("mp"),
            P("mp", None),
            P(),
            P(),
            P(),
            P(None, "mp"),
            P(),
            P(None, None, "mp"),
            P(None, "mp"),
            P("mp", None),
            P(None, "mp"),
            P("mp"),
            P("mp", None),
            P(),
            P(),
            P(),
        ),
        check_vma=False,
    )
```

```python
import functools
import math

import jax
import jax.numpy as jnp
from jax import lax
from jax.experimental import pallas as pl
from jax.experimental.pallas import tpu as pltpu
from jax.sharding import PartitionSpec as P

HEADS = 16
DHEADS = 16
norm_eps = 1e-06
f32 = jnp.float32
bf16 = jnp.bfloat16
MIB = 1 << 20
VMEM = pl.BlockSpec(memory_space=pltpu.VMEM)
SMEM = pl.BlockSpec(memory_space=pltpu.SMEM)
COST = pl.CostEstimate(flops=10**10, bytes_accessed=10**8, transcendentals=0)


def shaped(dims, kind):
    return jax.ShapeDtypeStruct(dims, kind)


def kept(shape):
    return pltpu.HBM(shape.shape, shape.dtype)


def in_hbm(value):
    return pltpu.with_memory_space_constraint(value, pltpu.HBM)


class Chain:
    token = jax.ShapeDtypeStruct((8, 128), jnp.float32)

    def __init__(self):
        self.last = None

    def __call__(self, body, outs, args, smem=0, scratch=(), limit=16, prefetch=None, grid=None, specs=None):
        args, outs = list(args), list(outs)
        extra = self.last is not None
        ins = len(args) + (prefetch is not None)
        many = len(outs)

        def inner(*refs):
            out_refs = refs[ins + extra :]
            out_refs[many][...] = jnp.zeros((8, 128), f32)
            return body(*refs[:ins], *out_refs[:many], *out_refs[many + 1 :])

        if extra:
            args.append(self.last)
        tail = [pl.BlockSpec(memory_space=pl.ANY)] * extra
        params = pltpu.CompilerParams(vmem_limit_bytes=limit * MIB)
        if prefetch is None:
            got = pl.pallas_call(
                inner,
                out_shape=outs + [self.token],
                in_specs=[SMEM] * smem + [VMEM] * (len(args) - smem - extra) + tail,
                out_specs=[VMEM] * (many + 1),
                scratch_shapes=scratch,
                compiler_params=params,
                cost_estimate=COST,
            )(*args)
        else:
            got = pl.pallas_call(
                inner,
                out_shape=outs + [self.token],
                grid_spec=pltpu.PrefetchScalarGridSpec(
                    num_scalar_prefetch=1,
                    grid=grid,
                    in_specs=specs[0] + tail,
                    out_specs=specs[1] + [pl.BlockSpec((8, 128), lambda i, p: (0, 0))],
                ),
                compiler_params=params,
                cost_estimate=COST,
            )(prefetch, *args)
        *got, self.last = got
        return got

    def pin(self, value):
        def body(value_ref, last_ref, out_ref, token_ref):
            token_ref[...] = jnp.zeros((8, 128), f32)

        any_space = pl.BlockSpec(memory_space=pl.ANY)
        got, self.last = pl.pallas_call(
            body,
            out_shape=[shaped(value.shape, value.dtype), self.token],
            in_specs=[any_space, any_space],
            out_specs=[any_space, VMEM],
            input_output_aliases={0: 0},
            compiler_params=pltpu.CompilerParams(vmem_limit_bytes=MIB),
            cost_estimate=COST,
        )(value, self.last)
        return got

    def gap(self):
        self(lambda: None, [], [], limit=1)


def nn(a, b):
    return lax.dot_general(a, b, (((1,), (0,)), ((), ())), preferred_element_type=f32)


def nt(a, b):
    return lax.dot_general(a, b, (((1,), (1,)), ((), ())), preferred_element_type=f32)


def tn(a, b):
    return lax.dot_general(a, b, (((0,), (0,)), ((), ())), preferred_element_type=f32)


def send(value, axis, pairs):
    return lax.ppermute(value, axis, pairs)


def swap(value, axis, mask):
    size = lax.axis_size(axis)
    return lax.ppermute(value, axis, [(i, i ^ mask) for i in range(size)])


def norm_parts(values):
    average = jnp.mean(values, axis=-1, keepdims=True)
    centred = values - average
    variance = jnp.mean(centred * centred, axis=-1, keepdims=True)
    scale = lax.rsqrt(variance + norm_eps)
    return centred * scale, scale


def norm_back(normal, scale, gain, grad):
    wide = grad * gain
    one = jnp.mean(wide, axis=-1, keepdims=True)
    two = jnp.mean(wide * normal, axis=-1, keepdims=True)
    return scale * (wide - one - normal * two)


def gelu_both(v):
    slope = math.sqrt(2.0 / math.pi)
    square = v * v
    t = jnp.tanh(slope * v * (1.0 + 0.044715 * square))
    half = 0.5 * (1.0 + t)
    return v * half, half + 0.5 * slope * v * (1.0 - t * t) * (1.0 + 3.0 * 0.044715 * square)


def sin_cos(x):
    turn = jnp.floor(x * (2.0 / math.pi) + 0.5)
    r = ((x - turn * 1.5703125) - turn * 4.837512969970703125e-4) - turn * 7.54978995489188216e-8
    z = r * r
    s = r + r * z * (-1.6666654611e-1 + z * (8.3321608736e-3 + z * -1.9515295891e-4))
    c = 1.0 - 0.5 * z + z * z * (
        4.166664568298827e-2 + z * (-1.388731625493765e-3 + z * 2.443315711809948e-5)
    )
    quarter = turn.astype(jnp.int32)
    odd = (quarter & 1) != 0
    sine = jnp.where(odd, c, s)
    cosine = jnp.where(odd, s, c)
    sine = jnp.where((quarter & 2) != 0, -sine, sine)
    cosine = jnp.where(((quarter + 1) & 2) != 0, -cosine, cosine)
    return sine, cosine


def head_masks(heads):
    size = 256 // heads
    lane = lax.broadcasted_iota(jnp.int32, (1, 256), 1)
    return [
        jnp.where((lane >= h * size) & (lane < (h + 1) * size), 1.0, 0.0).astype(bf16)
        for h in range(heads)
    ]


def attend(q, k, v, bias, heads, scale, keep):
    size = 256 // heads
    vt = v.astype(f32).T.astype(bf16)
    mixes = []
    for h, mask in enumerate(head_masks(heads)):
        s = nt(k, q * mask) + bias
        top = jnp.max(s, axis=0, keepdims=True)
        p = jnp.exp2((s - top) * (scale * math.log2(math.e)))
        total = jnp.sum(p, axis=0, keepdims=True)
        p = (p * (1.0 / total)).astype(bf16)
        keep(h, p)
        mixes.append(nn(vt[h * size : (h + 1) * size], p))
    return jnp.concatenate(mixes, axis=0).T


def attend_back(q, k, v, gm, probs, heads, scale):
    size = 256 // heads
    kt = k.astype(f32).T.astype(bf16)
    gq, gk, gv = [], 0.0, 0.0
    for h, mask in enumerate(head_masks(heads)):
        gmh = gm * mask
        p = probs(h)
        wide = p.astype(f32)
        t = wide * nt(v, gmh)
        gs = (t - wide * jnp.sum(t, axis=0, keepdims=True)).astype(bf16)
        gk = gk + nn(gs, q * mask)
        gv = gv + nn(p, gmh)
        gq.append(nn(kt[h * size : (h + 1) * size], gs))
    return jnp.concatenate(gq, axis=0).T * scale, gk * scale, gv


def place_of(slot, seg_ref, gsd_ref):
    n = seg_ref.shape[1]
    across = jnp.broadcast_to(seg_ref[pl.ds(slot, 1), :].astype(f32), (n, n))
    earlier = lax.broadcasted_iota(jnp.int32, (n, n), 1) < lax.broadcasted_iota(jnp.int32, (n, n), 0)
    rank = jnp.sum(jnp.where((across == across.T) & earlier, 1.0, 0.0), axis=1, keepdims=True)
    index = jnp.broadcast_to(gsd_ref[pl.ds(slot, 1), :].astype(f32), (n, n)).T[:, :1]
    return rank * (0.5 + 0.25 * index)


def start_body(slot_ref, seg_ref, gsd_ref, tokens_ref, gain_ref, shift_ref, wf_ref, normed_ref, stream_ref):
    place = place_of(slot_ref[0], seg_ref, gsd_ref)
    half = wf_ref.shape[1]
    sine, cosine = sin_cos(place * wf_ref[...])
    stream_ref[:, :half] = tokens_ref[:, :half].astype(f32) + sine
    stream_ref[:, half:] = tokens_ref[:, half:].astype(f32) + cosine
    normal, _ = norm_parts(stream_ref[...])
    normed_ref[...] = (normal * gain_ref[0:1] + shift_ref[0:1]).astype(bf16)


def mask_body(slot_ref, seg_ref, bias_a_ref, bias_b_ref):
    slot = slot_ref[0]
    n = seg_ref.shape[1]
    for j in range(4):
        across = jnp.broadcast_to(seg_ref[pl.ds(slot ^ j, 1), :].astype(f32), (n, n))
        (bias_a_ref, bias_b_ref)[j // 2][j % 2] = jnp.where(across == across.T, 0.0, -1e30)


def stream_body(slot_ref, seg_ref, gsd_ref, tokens_ref, eb_ref, wf_ref, nf_ref, pos_ref, stream_ref):
    place = place_of(slot_ref[0], seg_ref, gsd_ref)
    half = wf_ref.shape[1]
    sine, cosine = sin_cos(place * wf_ref[...])
    stream_ref[:, :half] = tokens_ref[:, :half].astype(f32) + sine
    stream_ref[:, half:] = tokens_ref[:, half:].astype(f32) + cosine
    half = nf_ref.shape[1]
    sine, cosine = sin_cos(place * nf_ref[...])
    pos_ref[:, :half] = sine + eb_ref[:, :half]
    pos_ref[:, half:] = cosine + eb_ref[:, half:]


def attn_body(scale, heads, first, *refs):
    count = (len(refs) - 9) // 2
    xs, rest = refs[:count], refs[count:]
    bias_ref, w_ref, qvb_ref, o_ref, q_ref, k_ref, v_ref, p_ref, mix_ref = rest[:9]
    for r, (x_ref, part_ref) in enumerate(zip(xs, rest[9:])):
        x = x_ref[...]
        q = (nn(x, w_ref[0]) + qvb_ref[0:1]).astype(bf16)
        k = nn(x, w_ref[1]).astype(bf16)
        v = (nn(x, w_ref[2]) + qvb_ref[1:2]).astype(bf16)
        q_ref[r], k_ref[r], v_ref[r] = q, k, v

        def keep(h, p):
            p_ref[r, h] = p

        mix = attend(q, k, v, bias_ref[first + r], heads, scale, keep).astype(bf16)
        mix_ref[r] = mix
        part_ref[...] = nn(mix, o_ref[...]).astype(bf16)


def attn_back_body(scale, heads, *refs):
    count = (len(refs) - 8) // 2
    gs, rest = refs[:count], refs[count:]
    q_ref, k_ref, v_ref, p_ref, w_ref, o_ref, g3_ref, sums_ref = rest[:8]
    total_q, total_v = 0.0, 0.0
    for r, (g_ref, part_ref) in enumerate(zip(gs, rest[8:])):
        gm = nt(g_ref[...], o_ref[...]).astype(bf16)
        gq, gk, gv = attend_back(
            q_ref[r], k_ref[r], v_ref[r], gm, lambda h: p_ref[r, h], heads, scale
        )
        total_q = total_q + jnp.sum(gq, axis=0, keepdims=True)
        total_v = total_v + jnp.sum(gv, axis=0, keepdims=True)
        acc = 0.0
        for c, g in enumerate((gq, gk, gv)):
            low = g.astype(bf16)
            g3_ref[r, :, c * 256 : (c + 1) * 256] = low
            acc = acc + nt(low, w_ref[c])
        part_ref[...] = acc.astype(bf16)
    sums_ref[0:1] = total_q
    sums_ref[1:2] = total_v


def mid_body(stream_ref, p_ref, near_ref, far_ref, ob_ref, gain_ref, shift_ref, mid_ref, normed_ref):
    total = p_ref[...].astype(f32) + near_ref[...].astype(f32) + far_ref[...].astype(f32)
    middle = stream_ref[...] + total + ob_ref[0:1]
    mid_ref[...] = middle
    normal, _ = norm_parts(middle)
    normed_ref[...] = (normal * gain_ref[1:2] + shift_ref[1:2]).astype(bf16)


def mlp_body(*refs):
    count = (len(refs) - 5) // 2
    xs, rest = refs[:count], refs[count:]
    up_ref, ub_ref, down_ref, hid_ref, dg_ref = rest[:5]
    width = up_ref.shape[1]
    for r, (x_ref, part_ref) in enumerate(zip(xs, rest[5:])):
        x = x_ref[...]
        for c in range(0, width, 256):
            cut = slice(c, c + 256)
            hidden, slope = gelu_both(nn(x, up_ref[:, cut]) + ub_ref[:, cut])
            hid_ref[r, :, cut] = hidden.astype(bf16)
            dg_ref[r, :, cut] = slope.astype(bf16)
        hidden = hid_ref[r]
        for c in range(0, down_ref.shape[1], 512):
            cut = slice(c, c + 512)
            part_ref[:, cut] = nn(hidden, down_ref[:, cut]).astype(bf16)


def mlp_back_body(*refs):
    count = (len(refs) - 5) // 2
    gs, rest = refs[:count], refs[count:]
    dg_ref, up_ref, down_ref, gp_ref, sums_ref = rest[:5]
    width = up_ref.shape[1]
    for r, (g_ref, part_ref) in enumerate(zip(gs, rest[5:])):
        g = g_ref[...]
        for c in range(0, width, 256):
            cut = slice(c, c + 256)
            grad = nt(g, down_ref[cut]) * dg_ref[r, :, cut].astype(f32)
            gp_ref[r, :, cut] = grad.astype(bf16)
            total = jnp.sum(grad, axis=0, keepdims=True)
            sums_ref[:, cut] = total if r == 0 else sums_ref[:, cut] + total
        gp = gp_ref[r]
        for c in range(0, up_ref.shape[0], 512):
            cut = slice(c, c + 512)
            part_ref[:, cut] = nt(gp, up_ref[cut]).astype(bf16)


def mlp_end_body(slot_ref, ge_ref, p_ref, near_ref, far_ref, mid_ref, gain_ref, ua_ref, ub_ref, uc_ref, dec_ref,
                 gmid_ref, gm_ref, pack_ref):
    slot = slot_ref[0]
    grad = p_ref[...].astype(f32) + near_ref[...].astype(f32) + far_ref[...].astype(f32)
    normal, scale = norm_parts(mid_ref[...])
    gmid = ge_ref[...] + norm_back(normal, scale, gain_ref[1:2], grad)
    gmid_ref[...] = gmid
    gm_ref[...] = gmid.astype(bf16)
    pack_ref[...] = jnp.zeros(pack_ref.shape, f32)
    pack_ref[0:1] = jnp.sum(gmid, axis=0, keepdims=True)
    pack_ref[1:2] = jnp.sum(grad * normal, axis=0, keepdims=True)
    pack_ref[2:3] = jnp.sum(grad, axis=0, keepdims=True)
    pack_ref[pl.ds(4 + slot, 1), :] = ua_ref[...] + ub_ref[...] + uc_ref[...]
    pack_ref[8:16] = dec_ref[...]


def last_body(slot_ref, gmid_ref, p_ref, near_ref, far_ref, stream_ref, gain_ref, sa_ref, sb_ref, sc_ref, mid_ref,
              gtok_ref, pack_ref):
    slot = slot_ref[0]
    grad = p_ref[...].astype(f32) + near_ref[...].astype(f32) + far_ref[...].astype(f32)
    normal, scale = norm_parts(stream_ref[...])
    gtok_ref[...] = gmid_ref[...] + norm_back(normal, scale, gain_ref[0:1], grad)
    pack_ref[:16] = mid_ref[...]
    pack_ref[16:] = jnp.zeros((8, pack_ref.shape[1]), f32)
    pack_ref[16:17] = jnp.sum(grad * normal, axis=0, keepdims=True)
    pack_ref[17:18] = jnp.sum(grad, axis=0, keepdims=True)
    share = sa_ref.shape[1]
    place = pl.ds(pl.multiple_of(slot * share, share), share)
    pack_ref[18:20, place] = sa_ref[...] + sb_ref[...] + sc_ref[...]


def decoder_body(slot_ref, mid_ref, p_ref, near_ref, far_ref, eob_ref, own_ref, by_ref, fa_ref, fb_ref, na_ref, nb_ref,
                 b0_ref, b1_ref, b2_ref, b3_ref, pos_ref, bias_ref, dob_ref, dgain_ref, dnb_ref, cot_ref,
                 encl_ref, out_ref, x1_ref, x2_ref, hid_ref, mix_ref, gp_ref, gm_ref, g3_ref, gz_ref,
                 gel_ref, ge_ref, sums_ref,
                 wup, wdown, wqkv, wout, wemb, pt, dg, qkv, wide, qvb_ref, upb_ref):
    slot, home = slot_ref[0], slot_ref[1]
    width = cot_ref.shape[1]
    block = width // 4
    heads = DHEADS * 256 // width
    groups = width // 256
    scale = (width // DHEADS) ** -0.5

    def place(j, base=0):
        return pl.ds(pl.multiple_of(base + (slot ^ j) * block, block), block)

    for j, ref in enumerate((b0_ref, b1_ref, b2_ref, b3_ref)):
        for c in range(2):
            qvb_ref[c : c + 1, j * block : (j + 1) * block] = ref[:, c * block : (c + 1) * block]
        upb_ref[:, j * width : (j + 1) * width] = ref[:, 2 * block :]
    piece, thin, tall = width // 8, block // 8, 2 * width // 8
    top = 2 * piece + thin
    step = top + piece + thin
    for j, (low_ref, high_ref) in enumerate(
        ((own_ref, own_ref), (by_ref, by_ref), (fa_ref, fb_ref), (na_ref, nb_ref))
    ):
        cut = slice(j * block, (j + 1) * block)
        for i in range(8):
            ref = (low_ref, high_ref)[i // 4]
            base = (i if j < 2 else i % 4) * step
            chunk = i if j < 2 else home ^ i

            def rows(size):
                return pl.ds(pl.multiple_of(chunk * size, size), size)

            wup[j, rows(piece)] = ref[base : base + piece]
            wdown[j, rows(piece)] = ref[base + piece : base + 2 * piece]
            wout[pl.ds(pl.multiple_of(j * block + chunk * thin, thin), thin)] = (
                ref[base + 2 * piece : base + top]
            )
            for c in range(3):
                wqkv[c, rows(piece), cut] = ref[base + top : base + top + piece, c * block : (c + 1) * block]
            wemb[pl.ds(pl.multiple_of(chunk * tall, tall), piece), cut] = (
                ref[base + top : base + top + piece, 3 * block :]
            )
            for c in range(4):
                wemb[pl.ds(pl.multiple_of(chunk * tall + piece + c * thin, thin), thin), cut] = (
                    ref[base + top + piece : base + step, c * block : (c + 1) * block]
                )
    encoded = mid_ref[...] + eob_ref[1:2]
    encoded = encoded + p_ref[...].astype(f32) + near_ref[...].astype(f32) + far_ref[...].astype(f32)
    encl_ref[...] = encoded.astype(bf16)
    embedded = nn(encl_ref[...], wemb[...])
    for j in range(4):
        wide[:, place(j)] = embedded[:, j * block : (j + 1) * block]
    stream = wide[...] + pos_ref[...]
    normal1, scale1 = norm_parts(stream)
    x1_ref[...] = (normal1 * dgain_ref[0:1] + dnb_ref[0:1]).astype(bf16)
    x1 = x1_ref[...]
    qkv[0] = (nn(x1, wqkv[0]) + qvb_ref[0:1]).astype(bf16)
    qkv[1] = nn(x1, wqkv[1]).astype(bf16)
    qkv[2] = (nn(x1, wqkv[2]) + qvb_ref[1:2]).astype(bf16)
    bias = bias_ref[0]
    for g in range(groups):
        cut = slice(g * 256, (g + 1) * 256)

        def keep(h, p):
            pt[g * heads + h] = p

        mix_ref[:, cut] = attend(
            qkv[0, :, cut], qkv[1, :, cut], qkv[2, :, cut], bias, heads, scale, keep
        ).astype(bf16)
    middle = stream + nn(mix_ref[...], wout[...]) + dob_ref[0:1]
    normal2, scale2 = norm_parts(middle)
    x2_ref[...] = (normal2 * dgain_ref[1:2] + dnb_ref[1:2]).astype(bf16)
    x2 = x2_ref[...]
    result = middle + dob_ref[1:2]
    for j in range(4):
        cut = slice(j * width, (j + 1) * width)
        hidden, slope = gelu_both(nn(x2, wup[j]) + upb_ref[:, cut])
        hid_ref[:, cut] = hidden.astype(bf16)
        dg[:, cut] = slope.astype(bf16)
        result = result + nn(hid_ref[:, cut], wdown[j])
    out_ref[...] = result

    cot = cot_ref[...]
    grad = 0.0
    sums_ref[...] = jnp.zeros(sums_ref.shape, f32)
    for j in range(4):
        cut = slice(j * width, (j + 1) * width)
        pre = nt(cot, wdown[j]) * dg[:, cut].astype(f32)
        gp_ref[:, cut] = pre.astype(bf16)
        block_sum = jnp.sum(pre, axis=0, keepdims=True)
        at = slot ^ j
        sums_ref[pl.ds(6 + (at >> 1), 1), pl.ds(pl.multiple_of((at & 1) * width, width), width)] = (
            block_sum
        )
        grad = grad + nt(gp_ref[:, cut], wup[j])
    cotf = cot.astype(f32)
    gmid = cotf + norm_back(normal2, scale2, dgain_ref[1:2], grad)
    gm_ref[...] = gmid.astype(bf16)
    sums_ref[1:2, :width] = jnp.sum(gmid, axis=0, keepdims=True)
    sums_ref[2:3, :width] = jnp.sum(cotf, axis=0, keepdims=True)
    sums_ref[2:3, width:] = jnp.sum(grad * normal2, axis=0, keepdims=True)
    sums_ref[4:5, :width] = jnp.sum(grad, axis=0, keepdims=True)
    gmix = nt(gm_ref[...], wout[...]).astype(bf16)
    grad = 0.0
    for g in range(groups):
        cut = slice(g * 256, (g + 1) * 256)
        three = attend_back(
            qkv[0, :, cut], qkv[1, :, cut], qkv[2, :, cut], gmix[:, cut],
            lambda h: pt[g * heads + h], heads, scale,
        )
        for c, part in enumerate(three):
            begin = c * width + g * 256
            low = part.astype(bf16)
            g3_ref[:, begin : begin + 256] = low
            grad = grad + nt(low, wqkv[c, :, cut])
        for c, row, base in ((0, 4, width), (2, 5, width)):
            total = jnp.sum(three[c], axis=0, keepdims=True)
            for i in range(256 // block):
                sums_ref[row : row + 1, place(g * (256 // block) + i, base)] = (
                    total[:, i * block : (i + 1) * block]
                )
    gstream = gmid + norm_back(normal1, scale1, dgain_ref[0:1], grad)
    sums_ref[3:4, width:] = jnp.sum(gstream, axis=0, keepdims=True)
    sums_ref[1:2, width:] = jnp.sum(grad * normal1, axis=0, keepdims=True)
    sums_ref[3:4, :width] = jnp.sum(grad, axis=0, keepdims=True)
    wide[...] = gstream
    for j in range(4):
        gz_ref[:, j * block : (j + 1) * block] = wide[:, place(j)].astype(bf16)
    ge = nt(gz_ref[...], wemb[...])
    ge_ref[...] = ge
    gel_ref[...] = ge.astype(bf16)
    sums_ref[0:1] = jnp.sum(ge, axis=0, keepdims=True)


def decoder_weights_body(x1_ref, x2_ref, hid_ref, mix_ref, gp_ref, gm_ref, g3_ref, gz_ref, encl_ref, cot_ref,
                         sent_ref, kept_ref):
    width = cot_ref.shape[1]
    block = width // 4
    cot, gm, x2 = cot_ref[...], gm_ref[...], x2_ref[...]
    piece, thin = width // 8, block // 8
    tall = encl_ref.shape[1] // 8
    top = 2 * piece + thin
    step = top + piece + thin

    def to(j):
        return sent_ref if j % 2 else kept_ref

    for j in (1, 3, 0, 2):
        w = to(j)
        i = j // 2
        cut = slice(j * width, (j + 1) * width)
        up = tn(x2, gp_ref[:, cut]).astype(bf16)
        down = tn(hid_ref[:, cut], cot).astype(bf16)
        out = tn(mix_ref[:, j * block : (j + 1) * block], gm).astype(bf16)
        for c in range(8):
            w[i, c * step : c * step + piece] = up[c * piece : (c + 1) * piece]
            w[i, c * step + piece : c * step + 2 * piece] = down[c * piece : (c + 1) * piece]
            w[i, c * step + 2 * piece : c * step + top] = out[c * thin : (c + 1) * thin]
    x1 = x1_ref[...]
    for k in range(3):
        full = tn(x1, g3_ref[:, k * width : (k + 1) * width]).astype(bf16)
        for j in range(4):
            for c in range(8):
                to(j)[j // 2, c * step + top : c * step + top + piece, k * block : (k + 1) * block] = (
                    full[c * piece : (c + 1) * piece, j * block : (j + 1) * block]
                )
    full = tn(encl_ref[...], gz_ref[...]).astype(bf16)
    for j in range(4):
        cut = slice(j * block, (j + 1) * block)
        for c in range(8):
            base = c * tall
            to(j)[j // 2, c * step + top : c * step + top + piece, 3 * block :] = full[base : base + piece, cut]
            base = base + piece
            for k in range(4):
                to(j)[j // 2, c * step + top + piece : (c + 1) * step, k * block : (k + 1) * block] = (
                    full[base + k * thin : base + (k + 1) * thin, cut]
                )


def pack_body(pick_ref, up_ref, down_ref, out_ref, qkv_ref, emb_ref, chunk_ref):
    piece, thin, block = up_ref.shape[0], out_ref.shape[0], emb_ref.shape[1]
    chunk_ref[:piece] = up_ref[...]
    chunk_ref[piece : 2 * piece] = down_ref[...]
    top = 2 * piece + thin
    chunk_ref[2 * piece : top] = out_ref[...]
    for c in range(3):
        chunk_ref[top : top + piece, c * block : (c + 1) * block] = qkv_ref[c]
    chunk_ref[top : top + piece, 3 * block :] = emb_ref[:piece]
    for c in range(4):
        base = piece + c * thin
        chunk_ref[top + piece :, c * block : (c + 1) * block] = emb_ref[base : base + thin]


def join_body(a_ref, b_ref, out_ref):
    rows = a_ref.shape[0]
    out_ref[:rows] = a_ref[...]
    out_ref[rows:] = b_ref[...]


def add_body(a_ref, b_ref, out_ref):
    out_ref[...] = (a_ref[...].astype(f32) + b_ref[...].astype(f32)).astype(out_ref.dtype)


def last_sums_body(slot_ref, *refs):
    terms, outs, total_ref = refs[:-12], refs[-12:-1], refs[-1]
    total = terms[0][...]
    for ref in terms[1:]:
        total = total + ref[...]
    total_ref[...] = total
    slot = slot_ref[0]
    e_qv, e_upb, e_ob, e_gain, e_nb, d_emb, d_qv, d_upb, d_ob, d_gain, d_nb = outs
    share, thin, width = e_qv.shape[1], d_qv.shape[1], d_emb.shape[1]
    e_qv[...] = total_ref[18:20, pl.ds(pl.multiple_of(slot * share, share), share)]
    e_upb[...] = total_ref[pl.ds(4 + slot, 1), :]
    e_ob[0:1] = total_ref[0:1]
    e_ob[1:2] = total_ref[8:9]
    e_gain[0:1] = total_ref[16:17]
    e_gain[1:2] = total_ref[1:2]
    e_nb[0:1] = total_ref[17:18]
    e_nb[1:2] = total_ref[2:3]
    d_ob[...] = total_ref[9:11, :width]
    d_gain[...] = total_ref[9:11, width:]
    d_nb[...] = total_ref[11:13, :width]
    d_emb[...] = total_ref[11:12, width:]
    d_qv[...] = total_ref[12:14, pl.ds(pl.multiple_of(width + slot * thin, thin), thin)]
    d_upb[...] = total_ref[pl.ds(14 + (slot >> 1), 1), pl.ds(pl.multiple_of((slot & 1) * width, width), width)]


def far_body(bit_ref, kept_ref, near_ref, out_ref):
    half = out_ref.shape[0]
    rows = pl.ds(pl.multiple_of(bit_ref[0] * half, half), half)
    out_ref[...] = (kept_ref[1, rows].astype(f32) + near_ref[1, rows].astype(f32)).astype(bf16)


def there_body(bit_ref, kept_ref, near_ref, *refs):
    *terms, out_ref = refs
    half = out_ref.shape[0]
    rows = pl.ds(pl.multiple_of(bit_ref[0] * half, half), half)
    total = kept_ref[0, rows].astype(f32) + near_ref[0, rows].astype(f32)
    for ref in terms:
        total = total + ref[...].astype(f32)
    out_ref[...] = total.astype(bf16)


def choose_body(bit_ref, keep_ref, got_ref, out_ref):
    @pl.when(bit_ref[0] == 0)
    def _():
        out_ref[...] = keep_ref[...]

    @pl.when(bit_ref[0] != 0)
    def _():
        out_ref[...] = got_ref[...]


def piece_of(refs, j):
    for ref in refs:
        if len(ref.shape) == 2:
            if j == 0:
                return ref[...]
            j -= 1
        elif j < ref.shape[0]:
            return ref[j]
        else:
            j -= ref.shape[0]


def tile_sum(xs, gs, more):
    acc = 0.0
    for j in range(4):
        acc = acc + tn(piece_of(xs, j), piece_of(gs, j))
    if not more:
        return [(slice(None), slice(None), acc)]
    rows, cols = acc.shape
    parts = [(slice(None), slice(0, cols), acc)]
    half, quarter = rows // 2, rows // 8
    wide = more[0].shape[1] // 4
    for c in range(2):
        for k in range(4):
            parts.append((
                slice(c * half + k * quarter, c * half + (k + 1) * quarter),
                slice(cols, cols + wide),
                more[0][c * quarter : (c + 1) * quarter, k * wide : (k + 1) * wide].astype(f32),
            ))
    return parts


def half_body(nx, ng, nm, pick_ref, *refs):
    xs, gs, more = refs[:nx], refs[nx : nx + ng], refs[nx + ng : nx + ng + nm]
    *add_ref, out_ref = refs[nx + ng + nm :]
    for rows, cols, value in tile_sum(xs, gs, more):
        if add_ref:
            value = value + add_ref[0][rows, cols].astype(f32)
        out_ref[rows, cols] = value.astype(bf16)


def weight_half(chain, xs, gs, more, pick, add=None):
    tile = xs[0].shape[-1] // 4
    out_cols = gs[0].shape[-1] + sum(m.shape[1] // 4 for m in more)

    def column(shape):
        lead = shape[:-1]
        return pl.BlockSpec(lead + (tile,), lambda i, p: (0,) * len(lead) + (p[i],))

    def whole(shape):
        return pl.BlockSpec(shape, lambda i, p: (0,) * len(shape))

    in_specs = [column(x.shape) for x in xs] + [whole(g.shape) for g in gs]
    in_specs += [pl.BlockSpec((tile // 4, m.shape[1]), lambda i, p: (p[i], 0)) for m in more]
    args = list(xs) + list(gs) + list(more)
    out_spec = pl.BlockSpec((tile, out_cols), lambda i, p: (i, 0))
    if add is not None:
        in_specs.append(out_spec)
        args.append(add)
    return chain(
        functools.partial(half_body, len(xs), len(gs), len(more)),
        [shaped((2 * tile, out_cols), bf16)],
        args,
        prefetch=pick,
        grid=(2,),
        specs=(in_specs, [out_spec]),
        limit=20,
    )[0]


def spread_body(writes, place_ref, *refs):
    sums = max(write[0] for write in writes) + 1
    out_refs = refs[2 * sums :]
    for i in range(8):
        for source, which, lead, first, every, row, rows, col, cols, at_col in writes:
            ref = refs[2 * source + i // 4]
            base = i % 4 * (ref.shape[0] // 4)
            at = place_ref[source] ^ i
            value = ref[base + row : base + row + rows, col : col + cols].astype(f32)
            to = pl.ds(pl.multiple_of(at * every + first, rows), rows)
            if lead is None:
                out_refs[which][to, at_col : at_col + cols] = value
            else:
                out_refs[which][lead, to] = value


def out_weight_body(*refs):
    mixes, gs, out_ref = refs[:3], refs[3:7], refs[7]
    acc = 0.0
    for j in range(4):
        acc = acc + tn(piece_of(mixes, j), piece_of(gs, j))
    out_ref[...] = acc.astype(bf16)


class Sum:
    def __init__(self, chain):
        self.chain = chain
        self.size = lax.axis_size("dp")
        me = lax.axis_index("dp").astype(jnp.int32)
        self.x, z = me & 1, me >> 1
        self.outer = jnp.where((z == 0) | (z == 3), 1, 0).astype(jnp.int32).reshape(1)
        self.place = 4 * self.x if self.size == 8 else jnp.int32(0)
        inward = [(0, 1), (3, 2)]
        self.inward = [(2 * a + x, 2 * b + x) for a, b in inward for x in range(2)]
        self.outward = [(b, a) for a, b in self.inward]
        self.middle = [(2 * a + x, 2 * b + x) for a, b in ((1, 2), (2, 1)) for x in range(2)]
        steps = [self.second, self.third, self.fourth, self.fifth]
        self.steps = iter(steps if self.size == 8 else [])

    def step(self):
        for todo in self.steps:
            todo()
            return

    def product(self, xs, gs, more=()):
        self.terms = (xs, gs, more)
        if self.size != 8:
            first = weight_half(self.chain, *self.terms, jnp.array([0, 1], jnp.int32))
            other = weight_half(self.chain, *self.terms, jnp.array([2, 3], jnp.int32))
            return self.general(jnp.concatenate([first, other], axis=0))
        there = 2 * (1 - self.x)
        self.got = swap(weight_half(self.chain, *self.terms, jnp.stack([there, there + 1])), "dp", 1)

    def shares(self, kept, near, there):
        self.terms = None
        self.held = (kept, near, there)
        if self.size == 8:
            half = shaped(there.shape, bf16)
            out = self.chain(there_body, [half], ((1 - self.x).reshape(1), kept, near, there), smem=1)[0]
            self.got = swap(out, "dp", 1)

    def other(self, mine):
        kept, near, there = self.held
        self.held = (kept, near, mine)
        if self.size != 8:
            total = kept[0].astype(f32) + near[0].astype(f32)
            total = total + jnp.concatenate([mine, there], axis=0).astype(f32)
            self.general(total.astype(bf16))

    def second(self):
        if self.terms is None:
            half = shaped(self.got.shape, bf16)
            self.keep = self.chain(there_body, [half], (self.x.reshape(1), *self.held, self.got), smem=1)[0]
        else:
            mine = 2 * self.x
            self.keep = weight_half(self.chain, *self.terms, jnp.stack([mine, mine + 1]), self.got)
        self.got = send(self.keep, "dp", self.inward)

    def plus(self):
        self.keep = self.chain(add_body, [shaped(self.keep.shape, bf16)], (self.keep, self.got))[0]

    def third(self):
        self.plus()
        self.got = send(self.keep, "dp", self.middle)

    def fourth(self):
        self.plus()
        self.got = send(self.keep, "dp", self.outward)

    def fifth(self):
        self.keep = self.chain(
            choose_body, [shaped(self.keep.shape, bf16)], (self.outer, self.keep, self.got), smem=1
        )[0]
        self.got = swap(self.keep, "dp", 1)

    def general(self, held):
        me = lax.axis_index("dp")
        bits = [1 << i for i in range(self.size.bit_length() - 1)]
        for bit in bits:
            mine = (me & bit) != 0
            half = held.shape[0] // 2
            other = lax.dynamic_slice_in_dim(held, jnp.where(mine, 0, half), half, 0)
            own = lax.dynamic_slice_in_dim(held, jnp.where(mine, half, 0), half, 0)
            held = (own.astype(f32) + swap(other, "dp", bit).astype(f32)).astype(bf16)
        for bit in reversed(bits):
            mine = (me & bit) != 0
            other = swap(held, "dp", bit)
            held = jnp.where(
                mine,
                jnp.concatenate([other, held], axis=0),
                jnp.concatenate([held, other], axis=0),
            )
        half = held.shape[0] // 2
        self.keep, self.got = held[:half], held[half:]


def per_device(
    tokens, segment_ids, gsd_index, enc_qkv, enc_qv_bias, enc_out_proj, enc_up, enc_up_bias,
    enc_down, enc_out_bias, enc_gain, enc_norm_bias, embed_weight, embed_bias, dec_qkv,
    dec_qv_bias, dec_out_proj, dec_up, dec_up_bias, dec_down, dec_out_bias, dec_gain,
    dec_norm_bias, cotangent,
):
    n, width = tokens.shape
    rows, length = segment_ids.shape
    assert rows == 4 and n == length == 256 and lax.axis_size("mp") == 4
    share, ff = enc_qkv.shape[2], enc_up.shape[1]
    dwidth, dff = cotangent.shape[1], dec_up.shape[1] * 4
    dshare = dwidth // 4
    heads = share // (width // HEADS)
    scale = (width // HEADS) ** -0.5
    slot = lax.axis_index("mp").astype(jnp.int32)
    at = slot.reshape(1)
    chain = Chain()
    dec = Sum(chain)
    group = lax.axis_index("dp").astype(jnp.int32)
    home = 4 * (group & 1) + (group & 2) + ((group >> 2) & 1) if dec.size == 8 else jnp.int32(0)

    def low(*dims):
        return shaped(dims, bf16)

    def full(*dims):
        return shaped(dims, f32)

    def waves(size):
        half = size // 2
        return jnp.power(10000.0, -jnp.arange(half, dtype=f32) / half).reshape(1, half)

    def near(value):
        return swap(value, "mp", 1)

    def far(value):
        return swap(value, "mp", 2)

    pack_rows = 3 * dwidth + 2 * dshare
    decoder_weights = [in_hbm(w) for w in (dec_up, dec_down, dec_out_proj, dec_qkv, embed_weight)]

    def pack(pick, steps):
        def block(shape):
            if len(shape) == 3:
                return pl.BlockSpec((shape[0], shape[1] // 8, shape[2]), lambda i, p: (0, p[i], 0))
            return pl.BlockSpec((shape[0] // 8, shape[1]), lambda i, p: (p[i], 0))

        rows = pack_rows // 8
        return chain(
            pack_body,
            [low(steps * rows, dwidth)],
            decoder_weights,
            prefetch=pick,
            grid=(steps,),
            specs=([block(w.shape) for w in decoder_weights], [pl.BlockSpec((rows, dwidth), lambda i, p: (i, 0))]),
        )[0]

    split = dec.size == 8
    got = far(pack(home.reshape(1), 1)) if split else None
    normed = chain(
        start_body,
        [low(n, width)],
        (at, in_hbm(segment_ids), in_hbm(gsd_index), in_hbm(tokens), in_hbm(enc_gain), in_hbm(enc_norm_bias), waves(width)),
        smem=1,
        scratch=[pltpu.VMEM((n, width), f32)],
    )[0]
    x = [normed, near(normed), far(normed)]
    bias_a, bias_b = chain(mask_body, [kept(full(2, n, n)), kept(full(2, n, n))], (at, in_hbm(segment_ids)), smem=1)

    def attention(bias, first, *blocks):
        count = len(blocks)
        return chain(
            functools.partial(attn_body, scale, heads, first),
            [kept(low(count, n, share))] * 3
            + [kept(low(count, heads, n, n)), kept(low(count, n, share))]
            + [low(n, width)] * count,
            (*blocks, bias, enc_qkv, enc_qv_bias, enc_out_proj),
        )

    def add(a, b):
        return chain(add_body, [shaped(a.shape, a.dtype)], (a, b))[0]

    def join(a, b):
        return chain(join_body, [low(a.shape[0] + b.shape[0], a.shape[1])], (a, b))[0]

    def both(blocks):
        blocks[2] = chain.pin(blocks[2])
        blocks.append(near(blocks[2]))

    *saved_a, mixa, part0, part1 = attention(bias_a, 0, x[0], x[1])
    part1 = near(part1)
    vector = jnp.concatenate([dec_qv_bias.reshape(-1), dec_up_bias]).reshape(1, -1)
    vector = chain.pin(vector)
    vectors = [vector, near(vector), far(vector)]
    part1 = chain.pin(part1)
    both(x)
    chain.gap()
    chain.gap()
    *saved_d, mixd, part3 = attention(bias_b, 1, x[3])
    part3 = near(part3)
    *saved_c, mixc, part2 = attention(bias_b, 0, x[2])
    if split:
        got = chain.pin(got)
        more = swap(got, "dp", 4)
    part2 = far(add(part2, part3))
    vectors[1] = chain.pin(vectors[1])
    both(vectors)
    packed = pack(jnp.arange(8, dtype=jnp.int32), 8)
    packed_near = near(packed)
    pos, stream = chain(
        stream_body,
        [kept(full(n, dwidth)), full(n, width)],
        (at, in_hbm(segment_ids), in_hbm(gsd_index), in_hbm(tokens), in_hbm(embed_bias.reshape(1, -1)), waves(width), waves(dwidth)),
        smem=1,
    )
    if split:
        got = join(got, more)
        more = swap(got, "dp", 2)
    else:
        got = far(packed)
    middle, normed2 = chain(
        mid_body,
        [kept(full(n, width)), low(n, width)],
        (stream, part0, part1, part2, enc_out_bias, enc_gain, enc_norm_bias),
    )
    y = [normed2, near(normed2), far(normed2)]
    packed_near = chain.pin(packed_near)
    vectors[3] = chain.pin(vectors[3])

    def feed(*blocks):
        count = len(blocks)
        return chain(
            mlp_body,
            [kept(low(count, n, ff))] * 2 + [low(n, width)] * count,
            (*blocks, enc_up, enc_up_bias.reshape(1, -1), enc_down),
        )

    hida, dga, part0, part1 = feed(y[0], y[1])
    part1 = near(part1)
    if split:
        got = join(got, more)
        more = swap(got, "dp", 1)
    else:
        more = got[pack_rows // 2 :]
        got = got[: pack_rows // 2]
    far_weights = [got, more]
    near_weights = [near(got)]
    both(y)
    part1 = chain.pin(part1)
    near_weights[0] = chain.pin(near_weights[0])
    hidd, dgd, part3 = feed(y[3])
    part3 = near(part3)
    hidc, dgc, part2 = feed(y[2])
    part2 = far(add(part2, part3))
    far_weights[1] = chain.pin(more)
    near_weights.append(near(far_weights[1]))
    part2 = chain.pin(part2)

    (enc_low, output, x1, x2, hid, mix, gp, gm, g3, gz, ge_low, ge, dec_sums) = chain(
        decoder_body,
        [low(n, width), kept(full(n, dwidth)), low(n, dwidth), low(n, dwidth), low(n, dff),
         low(n, dwidth), low(n, dff), low(n, dwidth), low(n, 3 * dwidth), low(n, dwidth),
         low(n, width), kept(full(n, width)), kept(full(8, width))],
        (jnp.stack([slot, home]), middle, part0, part1, part2, enc_out_bias, packed, packed_near,
         *far_weights, *near_weights, *vectors, pos, bias_a, dec_out_bias, dec_gain,
         dec_norm_bias, cotangent),
        smem=1,
        scratch=[
            pltpu.VMEM((4, dwidth, dwidth), bf16), pltpu.VMEM((4, dwidth, dwidth), bf16),
            pltpu.VMEM((3, dwidth, dwidth), bf16), pltpu.VMEM((dwidth, dwidth), bf16),
            pltpu.VMEM((width, dwidth), bf16), pltpu.VMEM((DHEADS, n, n), bf16),
            pltpu.VMEM((n, dff), bf16), pltpu.VMEM((3, n, dwidth), bf16), pltpu.VMEM((n, dwidth), f32),
            pltpu.VMEM((2, dwidth), f32), pltpu.VMEM((1, dff), f32),
        ],
        limit=40,
    )
    g = [ge_low, near(ge_low), far(ge_low)]

    def feed_back(slope, *blocks):
        count = len(blocks)
        return chain(
            mlp_back_body,
            [kept(low(count, n, ff)), kept(full(1, ff))] + [low(n, width)] * count,
            (*blocks, slope, enc_up, enc_down),
        )

    def attention_back(saved, *blocks):
        count = len(blocks)
        return chain(
            functools.partial(attn_back_body, scale, heads),
            [kept(low(count, n, 3 * share)), kept(full(2, share))] + [low(n, width)] * count,
            (*blocks, *saved, enc_qkv, enc_out_proj),
        )

    def far_share(bit):
        return far(chain(far_body, [low(pack_rows // 2, dwidth)], (bit.reshape(1), kept_share, sent), smem=1)[0])

    def hbm(*values):
        return [in_hbm(v) for v in values]

    down, up, attn = Sum(chain), Sum(chain), Sum(chain)

    def finish(sums, outs, writes):
        return chain(
            functools.partial(spread_body, writes),
            [kept(full(*dims)) for dims in outs],
            (jnp.stack([f.place for f in sums]), *[v for f in sums for v in (f.keep, f.got)]),
            smem=1,
            limit=24,
        )

    chain.gap()
    gpa, upa, part0, part1 = feed_back(dga, g[0], g[1])
    part1 = near(part1)
    sent, kept_share = chain(
        decoder_weights_body,
        [low(2, pack_rows, dwidth), kept(low(2, pack_rows, dwidth))],
        (x1, x2, hid, mix, gp, gm, g3, gz, enc_low, cotangent),
        limit=24,
    )
    sent = near(sent)
    part1 = chain.pin(part1)
    both(g)
    gpc, upc, part2 = feed_back(dgc, g[2])
    down.product(hbm(hida, hidc, hidd), g)
    gpd, upd, part3 = feed_back(dgd, g[3])
    part3 = near(part3)
    chain.gap()
    part2 = far(add(part2, part3))
    chain.gap()
    grad_middle, gm_low, sums_mid = chain(
        mlp_end_body,
        [kept(full(n, width)), low(n, width), kept(full(16, width))],
        (at, ge, part0, part1, part2, middle, enc_gain, upa, upc, upd, dec_sums),
        smem=1,
    )
    m = [gm_low, near(gm_low), far(gm_low)]
    up.product(hbm(*y), hbm(gpa, gpc, gpd))
    g3a, sa, part0, part1 = attention_back(saved_a, m[0], m[1])
    part1 = near(part1)
    down.step()
    part1 = chain.pin(part1)
    there = far_share(1 - dec.x)
    both(m)
    g3c, sc, part2 = attention_back(saved_c, m[2])
    out_full = chain(out_weight_body, [low(share, width)], (mixa, mixc, mixd, *m))[0]
    g3d, sd, part3 = attention_back(saved_d, m[3])
    part3 = near(part3)
    attn.product(hbm(*x), hbm(g3a, g3c, g3d), [out_full])
    part2 = far(add(part2, part3))
    up.step()
    down.step()
    grad_tokens, sums = chain(
        last_body,
        [kept(full(n, width)), full(24, width)],
        (at, grad_middle, part0, part1, part2, stream, enc_gain, sa, sc, sd, sums_mid),
        smem=1,
    )
    dec.shares(kept_share, sent, there)
    dec.other(far_share(dec.x))
    attn.step()
    up.step()
    down.step()
    hops = [("mp", 1), ("mp", 2)] + [("dp", 1 << i) for i in range(dec.size.bit_length() - 1)]
    hops = iter(hops)

    def hop(total, got=None):
        if got is not None:
            total = add(total, got)
        for axis, mask in hops:
            return total, swap(total, axis, mask)
        return total, None

    attn.step()
    up.step()
    dec.step()
    down.step()
    small = hop(sums)
    dec.step()
    small = hop(*small)
    attn.step()
    small = hop(*small)
    e_down = finish((down,), [(ff, width)], [(0, 0, None, 0, ff // 8, 0, ff // 8, 0, width, 0)])[0]
    up.step()
    small = hop(*small)
    dec.step()
    small = hop(*small)
    attn.step()
    e_up = finish((up,), [(width, ff)], [(0, 0, None, 0, width // 8, 0, width // 8, 0, ff, 0)])[0]
    while small[1] is not None:
        sums = small
        small = hop(*small)
    vectors = chain(
        last_sums_body,
        [full(2, share), full(1, ff), full(2, width), full(2, width), full(2, width), full(1, dwidth),
         full(2, dshare), full(1, dff // 4), full(2, dwidth), full(2, dwidth), full(2, dwidth)],
        (at, *sums),
        smem=1,
        scratch=[pltpu.VMEM((24, width), f32)],
    )
    dec.step()
    rows, fold = width // 8, share // 8
    e_qkv, e_out = finish(
        (attn,),
        [(3, width, share), (share, width)],
        [(0, 0, c, 0, rows, 0, rows, c * share, share, 0) for c in range(3)]
        + [(0, 1, None, 0, fold, k * fold, fold, 3 * share, width // 4, k * (width // 4)) for k in range(4)],
    )
    part, thin, tall = dwidth // 8, dshare // 8, width // 8
    top = 2 * part + thin
    d_up, d_down, d_out, d_qkv, e_embed = finish(
        (dec,),
        [(dwidth, dwidth), (dwidth, dwidth), (dshare, dwidth), (3, dwidth, dshare), (width, dshare)],
        [
            (0, 0, None, 0, part, 0, part, 0, dwidth, 0),
            (0, 1, None, 0, part, part, part, 0, dwidth, 0),
            (0, 2, None, 0, thin, 2 * part, thin, 0, dwidth, 0),
        ]
        + [(0, 3, c, 0, part, top, part, c * dshare, dshare, 0) for c in range(3)]
        + [(0, 4, None, 0, tall, top, part, 3 * dshare, dshare, 0)]
        + [(0, 4, None, part + k * thin, tall, top + part, thin, k * dshare, dshare, 0) for k in range(4)],
    )
    e_qv, e_upb, e_ob, e_gain, e_nb, d_emb, d_qv, d_upb, d_ob, d_gain, d_nb = vectors

    return (
        output,
        grad_tokens,
        e_qkv,
        e_qv,
        e_out,
        e_up,
        e_upb.reshape(-1),
        e_down,
        e_ob,
        e_gain,
        e_nb,
        e_embed,
        d_emb.reshape(-1),
        d_qkv,
        d_qv,
        d_out,
        d_up,
        d_upb.reshape(-1),
        d_down,
        d_ob,
        d_gain,
        d_nb,
    )


def solution(mesh):
    return jax.shard_map(
        per_device,
        mesh=mesh,
        in_specs=(
            P(("dp", "mp"), None),
            P("dp", None),
            P("dp", None),
            P(None, None, "mp"),
            P(None, "mp"),
            P("mp", None),
            P(None, "mp"),
            P("mp"),
            P("mp", None),
            P(),
            P(),
            P(),
            P(None, "mp"),
            P(),
            P(None, None, "mp"),
            P(None, "mp"),
            P("mp", None),
            P(None, "mp"),
            P("mp"),
            P("mp", None),
            P(),
            P(),
            P(),
            P(("dp", "mp"), None),
        ),
        out_specs=(
            P(("dp", "mp"), None),
            P(("dp", "mp"), None),
            P(None, None, "mp"),
            P(None, "mp"),
            P("mp", None),
            P(None, "mp"),
            P("mp"),
            P("mp", None),
            P(),
            P(),
            P(),
            P(None, "mp"),
            P(),
            P(None, None, "mp"),
            P(None, "mp"),
            P("mp", None),
            P(None, "mp"),
            P("mp"),
            P("mp", None),
            P(),
            P(),
            P(),
        ),
        check_vma=False,
    )
```

```python
import functools
import math

import jax
import jax.numpy as jnp
from jax import lax
from jax.experimental import pallas as pl
from jax.experimental.pallas import tpu as pltpu
from jax.sharding import PartitionSpec as P

HEADS = 16
DHEADS = 16
norm_eps = 1e-06
f32 = jnp.float32
bf16 = jnp.bfloat16
MIB = 1 << 20
VMEM = pl.BlockSpec(memory_space=pltpu.VMEM)
SMEM = pl.BlockSpec(memory_space=pltpu.SMEM)
COST = pl.CostEstimate(flops=10**10, bytes_accessed=10**8, transcendentals=0)


def shaped(dims, kind):
    return jax.ShapeDtypeStruct(dims, kind)


def kept(shape):
    return pltpu.HBM(shape.shape, shape.dtype)


def in_hbm(value):
    return pltpu.with_memory_space_constraint(value, pltpu.HBM)


class Chain:
    token = jax.ShapeDtypeStruct((8, 128), jnp.float32)

    def __init__(self):
        self.last = None

    def __call__(self, body, outs, args, smem=0, scratch=(), limit=16, prefetch=None, grid=None, specs=None):
        args, outs = list(args), list(outs)
        extra = self.last is not None
        ins = len(args) + (prefetch is not None)
        many = len(outs)

        def inner(*refs):
            out_refs = refs[ins + extra :]
            out_refs[many][...] = jnp.zeros((8, 128), f32)
            return body(*refs[:ins], *out_refs[:many], *out_refs[many + 1 :])

        if extra:
            args.append(self.last)
        tail = [pl.BlockSpec(memory_space=pl.ANY)] * extra
        params = pltpu.CompilerParams(vmem_limit_bytes=limit * MIB)
        if prefetch is None:
            got = pl.pallas_call(
                inner,
                out_shape=outs + [self.token],
                in_specs=[SMEM] * smem + [VMEM] * (len(args) - smem - extra) + tail,
                out_specs=[VMEM] * (many + 1),
                scratch_shapes=scratch,
                compiler_params=params,
                cost_estimate=COST,
            )(*args)
        else:
            got = pl.pallas_call(
                inner,
                out_shape=outs + [self.token],
                grid_spec=pltpu.PrefetchScalarGridSpec(
                    num_scalar_prefetch=1,
                    grid=grid,
                    in_specs=specs[0] + tail,
                    out_specs=specs[1] + [pl.BlockSpec((8, 128), lambda i, p: (0, 0))],
                ),
                compiler_params=params,
                cost_estimate=COST,
            )(prefetch, *args)
        *got, self.last = got
        return got

    def pin(self, value):
        def body(value_ref, last_ref, out_ref, token_ref):
            token_ref[...] = jnp.zeros((8, 128), f32)

        any_space = pl.BlockSpec(memory_space=pl.ANY)
        got, self.last = pl.pallas_call(
            body,
            out_shape=[shaped(value.shape, value.dtype), self.token],
            in_specs=[any_space, any_space],
            out_specs=[any_space, VMEM],
            input_output_aliases={0: 0},
            compiler_params=pltpu.CompilerParams(vmem_limit_bytes=MIB),
            cost_estimate=COST,
        )(value, self.last)
        return got

    def gap(self):
        self(lambda: None, [], [], limit=1)


def nn(a, b):
    return lax.dot_general(a, b, (((1,), (0,)), ((), ())), preferred_element_type=f32)


def nt(a, b):
    return lax.dot_general(a, b, (((1,), (1,)), ((), ())), preferred_element_type=f32)


def tn(a, b):
    return lax.dot_general(a, b, (((0,), (0,)), ((), ())), preferred_element_type=f32)


def send(value, axis, pairs):
    return lax.ppermute(value, axis, pairs)


def swap(value, axis, mask):
    size = lax.axis_size(axis)
    return lax.ppermute(value, axis, [(i, i ^ mask) for i in range(size)])


def norm_parts(values):
    average = jnp.mean(values, axis=-1, keepdims=True)
    centred = values - average
    variance = jnp.mean(centred * centred, axis=-1, keepdims=True)
    scale = lax.rsqrt(variance + norm_eps)
    return centred * scale, scale


def norm_back(normal, scale, gain, grad):
    wide = grad * gain
    one = jnp.mean(wide, axis=-1, keepdims=True)
    two = jnp.mean(wide * normal, axis=-1, keepdims=True)
    return scale * (wide - one - normal * two)


def gelu_both(v):
    slope = math.sqrt(2.0 / math.pi)
    square = v * v
    t = jnp.tanh(slope * v * (1.0 + 0.044715 * square))
    half = 0.5 * (1.0 + t)
    return v * half, half + 0.5 * slope * v * (1.0 - t * t) * (1.0 + 3.0 * 0.044715 * square)


def sin_cos(x):
    turn = jnp.floor(x * (2.0 / math.pi) + 0.5)
    r = ((x - turn * 1.5703125) - turn * 4.837512969970703125e-4) - turn * 7.54978995489188216e-8
    z = r * r
    s = r + r * z * (-1.6666654611e-1 + z * (8.3321608736e-3 + z * -1.9515295891e-4))
    c = 1.0 - 0.5 * z + z * z * (
        4.166664568298827e-2 + z * (-1.388731625493765e-3 + z * 2.443315711809948e-5)
    )
    quarter = turn.astype(jnp.int32)
    odd = (quarter & 1) != 0
    sine = jnp.where(odd, c, s)
    cosine = jnp.where(odd, s, c)
    sine = jnp.where((quarter & 2) != 0, -sine, sine)
    cosine = jnp.where(((quarter + 1) & 2) != 0, -cosine, cosine)
    return sine, cosine


def head_masks(heads):
    size = 256 // heads
    lane = lax.broadcasted_iota(jnp.int32, (1, 256), 1)
    return [
        jnp.where((lane >= h * size) & (lane < (h + 1) * size), 1.0, 0.0).astype(bf16)
        for h in range(heads)
    ]


def attend(q, k, v, bias, heads, scale, keep):
    size = 256 // heads
    vt = v.astype(f32).T.astype(bf16)
    mixes = []
    for h, mask in enumerate(head_masks(heads)):
        s = nt(k, q * mask) + bias
        top = jnp.max(s, axis=0, keepdims=True)
        p = jnp.exp2((s - top) * (scale * math.log2(math.e)))
        total = jnp.sum(p, axis=0, keepdims=True)
        p = (p * (1.0 / total)).astype(bf16)
        keep(h, p)
        mixes.append(nn(vt[h * size : (h + 1) * size], p))
    return jnp.concatenate(mixes, axis=0).T


def attend_back(q, k, v, gm, probs, heads, scale):
    size = 256 // heads
    kt = k.astype(f32).T.astype(bf16)
    gq, gk, gv = [], 0.0, 0.0
    for h, mask in enumerate(head_masks(heads)):
        gmh = gm * mask
        p = probs(h)
        wide = p.astype(f32)
        t = wide * nt(v, gmh)
        gs = (t - wide * jnp.sum(t, axis=0, keepdims=True)).astype(bf16)
        gk = gk + nn(gs, q * mask)
        gv = gv + nn(p, gmh)
        gq.append(nn(kt[h * size : (h + 1) * size], gs))
    return jnp.concatenate(gq, axis=0).T * scale, gk * scale, gv


def place_of(slot, seg_ref, gsd_ref):
    n = seg_ref.shape[1]
    across = jnp.broadcast_to(seg_ref[pl.ds(slot, 1), :].astype(f32), (n, n))
    earlier = lax.broadcasted_iota(jnp.int32, (n, n), 1) < lax.broadcasted_iota(jnp.int32, (n, n), 0)
    rank = jnp.sum(jnp.where((across == across.T) & earlier, 1.0, 0.0), axis=1, keepdims=True)
    index = jnp.broadcast_to(gsd_ref[pl.ds(slot, 1), :].astype(f32), (n, n)).T[:, :1]
    return rank * (0.5 + 0.25 * index)


def start_body(slot_ref, seg_ref, gsd_ref, tokens_ref, gain_ref, shift_ref, wf_ref, normed_ref, stream_ref):
    place = place_of(slot_ref[0], seg_ref, gsd_ref)
    half = wf_ref.shape[1]
    sine, cosine = sin_cos(place * wf_ref[...])
    stream_ref[:, :half] = tokens_ref[:, :half].astype(f32) + sine
    stream_ref[:, half:] = tokens_ref[:, half:].astype(f32) + cosine
    normal, _ = norm_parts(stream_ref[...])
    normed_ref[...] = (normal * gain_ref[0:1] + shift_ref[0:1]).astype(bf16)


def mask_body(slot_ref, seg_ref, bias_a_ref, bias_b_ref):
    slot = slot_ref[0]
    n = seg_ref.shape[1]
    for j in range(4):
        across = jnp.broadcast_to(seg_ref[pl.ds(slot ^ j, 1), :].astype(f32), (n, n))
        (bias_a_ref, bias_b_ref)[j // 2][j % 2] = jnp.where(across == across.T, 0.0, -1e30)


def stream_body(slot_ref, seg_ref, gsd_ref, tokens_ref, eb_ref, wf_ref, nf_ref, pos_ref, stream_ref):
    place = place_of(slot_ref[0], seg_ref, gsd_ref)
    half = wf_ref.shape[1]
    sine, cosine = sin_cos(place * wf_ref[...])
    stream_ref[:, :half] = tokens_ref[:, :half].astype(f32) + sine
    stream_ref[:, half:] = tokens_ref[:, half:].astype(f32) + cosine
    half = nf_ref.shape[1]
    sine, cosine = sin_cos(place * nf_ref[...])
    pos_ref[:, :half] = sine + eb_ref[:, :half]
    pos_ref[:, half:] = cosine + eb_ref[:, half:]


def attn_body(scale, heads, first, *refs):
    count = (len(refs) - 9) // 2
    xs, rest = refs[:count], refs[count:]
    bias_ref, w_ref, qvb_ref, o_ref, q_ref, k_ref, v_ref, p_ref, mix_ref = rest[:9]
    for r, (x_ref, part_ref) in enumerate(zip(xs, rest[9:])):
        x = x_ref[...]
        q = (nn(x, w_ref[0]) + qvb_ref[0:1]).astype(bf16)
        k = nn(x, w_ref[1]).astype(bf16)
        v = (nn(x, w_ref[2]) + qvb_ref[1:2]).astype(bf16)
        q_ref[r], k_ref[r], v_ref[r] = q, k, v

        def keep(h, p):
            p_ref[r, h] = p

        mix = attend(q, k, v, bias_ref[first + r], heads, scale, keep).astype(bf16)
        mix_ref[r] = mix
        part_ref[...] = nn(mix, o_ref[...]).astype(bf16)


def attn_back_body(scale, heads, *refs):
    count = (len(refs) - 8) // 2
    gs, rest = refs[:count], refs[count:]
    q_ref, k_ref, v_ref, p_ref, w_ref, o_ref, g3_ref, sums_ref = rest[:8]
    total_q, total_v = 0.0, 0.0
    for r, (g_ref, part_ref) in enumerate(zip(gs, rest[8:])):
        gm = nt(g_ref[...], o_ref[...]).astype(bf16)
        gq, gk, gv = attend_back(
            q_ref[r], k_ref[r], v_ref[r], gm, lambda h: p_ref[r, h], heads, scale
        )
        total_q = total_q + jnp.sum(gq, axis=0, keepdims=True)
        total_v = total_v + jnp.sum(gv, axis=0, keepdims=True)
        acc = 0.0
        for c, g in enumerate((gq, gk, gv)):
            low = g.astype(bf16)
            g3_ref[r, :, c * 256 : (c + 1) * 256] = low
            acc = acc + nt(low, w_ref[c])
        part_ref[...] = acc.astype(bf16)
    sums_ref[0:1] = total_q
    sums_ref[1:2] = total_v


def mid_body(stream_ref, p_ref, near_ref, far_ref, ob_ref, gain_ref, shift_ref, mid_ref, normed_ref):
    total = p_ref[...].astype(f32) + near_ref[...].astype(f32) + far_ref[...].astype(f32)
    middle = stream_ref[...] + total + ob_ref[0:1]
    mid_ref[...] = middle
    normal, _ = norm_parts(middle)
    normed_ref[...] = (normal * gain_ref[1:2] + shift_ref[1:2]).astype(bf16)


def mlp_body(*refs):
    count = (len(refs) - 5) // 2
    xs, rest = refs[:count], refs[count:]
    up_ref, ub_ref, down_ref, hid_ref, dg_ref = rest[:5]
    width = up_ref.shape[1]
    for r, (x_ref, part_ref) in enumerate(zip(xs, rest[5:])):
        x = x_ref[...]
        for c in range(0, width, 256):
            cut = slice(c, c + 256)
            hidden, slope = gelu_both(nn(x, up_ref[:, cut]) + ub_ref[:, cut])
            hid_ref[r, :, cut] = hidden.astype(bf16)
            dg_ref[r, :, cut] = slope.astype(bf16)
        hidden = hid_ref[r]
        for c in range(0, down_ref.shape[1], 512):
            cut = slice(c, c + 512)
            part_ref[:, cut] = nn(hidden, down_ref[:, cut]).astype(bf16)


def mlp_back_body(*refs):
    count = (len(refs) - 5) // 2
    gs, rest = refs[:count], refs[count:]
    dg_ref, up_ref, down_ref, gp_ref, sums_ref = rest[:5]
    width = up_ref.shape[1]
    for r, (g_ref, part_ref) in enumerate(zip(gs, rest[5:])):
        g = g_ref[...]
        for c in range(0, width, 256):
            cut = slice(c, c + 256)
            grad = nt(g, down_ref[cut]) * dg_ref[r, :, cut].astype(f32)
            gp_ref[r, :, cut] = grad.astype(bf16)
            total = jnp.sum(grad, axis=0, keepdims=True)
            sums_ref[:, cut] = total if r == 0 else sums_ref[:, cut] + total
        gp = gp_ref[r]
        for c in range(0, up_ref.shape[0], 512):
            cut = slice(c, c + 512)
            part_ref[:, cut] = nt(gp, up_ref[cut]).astype(bf16)


def mlp_end_body(slot_ref, ge_ref, p_ref, near_ref, far_ref, mid_ref, gain_ref, ua_ref, ub_ref, uc_ref, dec_ref,
                 gmid_ref, gm_ref, pack_ref):
    slot = slot_ref[0]
    grad = p_ref[...].astype(f32) + near_ref[...].astype(f32) + far_ref[...].astype(f32)
    normal, scale = norm_parts(mid_ref[...])
    gmid = ge_ref[...] + norm_back(normal, scale, gain_ref[1:2], grad)
    gmid_ref[...] = gmid
    gm_ref[...] = gmid.astype(bf16)
    pack_ref[...] = jnp.zeros(pack_ref.shape, f32)
    pack_ref[0:1] = jnp.sum(gmid, axis=0, keepdims=True)
    pack_ref[1:2] = jnp.sum(grad * normal, axis=0, keepdims=True)
    pack_ref[2:3] = jnp.sum(grad, axis=0, keepdims=True)
    pack_ref[pl.ds(4 + slot, 1), :] = ua_ref[...] + ub_ref[...] + uc_ref[...]
    pack_ref[8:16] = dec_ref[...]


def last_body(slot_ref, gmid_ref, p_ref, near_ref, far_ref, stream_ref, gain_ref, sa_ref, sb_ref, sc_ref, mid_ref,
              gtok_ref, pack_ref):
    slot = slot_ref[0]
    grad = p_ref[...].astype(f32) + near_ref[...].astype(f32) + far_ref[...].astype(f32)
    normal, scale = norm_parts(stream_ref[...])
    gtok_ref[...] = gmid_ref[...] + norm_back(normal, scale, gain_ref[0:1], grad)
    pack_ref[:16] = mid_ref[...]
    pack_ref[16:] = jnp.zeros((8, pack_ref.shape[1]), f32)
    pack_ref[16:17] = jnp.sum(grad * normal, axis=0, keepdims=True)
    pack_ref[17:18] = jnp.sum(grad, axis=0, keepdims=True)
    share = sa_ref.shape[1]
    place = pl.ds(pl.multiple_of(slot * share, share), share)
    pack_ref[18:20, place] = sa_ref[...] + sb_ref[...] + sc_ref[...]


def decoder_body(slot_ref, mid_ref, p_ref, near_ref, far_ref, eob_ref, own_ref, by_ref, fa_ref, fb_ref, na_ref, nb_ref,
                 b0_ref, b1_ref, b2_ref, b3_ref, pos_ref, bias_ref, dob_ref, dgain_ref, dnb_ref, cot_ref,
                 encl_ref, out_ref, x1_ref, x2_ref, hid_ref, mix_ref, gp_ref, gm_ref, g3_ref, gz_ref,
                 gel_ref, ge_ref, sums_ref,
                 wup, wdown, wqkv, wout, wemb, pt, dg, qkv, wide, qvb_ref, upb_ref):
    slot, home = slot_ref[0], slot_ref[1]
    width = cot_ref.shape[1]
    block = width // 4
    heads = DHEADS * 256 // width
    groups = width // 256
    scale = (width // DHEADS) ** -0.5

    def place(j, base=0):
        return pl.ds(pl.multiple_of(base + (slot ^ j) * block, block), block)

    for j, ref in enumerate((b0_ref, b1_ref, b2_ref, b3_ref)):
        for c in range(2):
            qvb_ref[c : c + 1, j * block : (j + 1) * block] = ref[:, c * block : (c + 1) * block]
        upb_ref[:, j * width : (j + 1) * width] = ref[:, 2 * block :]
    piece, thin, tall = width // 8, block // 8, 2 * width // 8
    top = 2 * piece + thin
    step = top + piece + thin
    for j, (low_ref, high_ref) in enumerate(
        ((own_ref, own_ref), (by_ref, by_ref), (fa_ref, fb_ref), (na_ref, nb_ref))
    ):
        cut = slice(j * block, (j + 1) * block)
        for i in range(8):
            ref = (low_ref, high_ref)[i // 4]
            base = (i if j < 2 else i % 4) * step
            chunk = i if j < 2 else home ^ i

            def rows(size):
                return pl.ds(pl.multiple_of(chunk * size, size), size)

            wup[j, rows(piece)] = ref[base : base + piece]
            wdown[j, rows(piece)] = ref[base + piece : base + 2 * piece]
            wout[pl.ds(pl.multiple_of(j * block + chunk * thin, thin), thin)] = (
                ref[base + 2 * piece : base + top]
            )
            for c in range(3):
                wqkv[c, rows(piece), cut] = ref[base + top : base + top + piece, c * block : (c + 1) * block]
            wemb[pl.ds(pl.multiple_of(chunk * tall, tall), piece), cut] = (
                ref[base + top : base + top + piece, 3 * block :]
            )
            for c in range(4):
                wemb[pl.ds(pl.multiple_of(chunk * tall + piece + c * thin, thin), thin), cut] = (
                    ref[base + top + piece : base + step, c * block : (c + 1) * block]
                )
    encoded = mid_ref[...] + eob_ref[1:2]
    encoded = encoded + p_ref[...].astype(f32) + near_ref[...].astype(f32) + far_ref[...].astype(f32)
    encl_ref[...] = encoded.astype(bf16)
    embedded = nn(encl_ref[...], wemb[...])
    for j in range(4):
        wide[:, place(j)] = embedded[:, j * block : (j + 1) * block]
    stream = wide[...] + pos_ref[...]
    normal1, scale1 = norm_parts(stream)
    x1_ref[...] = (normal1 * dgain_ref[0:1] + dnb_ref[0:1]).astype(bf16)
    x1 = x1_ref[...]
    qkv[0] = (nn(x1, wqkv[0]) + qvb_ref[0:1]).astype(bf16)
    qkv[1] = nn(x1, wqkv[1]).astype(bf16)
    qkv[2] = (nn(x1, wqkv[2]) + qvb_ref[1:2]).astype(bf16)
    bias = bias_ref[0]
    for g in range(groups):
        cut = slice(g * 256, (g + 1) * 256)

        def keep(h, p):
            pt[g * heads + h] = p

        mix_ref[:, cut] = attend(
            qkv[0, :, cut], qkv[1, :, cut], qkv[2, :, cut], bias, heads, scale, keep
        ).astype(bf16)
    middle = stream + nn(mix_ref[...], wout[...]) + dob_ref[0:1]
    normal2, scale2 = norm_parts(middle)
    x2_ref[...] = (normal2 * dgain_ref[1:2] + dnb_ref[1:2]).astype(bf16)
    x2 = x2_ref[...]
    result = middle + dob_ref[1:2]
    for j in range(4):
        cut = slice(j * width, (j + 1) * width)
        hidden, slope = gelu_both(nn(x2, wup[j]) + upb_ref[:, cut])
        hid_ref[:, cut] = hidden.astype(bf16)
        dg[:, cut] = slope.astype(bf16)
        result = result + nn(hid_ref[:, cut], wdown[j])
    out_ref[...] = result

    cot = cot_ref[...]
    grad = 0.0
    sums_ref[...] = jnp.zeros(sums_ref.shape, f32)
    for j in range(4):
        cut = slice(j * width, (j + 1) * width)
        pre = nt(cot, wdown[j]) * dg[:, cut].astype(f32)
        gp_ref[:, cut] = pre.astype(bf16)
        block_sum = jnp.sum(pre, axis=0, keepdims=True)
        at = slot ^ j
        sums_ref[pl.ds(6 + (at >> 1), 1), pl.ds(pl.multiple_of((at & 1) * width, width), width)] = (
            block_sum
        )
        grad = grad + nt(gp_ref[:, cut], wup[j])
    cotf = cot.astype(f32)
    gmid = cotf + norm_back(normal2, scale2, dgain_ref[1:2], grad)
    gm_ref[...] = gmid.astype(bf16)
    sums_ref[1:2, :width] = jnp.sum(gmid, axis=0, keepdims=True)
    sums_ref[2:3, :width] = jnp.sum(cotf, axis=0, keepdims=True)
    sums_ref[2:3, width:] = jnp.sum(grad * normal2, axis=0, keepdims=True)
    sums_ref[4:5, :width] = jnp.sum(grad, axis=0, keepdims=True)
    gmix = nt(gm_ref[...], wout[...]).astype(bf16)
    grad = 0.0
    for g in range(groups):
        cut = slice(g * 256, (g + 1) * 256)
        three = attend_back(
            qkv[0, :, cut], qkv[1, :, cut], qkv[2, :, cut], gmix[:, cut],
            lambda h: pt[g * heads + h], heads, scale,
        )
        for c, part in enumerate(three):
            begin = c * width + g * 256
            low = part.astype(bf16)
            g3_ref[:, begin : begin + 256] = low
            grad = grad + nt(low, wqkv[c, :, cut])
        for c, row, base in ((0, 4, width), (2, 5, width)):
            total = jnp.sum(three[c], axis=0, keepdims=True)
            for i in range(256 // block):
                sums_ref[row : row + 1, place(g * (256 // block) + i, base)] = (
                    total[:, i * block : (i + 1) * block]
                )
    gstream = gmid + norm_back(normal1, scale1, dgain_ref[0:1], grad)
    sums_ref[3:4, width:] = jnp.sum(gstream, axis=0, keepdims=True)
    sums_ref[1:2, width:] = jnp.sum(grad * normal1, axis=0, keepdims=True)
    sums_ref[3:4, :width] = jnp.sum(grad, axis=0, keepdims=True)
    wide[...] = gstream
    for j in range(4):
        gz_ref[:, j * block : (j + 1) * block] = wide[:, place(j)].astype(bf16)
    ge = nt(gz_ref[...], wemb[...])
    ge_ref[...] = ge
    gel_ref[...] = ge.astype(bf16)
    sums_ref[0:1] = jnp.sum(ge, axis=0, keepdims=True)


def decoder_weights_body(x1_ref, x2_ref, hid_ref, mix_ref, gp_ref, gm_ref, g3_ref, gz_ref, encl_ref, cot_ref,
                         sent_ref, kept_ref):
    width = cot_ref.shape[1]
    block = width // 4
    cot, gm, x2 = cot_ref[...], gm_ref[...], x2_ref[...]
    piece, thin = width // 8, block // 8
    tall = encl_ref.shape[1] // 8
    top = 2 * piece + thin
    step = top + piece + thin

    def to(j):
        return sent_ref if j % 2 else kept_ref

    for j in (1, 3, 0, 2):
        w = to(j)
        i = j // 2
        cut = slice(j * width, (j + 1) * width)
        up = tn(x2, gp_ref[:, cut]).astype(bf16)
        down = tn(hid_ref[:, cut], cot).astype(bf16)
        out = tn(mix_ref[:, j * block : (j + 1) * block], gm).astype(bf16)
        for c in range(8):
            w[i, c * step : c * step + piece] = up[c * piece : (c + 1) * piece]
            w[i, c * step + piece : c * step + 2 * piece] = down[c * piece : (c + 1) * piece]
            w[i, c * step + 2 * piece : c * step + top] = out[c * thin : (c + 1) * thin]
    x1 = x1_ref[...]
    for k in range(3):
        full = tn(x1, g3_ref[:, k * width : (k + 1) * width]).astype(bf16)
        for j in range(4):
            for c in range(8):
                to(j)[j // 2, c * step + top : c * step + top + piece, k * block : (k + 1) * block] = (
                    full[c * piece : (c + 1) * piece, j * block : (j + 1) * block]
                )
    full = tn(encl_ref[...], gz_ref[...]).astype(bf16)
    for j in range(4):
        cut = slice(j * block, (j + 1) * block)
        for c in range(8):
            base = c * tall
            to(j)[j // 2, c * step + top : c * step + top + piece, 3 * block :] = full[base : base + piece, cut]
            base = base + piece
            for k in range(4):
                to(j)[j // 2, c * step + top + piece : (c + 1) * step, k * block : (k + 1) * block] = (
                    full[base + k * thin : base + (k + 1) * thin, cut]
                )


def pack_body(pick_ref, up_ref, down_ref, out_ref, qkv_ref, emb_ref, chunk_ref):
    piece, thin, block = up_ref.shape[0], out_ref.shape[0], emb_ref.shape[1]
    chunk_ref[:piece] = up_ref[...]
    chunk_ref[piece : 2 * piece] = down_ref[...]
    top = 2 * piece + thin
    chunk_ref[2 * piece : top] = out_ref[...]
    for c in range(3):
        chunk_ref[top : top + piece, c * block : (c + 1) * block] = qkv_ref[c]
    chunk_ref[top : top + piece, 3 * block :] = emb_ref[:piece]
    for c in range(4):
        base = piece + c * thin
        chunk_ref[top + piece :, c * block : (c + 1) * block] = emb_ref[base : base + thin]


def join_body(a_ref, b_ref, out_ref):
    rows = a_ref.shape[0]
    out_ref[:rows] = a_ref[...]
    out_ref[rows:] = b_ref[...]


def add_body(a_ref, b_ref, out_ref):
    out_ref[...] = (a_ref[...].astype(f32) + b_ref[...].astype(f32)).astype(out_ref.dtype)


def last_sums_body(slot_ref, *refs):
    terms, outs, total_ref = refs[:-12], refs[-12:-1], refs[-1]
    total = terms[0][...]
    for ref in terms[1:]:
        total = total + ref[...]
    total_ref[...] = total
    slot = slot_ref[0]
    e_qv, e_upb, e_ob, e_gain, e_nb, d_emb, d_qv, d_upb, d_ob, d_gain, d_nb = outs
    share, thin, width = e_qv.shape[1], d_qv.shape[1], d_emb.shape[1]
    e_qv[...] = total_ref[18:20, pl.ds(pl.multiple_of(slot * share, share), share)]
    e_upb[...] = total_ref[pl.ds(4 + slot, 1), :]
    e_ob[0:1] = total_ref[0:1]
    e_ob[1:2] = total_ref[8:9]
    e_gain[0:1] = total_ref[16:17]
    e_gain[1:2] = total_ref[1:2]
    e_nb[0:1] = total_ref[17:18]
    e_nb[1:2] = total_ref[2:3]
    d_ob[...] = total_ref[9:11, :width]
    d_gain[...] = total_ref[9:11, width:]
    d_nb[...] = total_ref[11:13, :width]
    d_emb[...] = total_ref[11:12, width:]
    d_qv[...] = total_ref[12:14, pl.ds(pl.multiple_of(width + slot * thin, thin), thin)]
    d_upb[...] = total_ref[pl.ds(14 + (slot >> 1), 1), pl.ds(pl.multiple_of((slot & 1) * width, width), width)]


def far_body(bit_ref, kept_ref, near_ref, out_ref):
    half = out_ref.shape[0]
    rows = pl.ds(pl.multiple_of(bit_ref[0] * half, half), half)
    out_ref[...] = (kept_ref[1, rows].astype(f32) + near_ref[1, rows].astype(f32)).astype(bf16)


def there_body(bit_ref, kept_ref, near_ref, *refs):
    *terms, out_ref = refs
    half = out_ref.shape[0]
    rows = pl.ds(pl.multiple_of(bit_ref[0] * half, half), half)
    total = kept_ref[0, rows].astype(f32) + near_ref[0, rows].astype(f32)
    for ref in terms:
        total = total + ref[...].astype(f32)
    out_ref[...] = total.astype(bf16)


def choose_body(bit_ref, keep_ref, got_ref, out_ref):
    @pl.when(bit_ref[0] == 0)
    def _():
        out_ref[...] = keep_ref[...]

    @pl.when(bit_ref[0] != 0)
    def _():
        out_ref[...] = got_ref[...]


def piece_of(refs, j):
    for ref in refs:
        if len(ref.shape) == 2:
            if j == 0:
                return ref[...]
            j -= 1
        elif j < ref.shape[0]:
            return ref[j]
        else:
            j -= ref.shape[0]


def tile_sum(xs, gs, more):
    acc = 0.0
    for j in range(4):
        acc = acc + tn(piece_of(xs, j), piece_of(gs, j))
    if not more:
        return [(slice(None), slice(None), acc)]
    rows, cols = acc.shape
    parts = [(slice(None), slice(0, cols), acc)]
    half, quarter = rows // 2, rows // 8
    wide = more[0].shape[1] // 4
    for c in range(2):
        for k in range(4):
            parts.append((
                slice(c * half + k * quarter, c * half + (k + 1) * quarter),
                slice(cols, cols + wide),
                more[0][c * quarter : (c + 1) * quarter, k * wide : (k + 1) * wide].astype(f32),
            ))
    return parts


def half_body(nx, ng, nm, pick_ref, *refs):
    xs, gs, more = refs[:nx], refs[nx : nx + ng], refs[nx + ng : nx + ng + nm]
    *add_ref, out_ref = refs[nx + ng + nm :]
    for rows, cols, value in tile_sum(xs, gs, more):
        if add_ref:
            value = value + add_ref[0][rows, cols].astype(f32)
        out_ref[rows, cols] = value.astype(bf16)


def weight_half(chain, xs, gs, more, pick, add=None):
    tile = xs[0].shape[-1] // 4
    out_cols = gs[0].shape[-1] + sum(m.shape[1] // 4 for m in more)

    def column(shape):
        lead = shape[:-1]
        return pl.BlockSpec(lead + (tile,), lambda i, p: (0,) * len(lead) + (p[i],))

    def whole(shape):
        return pl.BlockSpec(shape, lambda i, p: (0,) * len(shape))

    in_specs = [column(x.shape) for x in xs] + [whole(g.shape) for g in gs]
    in_specs += [pl.BlockSpec((tile // 4, m.shape[1]), lambda i, p: (p[i], 0)) for m in more]
    args = list(xs) + list(gs) + list(more)
    out_spec = pl.BlockSpec((tile, out_cols), lambda i, p: (i, 0))
    if add is not None:
        in_specs.append(out_spec)
        args.append(add)
    return chain(
        functools.partial(half_body, len(xs), len(gs), len(more)),
        [shaped((2 * tile, out_cols), bf16)],
        args,
        prefetch=pick,
        grid=(2,),
        specs=(in_specs, [out_spec]),
        limit=20,
    )[0]


def spread_body(writes, place_ref, *refs):
    sums = max(write[0] for write in writes) + 1
    out_refs = refs[2 * sums :]
    for i in range(8):
        for source, which, lead, first, every, row, rows, col, cols, at_col in writes:
            ref = refs[2 * source + i // 4]
            base = i % 4 * (ref.shape[0] // 4)
            at = place_ref[source] ^ i
            value = ref[base + row : base + row + rows, col : col + cols].astype(f32)
            to = pl.ds(pl.multiple_of(at * every + first, rows), rows)
            if lead is None:
                out_refs[which][to, at_col : at_col + cols] = value
            else:
                out_refs[which][lead, to] = value


def out_weight_body(*refs):
    mixes, gs, out_ref = refs[:3], refs[3:7], refs[7]
    acc = 0.0
    for j in range(4):
        acc = acc + tn(piece_of(mixes, j), piece_of(gs, j))
    out_ref[...] = acc.astype(bf16)


class Sum:
    def __init__(self, chain):
        self.chain = chain
        self.size = lax.axis_size("dp")
        me = lax.axis_index("dp").astype(jnp.int32)
        self.x, z = me & 1, me >> 1
        self.outer = jnp.where((z == 0) | (z == 3), 1, 0).astype(jnp.int32).reshape(1)
        self.place = 4 * self.x if self.size == 8 else jnp.int32(0)
        inward = [(0, 1), (3, 2)]
        self.inward = [(2 * a + x, 2 * b + x) for a, b in inward for x in range(2)]
        self.outward = [(b, a) for a, b in self.inward]
        self.middle = [(2 * a + x, 2 * b + x) for a, b in ((1, 2), (2, 1)) for x in range(2)]
        steps = [self.second, self.third, self.fourth, self.fifth]
        self.steps = iter(steps if self.size == 8 else [])

    def step(self):
        for todo in self.steps:
            todo()
            return

    def product(self, xs, gs, more=()):
        self.terms = (xs, gs, more)
        if self.size != 8:
            first = weight_half(self.chain, *self.terms, jnp.array([0, 1], jnp.int32))
            other = weight_half(self.chain, *self.terms, jnp.array([2, 3], jnp.int32))
            return self.general(jnp.concatenate([first, other], axis=0))
        there = 2 * (1 - self.x)
        self.got = swap(weight_half(self.chain, *self.terms, jnp.stack([there, there + 1])), "dp", 1)

    def shares(self, kept, near, there):
        self.terms = None
        self.held = (kept, near, there)
        if self.size == 8:
            half = shaped(there.shape, bf16)
            out = self.chain(there_body, [half], ((1 - self.x).reshape(1), kept, near, there), smem=1)[0]
            self.got = swap(out, "dp", 1)

    def other(self, mine):
        kept, near, there = self.held
        self.held = (kept, near, mine)
        if self.size != 8:
            total = kept[0].astype(f32) + near[0].astype(f32)
            total = total + jnp.concatenate([mine, there], axis=0).astype(f32)
            self.general(total.astype(bf16))

    def second(self):
        if self.terms is None:
            half = shaped(self.got.shape, bf16)
            self.keep = self.chain(there_body, [half], (self.x.reshape(1), *self.held, self.got), smem=1)[0]
        else:
            mine = 2 * self.x
            self.keep = weight_half(self.chain, *self.terms, jnp.stack([mine, mine + 1]), self.got)
        self.got = send(self.keep, "dp", self.inward)

    def plus(self):
        self.keep = self.chain(add_body, [shaped(self.keep.shape, bf16)], (self.keep, self.got))[0]

    def third(self):
        self.plus()
        self.got = send(self.keep, "dp", self.middle)

    def fourth(self):
        self.plus()
        self.got = send(self.keep, "dp", self.outward)

    def fifth(self):
        self.keep = self.chain(
            choose_body, [shaped(self.keep.shape, bf16)], (self.outer, self.keep, self.got), smem=1
        )[0]
        self.got = swap(self.keep, "dp", 1)

    def general(self, held):
        me = lax.axis_index("dp")
        bits = [1 << i for i in range(self.size.bit_length() - 1)]
        for bit in bits:
            mine = (me & bit) != 0
            half = held.shape[0] // 2
            other = lax.dynamic_slice_in_dim(held, jnp.where(mine, 0, half), half, 0)
            own = lax.dynamic_slice_in_dim(held, jnp.where(mine, half, 0), half, 0)
            held = (own.astype(f32) + swap(other, "dp", bit).astype(f32)).astype(bf16)
        for bit in reversed(bits):
            mine = (me & bit) != 0
            other = swap(held, "dp", bit)
            held = jnp.where(
                mine,
                jnp.concatenate([other, held], axis=0),
                jnp.concatenate([held, other], axis=0),
            )
        half = held.shape[0] // 2
        self.keep, self.got = held[:half], held[half:]


def per_device(
    tokens, segment_ids, gsd_index, enc_qkv, enc_qv_bias, enc_out_proj, enc_up, enc_up_bias,
    enc_down, enc_out_bias, enc_gain, enc_norm_bias, embed_weight, embed_bias, dec_qkv,
    dec_qv_bias, dec_out_proj, dec_up, dec_up_bias, dec_down, dec_out_bias, dec_gain,
    dec_norm_bias, cotangent,
):
    n, width = tokens.shape
    rows, length = segment_ids.shape
    assert rows == 4 and n == length == 256 and lax.axis_size("mp") == 4
    share, ff = enc_qkv.shape[2], enc_up.shape[1]
    dwidth, dff = cotangent.shape[1], dec_up.shape[1] * 4
    dshare = dwidth // 4
    heads = share // (width // HEADS)
    scale = (width // HEADS) ** -0.5
    slot = lax.axis_index("mp").astype(jnp.int32)
    at = slot.reshape(1)
    chain = Chain()
    dec = Sum(chain)
    group = lax.axis_index("dp").astype(jnp.int32)
    home = 4 * (group & 1) + (group & 2) + ((group >> 2) & 1) if dec.size == 8 else jnp.int32(0)

    def low(*dims):
        return shaped(dims, bf16)

    def full(*dims):
        return shaped(dims, f32)

    def waves(size):
        half = size // 2
        return jnp.power(10000.0, -jnp.arange(half, dtype=f32) / half).reshape(1, half)

    def near(value):
        return swap(value, "mp", 1)

    def far(value):
        return swap(value, "mp", 2)

    pack_rows = 3 * dwidth + 2 * dshare
    decoder_weights = [in_hbm(w) for w in (dec_up, dec_down, dec_out_proj, dec_qkv, embed_weight)]

    def pack(pick, steps):
        def block(shape):
            if len(shape) == 3:
                return pl.BlockSpec((shape[0], shape[1] // 8, shape[2]), lambda i, p: (0, p[i], 0))
            return pl.BlockSpec((shape[0] // 8, shape[1]), lambda i, p: (p[i], 0))

        rows = pack_rows // 8
        return chain(
            pack_body,
            [low(steps * rows, dwidth)],
            decoder_weights,
            prefetch=pick,
            grid=(steps,),
            specs=([block(w.shape) for w in decoder_weights], [pl.BlockSpec((rows, dwidth), lambda i, p: (i, 0))]),
        )[0]

    split = dec.size == 8
    got = far(pack(home.reshape(1), 1)) if split else None
    normed = chain(
        start_body,
        [low(n, width)],
        (at, in_hbm(segment_ids), in_hbm(gsd_index), in_hbm(tokens), in_hbm(enc_gain), in_hbm(enc_norm_bias), waves(width)),
        smem=1,
        scratch=[pltpu.VMEM((n, width), f32)],
    )[0]
    x = [normed, near(normed), far(normed)]
    bias_a, bias_b = chain(mask_body, [kept(full(2, n, n)), kept(full(2, n, n))], (at, in_hbm(segment_ids)), smem=1)

    def attention(bias, first, *blocks):
        count = len(blocks)
        return chain(
            functools.partial(attn_body, scale, heads, first),
            [kept(low(count, n, share))] * 3
            + [kept(low(count, heads, n, n)), kept(low(count, n, share))]
            + [low(n, width)] * count,
            (*blocks, bias, enc_qkv, enc_qv_bias, enc_out_proj),
        )

    def add(a, b):
        return chain(add_body, [shaped(a.shape, a.dtype)], (a, b))[0]

    def join(a, b):
        return chain(join_body, [low(a.shape[0] + b.shape[0], a.shape[1])], (a, b))[0]

    def both(blocks):
        blocks[2] = chain.pin(blocks[2])
        blocks.append(near(blocks[2]))

    *saved_a, mixa, part0, part1 = attention(bias_a, 0, x[0], x[1])
    part1 = near(part1)
    vector = jnp.concatenate([dec_qv_bias.reshape(-1), dec_up_bias]).reshape(1, -1)
    vector = chain.pin(vector)
    vectors = [vector, near(vector), far(vector)]
    part1 = chain.pin(part1)
    both(x)
    chain.gap()
    chain.gap()
    *saved_d, mixd, part3 = attention(bias_b, 1, x[3])
    part3 = near(part3)
    *saved_c, mixc, part2 = attention(bias_b, 0, x[2])
    if split:
        got = chain.pin(got)
        more = swap(got, "dp", 4)
    part2 = far(add(part2, part3))
    vectors[1] = chain.pin(vectors[1])
    both(vectors)
    packed = pack(jnp.arange(8, dtype=jnp.int32), 8)
    packed_near = near(packed)
    pos, stream = chain(
        stream_body,
        [kept(full(n, dwidth)), full(n, width)],
        (at, in_hbm(segment_ids), in_hbm(gsd_index), in_hbm(tokens), in_hbm(embed_bias.reshape(1, -1)), waves(width), waves(dwidth)),
        smem=1,
    )
    if split:
        got = join(got, more)
        more = swap(got, "dp", 2)
    else:
        got = far(packed)
    middle, normed2 = chain(
        mid_body,
        [kept(full(n, width)), low(n, width)],
        (stream, part0, part1, part2, enc_out_bias, enc_gain, enc_norm_bias),
    )
    y = [normed2, near(normed2), far(normed2)]
    packed_near = chain.pin(packed_near)
    vectors[3] = chain.pin(vectors[3])

    def feed(*blocks):
        count = len(blocks)
        return chain(
            mlp_body,
            [kept(low(count, n, ff))] * 2 + [low(n, width)] * count,
            (*blocks, enc_up, enc_up_bias.reshape(1, -1), enc_down),
        )

    hida, dga, part0, part1 = feed(y[0], y[1])
    part1 = near(part1)
    if split:
        got = join(got, more)
        more = swap(got, "dp", 1)
    else:
        more = got[pack_rows // 2 :]
        got = got[: pack_rows // 2]
    far_weights = [got, more]
    near_weights = [near(got)]
    both(y)
    part1 = chain.pin(part1)
    near_weights[0] = chain.pin(near_weights[0])
    hidd, dgd, part3 = feed(y[3])
    part3 = near(part3)
    hidc, dgc, part2 = feed(y[2])
    part2 = far(add(part2, part3))
    far_weights[1] = chain.pin(more)
    near_weights.append(near(far_weights[1]))
    part2 = chain.pin(part2)

    (enc_low, output, x1, x2, hid, mix, gp, gm, g3, gz, ge_low, ge, dec_sums) = chain(
        decoder_body,
        [kept(o) for o in (low(n, width), full(n, dwidth), low(n, dwidth), low(n, dwidth), low(n, dff),
                           low(n, dwidth), low(n, dff), low(n, dwidth), low(n, 3 * dwidth), low(n, dwidth))]
        + [low(n, width), kept(full(n, width)), kept(full(8, width))],
        (jnp.stack([slot, home]), middle, part0, part1, part2, enc_out_bias, packed, packed_near,
         *far_weights, *near_weights, *vectors, pos, bias_a, dec_out_bias, dec_gain,
         dec_norm_bias, cotangent),
        smem=1,
        scratch=[
            pltpu.VMEM((4, dwidth, dwidth), bf16), pltpu.VMEM((4, dwidth, dwidth), bf16),
            pltpu.VMEM((3, dwidth, dwidth), bf16), pltpu.VMEM((dwidth, dwidth), bf16),
            pltpu.VMEM((width, dwidth), bf16), pltpu.VMEM((DHEADS, n, n), bf16),
            pltpu.VMEM((n, dff), bf16), pltpu.VMEM((3, n, dwidth), bf16), pltpu.VMEM((n, dwidth), f32),
            pltpu.VMEM((2, dwidth), f32), pltpu.VMEM((1, dff), f32),
        ],
        limit=40,
    )
    g = [ge_low, near(ge_low), far(ge_low)]

    def feed_back(slope, *blocks):
        count = len(blocks)
        return chain(
            mlp_back_body,
            [kept(low(count, n, ff)), kept(full(1, ff))] + [low(n, width)] * count,
            (*blocks, slope, enc_up, enc_down),
        )

    def attention_back(saved, *blocks):
        count = len(blocks)
        return chain(
            functools.partial(attn_back_body, scale, heads),
            [kept(low(count, n, 3 * share)), kept(full(2, share))] + [low(n, width)] * count,
            (*blocks, *saved, enc_qkv, enc_out_proj),
        )

    def far_share(bit):
        return far(chain(far_body, [low(pack_rows // 2, dwidth)], (bit.reshape(1), kept_share, sent), smem=1)[0])

    def hbm(*values):
        return [in_hbm(v) for v in values]

    down, up, attn = Sum(chain), Sum(chain), Sum(chain)

    def finish(sums, outs, writes):
        return chain(
            functools.partial(spread_body, writes),
            [kept(full(*dims)) for dims in outs],
            (jnp.stack([f.place for f in sums]), *[v for f in sums for v in (f.keep, f.got)]),
            smem=1,
            limit=24,
        )

    chain.gap()
    gpa, upa, part0, part1 = feed_back(dga, g[0], g[1])
    part1 = near(part1)
    sent, kept_share = chain(
        decoder_weights_body,
        [low(2, pack_rows, dwidth), kept(low(2, pack_rows, dwidth))],
        (x1, x2, hid, mix, gp, gm, g3, gz, enc_low, cotangent),
        limit=24,
    )
    sent = near(sent)
    part1 = chain.pin(part1)
    both(g)
    gpc, upc, part2 = feed_back(dgc, g[2])
    down.product(hbm(hida, hidc, hidd), g)
    gpd, upd, part3 = feed_back(dgd, g[3])
    part3 = near(part3)
    chain.gap()
    part2 = far(add(part2, part3))
    chain.gap()
    grad_middle, gm_low, sums_mid = chain(
        mlp_end_body,
        [kept(full(n, width)), low(n, width), kept(full(16, width))],
        (at, ge, part0, part1, part2, middle, enc_gain, upa, upc, upd, dec_sums),
        smem=1,
    )
    m = [gm_low, near(gm_low), far(gm_low)]
    hops = [("mp", 1), ("mp", 2)] + [("dp", 1 << i) for i in range(dec.size.bit_length() - 1)]
    hops = iter(hops)

    def hop(total, got=None):
        if got is not None:
            total = add(total, got)
        for axis, mask in hops:
            return total, swap(total, axis, mask)
        return total, None

    up.product(hbm(*y), hbm(gpa, gpc, gpd))
    down.step()
    g3a, sa, part0, part1 = attention_back(saved_a, m[0], m[1])
    part1 = near(part1)
    there = far_share(1 - dec.x)
    both(m)
    g3c, sc, part2 = attention_back(saved_c, m[2])
    g3d, sd, part3 = attention_back(saved_d, m[3])
    part3 = near(part3)
    part1 = chain.pin(part1)
    part2 = far(add(part2, part3))
    out_full = chain(out_weight_body, [low(share, width)], (mixa, mixc, mixd, *m))[0]
    attn.product(hbm(*x), hbm(g3a, g3c, g3d), [out_full])
    down.step()
    up.step()
    dec.shares(kept_share, sent, there)
    dec.other(far_share(dec.x))
    chain.gap()
    down.step()
    grad_tokens, sums = chain(
        last_body,
        [kept(full(n, width)), full(24, width)],
        (at, grad_middle, part0, part1, part2, stream, enc_gain, sa, sc, sd, sums_mid),
        smem=1,
    )
    up.step()
    attn.step()
    small = hop(sums)
    dec.step()
    down.step()
    small = hop(*small)
    up.step()
    attn.step()
    small = hop(*small)
    e_down = finish((down,), [(ff, width)], [(0, 0, None, 0, ff // 8, 0, ff // 8, 0, width, 0)])[0]
    dec.step()
    up.step()
    chain.gap()
    attn.step()
    small = hop(*small)
    dec.step()
    e_up = finish((up,), [(width, ff)], [(0, 0, None, 0, width // 8, 0, width // 8, 0, ff, 0)])[0]
    attn.step()
    dec.step()
    rows, fold = width // 8, share // 8
    e_qkv, e_out = finish(
        (attn,),
        [(3, width, share), (share, width)],
        [(0, 0, c, 0, rows, 0, rows, c * share, share, 0) for c in range(3)]
        + [(0, 1, None, 0, fold, k * fold, fold, 3 * share, width // 4, k * (width // 4)) for k in range(4)],
    )
    small = hop(*small)
    part, thin, tall = dwidth // 8, dshare // 8, width // 8
    top = 2 * part + thin
    d_up, d_down, d_out, d_qkv, e_embed = finish(
        (dec,),
        [(dwidth, dwidth), (dwidth, dwidth), (dshare, dwidth), (3, dwidth, dshare), (width, dshare)],
        [
            (0, 0, None, 0, part, 0, part, 0, dwidth, 0),
            (0, 1, None, 0, part, part, part, 0, dwidth, 0),
            (0, 2, None, 0, thin, 2 * part, thin, 0, dwidth, 0),
        ]
        + [(0, 3, c, 0, part, top, part, c * dshare, dshare, 0) for c in range(3)]
        + [(0, 4, None, 0, tall, top, part, 3 * dshare, dshare, 0)]
        + [(0, 4, None, part + k * thin, tall, top + part, thin, k * dshare, dshare, 0) for k in range(4)],
    )
    sums = small
    vectors = chain(
        last_sums_body,
        [full(2, share), full(1, ff), full(2, width), full(2, width), full(2, width), full(1, dwidth),
         full(2, dshare), full(1, dff // 4), full(2, dwidth), full(2, dwidth), full(2, dwidth)],
        (at, *sums),
        smem=1,
        scratch=[pltpu.VMEM((24, width), f32)],
    )
    e_qv, e_upb, e_ob, e_gain, e_nb, d_emb, d_qv, d_upb, d_ob, d_gain, d_nb = vectors

    return (
        output,
        grad_tokens,
        e_qkv,
        e_qv,
        e_out,
        e_up,
        e_upb.reshape(-1),
        e_down,
        e_ob,
        e_gain,
        e_nb,
        e_embed,
        d_emb.reshape(-1),
        d_qkv,
        d_qv,
        d_out,
        d_up,
        d_upb.reshape(-1),
        d_down,
        d_ob,
        d_gain,
        d_nb,
    )


def solution(mesh):
    return jax.shard_map(
        per_device,
        mesh=mesh,
        in_specs=(
            P(("dp", "mp"), None),
            P("dp", None),
            P("dp", None),
            P(None, None, "mp"),
            P(None, "mp"),
            P("mp", None),
            P(None, "mp"),
            P("mp"),
            P("mp", None),
            P(),
            P(),
            P(),
            P(None, "mp"),
            P(),
            P(None, None, "mp"),
            P(None, "mp"),
            P("mp", None),
            P(None, "mp"),
            P("mp"),
            P("mp", None),
            P(),
            P(),
            P(),
            P(("dp", "mp"), None),
        ),
        out_specs=(
            P(("dp", "mp"), None),
            P(("dp", "mp"), None),
            P(None, None, "mp"),
            P(None, "mp"),
            P("mp", None),
            P(None, "mp"),
            P("mp"),
            P("mp", None),
            P(),
            P(),
            P(),
            P(None, "mp"),
            P(),
            P(None, None, "mp"),
            P(None, "mp"),
            P("mp", None),
            P(None, "mp"),
            P("mp"),
            P("mp", None),
            P(),
            P(),
            P(),
        ),
        check_vma=False,
    )
```
